32 devices in a mesh: dp: 16 (over z, x, core), blk: 2 (over y).
Axes of the slice: x: 2, y: 2, z: 4, core: 2. Of those that a mesh axis runs over, the one named last changes fastest.
Arguments:
- tokens: bfloat16 [32, 2048, 768], P('dp', 'blk'), may hold values from -6 to 6
- lengths: int32 [32], P('dp'), may hold values from 8 to 2048, as said below
- w_qkv: bfloat16 [768, 2304], P(('dp', 'blk')), may hold values from -0.21875 to 0.21875
- w_out: bfloat16 [768, 768], P(('dp', 'blk')), may hold values from -1.5 to 1.5
- w_gate: bfloat16 [768, 3072], P(('dp', 'blk')), may hold values from -0.21875 to 0.21875
- w_up: bfloat16 [768, 3072], P(('dp', 'blk')), may hold values from -0.21875 to 0.21875
- w_down: bfloat16 [3072, 768], P(('dp', 'blk')), may hold values from -0.109375 to 0.109375
- gain_one: bfloat16 [768], P(('dp', 'blk')), may hold values from 0.25 to 1.75
- gain_two: bfloat16 [768], P(('dp', 'blk')), may hold values from 0.25 to 1.75
- cotangent: bfloat16 [32, 2048, 768], P('dp', 'blk'), may hold values from -6 to 6
Outputs:
- output: bfloat16 [32, 2048, 768], P('dp', 'blk')
- grad_tokens: bfloat16 [32, 2048, 768], P('dp', 'blk')
- grad_w_qkv: float32 [768, 2304], P(('dp', 'blk'))
- grad_w_out: float32 [768, 768], P(('dp', 'blk'))
- grad_w_gate: float32 [768, 3072], P('dp', 'blk')
- grad_w_up: float32 [768, 3072], P('dp', 'blk')
- grad_w_down: float32 [3072, 768], P('blk', 'dp')
- grad_gain_one: float32 [768], P(('dp', 'blk'))
- grad_gain_two: float32 [768], P(('dp', 'blk'))
The draws below stay inside these ranges and needn't reach their ends.
Inputs may be any that keep to these rules, and one draw needn't show every extreme that they name: `lengths`: among the 2 rows of each index of dp, one has length 2048; a row's positions from its length on are padding.
All inputs are finite; a program needn't handle non-finite values.
Results may differ from the reference program's by a relative error of at most 0.02.
Values may be sent and summed in bfloat16 or wider, within the bound.
A program may use at most 512 MiB of HBM per device.

```python
import jax
import jax.numpy as jnp
from jax import lax

D = 768
HEADS = 12
HEAD = 64
FF = 3072
SEQ = 2048
ROWS_DEV = 2
ROWS = 32


def draw_lengths(key, part):
    key = jax.random.fold_in(key, 7)
    key_short, key_long, key_kind, key_pick = jax.random.split(key, 4)
    short_len = jax.random.randint(key_short, (ROWS,), 8, max(9, min(65, SEQ // 2 + 1)))
    long_len = jax.random.randint(key_long, (ROWS,), 8, SEQ + 1)
    kinds = jax.random.randint(key_kind, (ROWS,), 0, 5)
    base_len = jnp.where(kinds < 2, short_len, long_len)
    picked = jax.random.randint(key_pick, (ROWS // ROWS_DEV,), 0, ROWS_DEV)
    full_row = jnp.arange(ROWS, dtype=jnp.int32) % ROWS_DEV == jnp.repeat(picked, ROWS_DEV)
    return jnp.where(full_row, SEQ, base_len).astype(jnp.int32)


def levels(key, extent, pieces, least, high):
    loudness = 1.0
    for dim, blocks in pieces:
        heights = jax.random.uniform(jax.random.fold_in(jax.random.fold_in(key, 6), dim), (blocks,), jnp.float32, least / len(pieces), high / len(pieces))
        loudness = loudness * jnp.repeat(jnp.exp(heights), extent[dim] // blocks).reshape((-1,) + (1,) * (len(extent) - 1 - dim))
    return loudness


def normal_values(own_key, dims, scale, bound, shards=(), held_as=jnp.bfloat16):
    array = scale * jax.random.normal(own_key, dims, jnp.float32)
    if shards:
        array = array * levels(own_key, dims, shards, -0.22, 0.18)
    return jnp.clip(array, -bound, bound).astype(held_as)


def setup_inputs(seed: int = 0) -> dict:
    key_list = jax.random.split(jax.random.key(seed), 11)
    tokens = normal_values(key_list[0], (ROWS, SEQ, D), 1.0, 6.0, ((0, 16), (1, 2)))
    lengths = draw_lengths(jax.random.fold_in(key_list[10], 71), 0)
    w_qkv = normal_values(key_list[2], (D, 3 * D), D ** -0.5, 0.21875, ((0, 32),))
    w_out = normal_values(key_list[3], (D, D), (D // 48) ** -0.5, 1.5, ((0, 32),))
    w_gate = normal_values(key_list[4], (D, FF), D ** -0.5, 0.21875, ((0, 32),))
    w_up = normal_values(key_list[5], (D, FF), D ** -0.5, 0.21875, ((0, 32),))
    w_down = normal_values(key_list[6], (FF, D), FF ** -0.5, 0.109375, ((0, 32),))
    gain_one = jnp.clip(1.0 + 0.15 * jax.random.normal(key_list[7], (D,), jnp.float32), 0.25, 1.75).astype(jnp.bfloat16)
    gain_two = jnp.clip(1.0 + 0.15 * jax.random.normal(key_list[8], (D,), jnp.float32), 0.25, 1.75).astype(jnp.bfloat16)
    cotangent = normal_values(key_list[9], (ROWS, SEQ, D), 1.0, 6.0, ((0, 16), (1, 2)))
    return {"tokens": tokens, "lengths": lengths, "w_qkv": w_qkv, "w_out": w_out, "w_gate": w_gate, "w_up": w_up, "w_down": w_down, "gain_one": gain_one, "gain_two": gain_two, "cotangent": cotangent}


@jax.custom_vjp
def low(v):
    return lax.optimization_barrier(v.astype(jnp.bfloat16)).astype(jnp.float32)

@jax.custom_vjp
def low_back(v):
    return v

def low_keep(v):
    return (low(v), None)

def low_pass(kept, grad):
    return (grad,)

def back_keep(v):
    return (v, None)

def back_low(kept, grad):
    return (low(grad),)
low.defvjp(low_keep, low_pass)
low_back.defvjp(back_keep, back_low)
epsilon = 1e-05
negative = -1e+30

def matmul(left, right):
    return jnp.dot(left, right, precision=lax.Precision.HIGHEST)

def tables(positions, head_size):
    half_size = head_size // 2
    index = jnp.arange(half_size, dtype=jnp.float32)
    inverse = jnp.power(1000.0, -2.0 * index / head_size)
    angles = positions.astype(jnp.float32)[:, None] * inverse[None, :]
    cosine = jnp.cos(angles)
    sine_part = jnp.sin(angles)
    return (jnp.concatenate([cosine, cosine], -1), jnp.concatenate([sine_part, sine_part], -1))

def rope(vector, cosine, sine_part):
    half_size = vector.shape[-1] // 2
    turned = jnp.concatenate([-vector[..., half_size:], vector[..., :half_size]], -1)
    return vector * cosine[:, None, :] + turned * sine_part[:, None, :]

def layer_norm(values, gain):
    mean_part = lax.optimization_barrier(jnp.mean(values, axis=-1, keepdims=True))
    centered = values - mean_part
    variance = lax.optimization_barrier(jnp.mean(centered * centered, axis=-1, keepdims=True))
    return centered * lax.rsqrt(variance + epsilon) * gain

def block_layer(seq_row, length, w_qkv, w_out, w_gate, w_up, w_down, gain_one, gain_two):
    seq_len = seq_row.shape[0]
    projected = low_back(matmul(seq_row, w_qkv)).reshape(seq_len, 3, HEADS, HEAD)
    positions = jnp.arange(seq_len, dtype=jnp.int32)
    cosine, sine_part = tables(positions, HEAD)
    queries = low(rope(projected[:, 0], cosine, sine_part))
    key_side = low(rope(projected[:, 1], cosine, sine_part))
    value_side = low(projected[:, 2])
    key_valid = positions < length
    block_size = min(512, seq_len)

    def attend(query_block):
        raw_scores = low_back(jnp.einsum('qhd,khd->hqk', query_block, key_side, precision=lax.Precision.HIGHEST))
        scores = jnp.where(key_valid[None, None, :], raw_scores * 0.125, negative)
        row_max = lax.optimization_barrier(jnp.max(scores, axis=-1, keepdims=True))
        weights = jnp.exp(scores - row_max)
        probs = weights / lax.optimization_barrier(jnp.sum(weights, axis=-1, keepdims=True))
        return jnp.einsum('hqk,khd->qhd', low(probs), value_side, precision=lax.Precision.HIGHEST)
    attended = lax.map(jax.checkpoint(attend), queries.reshape(seq_len // block_size, block_size, HEADS, HEAD))
    attended = low_back(low(attended.reshape(seq_len, HEADS * HEAD)))
    first = seq_row + low_back(matmul(attended, w_out))
    hidden = layer_norm(first, gain_one)
    hidden_low = low(hidden)
    gate = low_back(matmul(hidden_low, w_gate))
    up_part = low_back(matmul(hidden_low, w_up))
    active = low(jax.nn.silu(gate) * up_part)
    second = hidden + low_back(matmul(active, w_down))
    return layer_norm(second, gain_two)

def reference(tokens, lengths, w_qkv, w_out, w_gate, w_up, w_down, gain_one, gain_two, cotangent):
    params = (w_qkv.astype(jnp.float32), w_out.astype(jnp.float32), w_gate.astype(jnp.float32), w_up.astype(jnp.float32), w_down.astype(jnp.float32), gain_one.astype(jnp.float32), gain_two.astype(jnp.float32))

    def one_row(summed, inputs):
        seq_row, length, seed_grad = inputs

        def forward(row_input, *weights):
            return block_layer(row_input, length, *weights)
        result, pullback = jax.vjp(forward, seq_row, *params)
        grads = pullback(seed_grad)
        summed = tuple((left + right for left, right in zip(summed, grads[1:])))
        return (summed, (result.astype(jnp.bfloat16), grads[0].astype(jnp.bfloat16)))
    zero_grads = tuple((jnp.zeros(weight.shape, jnp.float32) for weight in params))
    summed, (output, grad_tokens) = lax.scan(one_row, zero_grads, (tokens.astype(jnp.float32), lengths, cotangent.astype(jnp.float32)))
    return (output, grad_tokens, summed[0], summed[1], summed[2], summed[3], summed[4], summed[5], summed[6])
```

```python
import functools

import jax
import jax.numpy as jnp
import numpy as np
from jax import lax
from jax.experimental import pallas as pl
from jax.experimental.pallas import tpu as pltpu
from jax.sharding import PartitionSpec as P

HEADS = 12
HEAD = 64
PAIR = 2 * HEAD
EPS = 1e-05
NEG = -1e30
LOG2E = 1.4426950408889634
LN2 = 0.6931471805599453
VMEM_LIMIT = 60 * 1024 * 1024

BF = jnp.bfloat16
F32 = jnp.float32


def dot(a, b):
    return lax.dot_general(a, b, (((1,), (0,)), ((), ())), preferred_element_type=F32)


def dot_nt(a, b):
    return lax.dot_general(a, b, (((1,), (1,)), ((), ())), preferred_element_type=F32)


def params(limit=VMEM_LIMIT):
    return pltpu.CompilerParams(vmem_limit_bytes=limit)


def lanes(shape):
    return lax.broadcasted_iota(jnp.int32, shape, 1)


def turn(u):
    low_half = (lanes(u.shape) % HEAD) < HEAD // 2
    return jnp.where(low_half, -pltpu.roll(u, PAIR - HEAD // 2, 1), pltpu.roll(u, HEAD // 2, 1))


def qkv_kernel(x_ref, w_ref, cos_ref, sin_ref, q_ref, k_ref, v_ref, xt_ref):
    x = x_ref[...]
    width = x.shape[1]
    cosine, sine = cos_ref[...], sin_ref[...]
    for part, out in ((0, q_ref), (1, k_ref), (2, v_ref)):
        for pair in range(width // PAIR):
            at = part * width + pair * PAIR
            if pair % 2 == 0:
                u2 = dot(x, w_ref[:, at : at + 2 * PAIR])
            u = u2[:, (pair % 2) * PAIR : (pair % 2 + 1) * PAIR]
            if part < 2:
                u = u * cosine + turn(u) * sine
            if part == 0:
                u = u * (0.125 * LOG2E)
            out[:, pair * PAIR : (pair + 1) * PAIR] = u.astype(BF)
    xt_ref[...] = x.T


def qkv_call(x, w, cosine, sine, tile=512):
    tokens, width = x.shape
    span = cosine.shape[0]
    tile = min(tile, span)
    row = pl.BlockSpec((tile, width), lambda i: (i, 0))
    table = pl.BlockSpec((tile, PAIR), lambda i: (i % (span // tile), 0))
    return pl.pallas_call(
        qkv_kernel,
        grid=(tokens // tile,),
        in_specs=[
            row,
            pl.BlockSpec(w.shape, lambda i: (0, 0), pipeline_mode=pl.Buffered(1)),
            table,
            table,
        ],
        out_specs=[row, row, row, pl.BlockSpec((width, tile), lambda i: (0, i))],
        out_shape=[jax.ShapeDtypeStruct((tokens, width), BF)] * 3
        + [jax.ShapeDtypeStruct((width, tokens), BF)],
        compiler_params=params(),
        name="qkv",
    )(x, w, cosine, sine)


def attend_kernel(q_ref, k_ref, v_ref, bias_ref, o_ref, aug_ref, ka, va):
    keys = k_ref.shape[1]

    @pl.when(pl.program_id(2) == 0)
    def _():
        lane = lanes((keys, PAIR))
        k, v = k_ref[0], v_ref[0]
        zero = jnp.zeros_like(k)
        for h in range(2):
            mine = (lane // HEAD) == h
            ka[h, :, :PAIR] = jnp.where(mine, k, zero)
            ka[h, :, PAIR:] = bias_ref[0]
            va[h, :, :PAIR] = jnp.where(mine, v, zero)
            va[h, :, PAIR:] = mine.astype(F32).astype(BF)

    q = q_ref[0]
    lane = lanes(q.shape)
    qa = jnp.concatenate([q, (lane == 3).astype(F32).astype(BF)], axis=1)
    acc = None
    tops = []
    for h in range(2):
        s = dot_nt(qa, ka[h])
        top = jnp.max(s, axis=1, keepdims=True)
        p = jnp.exp2(s - top).astype(BF)
        part = dot(p, va[h])
        acc = part if acc is None else acc + part
        tops.append(top)
    total = acc[:, PAIR:]
    o_ref[0] = (acc[:, :PAIR] / total).astype(BF)
    lse = jnp.where(lane < HEAD, tops[0], tops[1]) + jnp.log2(total)
    aug_ref[0] = spread(lse, jnp.where(lane == 3, 1.0, 0.0))


def spread(value, other):
    high = value.astype(BF).astype(F32)
    rest = value - high
    mid = rest.astype(BF).astype(F32)
    low = rest - mid
    sub = lanes(value.shape) % HEAD
    return jnp.where(
        sub == 0, high, jnp.where(sub == 1, mid, jnp.where(sub == 2, low, other))
    ).astype(BF)


def attend_call(q, k, v, bias, tile=256):
    rows, span, width = q.shape
    keys = k.shape[1]
    tile = min(tile, span)
    qs = pl.BlockSpec((1, tile, PAIR), lambda r, p, i: (r, i, p))
    ks = pl.BlockSpec((1, keys, PAIR), lambda r, p, i: (r, 0, p))
    return pl.pallas_call(
        attend_kernel,
        grid=(rows, width // PAIR, span // tile),
        in_specs=[qs, ks, ks, pl.BlockSpec((1, keys, PAIR), lambda r, p, i: (r, 0, 0))],
        out_specs=[qs, qs],
        out_shape=[jax.ShapeDtypeStruct(q.shape, BF)] * 2,
        scratch_shapes=[
            pltpu.VMEM((2, keys, 2 * PAIR), BF),
            pltpu.VMEM((2, keys, 2 * PAIR), BF),
        ],
        compiler_params=params(),
        name="attend",
    )(q, k, v, bias)


def attend_back_kernel(
    tk, tq, q_ref, k_ref, v_ref, bias_ref, o_ref, do_ref, aug_ref, cq_ref, sq_ref, ck_ref, sk_ref,
    dq_ref, dk_ref, dv_ref, qa, ka, va, da, qm, dm, kt, dqt, dk_acc, dv_acc,
):
    keys, span = k_ref.shape[1], q_ref.shape[1]

    lane_k = lanes((keys, PAIR))
    lane_q = lanes((span, PAIR))
    q, k, v, do = q_ref[0], k_ref[0], v_ref[0], do_ref[0]
    bias = bias_ref[0].astype(F32)
    prod = do.astype(F32) * o_ref[0].astype(F32)
    first = prod.astype(BF)
    second = (prod - first.astype(F32)).astype(BF)
    block = (
        (lax.broadcasted_iota(jnp.int32, (PAIR, PAIR), 0) // HEAD)
        == (lax.broadcasted_iota(jnp.int32, (PAIR, PAIR), 1) // HEAD)
    ).astype(F32).astype(BF)
    delta = dot(first, block) + dot(second, block)
    qa[:, :PAIR] = q
    qa[:, PAIR:] = aug_ref[0]
    da[:, :PAIR] = do
    da[:, PAIR:] = spread(delta, jnp.zeros_like(delta))
    for h in range(2):
        mine_k = (lane_k // HEAD) == h
        mine_q = (lane_q // HEAD) == h
        minus = jnp.where(mine_k & (lane_k % HEAD < 3), -1.0, 0.0)
        ka[h, :, :PAIR] = jnp.where(mine_k, k, jnp.zeros_like(k))
        ka[h, :, PAIR:] = (minus + bias).astype(BF)
        va[h, :, :PAIR] = jnp.where(mine_k, v, jnp.zeros_like(v))
        va[h, :, PAIR:] = minus.astype(BF)
        qm[h] = jnp.where(mine_q, q, jnp.zeros_like(q))
        dm[h] = jnp.where(mine_q, do, jnp.zeros_like(do))
    kt[...] = k.T
    dqt[...] = jnp.zeros_like(dqt)

    nq, nk = span // tq, keys // tk

    def key_step(j, _):
        at_k = pl.ds(pl.multiple_of(j * tk, tk), tk)
        dk_acc[...] = jnp.zeros_like(dk_acc)
        dv_acc[...] = jnp.zeros_like(dv_acc)

        def query_step(i, _):
            at_q = pl.ds(pl.multiple_of(i * tq, tq), tq)
            dv, dk = None, None
            for h in range(2):
                st = dot_nt(ka[h, at_k, :], qa[at_q, :])
                dpt = dot_nt(va[h, at_k, :], da[at_q, :])
                p = jnp.exp2(st)
                ds = (p * dpt).astype(BF)
                pv = dot(p.astype(BF), dm[h, at_q, :])
                pk = dot(ds, qm[h, at_q, :])
                dv = pv if dv is None else dv + pv
                dk = pk if dk is None else dk + pk
                head = slice(h * HEAD, (h + 1) * HEAD)
                dqt[head, at_q] += dot(kt[head, at_k], ds)
            dv_acc[...] += dv
            dk_acc[...] += dk
            return 0

        lax.fori_loop(0, nq, query_step, 0, unroll=True)
        dv_ref[0, at_k, :] = dv_acc[...].astype(dv_ref.dtype)
        g = dk_acc[...] * LN2
        if dk_ref.dtype == BF:
            g = back_turn(g, ck_ref[at_k, :], sk_ref[at_k, :])
        dk_ref[0, at_k, :] = g.astype(dk_ref.dtype)
        return 0

    lax.fori_loop(0, nk, key_step, 0)
    g = dqt[...].T * 0.125
    dq_ref[0] = back_turn(g, cq_ref[...], sq_ref[...]).astype(BF)


def back_turn(g, cosine, sine):
    return g * cosine - turn(g * sine)


def attend_back_call(q, k, v, bias, o, do, aug, cq, sq, ck, sk, whole, tk=512, tq=512):
    rows, span, width = q.shape
    keys = k.shape[1]
    tq = min(tq, span)
    tk = min(tk, keys)
    qs = pl.BlockSpec((1, span, PAIR), lambda r, p: (r, 0, p))
    ks = pl.BlockSpec((1, keys, PAIR), lambda r, p: (r, 0, p))
    tq_s = pl.BlockSpec((span, PAIR), lambda r, p: (0, 0))
    tk_s = pl.BlockSpec((keys, PAIR), lambda r, p: (0, 0))
    kv_type = BF if whole else F32
    return pl.pallas_call(
        functools.partial(attend_back_kernel, tk, tq),
        grid=(rows, width // PAIR),
        in_specs=[
            qs, ks, ks, pl.BlockSpec((1, keys, PAIR), lambda r, p: (r, 0, 0)), qs, qs, qs,
            tq_s, tq_s, tk_s, tk_s,
        ],
        out_specs=[qs, ks, ks],
        out_shape=[
            jax.ShapeDtypeStruct(q.shape, BF),
            jax.ShapeDtypeStruct(k.shape, kv_type),
            jax.ShapeDtypeStruct(k.shape, kv_type),
        ],
        scratch_shapes=[
            pltpu.VMEM((span, 2 * PAIR), BF),
            pltpu.VMEM((2, keys, 2 * PAIR), BF),
            pltpu.VMEM((2, keys, 2 * PAIR), BF),
            pltpu.VMEM((span, 2 * PAIR), BF),
            pltpu.VMEM((2, span, PAIR), BF),
            pltpu.VMEM((2, span, PAIR), BF),
            pltpu.VMEM((PAIR, keys), BF),
            pltpu.VMEM((PAIR, span), F32),
            pltpu.VMEM((tk, PAIR), F32),
            pltpu.VMEM((tk, PAIR), F32),
        ],
        compiler_params=params(),
        name="attend_back",
    )(q, k, v, bias, o, do, aug, cq, sq, ck, sk)


def middle_kernel(
    chunk, x_ref, att_ref, cot_ref, wo_ref, wg_ref, wu_ref, wd_ref, g1_ref, g2_ref,
    out_ref, dfirst_ref, datt_ref, act_ref, dg_ref, du_ref, ht_ref, dft_ref, at_ref, gg1_ref, gg2_ref,
    ca, cb,
):
    @pl.when(pl.program_id(0) == 0)
    def _():
        gg1_ref[...] = jnp.zeros_like(gg1_ref)
        gg2_ref[...] = jnp.zeros_like(gg2_ref)

    gain1, gain2 = g1_ref[...], g2_ref[...]
    att = att_ref[...]
    at_ref[...] = att.T
    first = x_ref[...].astype(F32) + dot(att, wo_ref[...])
    centered = first - jnp.mean(first, axis=1, keepdims=True)
    s1 = lax.rsqrt(jnp.mean(centered * centered, axis=1, keepdims=True) + EPS)
    n1 = centered * s1
    hidden = n1 * gain1
    low = hidden.astype(BF)
    ht_ref[...] = low.T
    hidden_width = wg_ref.shape[1]
    second = hidden
    for c in range(hidden_width // chunk):
        at = slice(c * chunk, (c + 1) * chunk)
        g = dot(low, wg_ref[:, at])
        u = dot(low, wu_ref[:, at])
        sig = jax.nn.sigmoid(g)
        silu = g * sig
        act = (silu * u).astype(BF)
        act_ref[:, at] = act
        ca[:, at] = (u * (sig + silu * (1.0 - sig))).astype(ca.dtype)
        cb[:, at] = silu.astype(cb.dtype)
        second = second + dot(act, wd_ref[at, :])
    centered = second - jnp.mean(second, axis=1, keepdims=True)
    s2 = lax.rsqrt(jnp.mean(centered * centered, axis=1, keepdims=True) + EPS)
    n2 = centered * s2
    out_ref[...] = (n2 * gain2).astype(BF)
    dy = cot_ref[...].astype(F32)
    gg2_ref[...] += jnp.sum(dy * n2, axis=0, keepdims=True)
    inner = dy * gain2
    d_second = s2 * (
        inner - jnp.mean(inner, axis=1, keepdims=True) - n2 * jnp.mean(inner * n2, axis=1, keepdims=True)
    )
    d_ffn = d_second.astype(BF)
    dft_ref[...] = d_ffn.T
    d_hidden = d_second
    for c in range(hidden_width // chunk):
        at = slice(c * chunk, (c + 1) * chunk)
        d_act = dot_nt(d_ffn, wd_ref[at, :])
        dg = (d_act * ca[:, at]).astype(BF)
        du = (d_act * cb[:, at]).astype(BF)
        dg_ref[:, at] = dg
        du_ref[:, at] = du
        d_hidden = d_hidden + dot_nt(dg, wg_ref[:, at]) + dot_nt(du, wu_ref[:, at])
    gg1_ref[...] += jnp.sum(d_hidden * n1, axis=0, keepdims=True)
    inner = d_hidden * gain1
    d_first = s1 * (
        inner - jnp.mean(inner, axis=1, keepdims=True) - n1 * jnp.mean(inner * n1, axis=1, keepdims=True)
    )
    low = d_first.astype(BF)
    dfirst_ref[...] = low
    datt_ref[...] = dot_nt(low, wo_ref[...]).astype(BF)


def middle_call(x, att, cot, wo, wg, wu, wd, g1, g2, tile=256, chunk=768):
    tokens, width = x.shape
    hidden_width = wg.shape[1]
    tile = min(tile, tokens)
    row = pl.BlockSpec((tile, width), lambda i: (i, 0))
    wide = pl.BlockSpec((tile, hidden_width), lambda i: (i, 0))
    column = pl.BlockSpec((width, tile), lambda i: (0, i))

    def whole(a):
        return pl.BlockSpec(a.shape, lambda i: (0, 0), pipeline_mode=pl.Buffered(1))

    gain = pl.BlockSpec((1, width), lambda i: (0, 0))
    return pl.pallas_call(
        functools.partial(middle_kernel, chunk),
        grid=(tokens // tile,),
        in_specs=[row, row, row, whole(wo), whole(wg), whole(wu), whole(wd), gain, gain],
        out_specs=[row, row, row, wide, wide, wide, column, column, column, gain, gain],
        out_shape=[jax.ShapeDtypeStruct((tokens, width), BF)] * 3
        + [jax.ShapeDtypeStruct((tokens, hidden_width), BF)] * 3
        + [jax.ShapeDtypeStruct((width, tokens), BF)] * 3
        + [jax.ShapeDtypeStruct((1, width), F32)] * 2,
        scratch_shapes=[pltpu.VMEM((tile, hidden_width), F32)] * 2,
        compiler_params=params(),
        name="middle",
    )(x, att, cot, wo, wg, wu, wd, g1, g2)


def outer_kernel(a_ref, b_ref, o_ref):
    o_ref[...] = dot(a_ref[...], b_ref[...]).astype(o_ref.dtype)


def outer_call(a, b, out_type, tile=512):
    rows, tokens = a.shape
    columns = b.shape[1]
    tile = tile if columns % tile == 0 else 256
    return pl.pallas_call(
        outer_kernel,
        grid=(columns // tile,),
        in_specs=[
            pl.BlockSpec((rows, tokens), lambda i: (0, 0), pipeline_mode=pl.Buffered(1)),
            pl.BlockSpec((tokens, tile), lambda i: (0, i)),
        ],
        out_specs=pl.BlockSpec((rows, tile), lambda i: (0, i)),
        out_shape=jax.ShapeDtypeStruct((rows, columns), out_type),
        compiler_params=params(),
        name="outer",
    )(a, b)


def tokens_kernel(dq_ref, dk_ref, dv_ref, dfirst_ref, w_ref, o_ref):
    width = dq_ref.shape[1]
    total = dfirst_ref[...].astype(F32)
    total += dot_nt(dq_ref[...], w_ref[:, :width])
    total += dot_nt(dk_ref[...], w_ref[:, width : 2 * width])
    total += dot_nt(dv_ref[...], w_ref[:, 2 * width :])
    o_ref[...] = total.astype(BF)


def tokens_call(dq, dk, dv, dfirst, w, tile=512):
    tokens, width = dq.shape
    tile = min(tile, tokens)
    row = pl.BlockSpec((tile, width), lambda i: (i, 0))
    return pl.pallas_call(
        tokens_kernel,
        grid=(tokens // tile,),
        in_specs=[row] * 4 + [pl.BlockSpec(w.shape, lambda i: (0, 0), pipeline_mode=pl.Buffered(1))],
        out_specs=row,
        out_shape=jax.ShapeDtypeStruct((tokens, width), BF),
        compiler_params=params(),
        name="grad_tokens",
    )(dq, dk, dv, dfirst, w)


def angle_tables(span):
    index = np.arange(HEAD // 2, dtype=np.float64)
    inverse = np.power(1000.0, -2.0 * index / HEAD)
    angles = np.arange(span, dtype=np.float64)[:, None] * inverse[None, :]
    repeat = (1, PAIR // (HEAD // 2))
    return (
        np.tile(np.cos(angles), repeat).astype(np.float32),
        np.tile(np.sin(angles), repeat).astype(np.float32),
    )


def swap(a, mine):
    keep = lax.dynamic_index_in_dim(a, mine, 0, keepdims=False)
    give = lax.dynamic_index_in_dim(a, 1 - mine, 0, keepdims=False)
    got = lax.ppermute(give, "blk", [(0, 1), (1, 0)])
    low = jnp.where(mine == 0, keep, got)
    high = jnp.where(mine == 0, got, keep)
    return jnp.stack([low, high])


def body(tokens, lengths, w_qkv, w_out, w_gate, w_up, w_down, gain_one, gain_two, cotangent):
    axes = ("dp", "blk")
    blk = lax.axis_size("blk")
    mine = lax.axis_index("blk")
    rows, span, width = tokens.shape
    seq = span * blk
    own = blk == 2 and rows == 2

    def gather(a):
        return lax.all_gather(a, axes, axis=0, tiled=True)

    f_qkv, f_out, f_gate, f_up, f_down = map(gather, (w_qkv, w_out, w_gate, w_up, w_down))
    gains = jnp.stack([gain_one, gain_two], 1)
    f_gains = gather(gains).astype(F32)
    g1, g2 = f_gains[:, 0][None], f_gains[:, 1][None]
    cosine, sine = map(jnp.asarray, angle_tables(seq))
    if own:
        x = swap(tokens, mine).reshape(1, seq, width)
        cot = swap(cotangent, mine).reshape(1, seq, width)
        length = lax.dynamic_slice_in_dim(lengths, mine, 1, 0)
        cq, sq = cosine, sine
    else:
        x, cot, length = tokens, cotangent, lengths
        cq = lax.dynamic_slice_in_dim(cosine, mine * span, span, 0)
        sq = lax.dynamic_slice_in_dim(sine, mine * span, span, 0)
    n, t = x.shape[:2]
    flat = x.reshape(n * t, width)
    q, k, v, xt = qkv_call(flat, f_qkv, cq, sq)
    q, k, v = (a.reshape(n, t, width) for a in (q, k, v))
    if not own:
        k = lax.all_gather(k, "blk", axis=1, tiled=True)
        v = lax.all_gather(v, "blk", axis=1, tiled=True)
    position = jnp.arange(seq, dtype=jnp.int32)[None, :, None]
    lane = jnp.arange(PAIR, dtype=jnp.int32)[None, None, :]
    bias = jnp.where((lane == 3) & (position >= length[:, None, None]), NEG, 0.0).astype(BF)
    att, aug = attend_call(q, k, v, bias)
    out, d_first, d_att, act, d_gate, d_up, h_t, df_t, att_t, gg1, gg2 = middle_call(
        flat, att.reshape(n * t, width), cot.reshape(n * t, width), f_out, f_gate, f_up, f_down, g1, g2
    )
    gw_gate = outer_call(h_t, d_gate, BF)
    gw_up = outer_call(h_t, d_up, BF)
    gw_down_t = outer_call(df_t, act, BF)
    gw_out = outer_call(att_t, d_first, BF)

    def scatter_wide(g):
        g = lax.psum_scatter(g, "blk", scatter_dimension=1, tiled=True)
        return lax.psum_scatter(g, "dp", scatter_dimension=0, tiled=True).astype(F32)

    s_gate, s_up, s_down_t = map(scatter_wide, (gw_gate, gw_up, gw_down_t))
    s_down = s_down_t.T
    dq, dk, dv = attend_back_call(
        q, k, v, bias, att, d_att.reshape(n, t, width), aug, cq, sq, cosine, sine, own
    )
    if not own:
        dk = lax.psum_scatter(dk, "blk", scatter_dimension=1, tiled=True)
        dv = lax.psum_scatter(dv, "blk", scatter_dimension=1, tiled=True)
        heads = (dk * jnp.tile(sq, (1, width // PAIR))).reshape(n, t, HEADS, HEAD)
        half = jnp.concatenate([heads[..., HEAD // 2 :], -heads[..., : HEAD // 2]], -1)
        dk = dk * jnp.tile(cq, (1, width // PAIR)) + half.reshape(n, t, width)
        dk, dv = dk.astype(BF), dv.astype(BF)
    dq, dk, dv = (a.reshape(n * t, width) for a in (dq, dk, dv))
    gw_qkv = jnp.concatenate([outer_call(xt, a, BF, 256) for a in (dq, dk, dv)], 1)
    g_tokens = tokens_call(dq, dk, dv, d_first, f_qkv)
    s_qkv = lax.psum_scatter(gw_qkv, axes, scatter_dimension=0, tiled=True).astype(F32)
    s_out = lax.psum_scatter(gw_out, axes, scatter_dimension=0, tiled=True).astype(F32)
    gg = jnp.concatenate([gg1, gg2]).T
    s_gg = lax.psum_scatter(gg, axes, scatter_dimension=0, tiled=True)
    if own:
        out = swap(out.reshape(2, span, width), mine)
        g_tokens = swap(g_tokens.reshape(2, span, width), mine)
    else:
        out = out.reshape(tokens.shape)
        g_tokens = g_tokens.reshape(tokens.shape)
    return (out, g_tokens, s_qkv, s_out, s_gate, s_up, s_down, s_gg[:, 0], s_gg[:, 1])


def solution(mesh):
    both = ("dp", "blk")
    return jax.shard_map(
        body,
        mesh=mesh,
        in_specs=(
            P("dp", "blk", None),
            P("dp"),
            P(both, None),
            P(both, None),
            P(both, None),
            P(both, None),
            P(both, None),
            P(both),
            P(both),
            P("dp", "blk", None),
        ),
        out_specs=(
            P("dp", "blk", None),
            P("dp", "blk", None),
            P(both, None),
            P(both, None),
            P("dp", "blk"),
            P("dp", "blk"),
            P("blk", "dp"),
            P(both),
            P(both),
        ),
        check_vma=False,
    )
```

```python
import functools

import jax
import jax.numpy as jnp
import numpy as np
from jax import lax
from jax.experimental import pallas as pl
from jax.experimental.pallas import tpu as pltpu
from jax.sharding import PartitionSpec as P

HEADS = 12
HEAD = 64
PAIR = 2 * HEAD
EPS = 1e-05
NEG = -1e30
LOG2E = 1.4426950408889634
LN2 = 0.6931471805599453
VMEM_LIMIT = 60 * 1024 * 1024

BF = jnp.bfloat16
F32 = jnp.float32


def dot(a, b):
    return lax.dot_general(a, b, (((1,), (0,)), ((), ())), preferred_element_type=F32)


def dot_nt(a, b):
    return lax.dot_general(a, b, (((1,), (1,)), ((), ())), preferred_element_type=F32)


def params(limit=VMEM_LIMIT):
    return pltpu.CompilerParams(vmem_limit_bytes=limit)


def lanes(shape):
    return lax.broadcasted_iota(jnp.int32, shape, 1)


def turn(u):
    low_half = (lanes(u.shape) % HEAD) < HEAD // 2
    return jnp.where(low_half, -pltpu.roll(u, PAIR - HEAD // 2, 1), pltpu.roll(u, HEAD // 2, 1))


MESH = pl.DeviceIdType.MESH
AXES = "zxcy"
SIZE = {"z": 4, "x": 2, "c": 2, "y": 2}


def place():
    dp, y = lax.axis_index("dp"), lax.axis_index("blk")
    return {"z": dp // 4, "x": dp // 2 % 2, "c": dp % 2, "y": y}


def moved(me, axis, by):
    return {**me, axis: lax.rem(me[axis] + by, SIZE[axis])}


def device(at):
    return ((at["z"] * 2 + at["x"]) * 2 + at["c"], at["y"])


def greet(me):
    barrier = pltpu.get_barrier_semaphore()
    peers = [moved(me, "y", 1), moved(me, "x", 1), moved(me, "c", 1)]
    peers += [moved(me, "z", d) for d in range(1, 4)]
    for peer in peers:
        pl.semaphore_signal(barrier, inc=1, device_id=device(peer), device_id_type=MESH)
    pl.semaphore_wait(barrier, len(peers))


class Gather:
    SEMS = 6

    def __init__(self, me, shard, full, send, recv, local, base, order):
        self.me, self.shard, self.full = me, shard, full
        self.send, self.recv, self.local, self.base, self.order = send, recv, local, base, order

    def view(self, at, got):
        return self.full.at[tuple(slice(None) if a in got else at[a] for a in AXES)]

    def copies(self, stage):
        got = self.order[:stage]
        axis = self.order[stage]
        slot = self.base + sum(SIZE[a] - 1 for a in got)
        out = []
        for d in range(1, SIZE[axis]):
            here = self.view(self.me, got)
            out.append(
                pltpu.make_async_remote_copy(
                    src_ref=self.shard if stage == 0 else here,
                    dst_ref=here,
                    send_sem=self.send.at[slot + d - 1],
                    recv_sem=self.recv.at[slot + d - 1],
                    device_id=device(moved(self.me, axis, d)),
                    device_id_type=MESH,
                )
            )
        return out

    def own(self):
        return pltpu.make_async_copy(self.shard, self.view(self.me, ""), self.local)

    def arrivals(self, stage):
        got = self.order[:stage]
        axis = self.order[stage]
        slot = self.base + sum(SIZE[a] - 1 for a in got)
        for d in range(1, SIZE[axis]):
            there = self.view(moved(self.me, axis, SIZE[axis] - d), got)
            pltpu.make_async_remote_copy(
                src_ref=there,
                dst_ref=there,
                send_sem=self.send.at[slot + d - 1],
                recv_sem=self.recv.at[slot + d - 1],
                device_id=device(moved(self.me, axis, d)),
                device_id_type=MESH,
            ).wait_recv()

    def start(self):
        self.own().start()
        for copy in self.copies(0):
            copy.start()

    def step(self, stage):
        self.arrivals(stage - 1)
        if stage == 1:
            self.own().wait()
        if stage < len(self.order):
            for copy in self.copies(stage):
                copy.start()

    def finish(self):
        for stage in range(len(self.order)):
            for copy in self.copies(stage):
                copy.wait_send()


def swap_copies(me, source, target, send, recv, local, slot):
    other = moved(me, "y", 1)
    y = me["y"]
    keep = pltpu.make_async_copy(source.at[y], target.at[y], local)
    give = pltpu.make_async_remote_copy(
        src_ref=source.at[1 - y],
        dst_ref=target.at[y],
        send_sem=send.at[slot],
        recv_sem=recv.at[slot],
        device_id=device(other),
        device_id_type=MESH,
    )
    take = pltpu.make_async_remote_copy(
        src_ref=target.at[1 - y],
        dst_ref=target.at[1 - y],
        send_sem=send.at[slot],
        recv_sem=recv.at[slot],
        device_id=device(other),
        device_id_type=MESH,
    )
    return keep, give, take


def opening_kernel(tok_ref, qkv_ref, x_ref, full_ref, send, recv, local):
    me = place()
    greet(me)
    keep, give, take = swap_copies(me, tok_ref, x_ref, send, recv, local.at[0], 0)
    gather = Gather(me, qkv_ref, full_ref, send, recv, local.at[1], 1, "yzxc")
    gather.start()
    give.start()
    keep.start()
    for stage in range(1, 5):
        gather.step(stage)
    gather.finish()
    take.wait_recv()
    give.wait_send()
    keep.wait()


def opening_call(tokens, w_qkv):
    hbm = pl.BlockSpec(memory_space=pl.ANY)
    return pl.pallas_call(
        opening_kernel,
        in_specs=[hbm, hbm],
        out_specs=[hbm, hbm],
        out_shape=[
            jax.ShapeDtypeStruct(tokens.shape, BF),
            jax.ShapeDtypeStruct((4, 2, 2, 2) + w_qkv.shape, BF),
        ],
        scratch_shapes=[
            pltpu.SemaphoreType.DMA((1 + Gather.SEMS,)),
            pltpu.SemaphoreType.DMA((1 + Gather.SEMS,)),
            pltpu.SemaphoreType.DMA((2,)),
        ],
        compiler_params=pltpu.CompilerParams(collective_id=0, has_side_effects=True),
        name="opening",
    )(tokens, w_qkv)


def qkv_kernel(x_ref, w_ref, cos_ref, sin_ref, q_ref, k_ref, v_ref, xt_ref):
    x = x_ref[...]
    width = x.shape[1]
    cosine, sine = cos_ref[...], sin_ref[...]
    for part, out in ((0, q_ref), (1, k_ref), (2, v_ref)):
        for pair in range(width // PAIR):
            at = part * width + pair * PAIR
            if pair % 2 == 0:
                u2 = dot(x, w_ref[:, at : at + 2 * PAIR])
            u = u2[:, (pair % 2) * PAIR : (pair % 2 + 1) * PAIR]
            if part < 2:
                u = u * cosine + turn(u) * sine
            if part == 0:
                u = u * (0.125 * LOG2E)
            out[:, pair * PAIR : (pair + 1) * PAIR] = u.astype(BF)
    xt_ref[...] = x.T


def qkv_call(x, w, cosine, sine, tile=512):
    tokens, width = x.shape
    span = cosine.shape[0]
    tile = min(tile, span)
    row = pl.BlockSpec((tile, width), lambda i: (i, 0))
    table = pl.BlockSpec((tile, PAIR), lambda i: (i % (span // tile), 0))
    return pl.pallas_call(
        qkv_kernel,
        grid=(tokens // tile,),
        in_specs=[
            row,
            pl.BlockSpec(w.shape, lambda i: (0, 0), pipeline_mode=pl.Buffered(1)),
            table,
            table,
        ],
        out_specs=[row, row, row, pl.BlockSpec((width, tile), lambda i: (0, i))],
        out_shape=[jax.ShapeDtypeStruct((tokens, width), BF)] * 3
        + [jax.ShapeDtypeStruct((width, tokens), BF)],
        compiler_params=params(),
        name="qkv",
    )(x, w, cosine, sine)


def attend_kernel(tile, chunk, moves, q_ref, k_ref, v_ref, bias_ref, *rest):
    inputs, rest = rest[: moves], rest[moves:]
    o_ref, aug_ref, rest = rest[0], rest[1], rest[2:]
    outputs, rest = rest[: moves], rest[moves:]
    ka, va, s_scr, m_scr = rest[:4]
    keys, span = k_ref.shape[1], q_ref.shape[1]
    tiles = span // tile
    events = {}
    if moves:
        events = attend_events(inputs, outputs, tiles * pl.num_programs(1), *rest[4:])
    lane = lanes((keys, PAIR))
    k, v = k_ref[0], v_ref[0]
    zero = jnp.zeros_like(k)
    for h in range(2):
        mine = (lane // HEAD) == h
        ka[h, :, :PAIR] = jnp.where(mine, k, zero)
        ka[h, :, PAIR:] = bias_ref[0]
        va[h, :, :PAIR] = jnp.where(mine, v, zero)
        va[h, :, PAIR:] = mine.astype(F32).astype(BF)
    lane = lanes((tile, PAIR))
    ones = (lane == 3).astype(F32).astype(BF)
    chunks = keys // chunk

    def score(i, h, c, top):
        at = pl.ds(pl.multiple_of(i * tile, tile), tile)
        qa = jnp.concatenate([q_ref[0, at, :], ones], axis=1)
        s = dot_nt(qa, ka[h, c * chunk : (c + 1) * chunk, :])
        s_scr[h, :, c * chunk : (c + 1) * chunk] = s
        for b in range(chunk // PAIR):
            part = s[:, b * PAIR : (b + 1) * PAIR]
            top = part if top is None else jnp.maximum(top, part)
        return top

    def close(h, top):
        m_scr[h] = jnp.broadcast_to(jnp.max(top, axis=1, keepdims=True), (tile, PAIR))

    def unit(h, later, other):
        m = m_scr[h]
        wide = jnp.concatenate([m] * (chunk // PAIR), axis=1)
        acc, top = None, None
        for c in range(chunks):
            top = score(later, other, c, top)
            p = jnp.exp2(s_scr[h, :, c * chunk : (c + 1) * chunk] - wide).astype(BF)
            part = dot(p, va[h, c * chunk : (c + 1) * chunk, :])
            acc = part if acc is None else acc + part
        return acc, top, m

    top = None
    for c in range(chunks):
        top = score(0, 0, c, top)
    close(0, top)

    def step(i, _):
        now = pl.program_id(1) * tiles + i
        for at_step, act in events.items():
            pl.when(now == at_step)(act)
        acc0, top, m0 = unit(0, i, 1)
        close(1, top)
        acc1, top, m1 = unit(1, jnp.minimum(i + 1, tiles - 1), 0)
        close(0, top)
        acc = acc0 + acc1
        total = acc[:, PAIR:]
        at = pl.ds(pl.multiple_of(i * tile, tile), tile)
        o_ref[0, at, :] = (acc[:, :PAIR] / total).astype(BF)
        lse = jnp.where(lane < HEAD, m0, m1) + jnp.log2(total)
        aug_ref[0, at, :] = spread(lse, jnp.where(lane == 3, 1.0, 0.0))
        return 0

    lax.fori_loop(0, tiles, step, 0)
    if moves:
        pl.when(pl.program_id(1) == pl.num_programs(1) - 1)(events.last)


class Events(dict):
    last = None


def attend_events(inputs, outputs, steps, send, recv, local):
    me = place()
    cot_in, shards = inputs[0], inputs[1:]
    cot_out, fulls = outputs[0], outputs[1:]
    keep, give, take = swap_copies(me, cot_in, cot_out, send, recv, local.at[0], 0)
    orders = ["zxyc", "zxyc", "zyxc", "yzxc"]
    gathers = [
        Gather(me, shard, full, send, recv, local.at[1 + i], 1 + i * Gather.SEMS, orders[i])
        for i, (shard, full) in enumerate(zip(shards, fulls))
    ]

    def begin():
        greet(me)
        for g in gathers:
            g.start()
        give.start()
        keep.start()

    def stage(g, n):
        return lambda: g.step(n)

    def last():
        for n, g in pending:
            g.step(n)
        for g in gathers:
            g.finish()
        take.wait_recv()
        give.wait_send()
        keep.wait()

    events = Events()
    events[0] = begin
    todo = [(n, g) for n in (1, 2, 3, 4) for g in gathers]
    times = [4, 6, 9, 5, 6, 9, 12, 11, 12, 16, 19, 20]
    for at, (n, g) in zip(times, todo):
        old = events.get(at)
        new = stage(g, n)
        events[at] = new if old is None else (lambda old=old, new=new: (old(), new(), None)[2])
    pending = todo[len(times) :]
    events.last = last
    return events


def spread(value, other):
    high = value.astype(BF).astype(F32)
    rest = value - high
    mid = rest.astype(BF).astype(F32)
    low = rest - mid
    sub = lanes(value.shape) % HEAD
    return jnp.where(
        sub == 0, high, jnp.where(sub == 1, mid, jnp.where(sub == 2, low, other))
    ).astype(BF)


def attend_call(q, k, v, bias, moving=(), tile=512, chunk=512):
    rows, span, width = q.shape
    keys = k.shape[1]
    tile = min(tile, span)
    moves = len(moving)
    qs = pl.BlockSpec((1, span, PAIR), lambda r, p: (r, 0, p))
    ks = pl.BlockSpec((1, keys, PAIR), lambda r, p: (r, 0, p))
    hbm = pl.BlockSpec(memory_space=pl.ANY)
    moved_shapes = [jax.ShapeDtypeStruct(a.shape, a.dtype) for a in moving[:1]] + [
        jax.ShapeDtypeStruct((4, 2, 2, 2) + a.shape, a.dtype) for a in moving[1:]
    ]
    sems = 1 + Gather.SEMS * max(moves - 1, 0)
    extra = [pltpu.SemaphoreType.DMA((sems,))] * 2 + [pltpu.SemaphoreType.DMA((moves,))]
    more = dict(collective_id=1, has_side_effects=True) if moves else {}
    return pl.pallas_call(
        functools.partial(attend_kernel, tile, chunk, moves),
        grid=(rows, width // PAIR),
        in_specs=[qs, ks, ks, pl.BlockSpec((1, keys, PAIR), lambda r, p: (r, 0, 0))] + [hbm] * moves,
        out_specs=[qs, qs] + [hbm] * moves,
        out_shape=[jax.ShapeDtypeStruct(q.shape, BF)] * 2 + moved_shapes,
        scratch_shapes=[
            pltpu.VMEM((2, keys, 2 * PAIR), BF),
            pltpu.VMEM((2, keys, 2 * PAIR), BF),
            pltpu.VMEM((2, tile, keys), F32),
            pltpu.VMEM((2, tile, PAIR), F32),
        ]
        + (extra if moves else []),
        compiler_params=pltpu.CompilerParams(vmem_limit_bytes=VMEM_LIMIT, **more),
        name="attend",
    )(q, k, v, bias, *moving)


def attend_back_kernel(
    tk, tq, q_ref, k_ref, v_ref, bias_ref, o_ref, do_ref, aug_ref, cq_ref, sq_ref, ck_ref, sk_ref,
    dq_ref, dk_ref, dv_ref, qa, ka, va, da, qm, dm, kt, dqt, dk_acc, dv_acc,
):
    keys, span = k_ref.shape[1], q_ref.shape[1]

    lane_k = lanes((keys, PAIR))
    lane_q = lanes((span, PAIR))
    q, k, v, do = q_ref[0], k_ref[0], v_ref[0], do_ref[0]
    bias = bias_ref[0].astype(F32)
    prod = do.astype(F32) * o_ref[0].astype(F32)
    first = prod.astype(BF)
    second = (prod - first.astype(F32)).astype(BF)
    block = (
        (lax.broadcasted_iota(jnp.int32, (PAIR, PAIR), 0) // HEAD)
        == (lax.broadcasted_iota(jnp.int32, (PAIR, PAIR), 1) // HEAD)
    ).astype(F32).astype(BF)
    delta = dot(first, block) + dot(second, block)
    qa[:, :PAIR] = q
    qa[:, PAIR:] = aug_ref[0]
    da[:, :PAIR] = do
    da[:, PAIR:] = spread(delta, jnp.zeros_like(delta))
    for h in range(2):
        mine_k = (lane_k // HEAD) == h
        mine_q = (lane_q // HEAD) == h
        minus = jnp.where(mine_k & (lane_k % HEAD < 3), -1.0, 0.0)
        ka[h, :, :PAIR] = jnp.where(mine_k, k, jnp.zeros_like(k))
        ka[h, :, PAIR:] = (minus + bias).astype(BF)
        va[h, :, :PAIR] = jnp.where(mine_k, v, jnp.zeros_like(v))
        va[h, :, PAIR:] = minus.astype(BF)
        qm[h] = jnp.where(mine_q, q, jnp.zeros_like(q))
        dm[h] = jnp.where(mine_q, do, jnp.zeros_like(do))
    kt[...] = k.T
    dqt[...] = jnp.zeros_like(dqt)

    nq, nk = span // tq, keys // tk

    def key_step(j, _):
        at_k = pl.ds(pl.multiple_of(j * tk, tk), tk)
        dk_acc[...] = jnp.zeros_like(dk_acc)
        dv_acc[...] = jnp.zeros_like(dv_acc)

        def query_step(i, _):
            at_q = pl.ds(pl.multiple_of(i * tq, tq), tq)
            dv, dk = None, None
            for h in range(2):
                st = dot_nt(ka[h, at_k, :], qa[at_q, :])
                dpt = dot_nt(va[h, at_k, :], da[at_q, :])
                p = jnp.exp2(st)
                ds = (p * dpt).astype(BF)
                pv = dot(p.astype(BF), dm[h, at_q, :])
                pk = dot(ds, qm[h, at_q, :])
                dv = pv if dv is None else dv + pv
                dk = pk if dk is None else dk + pk
                head = slice(h * HEAD, (h + 1) * HEAD)
                dqt[head, at_q] += dot(kt[head, at_k], ds)
            dv_acc[...] += dv
            dk_acc[...] += dk
            return 0

        lax.fori_loop(0, nq, query_step, 0, unroll=True)
        dv_ref[0, at_k, :] = dv_acc[...].astype(dv_ref.dtype)
        g = dk_acc[...] * LN2
        if dk_ref.dtype == BF:
            g = back_turn(g, ck_ref[at_k, :], sk_ref[at_k, :])
        dk_ref[0, at_k, :] = g.astype(dk_ref.dtype)
        return 0

    lax.fori_loop(0, nk, key_step, 0)
    g = dqt[...].T * 0.125
    dq_ref[0] = back_turn(g, cq_ref[...], sq_ref[...]).astype(BF)


def back_turn(g, cosine, sine):
    return g * cosine - turn(g * sine)


def attend_back_call(q, k, v, bias, o, do, aug, cq, sq, ck, sk, whole, tk=1024, tq=512):
    rows, span, width = q.shape
    keys = k.shape[1]
    tq = min(tq, span)
    tk = min(tk, keys)
    qs = pl.BlockSpec((1, span, PAIR), lambda r, p: (r, 0, p))
    ks = pl.BlockSpec((1, keys, PAIR), lambda r, p: (r, 0, p))
    tq_s = pl.BlockSpec((span, PAIR), lambda r, p: (0, 0))
    tk_s = pl.BlockSpec((keys, PAIR), lambda r, p: (0, 0))
    kv_type = BF if whole else F32
    return pl.pallas_call(
        functools.partial(attend_back_kernel, tk, tq),
        grid=(rows, width // PAIR),
        in_specs=[
            qs, ks, ks, pl.BlockSpec((1, keys, PAIR), lambda r, p: (r, 0, 0)), qs, qs, qs,
            tq_s, tq_s, tk_s, tk_s,
        ],
        out_specs=[qs, ks, ks],
        out_shape=[
            jax.ShapeDtypeStruct(q.shape, BF),
            jax.ShapeDtypeStruct(k.shape, kv_type),
            jax.ShapeDtypeStruct(k.shape, kv_type),
        ],
        scratch_shapes=[
            pltpu.VMEM((span, 2 * PAIR), BF),
            pltpu.VMEM((2, keys, 2 * PAIR), BF),
            pltpu.VMEM((2, keys, 2 * PAIR), BF),
            pltpu.VMEM((span, 2 * PAIR), BF),
            pltpu.VMEM((2, span, PAIR), BF),
            pltpu.VMEM((2, span, PAIR), BF),
            pltpu.VMEM((PAIR, keys), BF),
            pltpu.VMEM((PAIR, span), F32),
            pltpu.VMEM((tk, PAIR), F32),
            pltpu.VMEM((tk, PAIR), F32),
        ],
        compiler_params=params(),
        name="attend_back",
    )(q, k, v, bias, o, do, aug, cq, sq, ck, sk)


def middle_kernel(
    chunk, x_ref, att_ref, cot_ref, wo_ref, wg_ref, wu_ref, wd_ref, g1_ref, g2_ref,
    out_ref, dfirst_ref, datt_ref, act_ref, dg_ref, du_ref, ht_ref, dft_ref, at_ref, gg1_ref, gg2_ref,
    ca, cb,
):
    @pl.when(pl.program_id(0) == 0)
    def _():
        gg1_ref[...] = jnp.zeros_like(gg1_ref)
        gg2_ref[...] = jnp.zeros_like(gg2_ref)

    gain1, gain2 = g1_ref[...], g2_ref[...]
    att = att_ref[...]
    at_ref[...] = att.T
    first = x_ref[...].astype(F32) + dot(att, wo_ref[...])
    centered = first - jnp.mean(first, axis=1, keepdims=True)
    s1 = lax.rsqrt(jnp.mean(centered * centered, axis=1, keepdims=True) + EPS)
    n1 = centered * s1
    hidden = n1 * gain1
    low = hidden.astype(BF)
    ht_ref[...] = low.T
    hidden_width = wg_ref.shape[1]
    second = hidden
    for c in range(hidden_width // chunk):
        at = slice(c * chunk, (c + 1) * chunk)
        g = dot(low, wg_ref[:, at])
        u = dot(low, wu_ref[:, at])
        sig = jax.nn.sigmoid(g)
        silu = g * sig
        act = (silu * u).astype(BF)
        act_ref[:, at] = act
        ca[:, at] = (u * (sig + silu * (1.0 - sig))).astype(ca.dtype)
        cb[:, at] = silu.astype(cb.dtype)
        second = second + dot(act, wd_ref[at, :])
    centered = second - jnp.mean(second, axis=1, keepdims=True)
    s2 = lax.rsqrt(jnp.mean(centered * centered, axis=1, keepdims=True) + EPS)
    n2 = centered * s2
    out_ref[...] = (n2 * gain2).astype(BF)
    dy = cot_ref[...].astype(F32)
    gg2_ref[...] += jnp.sum(dy * n2, axis=0, keepdims=True)
    inner = dy * gain2
    d_second = s2 * (
        inner - jnp.mean(inner, axis=1, keepdims=True) - n2 * jnp.mean(inner * n2, axis=1, keepdims=True)
    )
    d_ffn = d_second.astype(BF)
    dft_ref[...] = d_ffn.T
    d_hidden = d_second
    for c in range(hidden_width // chunk):
        at = slice(c * chunk, (c + 1) * chunk)
        d_act = dot_nt(d_ffn, wd_ref[at, :])
        dg = (d_act * ca[:, at]).astype(BF)
        du = (d_act * cb[:, at]).astype(BF)
        dg_ref[:, at] = dg
        du_ref[:, at] = du
        d_hidden = d_hidden + dot_nt(dg, wg_ref[:, at]) + dot_nt(du, wu_ref[:, at])
    gg1_ref[...] += jnp.sum(d_hidden * n1, axis=0, keepdims=True)
    inner = d_hidden * gain1
    d_first = s1 * (
        inner - jnp.mean(inner, axis=1, keepdims=True) - n1 * jnp.mean(inner * n1, axis=1, keepdims=True)
    )
    low = d_first.astype(BF)
    dfirst_ref[...] = low
    datt_ref[...] = dot_nt(low, wo_ref[...]).astype(BF)


def middle_call(x, att, cot, wo, wg, wu, wd, g1, g2, tile=256, chunk=768):
    tokens, width = x.shape
    hidden_width = wg.shape[1]
    tile = min(tile, tokens)
    row = pl.BlockSpec((tile, width), lambda i: (i, 0))
    wide = pl.BlockSpec((tile, hidden_width), lambda i: (i, 0))
    column = pl.BlockSpec((width, tile), lambda i: (0, i))

    def whole(a):
        return pl.BlockSpec(a.shape, lambda i: (0, 0), pipeline_mode=pl.Buffered(1))

    gain = pl.BlockSpec((1, width), lambda i: (0, 0))
    return pl.pallas_call(
        functools.partial(middle_kernel, chunk),
        grid=(tokens // tile,),
        in_specs=[row, row, row, whole(wo), whole(wg), whole(wu), whole(wd), gain, gain],
        out_specs=[row, row, row, wide, wide, wide, column, column, column, gain, gain],
        out_shape=[jax.ShapeDtypeStruct((tokens, width), BF)] * 3
        + [jax.ShapeDtypeStruct((tokens, hidden_width), BF)] * 3
        + [jax.ShapeDtypeStruct((width, tokens), BF)] * 3
        + [jax.ShapeDtypeStruct((1, width), F32)] * 2,
        scratch_shapes=[pltpu.VMEM((tile, hidden_width), F32)] * 2,
        compiler_params=params(),
        name="middle",
    )(x, att, cot, wo, wg, wu, wd, g1, g2)


def outer_kernel(a_ref, b_ref, o_ref):
    o_ref[...] = dot(a_ref[...], b_ref[...]).astype(o_ref.dtype)


def outer_call(a, b, out_type, tile=512):
    rows, tokens = a.shape
    columns = b.shape[1]
    tile = tile if columns % tile == 0 else 256
    return pl.pallas_call(
        outer_kernel,
        grid=(columns // tile,),
        in_specs=[
            pl.BlockSpec((rows, tokens), lambda i: (0, 0), pipeline_mode=pl.Buffered(1)),
            pl.BlockSpec((tokens, tile), lambda i: (0, i)),
        ],
        out_specs=pl.BlockSpec((rows, tile), lambda i: (0, i)),
        out_shape=jax.ShapeDtypeStruct((rows, columns), out_type),
        compiler_params=params(),
        name="outer",
    )(a, b)


def tokens_kernel(dq_ref, dk_ref, dv_ref, dfirst_ref, w_ref, o_ref):
    width = dq_ref.shape[1]
    total = dfirst_ref[...].astype(F32)
    total += dot_nt(dq_ref[...], w_ref[:, :width])
    total += dot_nt(dk_ref[...], w_ref[:, width : 2 * width])
    total += dot_nt(dv_ref[...], w_ref[:, 2 * width :])
    o_ref[...] = total.astype(BF)


def tokens_call(dq, dk, dv, dfirst, w, tile=512):
    tokens, width = dq.shape
    tile = min(tile, tokens)
    row = pl.BlockSpec((tile, width), lambda i: (i, 0))
    return pl.pallas_call(
        tokens_kernel,
        grid=(tokens // tile,),
        in_specs=[row] * 4 + [pl.BlockSpec(w.shape, lambda i: (0, 0), pipeline_mode=pl.Buffered(1))],
        out_specs=row,
        out_shape=jax.ShapeDtypeStruct((tokens, width), BF),
        compiler_params=params(),
        name="grad_tokens",
    )(dq, dk, dv, dfirst, w)


def angle_tables(span):
    index = np.arange(HEAD // 2, dtype=np.float64)
    inverse = np.power(1000.0, -2.0 * index / HEAD)
    angles = np.arange(span, dtype=np.float64)[:, None] * inverse[None, :]
    repeat = (1, PAIR // (HEAD // 2))
    return (
        np.tile(np.cos(angles), repeat).astype(np.float32),
        np.tile(np.sin(angles), repeat).astype(np.float32),
    )


def swap(a, mine):
    keep = lax.dynamic_index_in_dim(a, mine, 0, keepdims=False)
    give = lax.dynamic_index_in_dim(a, 1 - mine, 0, keepdims=False)
    got = lax.ppermute(give, "blk", [(0, 1), (1, 0)])
    low = jnp.where(mine == 0, keep, got)
    high = jnp.where(mine == 0, got, keep)
    return jnp.stack([low, high])


def body(tokens, lengths, w_qkv, w_out, w_gate, w_up, w_down, gain_one, gain_two, cotangent):
    axes = ("dp", "blk")
    blk = lax.axis_size("blk")
    mine = lax.axis_index("blk")
    rows, span, width = tokens.shape
    seq = span * blk
    own = blk == 2 and rows == 2 and lax.axis_size("dp") == 16

    def gather(a):
        return lax.all_gather(a, axes, axis=0, tiled=True)

    cosine, sine = map(jnp.asarray, angle_tables(seq))
    gains = jnp.stack([gain_one, gain_two], 1)
    if own:
        x, f_qkv = opening_call(tokens, w_qkv)
        x = x.reshape(1, seq, width)
        f_qkv = f_qkv.reshape(width, -1)
        length = lax.dynamic_slice_in_dim(lengths, mine, 1, 0)
        cq, sq = cosine, sine
    else:
        f_qkv, f_out, f_gate, f_up, f_down = map(gather, (w_qkv, w_out, w_gate, w_up, w_down))
        f_gains = gather(gains).astype(F32)
        x, cot, length = tokens, cotangent, lengths
        cq = lax.dynamic_slice_in_dim(cosine, mine * span, span, 0)
        sq = lax.dynamic_slice_in_dim(sine, mine * span, span, 0)
    n, t = x.shape[:2]
    flat = x.reshape(n * t, width)
    q, k, v, xt = qkv_call(flat, f_qkv, cq, sq)
    q, k, v = (a.reshape(n, t, width) for a in (q, k, v))
    if not own:
        k = lax.all_gather(k, "blk", axis=1, tiled=True)
        v = lax.all_gather(v, "blk", axis=1, tiled=True)
    position = jnp.arange(seq, dtype=jnp.int32)[None, :, None]
    lane = jnp.arange(PAIR, dtype=jnp.int32)[None, None, :]
    bias = jnp.where((lane == 3) & (position >= length[:, None, None]), NEG, 0.0).astype(BF)
    if own:
        w_out = jnp.pad(jnp.concatenate([w_out, gains], 1), ((0, 0), (0, PAIR - 2)))
        att, aug, cot, f_out, f_gate, f_up, f_down = attend_call(
            q, k, v, bias, (cotangent, w_out, w_gate, w_up, w_down)
        )
        f_out = f_out.reshape(width, -1)
        f_out, f_gains = f_out[:, :width], f_out[:, width : width + 2].astype(F32)
        f_gate, f_up = f_gate.reshape(width, -1), f_up.reshape(width, -1)
        f_down = f_down.reshape(-1, width)
    else:
        att, aug = attend_call(q, k, v, bias)
    g1, g2 = f_gains[:, 0][None], f_gains[:, 1][None]
    out, d_first, d_att, act, d_gate, d_up, h_t, df_t, att_t, gg1, gg2 = middle_call(
        flat, att.reshape(n * t, width), cot.reshape(n * t, width), f_out, f_gate, f_up, f_down, g1, g2
    )
    gw_gate = outer_call(h_t, d_gate, BF)
    gw_up = outer_call(h_t, d_up, BF)
    gw_down_t = outer_call(df_t, act, BF)
    gw_out = outer_call(att_t, d_first, BF)

    def scatter_wide(g):
        g = lax.psum_scatter(g, "blk", scatter_dimension=1, tiled=True)
        return lax.psum_scatter(g, "dp", scatter_dimension=0, tiled=True).astype(F32)

    s_gate, s_up, s_down_t = map(scatter_wide, (gw_gate, gw_up, gw_down_t))
    s_down = s_down_t.T
    dq, dk, dv = attend_back_call(
        q, k, v, bias, att, d_att.reshape(n, t, width), aug, cq, sq, cosine, sine, own
    )
    if not own:
        dk = lax.psum_scatter(dk, "blk", scatter_dimension=1, tiled=True)
        dv = lax.psum_scatter(dv, "blk", scatter_dimension=1, tiled=True)
        heads = (dk * jnp.tile(sq, (1, width // PAIR))).reshape(n, t, HEADS, HEAD)
        half = jnp.concatenate([heads[..., HEAD // 2 :], -heads[..., : HEAD // 2]], -1)
        dk = dk * jnp.tile(cq, (1, width // PAIR)) + half.reshape(n, t, width)
        dk, dv = dk.astype(BF), dv.astype(BF)
    dq, dk, dv = (a.reshape(n * t, width) for a in (dq, dk, dv))
    gw_qkv = jnp.concatenate([outer_call(xt, a, BF, 256) for a in (dq, dk, dv)], 1)
    g_tokens = tokens_call(dq, dk, dv, d_first, f_qkv)
    s_qkv = lax.psum_scatter(gw_qkv, axes, scatter_dimension=0, tiled=True).astype(F32)
    s_out = lax.psum_scatter(gw_out, axes, scatter_dimension=0, tiled=True).astype(F32)
    gg = jnp.concatenate([gg1, gg2]).T
    s_gg = lax.psum_scatter(gg, axes, scatter_dimension=0, tiled=True)
    if own:
        out = swap(out.reshape(2, span, width), mine)
        g_tokens = swap(g_tokens.reshape(2, span, width), mine)
    else:
        out = out.reshape(tokens.shape)
        g_tokens = g_tokens.reshape(tokens.shape)
    return (out, g_tokens, s_qkv, s_out, s_gate, s_up, s_down, s_gg[:, 0], s_gg[:, 1])


def solution(mesh):
    both = ("dp", "blk")
    return jax.shard_map(
        body,
        mesh=mesh,
        in_specs=(
            P("dp", "blk", None),
            P("dp"),
            P(both, None),
            P(both, None),
            P(both, None),
            P(both, None),
            P(both, None),
            P(both),
            P(both),
            P("dp", "blk", None),
        ),
        out_specs=(
            P("dp", "blk", None),
            P("dp", "blk", None),
            P(both, None),
            P(both, None),
            P("dp", "blk"),
            P("dp", "blk"),
            P("blk", "dp"),
            P(both),
            P(both),
        ),
        check_vma=False,
    )
```

```python
import functools

import jax
import jax.numpy as jnp
import numpy as np
from jax import lax
from jax.experimental import pallas as pl
from jax.experimental.pallas import tpu as pltpu
from jax.sharding import PartitionSpec as P

HEADS = 12
HEAD = 64
PAIR = 2 * HEAD
EPS = 1e-05
NEG = -1e30
LOG2E = 1.4426950408889634
LN2 = 0.6931471805599453
VMEM_LIMIT = 60 * 1024 * 1024

BF = jnp.bfloat16
F32 = jnp.float32


def dot(a, b):
    return lax.dot_general(a, b, (((1,), (0,)), ((), ())), preferred_element_type=F32)


def dot_nt(a, b):
    return lax.dot_general(a, b, (((1,), (1,)), ((), ())), preferred_element_type=F32)


def params(limit=VMEM_LIMIT):
    return pltpu.CompilerParams(vmem_limit_bytes=limit)


def lanes(shape):
    return lax.broadcasted_iota(jnp.int32, shape, 1)


def turn(u):
    low_half = (lanes(u.shape) % HEAD) < HEAD // 2
    return jnp.where(low_half, -pltpu.roll(u, PAIR - HEAD // 2, 1), pltpu.roll(u, HEAD // 2, 1))


MESH = pl.DeviceIdType.MESH
AXES = "zxcy"
SIZE = {"z": 4, "x": 2, "c": 2, "y": 2}


def place():
    dp, y = lax.axis_index("dp"), lax.axis_index("blk")
    return {"z": dp // 4, "x": dp // 2 % 2, "c": dp % 2, "y": y}


def moved(me, axis, by):
    return {**me, axis: lax.rem(me[axis] + by, SIZE[axis])}


def device(at):
    return ((at["z"] * 2 + at["x"]) * 2 + at["c"], at["y"])


def greet(me):
    barrier = pltpu.get_barrier_semaphore()
    peers = [moved(me, "y", 1), moved(me, "x", 1), moved(me, "c", 1)]
    peers += [moved(me, "z", d) for d in range(1, 4)]
    for peer in peers:
        pl.semaphore_signal(barrier, inc=1, device_id=device(peer), device_id_type=MESH)
    pl.semaphore_wait(barrier, len(peers))


class Gather:
    SEMS = 6

    def __init__(self, me, shard, full, send, recv, local, base, order):
        self.me, self.shard, self.full = me, shard, full
        self.send, self.recv, self.local, self.base, self.order = send, recv, local, base, order

    def view(self, at, got):
        return self.full.at[tuple(slice(None) if a in got else at[a] for a in AXES)]

    def copies(self, stage):
        got = self.order[:stage]
        axis = self.order[stage]
        slot = self.base + sum(SIZE[a] - 1 for a in got)
        out = []
        for d in range(1, SIZE[axis]):
            here = self.view(self.me, got)
            out.append(
                pltpu.make_async_remote_copy(
                    src_ref=self.shard if stage == 0 else here,
                    dst_ref=here,
                    send_sem=self.send.at[slot + d - 1],
                    recv_sem=self.recv.at[slot + d - 1],
                    device_id=device(moved(self.me, axis, d)),
                    device_id_type=MESH,
                )
            )
        return out

    def own(self):
        return pltpu.make_async_copy(self.shard, self.view(self.me, ""), self.local)

    def arrivals(self, stage):
        got = self.order[:stage]
        axis = self.order[stage]
        slot = self.base + sum(SIZE[a] - 1 for a in got)
        for d in range(1, SIZE[axis]):
            there = self.view(moved(self.me, axis, SIZE[axis] - d), got)
            pltpu.make_async_remote_copy(
                src_ref=there,
                dst_ref=there,
                send_sem=self.send.at[slot + d - 1],
                recv_sem=self.recv.at[slot + d - 1],
                device_id=device(moved(self.me, axis, d)),
                device_id_type=MESH,
            ).wait_recv()

    def start(self):
        self.own().start()
        for copy in self.copies(0):
            copy.start()

    def step(self, stage):
        self.arrivals(stage - 1)
        if stage == 1:
            self.own().wait()
        if stage < len(self.order):
            for copy in self.copies(stage):
                copy.start()

    def finish(self):
        for stage in range(len(self.order)):
            for copy in self.copies(stage):
                copy.wait_send()


class Reduce:
    SEMS = 7

    def __init__(self, me, piece, bufs, out, send, recv, local, base, order):
        self.me, self.piece, self.out, self.order = me, piece, out, order
        self.b, self.r0, self.r1, self.r2, self.r3 = bufs
        self.send, self.recv, self.local, self.base = send, recv, local, base

    def copy(self, source, target, slot, axis, by=1):
        return pltpu.make_async_remote_copy(
            src_ref=source,
            dst_ref=target,
            send_sem=self.send.at[self.base + slot],
            recv_sem=self.recv.at[self.base + slot],
            device_id=device(moved(self.me, axis, by)),
            device_id_type=MESH,
        )

    def mine(self):
        c = self.me["c"]
        return [
            pltpu.make_async_copy(self.piece(c, y), self.b.at[y], self.local.at[y]) for y in range(2)
        ]

    def copies(self, stage):
        x, y, z = self.me["x"], self.me["y"], self.me["z"]
        if stage == 0:
            other = 1 - self.me["c"]
            return [self.copy(self.piece(other, i), self.r0.at[i], i, "c") for i in range(2)]
        if stage == 1:
            source = self.b.at[1 - y] if self.order[0] == "y" else self.b.at[:, :, 1 - x]
            return [self.copy(source, self.r1, 2, self.order[0])]
        if stage == 2:
            source = self.b.at[y, :, 1 - x] if self.order[0] == "y" else self.b.at[1 - y, :, x]
            return [self.copy(source, self.r2, 3, self.order[1])]
        return [
            self.copy(self.b.at[y, lax.rem(z + d, 4), x], self.r3.at[d - 1], 3 + d, "z", d)
            for d in range(1, 4)
        ]

    def start(self):
        for copy in self.copies(0) + self.mine():
            copy.start()

    def step(self, stage):
        x, y, z = self.me["x"], self.me["y"], self.me["z"]
        for copy in self.copies(stage - 1):
            copy.wait_recv()
        b, kind = self.b, self.b.dtype
        if stage == 1:
            for copy in self.mine():
                copy.wait()

            def add(i, _):
                at = (i // 4, i % 4)
                b[at] = (b[at].astype(F32) + self.r0[at].astype(F32)).astype(kind)
                return 0

            lax.fori_loop(0, 8, add, 0)
        if stage == 2:

            def add(i, _):
                if self.order[0] == "y":
                    for j in range(2):
                        b[y, i, j] = (b[y, i, j].astype(F32) + self.r1[i, j].astype(F32)).astype(kind)
                else:
                    for j in range(2):
                        b[j, i, x] = (b[j, i, x].astype(F32) + self.r1[j, i].astype(F32)).astype(kind)
                return 0

            lax.fori_loop(0, 4, add, 0)
        if stage == 3:

            def add(i, _):
                b[y, i, x] = (b[y, i, x].astype(F32) + self.r2[i].astype(F32)).astype(kind)
                return 0

            lax.fori_loop(0, 4, add, 0)
        if stage == 4:
            total = b[y, z, x].astype(F32)
            for d in range(3):
                total = total + self.r3[d].astype(F32)
            self.out[...] = total
            return
        for copy in self.copies(stage):
            copy.start()

    def finish(self):
        for stage in range(4):
            for copy in self.copies(stage):
                copy.wait_send()

    @staticmethod
    def scratch(rows, columns, kind, order):
        lead = (4, 2) if order[0] == "y" else (2, 4)
        return [
            pltpu.VMEM(shape + (rows, columns), kind)
            for shape in ((2, 4, 2), (2, 4, 2), lead, (4,), (3,))
        ]


def swap_copies(me, source, target, send, recv, local, slot):
    other = moved(me, "y", 1)
    y = me["y"]
    keep = pltpu.make_async_copy(source.at[y], target.at[y], local)
    give = pltpu.make_async_remote_copy(
        src_ref=source.at[1 - y],
        dst_ref=target.at[y],
        send_sem=send.at[slot],
        recv_sem=recv.at[slot],
        device_id=device(other),
        device_id_type=MESH,
    )
    take = pltpu.make_async_remote_copy(
        src_ref=target.at[1 - y],
        dst_ref=target.at[1 - y],
        send_sem=send.at[slot],
        recv_sem=recv.at[slot],
        device_id=device(other),
        device_id_type=MESH,
    )
    return keep, give, take


def opening_kernel(tok_ref, qkv_ref, x_ref, full_ref, send, recv, local):
    me = place()
    greet(me)
    keep, give, take = swap_copies(me, tok_ref, x_ref, send, recv, local.at[0], 0)
    gather = Gather(me, qkv_ref, full_ref, send, recv, local.at[1], 1, "yzxc")
    gather.start()
    give.start()
    keep.start()
    for stage in range(1, 5):
        gather.step(stage)
    gather.finish()
    take.wait_recv()
    give.wait_send()
    keep.wait()


def opening_call(tokens, w_qkv):
    hbm = pl.BlockSpec(memory_space=pl.ANY)
    return pl.pallas_call(
        opening_kernel,
        in_specs=[hbm, hbm],
        out_specs=[hbm, hbm],
        out_shape=[
            jax.ShapeDtypeStruct(tokens.shape, BF),
            jax.ShapeDtypeStruct((4, 2, 2, 2) + w_qkv.shape, BF),
        ],
        scratch_shapes=[
            pltpu.SemaphoreType.DMA((1 + Gather.SEMS,)),
            pltpu.SemaphoreType.DMA((1 + Gather.SEMS,)),
            pltpu.SemaphoreType.DMA((2,)),
        ],
        compiler_params=pltpu.CompilerParams(collective_id=0, has_side_effects=True),
        name="opening",
    )(tokens, w_qkv)


def qkv_kernel(x_ref, w_ref, cos_ref, sin_ref, q_ref, k_ref, v_ref, xt_ref):
    x = x_ref[...]
    width = x.shape[1]
    cosine, sine = cos_ref[...], sin_ref[...]
    for part, out in ((0, q_ref), (1, k_ref), (2, v_ref)):
        for pair in range(width // PAIR):
            at = part * width + pair * PAIR
            if pair % 2 == 0:
                u2 = dot(x, w_ref[:, at : at + 2 * PAIR])
            u = u2[:, (pair % 2) * PAIR : (pair % 2 + 1) * PAIR]
            if part < 2:
                u = u * cosine + turn(u) * sine
            if part == 0:
                u = u * (0.125 * LOG2E)
            out[:, pair * PAIR : (pair + 1) * PAIR] = u.astype(BF)
    xt_ref[...] = x.T


def qkv_call(x, w, cosine, sine, tile=512):
    tokens, width = x.shape
    span = cosine.shape[0]
    tile = min(tile, span)
    row = pl.BlockSpec((tile, width), lambda i: (i, 0))
    table = pl.BlockSpec((tile, PAIR), lambda i: (i % (span // tile), 0))
    return pl.pallas_call(
        qkv_kernel,
        grid=(tokens // tile,),
        in_specs=[
            row,
            pl.BlockSpec(w.shape, lambda i: (0, 0), pipeline_mode=pl.Buffered(1)),
            table,
            table,
        ],
        out_specs=[row, row, row, pl.BlockSpec((width, tile), lambda i: (0, i))],
        out_shape=[jax.ShapeDtypeStruct((tokens, width), BF)] * 3
        + [jax.ShapeDtypeStruct((width, tokens), BF)],
        compiler_params=params(),
        name="qkv",
    )(x, w, cosine, sine)


def attend_kernel(tile, chunk, moves, q_ref, k_ref, v_ref, bias_ref, *rest):
    inputs, rest = rest[: moves], rest[moves:]
    o_ref, aug_ref, rest = rest[0], rest[1], rest[2:]
    outputs, rest = rest[: moves], rest[moves:]
    ka, va, s_scr, m_scr = rest[:4]
    keys, span = k_ref.shape[1], q_ref.shape[1]
    tiles = span // tile
    events = {}
    if moves:
        events = attend_events(inputs, outputs, tiles * pl.num_programs(1), *rest[4:])
    lane = lanes((keys, PAIR))
    k, v = k_ref[0], v_ref[0]
    zero = jnp.zeros_like(k)
    for h in range(2):
        mine = (lane // HEAD) == h
        ka[h, :, :PAIR] = jnp.where(mine, k, zero)
        ka[h, :, PAIR:] = bias_ref[0]
        va[h, :, :PAIR] = jnp.where(mine, v, zero)
        va[h, :, PAIR:] = mine.astype(F32).astype(BF)
    lane = lanes((tile, PAIR))
    ones = (lane == 3).astype(F32).astype(BF)
    chunks = keys // chunk

    def score(i, h, c, top):
        at = pl.ds(pl.multiple_of(i * tile, tile), tile)
        qa = jnp.concatenate([q_ref[0, at, :], ones], axis=1)
        s = dot_nt(qa, ka[h, c * chunk : (c + 1) * chunk, :])
        s_scr[h, :, c * chunk : (c + 1) * chunk] = s
        for b in range(chunk // PAIR):
            part = s[:, b * PAIR : (b + 1) * PAIR]
            top = part if top is None else jnp.maximum(top, part)
        return top

    def close(h, top):
        m_scr[h] = jnp.broadcast_to(jnp.max(top, axis=1, keepdims=True), (tile, PAIR))

    def unit(h, later, other):
        m = m_scr[h]
        wide = jnp.concatenate([m] * (chunk // PAIR), axis=1)
        acc, top = None, None
        for c in range(chunks):
            top = score(later, other, c, top)
            p = jnp.exp2(s_scr[h, :, c * chunk : (c + 1) * chunk] - wide).astype(BF)
            part = dot(p, va[h, c * chunk : (c + 1) * chunk, :])
            acc = part if acc is None else acc + part
        return acc, top, m

    top = None
    for c in range(chunks):
        top = score(0, 0, c, top)
    close(0, top)

    def step(i, _):
        now = pl.program_id(1) * tiles + i
        for at_step, act in events.items():
            pl.when(now == at_step)(act)
        acc0, top, m0 = unit(0, i, 1)
        close(1, top)
        acc1, top, m1 = unit(1, jnp.minimum(i + 1, tiles - 1), 0)
        close(0, top)
        acc = acc0 + acc1
        total = acc[:, PAIR:]
        at = pl.ds(pl.multiple_of(i * tile, tile), tile)
        o_ref[0, at, :] = (acc[:, :PAIR] / total).astype(BF)
        lse = jnp.where(lane < HEAD, m0, m1) + jnp.log2(total)
        aug_ref[0, at, :] = spread(lse, jnp.where(lane == 3, 1.0, 0.0))
        return 0

    lax.fori_loop(0, tiles, step, 0)
    if moves:
        pl.when(pl.program_id(1) == pl.num_programs(1) - 1)(events.last)


class Events(dict):
    last = None


def attend_events(inputs, outputs, steps, send, recv, local):
    me = place()
    cot_in, shards = inputs[0], inputs[1:]
    cot_out, fulls = outputs[0], outputs[1:]
    keep, give, take = swap_copies(me, cot_in, cot_out, send, recv, local.at[0], 0)
    orders = ["zxyc", "zxyc", "zyxc", "yzxc"]
    gathers = [
        Gather(me, shard, full, send, recv, local.at[1 + i], 1 + i * Gather.SEMS, orders[i])
        for i, (shard, full) in enumerate(zip(shards, fulls))
    ]

    def begin():
        greet(me)
        for g in gathers:
            g.start()
        give.start()
        keep.start()

    def stage(g, n):
        return lambda: g.step(n)

    def last():
        for n, g in pending:
            g.step(n)
        for g in gathers:
            g.finish()
        take.wait_recv()
        give.wait_send()
        keep.wait()

    events = Events()
    events[0] = begin
    todo = [(n, g) for n in (1, 2, 3, 4) for g in gathers]
    times = [4, 6, 9, 5, 6, 9, 12, 11, 12, 16, 19, 20]
    for at, (n, g) in zip(times, todo):
        old = events.get(at)
        new = stage(g, n)
        events[at] = new if old is None else (lambda old=old, new=new: (old(), new(), None)[2])
    pending = todo[len(times) :]
    events.last = last
    return events


def spread(value, other):
    high = value.astype(BF).astype(F32)
    rest = value - high
    mid = rest.astype(BF).astype(F32)
    low = rest - mid
    sub = lanes(value.shape) % HEAD
    return jnp.where(
        sub == 0, high, jnp.where(sub == 1, mid, jnp.where(sub == 2, low, other))
    ).astype(BF)


def attend_call(q, k, v, bias, moving=(), tile=512, chunk=512):
    rows, span, width = q.shape
    keys = k.shape[1]
    tile = min(tile, span)
    moves = len(moving)
    qs = pl.BlockSpec((1, span, PAIR), lambda r, p: (r, 0, p))
    ks = pl.BlockSpec((1, keys, PAIR), lambda r, p: (r, 0, p))
    hbm = pl.BlockSpec(memory_space=pl.ANY)
    moved_shapes = [jax.ShapeDtypeStruct(a.shape, a.dtype) for a in moving[:1]] + [
        jax.ShapeDtypeStruct((4, 2, 2, 2) + a.shape, a.dtype) for a in moving[1:]
    ]
    sems = 1 + Gather.SEMS * max(moves - 1, 0)
    extra = [pltpu.SemaphoreType.DMA((sems,))] * 2 + [pltpu.SemaphoreType.DMA((moves,))]
    more = dict(collective_id=1, has_side_effects=True) if moves else {}
    return pl.pallas_call(
        functools.partial(attend_kernel, tile, chunk, moves),
        grid=(rows, width // PAIR),
        in_specs=[qs, ks, ks, pl.BlockSpec((1, keys, PAIR), lambda r, p: (r, 0, 0))] + [hbm] * moves,
        out_specs=[qs, qs] + [hbm] * moves,
        out_shape=[jax.ShapeDtypeStruct(q.shape, BF)] * 2 + moved_shapes,
        scratch_shapes=[
            pltpu.VMEM((2, keys, 2 * PAIR), BF),
            pltpu.VMEM((2, keys, 2 * PAIR), BF),
            pltpu.VMEM((2, tile, keys), F32),
            pltpu.VMEM((2, tile, PAIR), F32),
        ]
        + (extra if moves else []),
        compiler_params=pltpu.CompilerParams(vmem_limit_bytes=VMEM_LIMIT, **more),
        name="attend",
    )(q, k, v, bias, *moving)


def attend_back_kernel(
    tk, tq, moves, q_ref, k_ref, v_ref, bias_ref, o_ref, do_ref, aug_ref, cos_ref, sin_ref, *rest
):
    inputs, rest = rest[:moves], rest[moves:]
    dq_ref, dk_ref, dv_ref, rest = rest[0], rest[1], rest[2], rest[3:]
    outputs, rest = rest[:moves], rest[moves:]
    qa, ka, va, da, qm, dm, kt, dqt, dk_acc, dv_acc = rest[:10]
    keys, span = k_ref.shape[1], q_ref.shape[1]
    nq, nk = span // tq, keys // tk
    events = {}
    if moves:
        events = back_events(inputs, outputs, *rest[10:])

    lane_k = lanes((keys, PAIR))
    lane_q = lanes((span, PAIR))
    q, k, v, do = q_ref[0], k_ref[0], v_ref[0], do_ref[0]
    bias = bias_ref[0].astype(F32)
    prod = do.astype(F32) * o_ref[0].astype(F32)
    first = prod.astype(BF)
    second = (prod - first.astype(F32)).astype(BF)
    block = (
        (lax.broadcasted_iota(jnp.int32, (PAIR, PAIR), 0) // HEAD)
        == (lax.broadcasted_iota(jnp.int32, (PAIR, PAIR), 1) // HEAD)
    ).astype(F32).astype(BF)
    delta = dot(first, block) + dot(second, block)
    qa[:, :PAIR] = q
    qa[:, PAIR:] = aug_ref[0]
    da[:, :PAIR] = do
    da[:, PAIR:] = spread(delta, jnp.zeros_like(delta))
    for h in range(2):
        mine_k = (lane_k // HEAD) == h
        mine_q = (lane_q // HEAD) == h
        minus = jnp.where(mine_k & (lane_k % HEAD < 3), -1.0, 0.0)
        ka[h, :, :PAIR] = jnp.where(mine_k, k, jnp.zeros_like(k))
        ka[h, :, PAIR:] = (minus + bias).astype(BF)
        va[h, :, :PAIR] = jnp.where(mine_k, v, jnp.zeros_like(v))
        va[h, :, PAIR:] = minus.astype(BF)
        qm[h] = jnp.where(mine_q, q, jnp.zeros_like(q))
        dm[h] = jnp.where(mine_q, do, jnp.zeros_like(do))
    kt[...] = k.T
    dqt[...] = jnp.zeros_like(dqt)

    def key_step(j, _):
        at_k = pl.ds(pl.multiple_of(j * tk, tk), tk)
        dk_acc[...] = jnp.zeros_like(dk_acc)
        dv_acc[...] = jnp.zeros_like(dv_acc)

        def query_step(i, _):
            now = (pl.program_id(1) * nk + j) * nq + i
            for at_step, act in events.items():
                pl.when(now == at_step)(act)
            at_q = pl.ds(pl.multiple_of(i * tq, tq), tq)
            dv, dk = None, None
            for h in range(2):
                st = dot_nt(ka[h, at_k, :], qa[at_q, :])
                dpt = dot_nt(va[h, at_k, :], da[at_q, :])
                p = jnp.exp2(st)
                ds = (p * dpt).astype(BF)
                pv = dot(p.astype(BF), dm[h, at_q, :])
                pk = dot(ds, qm[h, at_q, :])
                dv = pv if dv is None else dv + pv
                dk = pk if dk is None else dk + pk
                head = slice(h * HEAD, (h + 1) * HEAD)
                dqt[head, at_q] += dot(kt[head, at_k], ds)
            dv_acc[...] += dv
            dk_acc[...] += dk
            return 0

        lax.fori_loop(0, nq, query_step, 0)
        dv_ref[0, at_k, :] = dv_acc[...].astype(dv_ref.dtype)
        g = dk_acc[...] * LN2
        if dk_ref.dtype == BF:
            g = back_turn(g, cos_ref[at_k, :], sin_ref[at_k, :])
        dk_ref[0, at_k, :] = g.astype(dk_ref.dtype)
        return 0

    lax.fori_loop(0, nk, key_step, 0)
    g = dqt[...].T * 0.125
    dq_ref[0] = back_turn(g, cos_ref[...], sin_ref[...]).astype(BF)
    if moves:
        pl.when(pl.program_id(1) == pl.num_programs(1) - 1)(events.last)


def back_turn(g, cosine, sine):
    return g * cosine - turn(g * sine)


def wide_piece(source, columns):
    return lambda c, y: source.at[:, :, c, :, pl.ds(y * columns, columns)]


def tall_piece(source):
    return lambda c, y: source.at[:, :, c, y]


BACK_ORDERS = ("yx", "xy", "xy", "yx")


def back_events(inputs, outputs, send, recv, local, *bufs):
    me = place()
    keep, give, take = swap_copies(me, inputs[0], outputs[0], send, recv, local.at[0], 0)
    reduces = []
    for i, (source, out) in enumerate(zip(inputs[1:], outputs[1:])):
        piece = wide_piece(source, source.shape[-1] // 2) if len(source.shape) == 5 else tall_piece(source)
        reduces.append(
            Reduce(
                me, piece, bufs[5 * i : 5 * i + 5], out, send, recv,
                local.at[pl.ds(1 + 2 * i, 2)], 1 + i * Reduce.SEMS, BACK_ORDERS[i],
            )
        )

    def begin():
        greet(me)
        for r in reduces:
            r.start()
        give.start()
        keep.start()

    def last():
        for r in reduces:
            r.step(4)
        for r in reduces:
            r.finish()
        take.wait_recv()
        give.wait_send()
        keep.wait()

    events = Events()
    events[0] = begin
    todo = [(n, r) for n in (1, 2, 3) for r in reduces]
    for at, (n, r) in zip(BACK_TIMES, todo):
        assert at not in events
        events[at] = functools.partial(r.step, n)
    events.last = last
    return events


BACK_TIMES = (5, 6, 7, 8, 16, 17, 21, 18, 24, 28, 32, 25)


def attend_back_call(q, k, v, bias, o, do, aug, cosine, sine, whole, moving=(), tk=1024, tq=512):
    rows, span, width = q.shape
    keys = k.shape[1]
    tq = min(tq, span)
    tk = min(tk, keys)
    moves = len(moving)
    qs = pl.BlockSpec((1, span, PAIR), lambda r, p: (r, 0, p))
    ks = pl.BlockSpec((1, keys, PAIR), lambda r, p: (r, 0, p))
    table = pl.BlockSpec((span, PAIR), lambda r, p: (0, 0), pipeline_mode=pl.Buffered(1))
    hbm = pl.BlockSpec(memory_space=pl.ANY)
    kv_type = BF if whole else F32
    results, result_specs, extra, more = [], [], [], {}
    if moves:
        results.append(jax.ShapeDtypeStruct(moving[0].shape, BF))
        result_specs.append(hbm)
        sems = 1 + Reduce.SEMS * (moves - 1)
        extra = [pltpu.SemaphoreType.DMA((sems,))] * 2 + [pltpu.SemaphoreType.DMA((2 * moves - 1,))]
        for a, order in zip(moving[1:], BACK_ORDERS):
            block = (a.shape[-2], a.shape[-1] // (2 if a.ndim == 5 else 1))
            results.append(jax.ShapeDtypeStruct(block, F32))
            result_specs.append(pl.BlockSpec(block, lambda r, p: (0, 0)))
            extra += Reduce.scratch(*block, a.dtype, order)
        more = dict(collective_id=2, has_side_effects=True)
    return pl.pallas_call(
        functools.partial(attend_back_kernel, tk, tq, moves),
        grid=(rows, width // PAIR),
        in_specs=[
            qs, ks, ks, pl.BlockSpec((1, keys, PAIR), lambda r, p: (r, 0, 0)), qs, qs, qs, table, table,
        ]
        + [hbm] * moves,
        out_specs=[qs, ks, ks] + result_specs,
        out_shape=[
            jax.ShapeDtypeStruct(q.shape, BF),
            jax.ShapeDtypeStruct(k.shape, kv_type),
            jax.ShapeDtypeStruct(k.shape, kv_type),
        ]
        + results,
        scratch_shapes=[
            pltpu.VMEM((span, 2 * PAIR), BF),
            pltpu.VMEM((2, keys, 2 * PAIR), BF),
            pltpu.VMEM((2, keys, 2 * PAIR), BF),
            pltpu.VMEM((span, 2 * PAIR), BF),
            pltpu.VMEM((2, span, PAIR), BF),
            pltpu.VMEM((2, span, PAIR), BF),
            pltpu.VMEM((PAIR, keys), BF),
            pltpu.VMEM((PAIR, span), F32),
            pltpu.VMEM((tk, PAIR), F32),
            pltpu.VMEM((tk, PAIR), F32),
        ]
        + extra,
        compiler_params=pltpu.CompilerParams(vmem_limit_bytes=VMEM_LIMIT, **more),
        name="attend_back",
    )(q, k, v, bias, o, do, aug, cosine, sine, *moving)


def middle_kernel(
    chunk, x_ref, att_ref, cot_ref, wo_ref, wg_ref, wu_ref, wd_ref, g1_ref, g2_ref,
    out_ref, dfirst_ref, datt_ref, act_ref, dg_ref, du_ref, ht_ref, dft_ref, at_ref, gg1_ref, gg2_ref,
    ca, cb,
):
    @pl.when(pl.program_id(0) == 0)
    def _():
        gg1_ref[...] = jnp.zeros_like(gg1_ref)
        gg2_ref[...] = jnp.zeros_like(gg2_ref)

    gain1, gain2 = g1_ref[...], g2_ref[...]
    att = att_ref[...]
    at_ref[...] = att.T
    first = x_ref[...].astype(F32) + dot(att, wo_ref[...])
    centered = first - jnp.mean(first, axis=1, keepdims=True)
    s1 = lax.rsqrt(jnp.mean(centered * centered, axis=1, keepdims=True) + EPS)
    n1 = centered * s1
    hidden = n1 * gain1
    low = hidden.astype(BF)
    ht_ref[...] = low.T
    hidden_width = wg_ref.shape[1]
    second = hidden
    for c in range(hidden_width // chunk):
        at = slice(c * chunk, (c + 1) * chunk)
        g = dot(low, wg_ref[:, at])
        u = dot(low, wu_ref[:, at])
        sig = jax.nn.sigmoid(g)
        silu = g * sig
        act = (silu * u).astype(BF)
        act_ref[:, at] = act
        ca[:, at] = (u * (sig + silu * (1.0 - sig))).astype(ca.dtype)
        cb[:, at] = silu.astype(cb.dtype)
        second = second + dot(act, wd_ref[at, :])
    centered = second - jnp.mean(second, axis=1, keepdims=True)
    s2 = lax.rsqrt(jnp.mean(centered * centered, axis=1, keepdims=True) + EPS)
    n2 = centered * s2
    out_ref[...] = (n2 * gain2).astype(BF)
    dy = cot_ref[...].astype(F32)
    gg2_ref[...] += jnp.sum(dy * n2, axis=0, keepdims=True)
    inner = dy * gain2
    d_second = s2 * (
        inner - jnp.mean(inner, axis=1, keepdims=True) - n2 * jnp.mean(inner * n2, axis=1, keepdims=True)
    )
    d_ffn = d_second.astype(BF)
    dft_ref[...] = d_ffn.T
    d_hidden = d_second
    for c in range(hidden_width // chunk):
        at = slice(c * chunk, (c + 1) * chunk)
        d_act = dot_nt(d_ffn, wd_ref[at, :])
        dg = (d_act * ca[:, at]).astype(BF)
        du = (d_act * cb[:, at]).astype(BF)
        dg_ref[:, at] = dg
        du_ref[:, at] = du
        d_hidden = d_hidden + dot_nt(dg, wg_ref[:, at]) + dot_nt(du, wu_ref[:, at])
    gg1_ref[...] += jnp.sum(d_hidden * n1, axis=0, keepdims=True)
    inner = d_hidden * gain1
    d_first = s1 * (
        inner - jnp.mean(inner, axis=1, keepdims=True) - n1 * jnp.mean(inner * n1, axis=1, keepdims=True)
    )
    low = d_first.astype(BF)
    dfirst_ref[...] = low
    datt_ref[...] = dot_nt(low, wo_ref[...]).astype(BF)


def middle_call(x, att, cot, wo, wg, wu, wd, g1, g2, tile=256, chunk=768):
    tokens, width = x.shape
    hidden_width = wg.shape[1]
    tile = min(tile, tokens)
    row = pl.BlockSpec((tile, width), lambda i: (i, 0))
    wide = pl.BlockSpec((tile, hidden_width), lambda i: (i, 0))
    column = pl.BlockSpec((width, tile), lambda i: (0, i))

    def whole(a):
        return pl.BlockSpec(a.shape, lambda i: (0, 0), pipeline_mode=pl.Buffered(1))

    gain = pl.BlockSpec((1, width), lambda i: (0, 0))
    return pl.pallas_call(
        functools.partial(middle_kernel, chunk),
        grid=(tokens // tile,),
        in_specs=[row, row, row, whole(wo), whole(wg), whole(wu), whole(wd), gain, gain],
        out_specs=[row, row, row, wide, wide, wide, column, column, column, gain, gain],
        out_shape=[jax.ShapeDtypeStruct((tokens, width), BF)] * 3
        + [jax.ShapeDtypeStruct((tokens, hidden_width), BF)] * 3
        + [jax.ShapeDtypeStruct((width, tokens), BF)] * 3
        + [jax.ShapeDtypeStruct((1, width), F32)] * 2,
        scratch_shapes=[pltpu.VMEM((tile, hidden_width), F32)] * 2,
        compiler_params=params(),
        name="middle",
    )(x, att, cot, wo, wg, wu, wd, g1, g2)


def outer_kernel(a_ref, b_ref, o_ref):
    o_ref[...] = dot(a_ref[...], b_ref[...]).astype(o_ref.dtype)


def outer_call(a, b, out_type, tile=512):
    rows, tokens = a.shape
    columns = b.shape[1]
    tile = tile if columns % tile == 0 else 256
    return pl.pallas_call(
        outer_kernel,
        grid=(columns // tile,),
        in_specs=[
            pl.BlockSpec((rows, tokens), lambda i: (0, 0), pipeline_mode=pl.Buffered(1)),
            pl.BlockSpec((tokens, tile), lambda i: (0, i)),
        ],
        out_specs=pl.BlockSpec((rows, tile), lambda i: (0, i)),
        out_shape=jax.ShapeDtypeStruct((rows, columns), out_type),
        compiler_params=params(),
        name="outer",
    )(a, b)


def tokens_kernel(dq_ref, dk_ref, dv_ref, dfirst_ref, w_ref, o_ref):
    width = dq_ref.shape[1]
    total = dfirst_ref[...].astype(F32)
    total += dot_nt(dq_ref[...], w_ref[:, :width])
    total += dot_nt(dk_ref[...], w_ref[:, width : 2 * width])
    total += dot_nt(dv_ref[...], w_ref[:, 2 * width :])
    o_ref[...] = total.astype(BF)


def tokens_call(dq, dk, dv, dfirst, w, tile=512):
    tokens, width = dq.shape
    tile = min(tile, tokens)
    row = pl.BlockSpec((tile, width), lambda i: (i, 0))
    return pl.pallas_call(
        tokens_kernel,
        grid=(tokens // tile,),
        in_specs=[row] * 4 + [pl.BlockSpec(w.shape, lambda i: (0, 0), pipeline_mode=pl.Buffered(1))],
        out_specs=row,
        out_shape=jax.ShapeDtypeStruct((tokens, width), BF),
        compiler_params=params(),
        name="grad_tokens",
    )(dq, dk, dv, dfirst, w)


def angle_tables(span):
    index = np.arange(HEAD // 2, dtype=np.float64)
    inverse = np.power(1000.0, -2.0 * index / HEAD)
    angles = np.arange(span, dtype=np.float64)[:, None] * inverse[None, :]
    repeat = (1, PAIR // (HEAD // 2))
    return (
        np.tile(np.cos(angles), repeat).astype(np.float32),
        np.tile(np.sin(angles), repeat).astype(np.float32),
    )


def swap(a, mine):
    keep = lax.dynamic_index_in_dim(a, mine, 0, keepdims=False)
    give = lax.dynamic_index_in_dim(a, 1 - mine, 0, keepdims=False)
    got = lax.ppermute(give, "blk", [(0, 1), (1, 0)])
    low = jnp.where(mine == 0, keep, got)
    high = jnp.where(mine == 0, got, keep)
    return jnp.stack([low, high])


def body(tokens, lengths, w_qkv, w_out, w_gate, w_up, w_down, gain_one, gain_two, cotangent):
    axes = ("dp", "blk")
    blk = lax.axis_size("blk")
    mine = lax.axis_index("blk")
    rows, span, width = tokens.shape
    seq = span * blk
    own = blk == 2 and rows == 2 and lax.axis_size("dp") == 16

    def gather(a):
        return lax.all_gather(a, axes, axis=0, tiled=True)

    cosine, sine = map(jnp.asarray, angle_tables(seq))
    gains = jnp.stack([gain_one, gain_two], 1)
    if own:
        x, f_qkv = opening_call(tokens, w_qkv)
        x = x.reshape(1, seq, width)
        f_qkv = f_qkv.reshape(width, -1)
        length = lax.dynamic_slice_in_dim(lengths, mine, 1, 0)
        cq, sq = cosine, sine
    else:
        f_qkv, f_out, f_gate, f_up, f_down = map(gather, (w_qkv, w_out, w_gate, w_up, w_down))
        f_gains = gather(gains).astype(F32)
        x, cot, length = tokens, cotangent, lengths
        cq = lax.dynamic_slice_in_dim(cosine, mine * span, span, 0)
        sq = lax.dynamic_slice_in_dim(sine, mine * span, span, 0)
    n, t = x.shape[:2]
    flat = x.reshape(n * t, width)
    q, k, v, xt = qkv_call(flat, f_qkv, cq, sq)
    q, k, v = (a.reshape(n, t, width) for a in (q, k, v))
    if not own:
        k = lax.all_gather(k, "blk", axis=1, tiled=True)
        v = lax.all_gather(v, "blk", axis=1, tiled=True)
    position = jnp.arange(seq, dtype=jnp.int32)[None, :, None]
    lane = jnp.arange(PAIR, dtype=jnp.int32)[None, None, :]
    bias = jnp.where((lane == 3) & (position >= length[:, None, None]), NEG, 0.0).astype(BF)
    if own:
        w_out = jnp.pad(jnp.concatenate([w_out, gains], 1), ((0, 0), (0, PAIR - 2)))
        att, aug, cot, f_out, f_gate, f_up, f_down = attend_call(
            q, k, v, bias, (cotangent, w_out, w_gate, w_up, w_down)
        )
        f_out = f_out.reshape(width, -1)
        f_out, f_gains = f_out[:, :width], f_out[:, width : width + 2].astype(F32)
        f_gate, f_up = f_gate.reshape(width, -1), f_up.reshape(width, -1)
        f_down = f_down.reshape(-1, width)
    else:
        att, aug = attend_call(q, k, v, bias)
    g1, g2 = f_gains[:, 0][None], f_gains[:, 1][None]
    out, d_first, d_att, act, d_gate, d_up, h_t, df_t, att_t, gg1, gg2 = middle_call(
        flat, att.reshape(n * t, width), cot.reshape(n * t, width), f_out, f_gate, f_up, f_down, g1, g2
    )
    gw_gate = outer_call(h_t, d_gate, BF)
    gw_up = outer_call(h_t, d_up, BF)
    gw_down_t = outer_call(df_t, act, BF)
    gw_out = outer_call(att_t, d_first, F32)
    gains = jnp.pad(jnp.concatenate([gg1, gg2]).T, ((0, 0), (0, PAIR - 2)))
    gw_out = jnp.concatenate([gw_out, gains], 1)
    d_att = d_att.reshape(n, t, width)
    if own:
        wide = tuple(g.reshape(4, 2, 2, width // 16, -1) for g in (gw_gate, gw_up, gw_down_t))
        dq, dk, dv, out, s_gate, s_up, s_down_t, s_out = attend_back_call(
            q, k, v, bias, att, d_att, aug, cq, sq, True,
            (out.reshape(2, span, width),) + wide + (gw_out.reshape(4, 2, 2, 2, width // 32, -1),),
        )
    else:

        def scatter_wide(g):
            g = lax.psum_scatter(g, "blk", scatter_dimension=1, tiled=True)
            return lax.psum_scatter(g, "dp", scatter_dimension=0, tiled=True).astype(F32)

        s_gate, s_up, s_down_t = map(scatter_wide, (gw_gate, gw_up, gw_down_t))
        s_out = lax.psum_scatter(gw_out, axes, scatter_dimension=0, tiled=True)
        dq, dk, dv = attend_back_call(q, k, v, bias, att, d_att, aug, cq, sq, False)
        dk = lax.psum_scatter(dk, "blk", scatter_dimension=1, tiled=True)
        dv = lax.psum_scatter(dv, "blk", scatter_dimension=1, tiled=True)
        heads = (dk * jnp.tile(sq, (1, width // PAIR))).reshape(n, t, HEADS, HEAD)
        half = jnp.concatenate([heads[..., HEAD // 2 :], -heads[..., : HEAD // 2]], -1)
        dk = dk * jnp.tile(cq, (1, width // PAIR)) + half.reshape(n, t, width)
        dk, dv = dk.astype(BF), dv.astype(BF)
    s_down = s_down_t.T
    s_out, s_gg = s_out[:, :width], s_out[:, width : width + 2]
    dq, dk, dv = (a.reshape(n * t, width) for a in (dq, dk, dv))
    gw_qkv = jnp.concatenate([outer_call(xt, a, BF, 256) for a in (dq, dk, dv)], 1)
    g_tokens = tokens_call(dq, dk, dv, d_first, f_qkv)
    s_qkv = lax.psum_scatter(gw_qkv, axes, scatter_dimension=0, tiled=True).astype(F32)
    if own:
        g_tokens = swap(g_tokens.reshape(2, span, width), mine)
    else:
        out = out.reshape(tokens.shape)
        g_tokens = g_tokens.reshape(tokens.shape)
    return (out, g_tokens, s_qkv, s_out, s_gate, s_up, s_down, s_gg[:, 0], s_gg[:, 1])


def solution(mesh):
    both = ("dp", "blk")
    return jax.shard_map(
        body,
        mesh=mesh,
        in_specs=(
            P("dp", "blk", None),
            P("dp"),
            P(both, None),
            P(both, None),
            P(both, None),
            P(both, None),
            P(both, None),
            P(both),
            P(both),
            P("dp", "blk", None),
        ),
        out_specs=(
            P("dp", "blk", None),
            P("dp", "blk", None),
            P(both, None),
            P(both, None),
            P("dp", "blk"),
            P("dp", "blk"),
            P("blk", "dp"),
            P(both),
            P(both),
        ),
        check_vma=False,
    )
```

```python
import functools

import jax
import jax.numpy as jnp
import numpy as np
from jax import lax
from jax.experimental import pallas as pl
from jax.experimental.pallas import tpu as pltpu
from jax.sharding import PartitionSpec as P

HEADS = 12
HEAD = 64
PAIR = 2 * HEAD
EPS = 1e-05
NEG = -1e30
LOG2E = 1.4426950408889634
LN2 = 0.6931471805599453
VMEM_LIMIT = 60 * 1024 * 1024

BF = jnp.bfloat16
F32 = jnp.float32


def dot(a, b):
    return lax.dot_general(a, b, (((1,), (0,)), ((), ())), preferred_element_type=F32)


def dot_nt(a, b):
    return lax.dot_general(a, b, (((1,), (1,)), ((), ())), preferred_element_type=F32)


def params(limit=VMEM_LIMIT):
    return pltpu.CompilerParams(vmem_limit_bytes=limit)


def lanes(shape):
    return lax.broadcasted_iota(jnp.int32, shape, 1)


def turn(u):
    low_half = (lanes(u.shape) % HEAD) < HEAD // 2
    return jnp.where(low_half, -pltpu.roll(u, PAIR - HEAD // 2, 1), pltpu.roll(u, HEAD // 2, 1))


MESH = pl.DeviceIdType.MESH
AXES = "zxcy"
SIZE = {"z": 4, "x": 2, "c": 2, "y": 2}


def place():
    dp, y = lax.axis_index("dp"), lax.axis_index("blk")
    return {"z": dp // 4, "x": dp // 2 % 2, "c": dp % 2, "y": y}


def moved(me, axis, by):
    return {**me, axis: lax.rem(me[axis] + by, SIZE[axis])}


def device(at):
    return ((at["z"] * 2 + at["x"]) * 2 + at["c"], at["y"])


def greet(me):
    barrier = pltpu.get_barrier_semaphore()
    peers = [moved(me, "y", 1), moved(me, "x", 1), moved(me, "c", 1)]
    peers += [moved(me, "z", d) for d in range(1, 4)]
    for peer in peers:
        pl.semaphore_signal(barrier, inc=1, device_id=device(peer), device_id_type=MESH)
    pl.semaphore_wait(barrier, len(peers))


class Gather:
    def __init__(self, me, shard, full, send, recv, local, base, order, held="", columns=None):
        self.me, self.full, self.held = me, full, held
        self.part = () if columns is None else (slice(None), pl.ds(*columns))
        lead = (slice(None),) * len(held)
        self.shard = shard.at[lead + self.part] if self.part else shard
        self.send, self.recv, self.local, self.base, self.order = send, recv, local, base, order

    @staticmethod
    def sems(order):
        return sum(SIZE[a] - 1 for a in order)

    def view(self, at, got):
        return self.full.at[tuple(slice(None) if a in got else at[a] for a in AXES if a in self.axes()) + self.part]

    def axes(self):
        return AXES if len(self.full.shape) == 6 else "z"

    def at_stage(self, stage):
        got = self.held + self.order[:stage]
        return got, self.order[stage], self.base + self.sems(self.order[:stage])

    def copies(self, stage):
        got, axis, slot = self.at_stage(stage)
        here = self.view(self.me, got)
        return [
            pltpu.make_async_remote_copy(
                src_ref=self.shard if stage == 0 else here,
                dst_ref=here,
                send_sem=self.send.at[slot + d - 1],
                recv_sem=self.recv.at[slot + d - 1],
                device_id=device(moved(self.me, axis, d)),
                device_id_type=MESH,
            )
            for d in range(1, SIZE[axis])
        ]

    def own(self):
        return pltpu.make_async_copy(self.shard, self.view(self.me, self.held), self.local)

    def arrivals(self, stage):
        got, axis, slot = self.at_stage(stage)
        for d in range(1, SIZE[axis]):
            there = self.view(moved(self.me, axis, SIZE[axis] - d), got)
            pltpu.make_async_remote_copy(
                src_ref=there,
                dst_ref=there,
                send_sem=self.send.at[slot + d - 1],
                recv_sem=self.recv.at[slot + d - 1],
                device_id=device(moved(self.me, axis, d)),
                device_id_type=MESH,
            ).wait_recv()

    def start(self):
        self.own().start()
        for copy in self.copies(0):
            copy.start()

    def step(self, stage):
        self.arrivals(stage - 1)
        if stage == 1:
            self.own().wait()
        if stage < len(self.order):
            for copy in self.copies(stage):
                copy.start()

    def finish(self):
        for stage in range(len(self.order)):
            for copy in self.copies(stage):
                copy.wait_send()


class Reduce:
    SEMS = 7

    def __init__(self, me, piece, bufs, out, send, recv, local, base, order):
        self.me, self.piece, self.out, self.order = me, piece, out, order
        self.b, self.r0, self.r1, self.r2, self.r3 = bufs
        self.send, self.recv, self.local, self.base = send, recv, local, base

    def copy(self, source, target, slot, axis, by=1):
        return pltpu.make_async_remote_copy(
            src_ref=source,
            dst_ref=target,
            send_sem=self.send.at[self.base + slot],
            recv_sem=self.recv.at[self.base + slot],
            device_id=device(moved(self.me, axis, by)),
            device_id_type=MESH,
        )

    def mine(self):
        c = self.me["c"]
        return [
            pltpu.make_async_copy(self.piece(c, y), self.b.at[y], self.local.at[y]) for y in range(2)
        ]

    def copies(self, stage):
        x, y, z = self.me["x"], self.me["y"], self.me["z"]
        if stage == 0:
            other = 1 - self.me["c"]
            return [self.copy(self.piece(other, i), self.r0.at[i], i, "c") for i in range(2)]
        if stage == 1:
            source = self.b.at[1 - y] if self.order[0] == "y" else self.b.at[:, :, 1 - x]
            return [self.copy(source, self.r1, 2, self.order[0])]
        if stage == 2:
            source = self.b.at[y, :, 1 - x] if self.order[0] == "y" else self.b.at[1 - y, :, x]
            return [self.copy(source, self.r2, 3, self.order[1])]
        return [
            self.copy(self.b.at[y, lax.rem(z + d, 4), x], self.r3.at[d - 1], 3 + d, "z", d)
            for d in range(1, 4)
        ]

    def start(self):
        for copy in self.copies(0) + self.mine():
            copy.start()

    def step(self, stage):
        x, y, z = self.me["x"], self.me["y"], self.me["z"]
        for copy in self.copies(stage - 1):
            copy.wait_recv()
        b, kind = self.b, self.b.dtype
        if stage == 1:
            for copy in self.mine():
                copy.wait()

            def add(i, _):
                at = (i // 4, i % 4)
                b[at] = (b[at].astype(F32) + self.r0[at].astype(F32)).astype(kind)
                return 0

            lax.fori_loop(0, 8, add, 0)
        if stage == 2:

            def add(i, _):
                if self.order[0] == "y":
                    for j in range(2):
                        b[y, i, j] = (b[y, i, j].astype(F32) + self.r1[i, j].astype(F32)).astype(kind)
                else:
                    for j in range(2):
                        b[j, i, x] = (b[j, i, x].astype(F32) + self.r1[j, i].astype(F32)).astype(kind)
                return 0

            lax.fori_loop(0, 4, add, 0)
        if stage == 3:

            def add(i, _):
                b[y, i, x] = (b[y, i, x].astype(F32) + self.r2[i].astype(F32)).astype(kind)
                return 0

            lax.fori_loop(0, 4, add, 0)
        if stage == 4:
            total = b[y, z, x].astype(F32)
            for d in range(3):
                total = total + self.r3[d].astype(F32)
            self.out[...] = total
            return
        for copy in self.copies(stage):
            copy.start()

    def finish(self):
        for stage in range(4):
            for copy in self.copies(stage):
                copy.wait_send()

    @staticmethod
    def scratch(rows, columns, kind, order):
        lead = (4, 2) if order[0] == "y" else (2, 4)
        return [
            pltpu.VMEM(shape + (rows, columns), kind)
            for shape in ((2, 4, 2), (2, 4, 2), lead, (4,), (3,))
        ]


def swap_copies(me, source, target, send, recv, local, slot):
    other = moved(me, "y", 1)
    y = me["y"]
    keep = pltpu.make_async_copy(source.at[y], target.at[y], local)
    give = pltpu.make_async_remote_copy(
        src_ref=source.at[1 - y],
        dst_ref=target.at[y],
        send_sem=send.at[slot],
        recv_sem=recv.at[slot],
        device_id=device(other),
        device_id_type=MESH,
    )
    take = pltpu.make_async_remote_copy(
        src_ref=target.at[1 - y],
        dst_ref=target.at[1 - y],
        send_sem=send.at[slot],
        recv_sem=recv.at[slot],
        device_id=device(other),
        device_id_type=MESH,
    )
    return keep, give, take


OPENING_ORDERS = ("yzxc", "zyxc", "z", "z", "z")


def opening_kernel(tok_ref, qkv_ref, *rest):
    early, rest = rest[:3], rest[3:]
    x_ref, full_ref, rest = rest[0], rest[1], rest[2:]
    early_out, (send, recv, local) = rest[:3], rest[3:]
    me = place()
    greet(me)
    keep, give, take = swap_copies(me, tok_ref, x_ref, send, recv, local.at[0], 0)
    half = qkv_ref.shape[-1] // 2
    sources = [(qkv_ref, full_ref, (0, half)), (qkv_ref, full_ref, (half, half))]
    sources += [(a, b, None) for a, b in zip(early, early_out)]
    gathers, base = [], 1
    for i, (source, full, columns) in enumerate(sources):
        order = OPENING_ORDERS[i]
        gathers.append(
            Gather(me, source, full, send, recv, local.at[1 + i], base, order, "", columns)
        )
        base += Gather.sems(order)
    first, second, later = gathers[0], gathers[1], gathers[2:]
    first.start()
    second.start()
    give.start()
    keep.start()
    first.step(1)
    second.step(1)
    first.step(2)
    for g in later:
        g.start()
    second.step(2)
    first.step(3)
    second.step(3)
    first.step(4)
    second.step(4)
    for g in later:
        g.step(1)
    for g in gathers:
        g.finish()
    take.wait_recv()
    give.wait_send()
    keep.wait()


def opening_call(tokens, w_qkv, early):
    hbm = pl.BlockSpec(memory_space=pl.ANY)
    sems = 1 + sum(map(Gather.sems, OPENING_ORDERS))
    return pl.pallas_call(
        opening_kernel,
        in_specs=[hbm] * 5,
        out_specs=[hbm] * 5,
        out_shape=[
            jax.ShapeDtypeStruct(tokens.shape, BF),
            jax.ShapeDtypeStruct((4, 2, 2, 2) + w_qkv.shape, BF),
        ]
        + [jax.ShapeDtypeStruct((4,) + a.shape, BF) for a in early],
        scratch_shapes=[
            pltpu.SemaphoreType.DMA((sems,)),
            pltpu.SemaphoreType.DMA((sems,)),
            pltpu.SemaphoreType.DMA((6,)),
        ],
        compiler_params=pltpu.CompilerParams(collective_id=0, has_side_effects=True),
        name="opening",
    )(tokens, w_qkv, *early)


def qkv_kernel(x_ref, w_ref, cos_ref, sin_ref, q_ref, k_ref, v_ref, xt_ref):
    x = x_ref[...]
    width = x.shape[1]
    cosine, sine = cos_ref[...], sin_ref[...]
    for part, out in ((0, q_ref), (1, k_ref), (2, v_ref)):
        for pair in range(width // PAIR):
            at = part * width + pair * PAIR
            if pair % 2 == 0:
                u2 = dot(x, w_ref[:, at : at + 2 * PAIR])
            u = u2[:, (pair % 2) * PAIR : (pair % 2 + 1) * PAIR]
            if part < 2:
                u = u * cosine + turn(u) * sine
            if part == 0:
                u = u * (0.125 * LOG2E)
            out[:, pair * PAIR : (pair + 1) * PAIR] = u.astype(BF)
    xt_ref[...] = x.T


def qkv_call(x, w, cosine, sine, tile=512):
    tokens, width = x.shape
    span = cosine.shape[0]
    tile = min(tile, span)
    row = pl.BlockSpec((tile, width), lambda i: (i, 0))
    table = pl.BlockSpec((tile, PAIR), lambda i: (i % (span // tile), 0))
    return pl.pallas_call(
        qkv_kernel,
        grid=(tokens // tile,),
        in_specs=[
            row,
            pl.BlockSpec(w.shape, lambda i: (0, 0), pipeline_mode=pl.Buffered(1)),
            table,
            table,
        ],
        out_specs=[row, row, row, pl.BlockSpec((width, tile), lambda i: (0, i))],
        out_shape=[jax.ShapeDtypeStruct((tokens, width), BF)] * 3
        + [jax.ShapeDtypeStruct((width, tokens), BF)],
        compiler_params=params(),
        name="qkv",
    )(x, w, cosine, sine)


def attend_kernel(tile, chunk, moves, q_ref, k_ref, v_ref, bias_ref, *rest):
    inputs, rest = rest[: moves], rest[moves:]
    o_ref, aug_ref, rest = rest[0], rest[1], rest[2:]
    outputs, rest = rest[: moves], rest[moves:]
    ka, va, s_scr, m_scr = rest[:4]
    keys, span = k_ref.shape[1], q_ref.shape[1]
    tiles = span // tile
    events = {}
    if moves:
        events = attend_events(inputs, outputs, *rest[4:])

    @pl.when(pl.program_id(1) == 0)
    def _():
        ka[:, PAIR:] = bias_ref[0]
        va[:, PAIR:] = jnp.ones((keys, PAIR), BF)

    ka[:, :PAIR] = k_ref[0]
    va[:, :PAIR] = v_ref[0]
    lane = lanes((tile, PAIR))
    side = lanes((tile, 2 * PAIR)) // HEAD % 2
    ones = (lane % HEAD == 3).astype(F32).astype(BF)
    chunks = keys // chunk

    def query(i, h):
        at = pl.ds(pl.multiple_of(i * tile, tile), tile)
        both = jnp.concatenate([q_ref[0, at, :], ones], axis=1)
        return jnp.where(side == h, both, jnp.zeros_like(both))

    def score(qa, h, c, top):
        s = dot_nt(qa, ka[c * chunk : (c + 1) * chunk, :])
        s_scr[h, :, c * chunk : (c + 1) * chunk] = s
        for b in range(chunk // PAIR):
            part = s[:, b * PAIR : (b + 1) * PAIR]
            top = part if top is None else jnp.maximum(top, part)
        return top

    def close(h, top):
        m_scr[h] = jnp.broadcast_to(jnp.max(top, axis=1, keepdims=True), (tile, PAIR))

    def unit(h, later, other):
        m = m_scr[h]
        wide = jnp.concatenate([m] * (chunk // PAIR), axis=1)
        qa = query(later, other)
        acc, top = None, None
        for c in range(chunks):
            top = score(qa, other, c, top)
            p = jnp.exp2(s_scr[h, :, c * chunk : (c + 1) * chunk] - wide).astype(BF)
            part = dot(p, va[c * chunk : (c + 1) * chunk, :])
            acc = part if acc is None else acc + part
        return acc, top, m

    top = None
    qa = query(0, 0)
    for c in range(chunks):
        top = score(qa, 0, c, top)
    close(0, top)

    def step(i, _):
        now = pl.program_id(1) * tiles + i
        for at_step, acts in events.items():

            @pl.when(now == at_step)
            def _():
                for act in acts:
                    act()

        acc0, top, m0 = unit(0, i, 1)
        close(1, top)
        acc1, top, m1 = unit(1, jnp.minimum(i + 1, tiles - 1), 0)
        close(0, top)
        mine = lane < HEAD
        total = jnp.where(mine, acc0[:, PAIR:], acc1[:, PAIR:])
        at = pl.ds(pl.multiple_of(i * tile, tile), tile)
        o_ref[0, at, :] = (jnp.where(mine, acc0[:, :PAIR], acc1[:, :PAIR]) / total).astype(BF)
        lse = jnp.where(mine, m0, m1) + jnp.log2(total)
        aug_ref[0, at, :] = spread(lse, jnp.where(lane % HEAD == 3, 1.0, 0.0))
        return 0

    lax.fori_loop(0, tiles, step, 0)
    if moves:

        @pl.when(pl.program_id(1) == pl.num_programs(1) - 1)
        def _():
            for act in events.last:
                act()


class Events(dict):
    def __init__(self):
        self.last = []

    def put(self, at, *acts):
        self.setdefault(at, []).extend(acts)


ATTEND_ORDERS = ("xyc", "xyc", "yxc", "yzxc")
ATTEND_PLAN = (
    (3, 3, 1), (7, 1, 1), (7, 2, 1), (8, 0, 1), (13, 3, 2), (16, 0, 2), (17, 1, 2), (18, 2, 2),
)
ATTEND_SWAP = 9


def attend_events(inputs, outputs, send, recv, local):
    me = place()
    keep, give, take = swap_copies(me, inputs[0], outputs[0], send, recv, local.at[0], 0)
    gathers, base = [], 1
    for i, (shard, full) in enumerate(zip(inputs[1:], outputs[1:])):
        held = "z" if i < 3 else ""
        gathers.append(
            Gather(me, shard, full, send, recv, local.at[1 + i], base, ATTEND_ORDERS[i], held)
        )
        base += Gather.sems(ATTEND_ORDERS[i])
    events = Events()
    events.put(0, functools.partial(greet, me), *(gathers[i].start for i in (3, 1, 2, 0)))
    events.put(ATTEND_SWAP, give.start, keep.start)
    done = [1] * len(gathers)
    for at, i, stage in ATTEND_PLAN:
        events.put(at, functools.partial(gathers[i].step, stage))
        done[i] = stage + 1
    for stage in range(1, 5):
        for i, g in enumerate(gathers):
            if done[i] <= stage <= len(ATTEND_ORDERS[i]):
                events.last.append(functools.partial(g.step, stage))
    events.last += [g.finish for g in gathers] + [take.wait_recv, give.wait_send, keep.wait]
    return events


def spread(value, other):
    high = value.astype(BF).astype(F32)
    rest = value - high
    mid = rest.astype(BF).astype(F32)
    low = rest - mid
    sub = lanes(value.shape) % HEAD
    return jnp.where(
        sub == 0, high, jnp.where(sub == 1, mid, jnp.where(sub == 2, low, other))
    ).astype(BF)


def attend_call(q, k, v, bias, moving=(), tile=512, chunk=512):
    rows, span, width = q.shape
    keys = k.shape[1]
    tile = min(tile, span)
    moves = len(moving)
    qs = pl.BlockSpec((1, span, PAIR), lambda r, p: (r, 0, p))
    ks = pl.BlockSpec((1, keys, PAIR), lambda r, p: (r, 0, p))
    hbm = pl.BlockSpec(memory_space=pl.ANY)
    moved_shapes = [jax.ShapeDtypeStruct(a.shape, a.dtype) for a in moving[:1]] + [
        jax.ShapeDtypeStruct((4, 2, 2, 2) + a.shape[-2:], a.dtype) for a in moving[1:]
    ]
    sems = 1 + sum(map(Gather.sems, ATTEND_ORDERS))
    extra = [pltpu.SemaphoreType.DMA((sems,))] * 2 + [pltpu.SemaphoreType.DMA((moves,))]
    more = dict(collective_id=1, has_side_effects=True) if moves else {}
    return pl.pallas_call(
        functools.partial(attend_kernel, tile, chunk, moves),
        grid=(rows, width // PAIR),
        in_specs=[qs, ks, ks, pl.BlockSpec((1, keys, PAIR), lambda r, p: (r, 0, 0))] + [hbm] * moves,
        out_specs=[qs, qs] + [hbm] * moves,
        out_shape=[jax.ShapeDtypeStruct(q.shape, BF)] * 2 + moved_shapes,
        scratch_shapes=[
            pltpu.VMEM((keys, 2 * PAIR), BF),
            pltpu.VMEM((keys, 2 * PAIR), BF),
            pltpu.VMEM((2, tile, keys), F32),
            pltpu.VMEM((2, tile, PAIR), F32),
        ]
        + (extra if moves else []),
        compiler_params=pltpu.CompilerParams(vmem_limit_bytes=VMEM_LIMIT, **more),
        name="attend",
    )(q, k, v, bias, *moving)


def attend_back_kernel(
    tk, tq, moves, q_ref, k_ref, v_ref, bias_ref, o_ref, do_ref, aug_ref, cos_ref, sin_ref, *rest
):
    inputs, rest = rest[:moves], rest[moves:]
    dq_ref, dk_ref, dv_ref, rest = rest[0], rest[1], rest[2], rest[3:]
    outputs, rest = rest[:moves], rest[moves:]
    qa, da, ka, va, kt, dqt, dk_acc, dv_acc = rest[:8]
    keys, span = k_ref.shape[1], q_ref.shape[1]
    nq, nk = span // tq, keys // tk
    events = {}
    if moves:
        events = back_events(inputs, outputs, *rest[8:])

    @pl.when(pl.program_id(1) == 0)
    def _():
        minus = jnp.where(lanes((keys, PAIR)) % HEAD < 3, -1.0, 0.0)
        ka[:, PAIR:] = (minus + bias_ref[0].astype(F32)).astype(BF)
        va[:, PAIR:] = minus.astype(BF)

    k, do = k_ref[0], do_ref[0]
    ka[:, :PAIR] = k
    va[:, :PAIR] = v_ref[0]
    kt[...] = k.T
    prod = do.astype(F32) * o_ref[0].astype(F32)
    first = prod.astype(BF)
    second = (prod - first.astype(F32)).astype(BF)
    block = (
        (lax.broadcasted_iota(jnp.int32, (PAIR, PAIR), 0) // HEAD)
        == (lax.broadcasted_iota(jnp.int32, (PAIR, PAIR), 1) // HEAD)
    ).astype(F32).astype(BF)
    delta = dot(first, block) + dot(second, block)
    q_both = jnp.concatenate([q_ref[0], aug_ref[0]], axis=1)
    d_both = jnp.concatenate([do, spread(delta, jnp.zeros_like(delta))], axis=1)
    side = lanes(q_both.shape) // HEAD % 2
    for h in range(2):
        qa[h] = jnp.where(side == h, q_both, jnp.zeros_like(q_both))
        da[h] = jnp.where(side == h, d_both, jnp.zeros_like(d_both))
    dqt[...] = jnp.zeros_like(dqt)

    def key_step(j, _):
        now = pl.program_id(1) * nk + j
        for at_step, acts in events.items():

            @pl.when(now == at_step)
            def _():
                for act in acts:
                    act()

        at_k = pl.ds(pl.multiple_of(j * tk, tk), tk)
        dk_acc[...] = jnp.zeros_like(dk_acc)
        dv_acc[...] = jnp.zeros_like(dv_acc)

        def query_step(i, _):
            at_q = pl.ds(pl.multiple_of(i * tq, tq), tq)
            dv, dk = None, None
            for h in range(2):
                st = dot_nt(ka[at_k, :], qa[h, at_q, :])
                dpt = dot_nt(va[at_k, :], da[h, at_q, :])
                p = jnp.exp2(st)
                ds = (p * dpt).astype(BF)
                pv = dot(p.astype(BF), da[h, at_q, :PAIR])
                pk = dot(ds, qa[h, at_q, :PAIR])
                dv = pv if dv is None else dv + pv
                dk = pk if dk is None else dk + pk
                head = slice(h * HEAD, (h + 1) * HEAD)
                dqt[head, at_q] += dot(kt[head, at_k], ds)
            dv_acc[...] += dv
            dk_acc[...] += dk
            return 0

        lax.fori_loop(0, nq, query_step, 0, unroll=True)
        dv_ref[0, at_k, :] = dv_acc[...].astype(dv_ref.dtype)
        g = dk_acc[...] * LN2
        if dk_ref.dtype == BF:
            g = back_turn(g, cos_ref[at_k, :], sin_ref[at_k, :])
        dk_ref[0, at_k, :] = g.astype(dk_ref.dtype)
        return 0

    lax.fori_loop(0, nk, key_step, 0)
    g = dqt[...].T * 0.125
    dq_ref[0] = back_turn(g, cos_ref[...], sin_ref[...]).astype(BF)
    if moves:

        @pl.when(pl.program_id(1) == pl.num_programs(1) - 1)
        def _():
            for act in events.last:
                act()


def back_turn(g, cosine, sine):
    return g * cosine - turn(g * sine)


def wide_piece(source, columns):
    return lambda c, y: source.at[:, :, c, :, pl.ds(y * columns, columns)]


def tall_piece(source):
    return lambda c, y: source.at[:, :, c, y]


BACK_ORDERS = ("yx", "yx", "xy", "xy")
BACK_PLAN = (
    (1, 0, 1), (1, 2, 1), (4, 0, 2), (4, 1, 1), (5, 3, 1), (5, 0, 3), (7, 1, 2), (7, 2, 2),
    (8, 3, 2), (9, 1, 3), (9, 2, 3), (10, 3, 3),
)
BACK_SWAP = 8


def back_events(inputs, outputs, send, recv, local, *bufs):
    me = place()
    keep, give, take = swap_copies(me, inputs[0], outputs[0], send, recv, local.at[0], 0)
    reduces = []
    for i, (source, out) in enumerate(zip(inputs[1:], outputs[1:])):
        piece = wide_piece(source, source.shape[-1] // 2) if len(source.shape) == 5 else tall_piece(source)
        reduces.append(
            Reduce(
                me, piece, bufs[5 * i : 5 * i + 5], out, send, recv,
                local.at[pl.ds(1 + 2 * i, 2)], 1 + i * Reduce.SEMS, BACK_ORDERS[i],
            )
        )
    events = Events()
    events.put(0, functools.partial(greet, me), *(reduces[i].start for i in (0, 2, 1, 3)))
    for at, i, stage in BACK_PLAN:
        events.put(at, functools.partial(reduces[i].step, stage))
    events.put(BACK_SWAP, give.start, keep.start)
    events.last += [functools.partial(r.step, 4) for r in reduces] + [r.finish for r in reduces]
    events.last += [take.wait_recv, give.wait_send, keep.wait]
    return events


def attend_back_call(q, k, v, bias, o, do, aug, cosine, sine, whole, moving=(), tk=1024, tq=512):
    rows, span, width = q.shape
    keys = k.shape[1]
    tq = min(tq, span)
    tk = min(tk, keys)
    moves = len(moving)
    qs = pl.BlockSpec((1, span, PAIR), lambda r, p: (r, 0, p))
    ks = pl.BlockSpec((1, keys, PAIR), lambda r, p: (r, 0, p))
    table = pl.BlockSpec((span, PAIR), lambda r, p: (0, 0), pipeline_mode=pl.Buffered(1))
    hbm = pl.BlockSpec(memory_space=pl.ANY)
    kv_type = BF if whole else F32
    results, result_specs, extra, more = [], [], [], {}
    if moves:
        results.append(jax.ShapeDtypeStruct(moving[0].shape, BF))
        result_specs.append(hbm)
        sems = 1 + Reduce.SEMS * (moves - 1)
        extra = [pltpu.SemaphoreType.DMA((sems,))] * 2 + [pltpu.SemaphoreType.DMA((2 * moves - 1,))]
        for a, order in zip(moving[1:], BACK_ORDERS):
            block = (a.shape[-2], a.shape[-1] // (2 if a.ndim == 5 else 1))
            results.append(jax.ShapeDtypeStruct(block, F32))
            result_specs.append(pl.BlockSpec(block, lambda r, p: (0, 0)))
            extra += Reduce.scratch(*block, a.dtype, order)
        more = dict(collective_id=2, has_side_effects=True)
    return pl.pallas_call(
        functools.partial(attend_back_kernel, tk, tq, moves),
        grid=(rows, width // PAIR),
        in_specs=[
            qs, ks, ks, pl.BlockSpec((1, keys, PAIR), lambda r, p: (r, 0, 0)), qs, qs, qs, table, table,
        ]
        + [hbm] * moves,
        out_specs=[qs, ks, ks] + result_specs,
        out_shape=[
            jax.ShapeDtypeStruct(q.shape, BF),
            jax.ShapeDtypeStruct(k.shape, kv_type),
            jax.ShapeDtypeStruct(k.shape, kv_type),
        ]
        + results,
        scratch_shapes=[
            pltpu.VMEM((2, span, 2 * PAIR), BF),
            pltpu.VMEM((2, span, 2 * PAIR), BF),
            pltpu.VMEM((keys, 2 * PAIR), BF),
            pltpu.VMEM((keys, 2 * PAIR), BF),
            pltpu.VMEM((PAIR, keys), BF),
            pltpu.VMEM((PAIR, span), F32),
            pltpu.VMEM((tk, PAIR), F32),
            pltpu.VMEM((tk, PAIR), F32),
        ]
        + extra,
        compiler_params=pltpu.CompilerParams(vmem_limit_bytes=VMEM_LIMIT, **more),
        name="attend_back",
    )(q, k, v, bias, o, do, aug, cosine, sine, *moving)


def middle_kernel(
    chunk, x_ref, att_ref, cot_ref, wo_ref, wg_ref, wu_ref, wd_ref, g1_ref, g2_ref,
    out_ref, dfirst_ref, datt_ref, act_ref, dg_ref, du_ref, ht_ref, dft_ref, at_ref, gg1_ref, gg2_ref,
    ca, cb,
):
    @pl.when(pl.program_id(0) == 0)
    def _():
        gg1_ref[...] = jnp.zeros_like(gg1_ref)
        gg2_ref[...] = jnp.zeros_like(gg2_ref)

    gain1, gain2 = g1_ref[...], g2_ref[...]
    att = att_ref[...]
    at_ref[...] = att.T
    first = x_ref[...].astype(F32) + dot(att, wo_ref[...])
    centered = first - jnp.mean(first, axis=1, keepdims=True)
    s1 = lax.rsqrt(jnp.mean(centered * centered, axis=1, keepdims=True) + EPS)
    n1 = centered * s1
    hidden = n1 * gain1
    low = hidden.astype(BF)
    ht_ref[...] = low.T
    hidden_width = wg_ref.shape[1]
    second = hidden
    for c in range(hidden_width // chunk):
        at = slice(c * chunk, (c + 1) * chunk)
        g = dot(low, wg_ref[:, at])
        u = dot(low, wu_ref[:, at])
        sig = jax.nn.sigmoid(g)
        silu = g * sig
        act = (silu * u).astype(BF)
        act_ref[:, at] = act
        ca[:, at] = (u * (sig + silu * (1.0 - sig))).astype(ca.dtype)
        cb[:, at] = silu.astype(cb.dtype)
        second = second + dot(act, wd_ref[at, :])
    centered = second - jnp.mean(second, axis=1, keepdims=True)
    s2 = lax.rsqrt(jnp.mean(centered * centered, axis=1, keepdims=True) + EPS)
    n2 = centered * s2
    out_ref[...] = (n2 * gain2).astype(BF)
    dy = cot_ref[...].astype(F32)
    gg2_ref[...] += jnp.sum(dy * n2, axis=0, keepdims=True)
    inner = dy * gain2
    d_second = s2 * (
        inner - jnp.mean(inner, axis=1, keepdims=True) - n2 * jnp.mean(inner * n2, axis=1, keepdims=True)
    )
    d_ffn = d_second.astype(BF)
    dft_ref[...] = d_ffn.T
    d_hidden = d_second
    for c in range(hidden_width // chunk):
        at = slice(c * chunk, (c + 1) * chunk)
        d_act = dot_nt(d_ffn, wd_ref[at, :])
        dg = (d_act * ca[:, at]).astype(BF)
        du = (d_act * cb[:, at]).astype(BF)
        dg_ref[:, at] = dg
        du_ref[:, at] = du
        d_hidden = d_hidden + dot_nt(dg, wg_ref[:, at]) + dot_nt(du, wu_ref[:, at])
    gg1_ref[...] += jnp.sum(d_hidden * n1, axis=0, keepdims=True)
    inner = d_hidden * gain1
    d_first = s1 * (
        inner - jnp.mean(inner, axis=1, keepdims=True) - n1 * jnp.mean(inner * n1, axis=1, keepdims=True)
    )
    low = d_first.astype(BF)
    dfirst_ref[...] = low
    datt_ref[...] = dot_nt(low, wo_ref[...]).astype(BF)


def middle_call(x, att, cot, wo, wg, wu, wd, g1, g2, tile=256, chunk=768):
    tokens, width = x.shape
    hidden_width = wg.shape[1]
    tile = min(tile, tokens)
    row = pl.BlockSpec((tile, width), lambda i: (i, 0))
    wide = pl.BlockSpec((tile, hidden_width), lambda i: (i, 0))
    column = pl.BlockSpec((width, tile), lambda i: (0, i))

    def whole(a):
        return pl.BlockSpec(a.shape, lambda i: (0, 0), pipeline_mode=pl.Buffered(1))

    gain = pl.BlockSpec((1, width), lambda i: (0, 0))
    return pl.pallas_call(
        functools.partial(middle_kernel, chunk),
        grid=(tokens // tile,),
        in_specs=[row, row, row, whole(wo), whole(wg), whole(wu), whole(wd), gain, gain],
        out_specs=[row, row, row, wide, wide, wide, column, column, column, gain, gain],
        out_shape=[jax.ShapeDtypeStruct((tokens, width), BF)] * 3
        + [jax.ShapeDtypeStruct((tokens, hidden_width), BF)] * 3
        + [jax.ShapeDtypeStruct((width, tokens), BF)] * 3
        + [jax.ShapeDtypeStruct((1, width), F32)] * 2,
        scratch_shapes=[pltpu.VMEM((tile, hidden_width), F32)] * 2,
        compiler_params=params(),
        name="middle",
    )(x, att, cot, wo, wg, wu, wd, g1, g2)


def outer_kernel(a_ref, b_ref, o_ref):
    o_ref[...] = dot(a_ref[...], b_ref[...]).astype(o_ref.dtype)


def outer_call(a, b, out_type, tile=512):
    rows, tokens = a.shape
    columns = b.shape[1]
    tile = tile if columns % tile == 0 else 256
    return pl.pallas_call(
        outer_kernel,
        grid=(columns // tile,),
        in_specs=[
            pl.BlockSpec((rows, tokens), lambda i: (0, 0), pipeline_mode=pl.Buffered(1)),
            pl.BlockSpec((tokens, tile), lambda i: (0, i)),
        ],
        out_specs=pl.BlockSpec((rows, tile), lambda i: (0, i)),
        out_shape=jax.ShapeDtypeStruct((rows, columns), out_type),
        compiler_params=params(),
        name="outer",
    )(a, b)


def outers_kernel(steps, a1_ref, a2_ref, a3_ref, b1_ref, b2_ref, b3_ref, b4_ref, gains_ref, o1_ref, o2_ref, o3_ref, o4_ref):
    now = pl.program_id(0)

    @pl.when(now < steps)
    def _():
        o1_ref[...] = dot(a1_ref[...], b1_ref[...]).astype(BF)

    @pl.when((now >= steps) & (now < 2 * steps))
    def _():
        o2_ref[...] = dot(a1_ref[...], b2_ref[...]).astype(BF)

    @pl.when((now >= 2 * steps) & (now < 3 * steps))
    def _():
        o3_ref[...] = dot(a2_ref[...], b3_ref[...]).astype(BF)

    @pl.when(now == 3 * steps)
    def _():
        width = b4_ref.shape[1]
        o4_ref[:, :width] = dot(a3_ref[...], b4_ref[...])
        o4_ref[:, width:] = gains_ref[...]


def outers_call(h_t, df_t, att_t, d_gate, d_up, act, d_first, gains, tile=512):
    width, tokens = h_t.shape
    hidden = d_gate.shape[1]
    steps = hidden // tile

    def whole(a):
        return pl.BlockSpec(a.shape, lambda i: (0, 0), pipeline_mode=pl.Buffered(1))

    def part(rows, n):
        return pl.BlockSpec((rows, tile), lambda i: (0, jnp.clip(i - n * steps, 0, steps - 1)))

    return pl.pallas_call(
        functools.partial(outers_kernel, steps),
        grid=(3 * steps + 1,),
        in_specs=[whole(h_t), whole(df_t), whole(att_t)]
        + [part(tokens, n) for n in range(3)]
        + [whole(d_first), whole(gains)],
        out_specs=[part(width, n) for n in range(3)]
        + [pl.BlockSpec((width, width + gains.shape[1]), lambda i: (0, 0), pipeline_mode=pl.Buffered(1))],
        out_shape=[jax.ShapeDtypeStruct((width, hidden), BF)] * 3
        + [jax.ShapeDtypeStruct((width, width + gains.shape[1]), F32)],
        compiler_params=params(),
        name="outers",
    )(h_t, df_t, att_t, d_gate, d_up, act, d_first, gains)


CLOSING_ORDERS = ("xy", "yx", "xy")


def closing_kernel(
    dq_hbm, dk_hbm, dv_hbm, first_hbm, xt_hbm, w_hbm, g_out, sum_ref,
    dq, dk, dv, first, xt, w, g, w0, w1, w2, send, recv, local, mine_sem, *bufs,
):
    me = place()
    y = me["y"]
    loads = [
        pltpu.make_async_copy(a, b, local.at[i])
        for i, (a, b) in enumerate(
            ((w_hbm, w), (dq_hbm, dq), (dk_hbm, dk), (dv_hbm, dv), (first_hbm, first), (xt_hbm, xt))
        )
    ]
    for load in loads:
        load.start()
    greet(me)
    width = dq.shape[1]
    half = g.shape[1]
    tile = half // 2

    def rows_of(which, t):
        at = pl.ds(pl.multiple_of(which * half + t * tile, tile), tile)
        total = first[at, :].astype(F32)
        for n, a in enumerate((dq, dk, dv)):
            total += dot_nt(a[at, :], w[:, n * width : (n + 1) * width])
        g[which, pl.ds(t * tile, tile), :] = total.astype(BF)

    for load in loads[:5]:
        load.wait()
    gives = []
    for t in range(2):
        rows_of(1 - y, t)
        part = pl.ds(t * tile, tile)
        gives.append(
            pltpu.make_async_remote_copy(
                src_ref=g.at[1 - y, part],
                dst_ref=g_out.at[y, part],
                send_sem=send.at[t],
                recv_sem=recv.at[t],
                device_id=device(moved(me, "y", 1)),
                device_id_type=MESH,
            )
        )
        gives[-1].start()
    for t in range(2):
        rows_of(y, t)
    keep = pltpu.make_async_copy(g.at[y], g_out.at[y], local.at[0])
    keep.start()
    loads[5].wait()
    reduces = []
    for n, (a, target) in enumerate(((dq, w0), (dk, w1), (dv, w2))):
        reduces.append(
            Reduce(
                me, tall_piece(target), bufs[5 * n : 5 * n + 5], sum_ref.at[:, pl.ds(n * width, width)],
                send, recv, mine_sem.at[pl.ds(2 * n, 2)], 2 + n * Reduce.SEMS, CLOSING_ORDERS[n],
            )
        )

    def products(n, a, target):
        step = 2 * PAIR

        def part(i, _):
            at = pl.ds(pl.multiple_of(i * step, step), step)
            value = dot(xt[...], a[:, at])
            target[:, :, :, :, :, at] = value.reshape(target.shape[:-1] + (step,)).astype(BF)
            return 0

        lax.fori_loop(0, width // step, part, 0)

    products(0, dq, w0)
    reduces[0].start()
    products(1, dk, w1)
    reduces[1].start()
    reduces[0].step(1)
    products(2, dv, w2)
    reduces[2].start()
    reduces[1].step(1)
    reduces[0].step(2)
    reduces[2].step(1)
    reduces[1].step(2)
    reduces[0].step(3)
    reduces[2].step(2)
    reduces[1].step(3)
    reduces[0].step(4)
    reduces[2].step(3)
    reduces[1].step(4)
    reduces[2].step(4)
    for r in reduces:
        r.finish()
    for t in range(2):
        part = pl.ds(t * tile, tile)
        pltpu.make_async_remote_copy(
            src_ref=g.at[1 - y, part],
            dst_ref=g_out.at[1 - y, part],
            send_sem=send.at[t],
            recv_sem=recv.at[t],
            device_id=device(moved(me, "y", 1)),
            device_id_type=MESH,
        ).wait_recv()
        gives[t].wait_send()
    keep.wait()


def closing_call(dq, dk, dv, first, xt, w):
    tokens, width = dq.shape
    hbm = pl.BlockSpec(memory_space=pl.ANY)
    block = (width // 32, width)
    full = pltpu.VMEM((4, 2, 2, 2) + block, BF)
    scratch = [pltpu.VMEM(a.shape, BF) for a in (dq, dk, dv, first, xt, w)]
    scratch += [pltpu.VMEM((2, tokens // 2, width), BF), full, full, full]
    sems = 2 + 3 * Reduce.SEMS
    scratch += [pltpu.SemaphoreType.DMA((sems,))] * 2
    scratch += [pltpu.SemaphoreType.DMA((6,)), pltpu.SemaphoreType.DMA((6,))]
    for order in CLOSING_ORDERS:
        scratch += Reduce.scratch(*block, BF, order)
    return pl.pallas_call(
        closing_kernel,
        in_specs=[hbm] * 6,
        out_specs=[hbm, pl.BlockSpec(memory_space=pltpu.VMEM)],
        out_shape=[
            jax.ShapeDtypeStruct((2, tokens // 2, width), BF),
            jax.ShapeDtypeStruct((block[0], 3 * width), F32),
        ],
        scratch_shapes=scratch,
        compiler_params=pltpu.CompilerParams(
            vmem_limit_bytes=VMEM_LIMIT, collective_id=3, has_side_effects=True
        ),
        name="closing",
    )(dq, dk, dv, first, xt, w)


def tokens_kernel(dq_ref, dk_ref, dv_ref, dfirst_ref, w_ref, o_ref):
    width = dq_ref.shape[1]
    total = dfirst_ref[...].astype(F32)
    total += dot_nt(dq_ref[...], w_ref[:, :width])
    total += dot_nt(dk_ref[...], w_ref[:, width : 2 * width])
    total += dot_nt(dv_ref[...], w_ref[:, 2 * width :])
    o_ref[...] = total.astype(BF)


def tokens_call(dq, dk, dv, dfirst, w, tile=512):
    tokens, width = dq.shape
    tile = min(tile, tokens)
    row = pl.BlockSpec((tile, width), lambda i: (i, 0))
    return pl.pallas_call(
        tokens_kernel,
        grid=(tokens // tile,),
        in_specs=[row] * 4 + [pl.BlockSpec(w.shape, lambda i: (0, 0), pipeline_mode=pl.Buffered(1))],
        out_specs=row,
        out_shape=jax.ShapeDtypeStruct((tokens, width), BF),
        compiler_params=params(),
        name="grad_tokens",
    )(dq, dk, dv, dfirst, w)


def angle_tables(span):
    index = np.arange(HEAD // 2, dtype=np.float64)
    inverse = np.power(1000.0, -2.0 * index / HEAD)
    angles = np.arange(span, dtype=np.float64)[:, None] * inverse[None, :]
    repeat = (1, PAIR // (HEAD // 2))
    return (
        np.tile(np.cos(angles), repeat).astype(np.float32),
        np.tile(np.sin(angles), repeat).astype(np.float32),
    )


def body(tokens, lengths, w_qkv, w_out, w_gate, w_up, w_down, gain_one, gain_two, cotangent):
    axes = ("dp", "blk")
    blk = lax.axis_size("blk")
    mine = lax.axis_index("blk")
    rows, span, width = tokens.shape
    seq = span * blk
    own = blk == 2 and rows == 2 and lax.axis_size("dp") == 16

    def gather(a):
        return lax.all_gather(a, axes, axis=0, tiled=True)

    cosine, sine = map(jnp.asarray, angle_tables(seq))
    gains = jnp.stack([gain_one, gain_two], 1)
    if own:
        w_out = jnp.pad(jnp.concatenate([w_out, gains], 1), ((0, 0), (0, PAIR - 2)))
        x, f_qkv, w_out, w_gate, w_up = opening_call(tokens, w_qkv, (w_out, w_gate, w_up))
        x = x.reshape(1, seq, width)
        f_qkv = f_qkv.reshape(width, -1)
        length = lax.dynamic_slice_in_dim(lengths, mine, 1, 0)
        cq, sq = cosine, sine
    else:
        f_qkv, f_out, f_gate, f_up, f_down = map(gather, (w_qkv, w_out, w_gate, w_up, w_down))
        f_gains = gather(gains).astype(F32)
        x, cot, length = tokens, cotangent, lengths
        cq = lax.dynamic_slice_in_dim(cosine, mine * span, span, 0)
        sq = lax.dynamic_slice_in_dim(sine, mine * span, span, 0)
    n, t = x.shape[:2]
    flat = x.reshape(n * t, width)
    q, k, v, xt = qkv_call(flat, f_qkv, cq, sq)
    q, k, v = (a.reshape(n, t, width) for a in (q, k, v))
    if not own:
        k = lax.all_gather(k, "blk", axis=1, tiled=True)
        v = lax.all_gather(v, "blk", axis=1, tiled=True)
    position = jnp.arange(seq, dtype=jnp.int32)[None, :, None]
    lane = jnp.arange(PAIR, dtype=jnp.int32)[None, None, :]
    bias = jnp.where((lane % HEAD == 3) & (position >= length[:, None, None]), NEG, 0.0).astype(BF)
    if own:
        att, aug, cot, f_out, f_gate, f_up, f_down = attend_call(
            q, k, v, bias, (cotangent, w_out, w_gate, w_up, w_down)
        )
        f_out = f_out.reshape(width, -1)
        f_out, f_gains = f_out[:, :width], f_out[:, width : width + 2].astype(F32)
        f_gate, f_up = f_gate.reshape(width, -1), f_up.reshape(width, -1)
        f_down = f_down.reshape(-1, width)
    else:
        att, aug = attend_call(q, k, v, bias)
    g1, g2 = f_gains[:, 0][None], f_gains[:, 1][None]
    out, d_first, d_att, act, d_gate, d_up, h_t, df_t, att_t, gg1, gg2 = middle_call(
        flat, att.reshape(n * t, width), cot.reshape(n * t, width), f_out, f_gate, f_up, f_down, g1, g2
    )
    gains = jnp.pad(jnp.concatenate([gg1, gg2]).T, ((0, 0), (0, PAIR - 2)))
    gw_gate, gw_up, gw_down_t, gw_out = outers_call(h_t, df_t, att_t, d_gate, d_up, act, d_first, gains)
    d_att = d_att.reshape(n, t, width)
    if own:
        wide = tuple(g.reshape(4, 2, 2, width // 16, -1) for g in (gw_gate, gw_up, gw_down_t))
        dq, dk, dv, out, s_gate, s_up, s_down_t, s_out = attend_back_call(
            q, k, v, bias, att, d_att, aug, cq, sq, True,
            (out.reshape(2, span, width),) + wide + (gw_out.reshape(4, 2, 2, 2, width // 32, -1),),
        )
    else:

        def scatter_wide(g):
            g = lax.psum_scatter(g, "blk", scatter_dimension=1, tiled=True)
            return lax.psum_scatter(g, "dp", scatter_dimension=0, tiled=True).astype(F32)

        s_gate, s_up, s_down_t = map(scatter_wide, (gw_gate, gw_up, gw_down_t))
        s_out = lax.psum_scatter(gw_out, axes, scatter_dimension=0, tiled=True)
        dq, dk, dv = attend_back_call(q, k, v, bias, att, d_att, aug, cq, sq, False)
        dk = lax.psum_scatter(dk, "blk", scatter_dimension=1, tiled=True)
        dv = lax.psum_scatter(dv, "blk", scatter_dimension=1, tiled=True)
        heads = (dk * jnp.tile(sq, (1, width // PAIR))).reshape(n, t, HEADS, HEAD)
        half = jnp.concatenate([heads[..., HEAD // 2 :], -heads[..., : HEAD // 2]], -1)
        dk = dk * jnp.tile(cq, (1, width // PAIR)) + half.reshape(n, t, width)
        dk, dv = dk.astype(BF), dv.astype(BF)
    s_down = s_down_t.T
    s_out, s_gg = s_out[:, :width], s_out[:, width : width + 2]
    dq, dk, dv = (a.reshape(n * t, width) for a in (dq, dk, dv))
    if own:
        g_tokens, s_qkv = closing_call(dq, dk, dv, d_first, xt, f_qkv)
    else:
        gw_qkv = jnp.concatenate([outer_call(xt, a, BF, 256) for a in (dq, dk, dv)], 1)
        s_qkv = lax.psum_scatter(gw_qkv, axes, scatter_dimension=0, tiled=True).astype(F32)
        g_tokens = tokens_call(dq, dk, dv, d_first, f_qkv).reshape(tokens.shape)
        out = out.reshape(tokens.shape)
    return (out, g_tokens, s_qkv, s_out, s_gate, s_up, s_down, s_gg[:, 0], s_gg[:, 1])


def solution(mesh):
    both = ("dp", "blk")
    return jax.shard_map(
        body,
        mesh=mesh,
        in_specs=(
            P("dp", "blk", None),
            P("dp"),
            P(both, None),
            P(both, None),
            P(both, None),
            P(both, None),
            P(both, None),
            P(both),
            P(both),
            P("dp", "blk", None),
        ),
        out_specs=(
            P("dp", "blk", None),
            P("dp", "blk", None),
            P(both, None),
            P(both, None),
            P("dp", "blk"),
            P("dp", "blk"),
            P("blk", "dp"),
            P(both),
            P(both),
        ),
        check_vma=False,
    )
```

```python
import functools

import jax
import jax.numpy as jnp
import numpy as np
from jax import lax
from jax.experimental import pallas as pl
from jax.experimental.pallas import tpu as pltpu
from jax.sharding import PartitionSpec as P

HEADS = 12
HEAD = 64
PAIR = 2 * HEAD
EPS = 1e-05
NEG = -1e30
LOG2E = 1.4426950408889634
LN2 = 0.6931471805599453
VMEM_LIMIT = 60 * 1024 * 1024

BF = jnp.bfloat16
F32 = jnp.float32


def dot(a, b):
    return lax.dot_general(a, b, (((1,), (0,)), ((), ())), preferred_element_type=F32)


def dot_nt(a, b):
    return lax.dot_general(a, b, (((1,), (1,)), ((), ())), preferred_element_type=F32)


def params(limit=VMEM_LIMIT):
    return pltpu.CompilerParams(vmem_limit_bytes=limit)


def lanes(shape):
    return lax.broadcasted_iota(jnp.int32, shape, 1)


def turn(u):
    low_half = (lanes(u.shape) % HEAD) < HEAD // 2
    return jnp.where(low_half, -pltpu.roll(u, PAIR - HEAD // 2, 1), pltpu.roll(u, HEAD // 2, 1))


MESH = pl.DeviceIdType.MESH
AXES = "zxcy"
SIZE = {"z": 4, "x": 2, "c": 2, "y": 2}


def place():
    dp, y = lax.axis_index("dp"), lax.axis_index("blk")
    return {"z": dp // 4, "x": dp // 2 % 2, "c": dp % 2, "y": y}


def moved(me, axis, by):
    return {**me, axis: lax.rem(me[axis] + by, SIZE[axis])}


def device(at):
    return ((at["z"] * 2 + at["x"]) * 2 + at["c"], at["y"])


def greet(me):
    barrier = pltpu.get_barrier_semaphore()
    peers = [moved(me, "y", 1), moved(me, "x", 1), moved(me, "c", 1)]
    peers += [moved(me, "z", d) for d in range(1, 4)]
    for peer in peers:
        pl.semaphore_signal(barrier, inc=1, device_id=device(peer), device_id_type=MESH)
    pl.semaphore_wait(barrier, len(peers))


class Gather:
    def __init__(self, me, shard, full, send, recv, local, base, order, held="", columns=None):
        self.me, self.full, self.held = me, full, held
        self.part = () if columns is None else (slice(None), pl.ds(*columns))
        lead = (slice(None),) * len(held)
        self.shard = shard.at[lead + self.part] if self.part else shard
        self.send, self.recv, self.local, self.base, self.order = send, recv, local, base, order

    @staticmethod
    def sems(order):
        return sum(SIZE[a] - 1 for a in order)

    def view(self, at, got):
        return self.full.at[tuple(slice(None) if a in got else at[a] for a in AXES if a in self.axes()) + self.part]

    def axes(self):
        return AXES if len(self.full.shape) == 6 else "z"

    def at_stage(self, stage):
        got = self.held + self.order[:stage]
        return got, self.order[stage], self.base + self.sems(self.order[:stage])

    def copies(self, stage):
        got, axis, slot = self.at_stage(stage)
        here = self.view(self.me, got)
        return [
            pltpu.make_async_remote_copy(
                src_ref=self.shard if stage == 0 else here,
                dst_ref=here,
                send_sem=self.send.at[slot + d - 1],
                recv_sem=self.recv.at[slot + d - 1],
                device_id=device(moved(self.me, axis, d)),
                device_id_type=MESH,
            )
            for d in range(1, SIZE[axis])
        ]

    def own(self):
        return pltpu.make_async_copy(self.shard, self.view(self.me, self.held), self.local)

    def arrivals(self, stage):
        got, axis, slot = self.at_stage(stage)
        for d in range(1, SIZE[axis]):
            there = self.view(moved(self.me, axis, SIZE[axis] - d), got)
            pltpu.make_async_remote_copy(
                src_ref=there,
                dst_ref=there,
                send_sem=self.send.at[slot + d - 1],
                recv_sem=self.recv.at[slot + d - 1],
                device_id=device(moved(self.me, axis, d)),
                device_id_type=MESH,
            ).wait_recv()

    def start(self):
        self.own().start()
        for copy in self.copies(0):
            copy.start()

    def step(self, stage):
        self.arrivals(stage - 1)
        if stage == 1:
            self.own().wait()
        if stage < len(self.order):
            for copy in self.copies(stage):
                copy.start()

    def finish(self):
        for stage in range(len(self.order)):
            for copy in self.copies(stage):
                copy.wait_send()


class Reduce:
    SEMS = 7

    def __init__(self, me, piece, bufs, out, send, recv, local, base, order):
        self.me, self.piece, self.out, self.order = me, piece, out, order
        self.b, self.r0, self.r1, self.r2, self.r3 = bufs
        self.send, self.recv, self.local, self.base = send, recv, local, base

    def copy(self, source, target, slot, axis, by=1):
        return pltpu.make_async_remote_copy(
            src_ref=source,
            dst_ref=target,
            send_sem=self.send.at[self.base + slot],
            recv_sem=self.recv.at[self.base + slot],
            device_id=device(moved(self.me, axis, by)),
            device_id_type=MESH,
        )

    def mine(self):
        c = self.me["c"]
        return [
            pltpu.make_async_copy(self.piece(c, y), self.b.at[y], self.local.at[y]) for y in range(2)
        ]

    def copies(self, stage):
        x, y, z = self.me["x"], self.me["y"], self.me["z"]
        if stage == 0:
            other = 1 - self.me["c"]
            return [self.copy(self.piece(other, i), self.r0.at[i], i, "c") for i in range(2)]
        if stage == 1:
            source = self.b.at[1 - y] if self.order[0] == "y" else self.b.at[:, :, 1 - x]
            return [self.copy(source, self.r1, 2, self.order[0])]
        if stage == 2:
            source = self.b.at[y, :, 1 - x] if self.order[0] == "y" else self.b.at[1 - y, :, x]
            return [self.copy(source, self.r2, 3, self.order[1])]
        return [
            self.copy(self.b.at[y, lax.rem(z + d, 4), x], self.r3.at[d - 1], 3 + d, "z", d)
            for d in range(1, 4)
        ]

    def start(self):
        for copy in self.copies(0) + self.mine():
            copy.start()

    def step(self, stage):
        x, y, z = self.me["x"], self.me["y"], self.me["z"]
        for copy in self.copies(stage - 1):
            copy.wait_recv()
        b, kind = self.b, self.b.dtype
        if stage == 1:
            for copy in self.mine():
                copy.wait()

            def add(i, _):
                at = (i // 4, i % 4)
                b[at] = (b[at].astype(F32) + self.r0[at].astype(F32)).astype(kind)
                return 0

            lax.fori_loop(0, 8, add, 0)
        if stage == 2:

            def add(i, _):
                if self.order[0] == "y":
                    for j in range(2):
                        b[y, i, j] = (b[y, i, j].astype(F32) + self.r1[i, j].astype(F32)).astype(kind)
                else:
                    for j in range(2):
                        b[j, i, x] = (b[j, i, x].astype(F32) + self.r1[j, i].astype(F32)).astype(kind)
                return 0

            lax.fori_loop(0, 4, add, 0)
        if stage == 3:

            def add(i, _):
                b[y, i, x] = (b[y, i, x].astype(F32) + self.r2[i].astype(F32)).astype(kind)
                return 0

            lax.fori_loop(0, 4, add, 0)
        if stage == 4:
            total = b[y, z, x].astype(F32)
            for d in range(3):
                total = total + self.r3[d].astype(F32)
            self.out[...] = total
            return
        for copy in self.copies(stage):
            copy.start()

    def finish(self):
        for stage in range(4):
            for copy in self.copies(stage):
                copy.wait_send()

    @staticmethod
    def scratch(rows, columns, kind, order):
        lead = (4, 2) if order[0] == "y" else (2, 4)
        return [
            pltpu.VMEM(shape + (rows, columns), kind)
            for shape in ((2, 4, 2), (2, 4, 2), lead, (4,), (3,))
        ]


class Swap:
    def __init__(self, me, source, target, bounce, send, recv, local, slots, parts):
        self.me, self.source, self.target, self.bounce = me, source, target, bounce
        self.send, self.recv, self.local, self.slots, self.parts = send, recv, local, slots, parts

    def copy(self, n, row, half):
        begin, size = self.parts[n]
        part = pl.ds(begin, size)
        return pltpu.make_async_remote_copy(
            src_ref=self.source.at[row, part],
            dst_ref=self.target.at[half, part],
            send_sem=self.send.at[self.slots + n],
            recv_sem=self.recv.at[self.slots + n],
            device_id=device(moved(self.me, "y", 1)),
            device_id_type=MESH,
        )

    def give(self, n):
        y = self.me["y"]
        self.copy(n, 1 - y, y).start()

    def keep_in(self):
        return pltpu.make_async_copy(self.source.at[self.me["y"]], self.bounce, self.local)

    def keep_out(self):
        return pltpu.make_async_copy(self.bounce, self.target.at[self.me["y"]], self.local)

    def keep_begin(self):
        self.keep_in().start()

    def keep_turn(self):
        self.keep_in().wait()
        self.keep_out().start()

    def finish(self):
        y = self.me["y"]
        for n in range(len(self.parts)):
            self.copy(n, 1 - y, 1 - y).wait_recv()
            self.copy(n, 1 - y, y).wait_send()
        self.keep_out().wait()


OPENING_ORDERS = ("yzxc", "zyxc", "z", "z", "z")


def opening_kernel(tok_ref, qkv_ref, *rest):
    early, rest = rest[:3], rest[3:]
    x_ref, full_ref, rest = rest[0], rest[1], rest[2:]
    early_out, (bounce, send, recv, local) = rest[:3], rest[3:]
    me = place()
    greet(me)
    rows = tok_ref.shape[1]
    swap = Swap(me, tok_ref, x_ref, bounce, send, recv, local.at[0], 0, ((0, rows // 8), (rows // 8, rows - rows // 8)))
    half = qkv_ref.shape[-1] // 2
    sources = [(qkv_ref, full_ref, (0, half)), (qkv_ref, full_ref, (half, half))]
    sources += [(a, b, None) for a, b in zip(early, early_out)]
    gathers, base = [], 2
    for i, (source, full, columns) in enumerate(sources):
        order = OPENING_ORDERS[i]
        gathers.append(
            Gather(me, source, full, send, recv, local.at[1 + i], base, order, "", columns)
        )
        base += Gather.sems(order)
    first, second, later = gathers[0], gathers[1], gathers[2:]
    first.start()
    second.start()
    swap.give(0)
    swap.keep_begin()
    first.step(1)
    second.step(1)
    swap.give(1)
    swap.keep_turn()
    first.step(2)
    for g in later:
        g.start()
    second.step(2)
    first.step(3)
    second.step(3)
    first.step(4)
    second.step(4)
    for g in later:
        g.step(1)
    for g in gathers:
        g.finish()
    swap.finish()


def opening_call(tokens, w_qkv, early):
    hbm = pl.BlockSpec(memory_space=pl.ANY)
    sems = 2 + sum(map(Gather.sems, OPENING_ORDERS))
    return pl.pallas_call(
        opening_kernel,
        in_specs=[hbm] + [pl.BlockSpec(memory_space=pltpu.VMEM)] * 4,
        out_specs=[hbm] * 5,
        out_shape=[
            jax.ShapeDtypeStruct(tokens.shape, BF),
            jax.ShapeDtypeStruct((4, 2, 2, 2) + w_qkv.shape, BF),
        ]
        + [jax.ShapeDtypeStruct((4,) + a.shape, BF) for a in early],
        scratch_shapes=[
            pltpu.VMEM(tokens.shape[1:], BF),
            pltpu.SemaphoreType.DMA((sems,)),
            pltpu.SemaphoreType.DMA((sems,)),
            pltpu.SemaphoreType.DMA((6,)),
        ],
        compiler_params=pltpu.CompilerParams(
            vmem_limit_bytes=VMEM_LIMIT, collective_id=0, has_side_effects=True
        ),
        name="opening",
    )(tokens, w_qkv, *early)


def qkv_kernel(x_ref, w_ref, cos_ref, sin_ref, q_ref, k_ref, v_ref, xt_ref):
    x = x_ref[...]
    width = x.shape[1]
    cosine, sine = cos_ref[...], sin_ref[...]
    for part, out in ((0, q_ref), (1, k_ref), (2, v_ref)):
        for pair in range(width // PAIR):
            at = part * width + pair * PAIR
            if pair % 2 == 0:
                u2 = dot(x, w_ref[:, at : at + 2 * PAIR])
            u = u2[:, (pair % 2) * PAIR : (pair % 2 + 1) * PAIR]
            if part < 2:
                u = u * cosine + turn(u) * sine
            if part == 0:
                u = u * (0.125 * LOG2E)
            out[:, pair * PAIR : (pair + 1) * PAIR] = u.astype(BF)
    xt_ref[...] = x.T


def qkv_call(x, w, cosine, sine, tile=512):
    tokens, width = x.shape
    span = cosine.shape[0]
    tile = min(tile, span)
    row = pl.BlockSpec((tile, width), lambda i: (i, 0))
    table = pl.BlockSpec((tile, PAIR), lambda i: (i % (span // tile), 0))
    return pl.pallas_call(
        qkv_kernel,
        grid=(tokens // tile,),
        in_specs=[
            row,
            pl.BlockSpec(w.shape, lambda i: (0, 0), pipeline_mode=pl.Buffered(1)),
            table,
            table,
        ],
        out_specs=[row, row, row, pl.BlockSpec((width, tile), lambda i: (0, i))],
        out_shape=[jax.ShapeDtypeStruct((tokens, width), BF)] * 3
        + [jax.ShapeDtypeStruct((width, tokens), BF)],
        compiler_params=params(),
        name="qkv",
    )(x, w, cosine, sine)


def attend_kernel(tile, chunk, moves, q_ref, k_ref, v_ref, bias_ref, *rest):
    inputs, rest = rest[: moves], rest[moves:]
    o_ref, aug_ref, rest = rest[0], rest[1], rest[2:]
    outputs, rest = rest[: moves], rest[moves:]
    ka, va, s_scr, m_scr = rest[:4]
    keys, span = k_ref.shape[1], q_ref.shape[1]
    tiles = span // tile
    events = {}
    if moves:
        events = attend_events(inputs, outputs, *rest[4:])

    @pl.when(pl.program_id(1) == 0)
    def _():
        ka[:, PAIR:] = bias_ref[0]
        va[:, PAIR:] = jnp.ones((keys, PAIR), BF)

    ka[:, :PAIR] = k_ref[0]
    va[:, :PAIR] = v_ref[0]
    lane = lanes((tile, PAIR))
    side = lanes((tile, 2 * PAIR)) // HEAD % 2
    ones = (lane % HEAD == 3).astype(F32).astype(BF)
    chunks = keys // chunk

    def query(i, h):
        at = pl.ds(pl.multiple_of(i * tile, tile), tile)
        both = jnp.concatenate([q_ref[0, at, :], ones], axis=1)
        return jnp.where(side == h, both, jnp.zeros_like(both))

    def score(qa, h, c, top):
        s = dot_nt(qa, ka[c * chunk : (c + 1) * chunk, :])
        s_scr[h, :, c * chunk : (c + 1) * chunk] = s
        for b in range(chunk // PAIR):
            part = s[:, b * PAIR : (b + 1) * PAIR]
            top = part if top is None else jnp.maximum(top, part)
        return top

    def close(h, top):
        m_scr[h] = jnp.broadcast_to(jnp.max(top, axis=1, keepdims=True), (tile, PAIR))

    def unit(h, later, other):
        m = m_scr[h]
        wide = jnp.concatenate([m] * (chunk // PAIR), axis=1)
        qa = query(later, other)
        acc, top = None, None
        for c in range(chunks):
            top = score(qa, other, c, top)
            p = jnp.exp2(s_scr[h, :, c * chunk : (c + 1) * chunk] - wide).astype(BF)
            part = dot(p, va[c * chunk : (c + 1) * chunk, :])
            acc = part if acc is None else acc + part
        return acc, top, m

    top = None
    qa = query(0, 0)
    for c in range(chunks):
        top = score(qa, 0, c, top)
    close(0, top)

    def step(i, _):
        now = pl.program_id(1) * tiles + i
        for at_step, acts in events.items():

            @pl.when(now == at_step)
            def _():
                for act in acts:
                    act()

        acc0, top, m0 = unit(0, i, 1)
        close(1, top)
        acc1, top, m1 = unit(1, jnp.minimum(i + 1, tiles - 1), 0)
        close(0, top)
        mine = lane < HEAD
        total = jnp.where(mine, acc0[:, PAIR:], acc1[:, PAIR:])
        at = pl.ds(pl.multiple_of(i * tile, tile), tile)
        o_ref[0, at, :] = (jnp.where(mine, acc0[:, :PAIR], acc1[:, :PAIR]) / total).astype(BF)
        lse = jnp.where(mine, m0, m1) + jnp.log2(total)
        aug_ref[0, at, :] = spread(lse, jnp.where(lane % HEAD == 3, 1.0, 0.0))
        return 0

    lax.fori_loop(0, tiles, step, 0)
    if moves:

        @pl.when(pl.program_id(1) == pl.num_programs(1) - 1)
        def _():
            for act in events.last:
                act()


class Events(dict):
    def __init__(self):
        self.last = []

    def put(self, at, *acts):
        self.setdefault(at, []).extend(acts)


ATTEND_ORDERS = ("yxc", "xyc", "yxc", "yzxc")
ATTEND_PLAN = (
    (3, 3, 1), (4, 0, 1), (6, 1, 1), (8, 2, 1), (9, 0, 2), (12, 3, 2), (17, 1, 2), (18, 2, 2),
)
ATTEND_SWAP = 8


def attend_events(inputs, outputs, bounce, send, recv, local):
    me = place()
    rows = inputs[0].shape[1]
    swap = Swap(me, inputs[0], outputs[0], bounce, send, recv, local.at[0], 0, ((0, rows),))
    gathers, base = [], 1
    for i, (shard, full) in enumerate(zip(inputs[1:], outputs[1:])):
        held = "z" if i < 3 else ""
        gathers.append(
            Gather(me, shard, full, send, recv, local.at[1 + i], base, ATTEND_ORDERS[i], held)
        )
        base += Gather.sems(ATTEND_ORDERS[i])
    events = Events()
    events.put(0, functools.partial(greet, me), *(gathers[i].start for i in (3, 0, 2, 1)))
    done = [1] * len(gathers)
    for at, i, stage in ATTEND_PLAN:
        events.put(at, functools.partial(gathers[i].step, stage))
        done[i] = stage + 1
    events.put(ATTEND_SWAP, functools.partial(swap.give, 0), swap.keep_begin)
    events.put(ATTEND_SWAP + 3, swap.keep_turn)
    for stage in range(1, 5):
        for i, g in enumerate(gathers):
            if done[i] <= stage <= len(ATTEND_ORDERS[i]):
                events.last.append(functools.partial(g.step, stage))
    events.last += [g.finish for g in gathers] + [swap.finish]
    return events


def spread(value, other):
    high = value.astype(BF).astype(F32)
    rest = value - high
    mid = rest.astype(BF).astype(F32)
    low = rest - mid
    sub = lanes(value.shape) % HEAD
    return jnp.where(
        sub == 0, high, jnp.where(sub == 1, mid, jnp.where(sub == 2, low, other))
    ).astype(BF)


def attend_call(q, k, v, bias, moving=(), tile=512, chunk=512):
    rows, span, width = q.shape
    keys = k.shape[1]
    tile = min(tile, span)
    moves = len(moving)
    qs = pl.BlockSpec((1, span, PAIR), lambda r, p: (r, 0, p))
    ks = pl.BlockSpec((1, keys, PAIR), lambda r, p: (r, 0, p))
    hbm = pl.BlockSpec(memory_space=pl.ANY)
    moved_shapes = [jax.ShapeDtypeStruct(a.shape, a.dtype) for a in moving[:1]] + [
        jax.ShapeDtypeStruct((4, 2, 2, 2) + a.shape[-2:], a.dtype) for a in moving[1:]
    ]
    sems = 1 + sum(map(Gather.sems, ATTEND_ORDERS))
    extra = [pltpu.VMEM(moving[0].shape[1:], BF)] if moves else []
    extra += [pltpu.SemaphoreType.DMA((sems,))] * 2 + [pltpu.SemaphoreType.DMA((moves,))]
    held = [
        pl.BlockSpec(a.shape, lambda r, p, n=a.ndim: (0,) * n, pipeline_mode=pl.Buffered(1))
        for a in moving[1:]
    ]
    more = dict(collective_id=1, has_side_effects=True) if moves else {}
    return pl.pallas_call(
        functools.partial(attend_kernel, tile, chunk, moves),
        grid=(rows, width // PAIR),
        in_specs=[qs, ks, ks, pl.BlockSpec((1, keys, PAIR), lambda r, p: (r, 0, 0))]
        + [hbm] * min(moves, 1)
        + held,
        out_specs=[qs, qs] + [hbm] * moves,
        out_shape=[jax.ShapeDtypeStruct(q.shape, BF)] * 2 + moved_shapes,
        scratch_shapes=[
            pltpu.VMEM((keys, 2 * PAIR), BF),
            pltpu.VMEM((keys, 2 * PAIR), BF),
            pltpu.VMEM((2, tile, keys), F32),
            pltpu.VMEM((2, tile, PAIR), F32),
        ]
        + (extra if moves else []),
        compiler_params=pltpu.CompilerParams(vmem_limit_bytes=VMEM_LIMIT, **more),
        name="attend",
    )(q, k, v, bias, *moving)


def attend_back_kernel(
    tq, moves, q_ref, k_ref, v_ref, bias_ref, o_ref, do_ref, aug_ref, cos_ref, sin_ref, *rest
):
    inputs, rest = rest[:moves], rest[moves:]
    dq_ref, dk_ref, dv_ref, rest = rest[0], rest[1], rest[2], rest[3:]
    outputs, rest = rest[:moves], rest[moves:]
    qa, da, ka, va, kt, dk_acc, dv_acc = rest[:7]
    keys, span = k_ref.shape[1], q_ref.shape[1]
    tiles = span // tq
    events = {}
    if moves:
        events = back_events(inputs, outputs, *rest[7:])

    @pl.when(pl.program_id(1) == 0)
    def _():
        minus = jnp.where(lanes((keys, PAIR)) % HEAD < 3, -1.0, 0.0)
        ka[:, PAIR:] = (minus + bias_ref[0].astype(F32)).astype(BF)
        va[:, PAIR:] = minus.astype(BF)

    k, do = k_ref[0], do_ref[0]
    ka[:, :PAIR] = k
    va[:, :PAIR] = v_ref[0]
    kt[...] = k.T
    prod = do.astype(F32) * o_ref[0].astype(F32)
    first = prod.astype(BF)
    second = (prod - first.astype(F32)).astype(BF)
    block = (
        (lax.broadcasted_iota(jnp.int32, (PAIR, PAIR), 0) // HEAD)
        == (lax.broadcasted_iota(jnp.int32, (PAIR, PAIR), 1) // HEAD)
    ).astype(F32).astype(BF)
    delta = dot(first, block) + dot(second, block)
    q_both = jnp.concatenate([q_ref[0], aug_ref[0]], axis=1)
    d_both = jnp.concatenate([do, spread(delta, jnp.zeros_like(delta))], axis=1)
    side = lanes(q_both.shape) // HEAD % 2
    for h in range(2):
        qa[h] = jnp.where(side == h, q_both, jnp.zeros_like(q_both))
        da[h] = jnp.where(side == h, d_both, jnp.zeros_like(d_both))
    dk_acc[...] = jnp.zeros_like(dk_acc)
    dv_acc[...] = jnp.zeros_like(dv_acc)

    def query_step(i, _):
        now = pl.program_id(1) * tiles + i
        for at_step, acts in events.items():

            @pl.when(now == at_step)
            def _():
                for act in acts:
                    act()

        at_q = pl.ds(pl.multiple_of(i * tq, tq), tq)
        dv, dk, dq = None, None, []
        for h in range(2):
            st = dot_nt(ka[...], qa[h, at_q, :])
            dpt = dot_nt(va[...], da[h, at_q, :])
            p = jnp.exp2(st)
            ds = (p * dpt).astype(BF)
            pv = dot(p.astype(BF), da[h, at_q, :PAIR])
            pk = dot(ds, qa[h, at_q, :PAIR])
            dv = pv if dv is None else dv + pv
            dk = pk if dk is None else dk + pk
            dq.append(dot(kt[h * HEAD : (h + 1) * HEAD, :], ds))
        dv_acc[...] += dv
        dk_acc[...] += dk
        g = jnp.concatenate(dq, axis=0).T * 0.125
        dq_ref[0, at_q, :] = back_turn(g, cos_ref[at_q, :], sin_ref[at_q, :]).astype(BF)
        return 0

    lax.fori_loop(0, tiles, query_step, 0)
    dv_ref[0] = dv_acc[...].astype(dv_ref.dtype)
    g = dk_acc[...] * LN2
    if dk_ref.dtype == BF:
        g = back_turn(g, cos_ref[...], sin_ref[...])
    dk_ref[0] = g.astype(dk_ref.dtype)
    if moves:

        @pl.when(pl.program_id(1) == pl.num_programs(1) - 1)
        def _():
            for act in events.last:
                act()


def back_turn(g, cosine, sine):
    return g * cosine - turn(g * sine)


def wide_piece(source, columns):
    return lambda c, y: source.at[:, :, c, :, pl.ds(y * columns, columns)]


def tall_piece(source):
    return lambda c, y: source.at[:, :, c, y]


BACK_ORDERS = ("yx", "yx", "xy", "xy")
BACK_PLAN = (
    (2, 0, 1), (2, 2, 1), (3, 1, 1), (3, 3, 1), (7, 0, 2), (7, 2, 2), (10, 3, 2), (12, 0, 3), (12, 1, 2),
    (14, 2, 3), (15, 1, 3), (16, 3, 3), (18, 0, 4), (19, 2, 4), (20, 1, 4), (21, 3, 4),
)


def back_events(inputs, outputs, send, recv, local, *bufs):
    me = place()
    reduces = []
    for i, (source, out) in enumerate(zip(inputs, outputs)):
        piece = wide_piece(source, source.shape[-1] // 2) if len(source.shape) == 5 else tall_piece(source)
        reduces.append(
            Reduce(
                me, piece, bufs[5 * i : 5 * i + 5], out, send, recv,
                local.at[pl.ds(2 * i, 2)], i * Reduce.SEMS, BACK_ORDERS[i],
            )
        )
    events = Events()
    events.put(0, functools.partial(greet, me), *(reduces[i].start for i in (0, 2, 1, 3)))
    for at, i, stage in BACK_PLAN:
        events.put(at, functools.partial(reduces[i].step, stage))
    events.last += [r.finish for r in reduces]
    return events


def attend_back_call(q, k, v, bias, o, do, aug, cosine, sine, whole, moving=(), tq=512):
    rows, span, width = q.shape
    keys = k.shape[1]
    tq = min(tq, span)
    moves = len(moving)
    qs = pl.BlockSpec((1, span, PAIR), lambda r, p: (r, 0, p))
    ks = pl.BlockSpec((1, keys, PAIR), lambda r, p: (r, 0, p))
    table = pl.BlockSpec((span, PAIR), lambda r, p: (0, 0), pipeline_mode=pl.Buffered(1))
    hbm = pl.BlockSpec(memory_space=pl.ANY)
    kv_type = BF if whole else F32
    results, result_specs, extra, more = [], [], [], {}
    if moves:
        extra = [pltpu.SemaphoreType.DMA((Reduce.SEMS * moves,))] * 2
        extra += [pltpu.SemaphoreType.DMA((2 * moves,))]
        for a, order in zip(moving, BACK_ORDERS):
            block = (a.shape[-2], a.shape[-1] // (2 if a.ndim == 5 else 1))
            results.append(jax.ShapeDtypeStruct(block, F32))
            result_specs.append(pl.BlockSpec(block, lambda r, p: (0, 0), pipeline_mode=pl.Buffered(1)))
            extra += Reduce.scratch(*block, a.dtype, order)
        more = dict(collective_id=2, has_side_effects=True)
    return pl.pallas_call(
        functools.partial(attend_back_kernel, tq, moves),
        grid=(rows, width // PAIR),
        in_specs=[
            qs, ks, ks,
            pl.BlockSpec((1, keys, PAIR), lambda r, p: (r, 0, 0), pipeline_mode=pl.Buffered(1)),
            qs, qs, qs, table, table,
        ]
        + [hbm] * moves,
        out_specs=[qs, ks, ks] + result_specs,
        out_shape=[
            jax.ShapeDtypeStruct(q.shape, BF),
            jax.ShapeDtypeStruct(k.shape, kv_type),
            jax.ShapeDtypeStruct(k.shape, kv_type),
        ]
        + results,
        scratch_shapes=[
            pltpu.VMEM((2, span, 2 * PAIR), BF),
            pltpu.VMEM((2, span, 2 * PAIR), BF),
            pltpu.VMEM((keys, 2 * PAIR), BF),
            pltpu.VMEM((keys, 2 * PAIR), BF),
            pltpu.VMEM((PAIR, keys), BF),
            pltpu.VMEM((keys, PAIR), F32),
            pltpu.VMEM((keys, PAIR), F32),
        ]
        + extra,
        compiler_params=pltpu.CompilerParams(vmem_limit_bytes=VMEM_LIMIT, **more),
        name="attend_back",
    )(q, k, v, bias, o, do, aug, cosine, sine, *moving)


def middle_kernel(
    chunk, x_ref, att_ref, cot_ref, wo_ref, wg_ref, wu_ref, wd_ref, g1_ref, g2_ref,
    out_ref, dfirst_ref, datt_ref, act_ref, dg_ref, du_ref, ht_ref, dft_ref, at_ref, gg1_ref, gg2_ref,
    ca, cb,
):
    @pl.when(pl.program_id(0) == 0)
    def _():
        gg1_ref[...] = jnp.zeros_like(gg1_ref)
        gg2_ref[...] = jnp.zeros_like(gg2_ref)

    gain1, gain2 = g1_ref[...], g2_ref[...]
    att = att_ref[...]
    at_ref[...] = att.T
    first = x_ref[...].astype(F32) + dot(att, wo_ref[...])
    centered = first - jnp.mean(first, axis=1, keepdims=True)
    s1 = lax.rsqrt(jnp.mean(centered * centered, axis=1, keepdims=True) + EPS)
    n1 = centered * s1
    hidden = n1 * gain1
    low = hidden.astype(BF)
    ht_ref[...] = low.T
    hidden_width = wg_ref.shape[1]
    second = hidden
    for c in range(hidden_width // chunk):
        at = slice(c * chunk, (c + 1) * chunk)
        g = dot(low, wg_ref[:, at])
        u = dot(low, wu_ref[:, at])
        sig = jax.nn.sigmoid(g)
        silu = g * sig
        act = (silu * u).astype(BF)
        act_ref[:, at] = act
        ca[:, at] = (u * (sig + silu * (1.0 - sig))).astype(ca.dtype)
        cb[:, at] = silu.astype(cb.dtype)
        second = second + dot(act, wd_ref[at, :])
    centered = second - jnp.mean(second, axis=1, keepdims=True)
    s2 = lax.rsqrt(jnp.mean(centered * centered, axis=1, keepdims=True) + EPS)
    n2 = centered * s2
    out_ref[...] = (n2 * gain2).astype(BF)
    dy = cot_ref[...].astype(F32)
    gg2_ref[...] += jnp.sum(dy * n2, axis=0, keepdims=True)
    inner = dy * gain2
    d_second = s2 * (
        inner - jnp.mean(inner, axis=1, keepdims=True) - n2 * jnp.mean(inner * n2, axis=1, keepdims=True)
    )
    d_ffn = d_second.astype(BF)
    dft_ref[...] = d_ffn.T
    d_hidden = d_second
    for c in range(hidden_width // chunk):
        at = slice(c * chunk, (c + 1) * chunk)
        d_act = dot_nt(d_ffn, wd_ref[at, :])
        dg = (d_act * ca[:, at]).astype(BF)
        du = (d_act * cb[:, at]).astype(BF)
        dg_ref[:, at] = dg
        du_ref[:, at] = du
        d_hidden = d_hidden + dot_nt(dg, wg_ref[:, at]) + dot_nt(du, wu_ref[:, at])
    gg1_ref[...] += jnp.sum(d_hidden * n1, axis=0, keepdims=True)
    inner = d_hidden * gain1
    d_first = s1 * (
        inner - jnp.mean(inner, axis=1, keepdims=True) - n1 * jnp.mean(inner * n1, axis=1, keepdims=True)
    )
    low = d_first.astype(BF)
    dfirst_ref[...] = low
    datt_ref[...] = dot_nt(low, wo_ref[...]).astype(BF)


def middle_call(x, att, cot, wo, wg, wu, wd, g1, g2, tile=256, chunk=768):
    tokens, width = x.shape
    hidden_width = wg.shape[1]
    tile = min(tile, tokens)
    row = pl.BlockSpec((tile, width), lambda i: (i, 0))
    wide = pl.BlockSpec((tile, hidden_width), lambda i: (i, 0))
    column = pl.BlockSpec((width, tile), lambda i: (0, i))

    def whole(a):
        return pl.BlockSpec(a.shape, lambda i: (0, 0), pipeline_mode=pl.Buffered(1))

    gain = pl.BlockSpec((1, width), lambda i: (0, 0))
    return pl.pallas_call(
        functools.partial(middle_kernel, chunk),
        grid=(tokens // tile,),
        in_specs=[row, row, row, whole(wo), whole(wg), whole(wu), whole(wd), gain, gain],
        out_specs=[row, row, row, wide, wide, wide, column, column, column, gain, gain],
        out_shape=[jax.ShapeDtypeStruct((tokens, width), BF)] * 3
        + [jax.ShapeDtypeStruct((tokens, hidden_width), BF)] * 3
        + [jax.ShapeDtypeStruct((width, tokens), BF)] * 3
        + [jax.ShapeDtypeStruct((1, width), F32)] * 2,
        scratch_shapes=[pltpu.VMEM((tile, hidden_width), F32)] * 2,
        compiler_params=params(),
        name="middle",
    )(x, att, cot, wo, wg, wu, wd, g1, g2)


def outer_kernel(a_ref, b_ref, o_ref):
    o_ref[...] = dot(a_ref[...], b_ref[...]).astype(o_ref.dtype)


def outer_call(a, b, out_type, tile=512):
    rows, tokens = a.shape
    columns = b.shape[1]
    tile = tile if columns % tile == 0 else 256
    return pl.pallas_call(
        outer_kernel,
        grid=(columns // tile,),
        in_specs=[
            pl.BlockSpec((rows, tokens), lambda i: (0, 0), pipeline_mode=pl.Buffered(1)),
            pl.BlockSpec((tokens, tile), lambda i: (0, i)),
        ],
        out_specs=pl.BlockSpec((rows, tile), lambda i: (0, i)),
        out_shape=jax.ShapeDtypeStruct((rows, columns), out_type),
        compiler_params=params(),
        name="outer",
    )(a, b)


def outers_kernel(steps, moves, a1_ref, a2_ref, a3_ref, b1_ref, b2_ref, b3_ref, b4_ref, gains_ref, *rest):
    source, rest = rest[:moves], rest[moves:]
    o1_ref, o2_ref, o3_ref, o4_ref, rest = rest[0], rest[1], rest[2], rest[3], rest[4:]
    now = pl.program_id(0)
    if moves:
        target, bounce, send, recv, local = rest
        me = place()
        swap = Swap(me, source[0], target, bounce, send, recv, local.at[0], 0, ((0, target.shape[1]),))

        @pl.when(now == 0)
        def _():
            greet(me)
            swap.give(0)
            swap.keep_begin()

        pl.when(now == 3)(swap.keep_turn)
        pl.when(now == 3 * steps)(swap.finish)

    @pl.when(now < steps)
    def _():
        o1_ref[...] = dot(a1_ref[...], b1_ref[...]).astype(BF)

    @pl.when((now >= steps) & (now < 2 * steps))
    def _():
        o2_ref[...] = dot(a1_ref[...], b2_ref[...]).astype(BF)

    @pl.when((now >= 2 * steps) & (now < 3 * steps))
    def _():
        o3_ref[...] = dot(a2_ref[...], b3_ref[...]).astype(BF)

    @pl.when(now == 3 * steps)
    def _():
        width = b4_ref.shape[1]
        o4_ref[:, :width] = dot(a3_ref[...], b4_ref[...])
        o4_ref[:, width:] = gains_ref[...]


def outers_call(h_t, df_t, att_t, d_gate, d_up, act, d_first, gains, moving=(), tile=512):
    width, tokens = h_t.shape
    hidden = d_gate.shape[1]
    steps = hidden // tile

    def whole(a):
        return pl.BlockSpec(a.shape, lambda i: (0, 0), pipeline_mode=pl.Buffered(1))

    def part(rows, n):
        return pl.BlockSpec((rows, tile), lambda i: (0, jnp.clip(i - n * steps, 0, steps - 1)))

    moves = len(moving)
    hbm = pl.BlockSpec(memory_space=pl.ANY)
    extra = [pltpu.VMEM(a.shape[1:], BF) for a in moving]
    extra += [pltpu.SemaphoreType.DMA((1,))] * (3 * moves)
    more = dict(collective_id=4, has_side_effects=True) if moves else {}
    return pl.pallas_call(
        functools.partial(outers_kernel, steps, moves),
        grid=(3 * steps + 1,),
        in_specs=[whole(h_t), whole(df_t), whole(att_t)]
        + [part(tokens, n) for n in range(3)]
        + [whole(d_first), whole(gains)]
        + [hbm] * moves,
        out_specs=[part(width, n) for n in range(3)]
        + [pl.BlockSpec((width, width + gains.shape[1]), lambda i: (0, 0), pipeline_mode=pl.Buffered(1))]
        + [hbm] * moves,
        out_shape=[jax.ShapeDtypeStruct((width, hidden), BF)] * 3
        + [jax.ShapeDtypeStruct((width, width + gains.shape[1]), F32)]
        + [jax.ShapeDtypeStruct(a.shape, BF) for a in moving],
        scratch_shapes=extra,
        compiler_params=pltpu.CompilerParams(vmem_limit_bytes=VMEM_LIMIT, **more),
        name="outers",
    )(h_t, df_t, att_t, d_gate, d_up, act, d_first, gains, *moving)


CLOSING_ORDERS = ("xy", "xy", "xy")


def closing_kernel(
    dq_hbm, dk_hbm, dv_hbm, first_hbm, xt_hbm, w_hbm, g_out, sum_ref,
    dq, dk, dv, first, xt, w, g, w0, w1, w2, send, recv, local, mine_sem, *bufs,
):
    me = place()
    y = me["y"]
    loads = [
        pltpu.make_async_copy(a, b, local.at[i])
        for i, (a, b) in enumerate(
            ((w_hbm, w), (dq_hbm, dq), (dk_hbm, dk), (dv_hbm, dv), (first_hbm, first), (xt_hbm, xt))
        )
    ]
    for load in loads:
        load.start()
    greet(me)
    width = dq.shape[1]
    half = g.shape[1]
    tile = half // 2

    def rows_of(which, t):
        at = pl.ds(pl.multiple_of(which * half + t * tile, tile), tile)
        total = first[at, :].astype(F32)
        for n, a in enumerate((dq, dk, dv)):
            total += dot_nt(a[at, :], w[:, n * width : (n + 1) * width])
        g[which, pl.ds(t * tile, tile), :] = total.astype(BF)

    for load in loads[:5]:
        load.wait()
    quarter = half // 4

    def give(n, target_half):
        part = pl.ds(n * quarter, quarter)
        return pltpu.make_async_remote_copy(
            src_ref=g.at[1 - y, part],
            dst_ref=g_out.at[target_half, part],
            send_sem=send.at[n],
            recv_sem=recv.at[n],
            device_id=device(moved(me, "y", 1)),
            device_id_type=MESH,
        )

    rows_of(1 - y, 0)
    give(0, y).start()
    give(1, y).start()
    rows_of(1 - y, 1)
    for t in range(2):
        rows_of(y, t)
    keep = pltpu.make_async_copy(g.at[y], g_out.at[y], local.at[0])
    keep.start()
    loads[5].wait()
    reduces = []
    for n, (a, target) in enumerate(((dq, w0), (dk, w1), (dv, w2))):
        reduces.append(
            Reduce(
                me, tall_piece(target), bufs[5 * n : 5 * n + 5], sum_ref.at[:, pl.ds(n * width, width)],
                send, recv, mine_sem.at[pl.ds(2 * n, 2)], 4 + n * Reduce.SEMS, CLOSING_ORDERS[n],
            )
        )

    def products(n, a, target):
        step = 2 * PAIR

        def part(i, _):
            at = pl.ds(pl.multiple_of(i * step, step), step)
            value = dot(xt[...], a[:, at])
            target[:, :, :, :, :, at] = value.reshape(target.shape[:-1] + (step,)).astype(BF)
            return 0

        lax.fori_loop(0, width // step, part, 0)

    products(0, dq, w0)
    reduces[0].start()
    give(2, y).start()
    products(1, dk, w1)
    reduces[1].start()
    reduces[0].step(1)
    products(2, dv, w2)
    reduces[2].start()
    reduces[1].step(1)
    reduces[0].step(2)
    reduces[2].step(1)
    reduces[1].step(2)
    reduces[0].step(3)
    reduces[2].step(2)
    give(3, y).start()
    reduces[1].step(3)
    reduces[0].step(4)
    reduces[2].step(3)
    reduces[1].step(4)
    reduces[2].step(4)
    for r in reduces:
        r.finish()
    for n in range(4):
        give(n, 1 - y).wait_recv()
        give(n, y).wait_send()
    keep.wait()


def closing_call(dq, dk, dv, first, xt, w):
    tokens, width = dq.shape
    hbm = pl.BlockSpec(memory_space=pl.ANY)
    block = (width // 32, width)
    full = pltpu.VMEM((4, 2, 2, 2) + block, BF)
    scratch = [pltpu.VMEM(a.shape, BF) for a in (dq, dk, dv, first, xt, w)]
    scratch += [pltpu.VMEM((2, tokens // 2, width), BF), full, full, full]
    sems = 4 + 3 * Reduce.SEMS
    scratch += [pltpu.SemaphoreType.DMA((sems,))] * 2
    scratch += [pltpu.SemaphoreType.DMA((6,)), pltpu.SemaphoreType.DMA((6,))]
    for order in CLOSING_ORDERS:
        scratch += Reduce.scratch(*block, BF, order)
    return pl.pallas_call(
        closing_kernel,
        in_specs=[hbm] * 6,
        out_specs=[hbm, pl.BlockSpec(memory_space=pltpu.VMEM)],
        out_shape=[
            jax.ShapeDtypeStruct((2, tokens // 2, width), BF),
            jax.ShapeDtypeStruct((block[0], 3 * width), F32),
        ],
        scratch_shapes=scratch,
        compiler_params=pltpu.CompilerParams(
            vmem_limit_bytes=VMEM_LIMIT, collective_id=3, has_side_effects=True
        ),
        name="closing",
    )(dq, dk, dv, first, xt, w)


def tokens_kernel(dq_ref, dk_ref, dv_ref, dfirst_ref, w_ref, o_ref):
    width = dq_ref.shape[1]
    total = dfirst_ref[...].astype(F32)
    total += dot_nt(dq_ref[...], w_ref[:, :width])
    total += dot_nt(dk_ref[...], w_ref[:, width : 2 * width])
    total += dot_nt(dv_ref[...], w_ref[:, 2 * width :])
    o_ref[...] = total.astype(BF)


def tokens_call(dq, dk, dv, dfirst, w, tile=512):
    tokens, width = dq.shape
    tile = min(tile, tokens)
    row = pl.BlockSpec((tile, width), lambda i: (i, 0))
    return pl.pallas_call(
        tokens_kernel,
        grid=(tokens // tile,),
        in_specs=[row] * 4 + [pl.BlockSpec(w.shape, lambda i: (0, 0), pipeline_mode=pl.Buffered(1))],
        out_specs=row,
        out_shape=jax.ShapeDtypeStruct((tokens, width), BF),
        compiler_params=params(),
        name="grad_tokens",
    )(dq, dk, dv, dfirst, w)


def angle_tables(span):
    index = np.arange(HEAD // 2, dtype=np.float64)
    inverse = np.power(1000.0, -2.0 * index / HEAD)
    angles = np.arange(span, dtype=np.float64)[:, None] * inverse[None, :]
    repeat = (1, PAIR // (HEAD // 2))
    return (
        np.tile(np.cos(angles), repeat).astype(np.float32),
        np.tile(np.sin(angles), repeat).astype(np.float32),
    )


def body(tokens, lengths, w_qkv, w_out, w_gate, w_up, w_down, gain_one, gain_two, cotangent):
    axes = ("dp", "blk")
    blk = lax.axis_size("blk")
    mine = lax.axis_index("blk")
    rows, span, width = tokens.shape
    seq = span * blk
    own = blk == 2 and rows == 2 and lax.axis_size("dp") == 16

    def gather(a):
        return lax.all_gather(a, axes, axis=0, tiled=True)

    cosine, sine = map(jnp.asarray, angle_tables(seq))
    gains = jnp.stack([gain_one, gain_two], 1)
    if own:
        w_out = jnp.pad(jnp.concatenate([w_out, gains], 1), ((0, 0), (0, PAIR - 2)))
        x, f_qkv, w_out, w_gate, w_up = opening_call(tokens, w_qkv, (w_out, w_gate, w_up))
        x = x.reshape(1, seq, width)
        f_qkv = f_qkv.reshape(width, -1)
        length = lax.dynamic_slice_in_dim(lengths, mine, 1, 0)
        cq, sq = cosine, sine
    else:
        f_qkv, f_out, f_gate, f_up, f_down = map(gather, (w_qkv, w_out, w_gate, w_up, w_down))
        f_gains = gather(gains).astype(F32)
        x, cot, length = tokens, cotangent, lengths
        cq = lax.dynamic_slice_in_dim(cosine, mine * span, span, 0)
        sq = lax.dynamic_slice_in_dim(sine, mine * span, span, 0)
    n, t = x.shape[:2]
    flat = x.reshape(n * t, width)
    q, k, v, xt = qkv_call(flat, f_qkv, cq, sq)
    q, k, v = (a.reshape(n, t, width) for a in (q, k, v))
    if not own:
        k = lax.all_gather(k, "blk", axis=1, tiled=True)
        v = lax.all_gather(v, "blk", axis=1, tiled=True)
    position = jnp.arange(seq, dtype=jnp.int32)[None, :, None]
    lane = jnp.arange(PAIR, dtype=jnp.int32)[None, None, :]
    bias = jnp.where((lane % HEAD == 3) & (position >= length[:, None, None]), NEG, 0.0).astype(BF)
    if own:
        att, aug, cot, f_out, f_gate, f_up, f_down = attend_call(
            q, k, v, bias, (cotangent, w_out, w_gate, w_up, w_down)
        )
        f_out = f_out.reshape(width, -1)
        f_out, f_gains = f_out[:, :width], f_out[:, width : width + 2].astype(F32)
        f_gate, f_up = f_gate.reshape(width, -1), f_up.reshape(width, -1)
        f_down = f_down.reshape(-1, width)
    else:
        att, aug = attend_call(q, k, v, bias)
    g1, g2 = f_gains[:, 0][None], f_gains[:, 1][None]
    out, d_first, d_att, act, d_gate, d_up, h_t, df_t, att_t, gg1, gg2 = middle_call(
        flat, att.reshape(n * t, width), cot.reshape(n * t, width), f_out, f_gate, f_up, f_down, g1, g2
    )
    gains = jnp.pad(jnp.concatenate([gg1, gg2]).T, ((0, 0), (0, PAIR - 2)))
    moving = (out.reshape(2, span, width),) if own else ()
    gw_gate, gw_up, gw_down_t, gw_out, *moving = outers_call(
        h_t, df_t, att_t, d_gate, d_up, act, d_first, gains, moving
    )
    d_att = d_att.reshape(n, t, width)
    if own:
        wide = tuple(g.reshape(4, 2, 2, width // 16, -1) for g in (gw_gate, gw_up, gw_down_t))
        out = moving[0]
        dq, dk, dv, s_gate, s_up, s_down_t, s_out = attend_back_call(
            q, k, v, bias, att, d_att, aug, cq, sq, True,
            wide + (gw_out.reshape(4, 2, 2, 2, width // 32, -1),),
        )
    else:

        def scatter_wide(g):
            g = lax.psum_scatter(g, "blk", scatter_dimension=1, tiled=True)
            return lax.psum_scatter(g, "dp", scatter_dimension=0, tiled=True).astype(F32)

        s_gate, s_up, s_down_t = map(scatter_wide, (gw_gate, gw_up, gw_down_t))
        s_out = lax.psum_scatter(gw_out, axes, scatter_dimension=0, tiled=True)
        dq, dk, dv = attend_back_call(q, k, v, bias, att, d_att, aug, cq, sq, False)
        dk = lax.psum_scatter(dk, "blk", scatter_dimension=1, tiled=True)
        dv = lax.psum_scatter(dv, "blk", scatter_dimension=1, tiled=True)
        heads = (dk * jnp.tile(sq, (1, width // PAIR))).reshape(n, t, HEADS, HEAD)
        half = jnp.concatenate([heads[..., HEAD // 2 :], -heads[..., : HEAD // 2]], -1)
        dk = dk * jnp.tile(cq, (1, width // PAIR)) + half.reshape(n, t, width)
        dk, dv = dk.astype(BF), dv.astype(BF)
    s_down = s_down_t.T
    s_out, s_gg = s_out[:, :width], s_out[:, width : width + 2]
    dq, dk, dv = (a.reshape(n * t, width) for a in (dq, dk, dv))
    if own:
        g_tokens, s_qkv = closing_call(dq, dk, dv, d_first, xt, f_qkv)
    else:
        gw_qkv = jnp.concatenate([outer_call(xt, a, BF, 256) for a in (dq, dk, dv)], 1)
        s_qkv = lax.psum_scatter(gw_qkv, axes, scatter_dimension=0, tiled=True).astype(F32)
        g_tokens = tokens_call(dq, dk, dv, d_first, f_qkv).reshape(tokens.shape)
        out = out.reshape(tokens.shape)
    return (out, g_tokens, s_qkv, s_out, s_gate, s_up, s_down, s_gg[:, 0], s_gg[:, 1])


def solution(mesh):
    both = ("dp", "blk")
    return jax.shard_map(
        body,
        mesh=mesh,
        in_specs=(
            P("dp", "blk", None),
            P("dp"),
            P(both, None),
            P(both, None),
            P(both, None),
            P(both, None),
            P(both, None),
            P(both),
            P(both),
            P("dp", "blk", None),
        ),
        out_specs=(
            P("dp", "blk", None),
            P("dp", "blk", None),
            P(both, None),
            P(both, None),
            P("dp", "blk"),
            P("dp", "blk"),
            P("blk", "dp"),
            P(both),
            P(both),
        ),
        check_vma=False,
    )
```

```python
import functools

import jax
import jax.numpy as jnp
import numpy as np
from jax import lax
from jax.experimental import pallas as pl
from jax.experimental.pallas import tpu as pltpu
from jax.sharding import PartitionSpec as P

HEADS = 12
HEAD = 64
PAIR = 2 * HEAD
EPS = 1e-05
NEG = -1e30
LOG2E = 1.4426950408889634
LN2 = 0.6931471805599453
VMEM_LIMIT = 60 * 1024 * 1024

BF = jnp.bfloat16
F32 = jnp.float32


def dot(a, b):
    return lax.dot_general(a, b, (((1,), (0,)), ((), ())), preferred_element_type=F32)


def dot_nt(a, b):
    return lax.dot_general(a, b, (((1,), (1,)), ((), ())), preferred_element_type=F32)


def params(limit=VMEM_LIMIT):
    return pltpu.CompilerParams(vmem_limit_bytes=limit)


def lanes(shape):
    return lax.broadcasted_iota(jnp.int32, shape, 1)


def turn(u):
    low_half = (lanes(u.shape) % HEAD) < HEAD // 2
    return jnp.where(low_half, -pltpu.roll(u, PAIR - HEAD // 2, 1), pltpu.roll(u, HEAD // 2, 1))


MESH = pl.DeviceIdType.MESH
AXES = "zxcy"
SIZE = {"z": 4, "x": 2, "c": 2, "y": 2}


def place():
    dp, y = lax.axis_index("dp"), lax.axis_index("blk")
    return {"z": dp // 4, "x": dp // 2 % 2, "c": dp % 2, "y": y}


def moved(me, axis, by):
    return {**me, axis: lax.rem(me[axis] + by, SIZE[axis])}


def device(at):
    return ((at["z"] * 2 + at["x"]) * 2 + at["c"], at["y"])


def greet(me):
    barrier = pltpu.get_barrier_semaphore()
    peers = [moved(me, "y", 1), moved(me, "x", 1), moved(me, "c", 1)]
    peers += [moved(me, "z", d) for d in range(1, 4)]
    for peer in peers:
        pl.semaphore_signal(barrier, inc=1, device_id=device(peer), device_id_type=MESH)
    pl.semaphore_wait(barrier, len(peers))


class Gather:
    def __init__(self, me, shard, full, send, recv, local, base, order, held="", columns=None):
        self.me, self.shard, self.full, self.held = me, shard, full, held
        self.part = () if columns is None else (slice(None), pl.ds(*columns))
        self.spans = [a for a in AXES if a in held + order]
        self.send, self.recv, self.local, self.base, self.order = send, recv, local, base, order

    @staticmethod
    def sems(order):
        return sum(SIZE[a] - 1 for a in order)

    def view(self, at, got):
        return self.full.at[tuple(slice(None) if a in got else at[a] for a in self.spans) + self.part]

    def at_stage(self, stage):
        got = self.held + self.order[:stage]
        return got, self.order[stage], self.base + self.sems(self.order[:stage])

    def copies(self, stage):
        got, axis, slot = self.at_stage(stage)
        here = self.view(self.me, got)
        return [
            pltpu.make_async_remote_copy(
                src_ref=self.shard if stage == 0 else here,
                dst_ref=here,
                send_sem=self.send.at[slot + d - 1],
                recv_sem=self.recv.at[slot + d - 1],
                device_id=device(moved(self.me, axis, d)),
                device_id_type=MESH,
            )
            for d in range(1, SIZE[axis])
        ]

    def own(self):
        return pltpu.make_async_copy(self.shard, self.view(self.me, self.held), self.local)

    def arrivals(self, stage):
        got, axis, slot = self.at_stage(stage)
        for d in range(1, SIZE[axis]):
            there = self.view(moved(self.me, axis, SIZE[axis] - d), got)
            pltpu.make_async_remote_copy(
                src_ref=there,
                dst_ref=there,
                send_sem=self.send.at[slot + d - 1],
                recv_sem=self.recv.at[slot + d - 1],
                device_id=device(moved(self.me, axis, d)),
                device_id_type=MESH,
            ).wait_recv()

    def start(self):
        self.own().start()
        for copy in self.copies(0):
            copy.start()

    def step(self, stage):
        self.arrivals(stage - 1)
        if stage == 1:
            self.own().wait()
        if stage < len(self.order):
            for copy in self.copies(stage):
                copy.start()

    def finish(self):
        for stage in range(len(self.order)):
            for copy in self.copies(stage):
                copy.wait_send()


class Reduce:
    SEMS = 7

    def __init__(self, me, piece, bufs, out, send, recv, local, base, order):
        self.me, self.piece, self.out, self.order = me, piece, out, order
        self.b, self.r0, self.r1, self.r2, self.r3 = bufs
        self.send, self.recv, self.local, self.base = send, recv, local, base

    def copy(self, source, target, slot, axis, by=1):
        return pltpu.make_async_remote_copy(
            src_ref=source,
            dst_ref=target,
            send_sem=self.send.at[self.base + slot],
            recv_sem=self.recv.at[self.base + slot],
            device_id=device(moved(self.me, axis, by)),
            device_id_type=MESH,
        )

    def mine(self):
        c = self.me["c"]
        return [
            pltpu.make_async_copy(self.piece(c, y), self.b.at[y], self.local.at[y]) for y in range(2)
        ]

    def copies(self, stage):
        x, y, z = self.me["x"], self.me["y"], self.me["z"]
        if stage == 0:
            other = 1 - self.me["c"]
            return [self.copy(self.piece(other, i), self.r0.at[i], i, "c") for i in range(2)]
        if stage == 1:
            source = self.b.at[1 - y] if self.order[0] == "y" else self.b.at[:, :, 1 - x]
            return [self.copy(source, self.r1, 2, self.order[0])]
        if stage == 2:
            source = self.b.at[y, :, 1 - x] if self.order[0] == "y" else self.b.at[1 - y, :, x]
            return [self.copy(source, self.r2, 3, self.order[1])]
        return [
            self.copy(self.b.at[y, lax.rem(z + d, 4), x], self.r3.at[d - 1], 3 + d, "z", d)
            for d in range(1, 4)
        ]

    def start(self):
        for copy in self.copies(0) + self.mine():
            copy.start()

    def step(self, stage):
        x, y, z = self.me["x"], self.me["y"], self.me["z"]
        for copy in self.copies(stage - 1):
            copy.wait_recv()
        b, kind = self.b, self.b.dtype
        if stage == 1:
            for copy in self.mine():
                copy.wait()

            def add(i, _):
                at = (i // 4, i % 4)
                b[at] = (b[at].astype(F32) + self.r0[at].astype(F32)).astype(kind)
                return 0

            lax.fori_loop(0, 8, add, 0)
        if stage == 2:

            def add(i, _):
                if self.order[0] == "y":
                    for j in range(2):
                        b[y, i, j] = (b[y, i, j].astype(F32) + self.r1[i, j].astype(F32)).astype(kind)
                else:
                    for j in range(2):
                        b[j, i, x] = (b[j, i, x].astype(F32) + self.r1[j, i].astype(F32)).astype(kind)
                return 0

            lax.fori_loop(0, 4, add, 0)
        if stage == 3:

            def add(i, _):
                b[y, i, x] = (b[y, i, x].astype(F32) + self.r2[i].astype(F32)).astype(kind)
                return 0

            lax.fori_loop(0, 4, add, 0)
        if stage == 4:
            total = b[y, z, x].astype(F32)
            for d in range(3):
                total = total + self.r3[d].astype(F32)
            self.out[...] = total
            return
        for copy in self.copies(stage):
            copy.start()

    def finish(self):
        for stage in range(4):
            for copy in self.copies(stage):
                copy.wait_send()

    @staticmethod
    def scratch(rows, columns, kind, order):
        lead = (4, 2) if order[0] == "y" else (2, 4)
        return [
            pltpu.VMEM(shape + (rows, columns), kind)
            for shape in ((2, 4, 2), (2, 4, 2), lead, (4,), (3,))
        ]


class Swap:
    def __init__(self, me, source, target, bounce, send, recv, local, slots, parts):
        self.me, self.source, self.target, self.bounce = me, source, target, bounce
        self.send, self.recv, self.local, self.slots, self.parts = send, recv, local, slots, parts

    def copy(self, n, row, half):
        begin, size = self.parts[n]
        part = pl.ds(begin, size)
        return pltpu.make_async_remote_copy(
            src_ref=self.source.at[row, part],
            dst_ref=self.target.at[half, part],
            send_sem=self.send.at[self.slots + n],
            recv_sem=self.recv.at[self.slots + n],
            device_id=device(moved(self.me, "y", 1)),
            device_id_type=MESH,
        )

    def give(self, n):
        y = self.me["y"]
        self.copy(n, 1 - y, y).start()

    def keep_in(self):
        return pltpu.make_async_copy(self.source.at[self.me["y"]], self.bounce, self.local)

    def keep_out(self):
        return pltpu.make_async_copy(self.bounce, self.target.at[self.me["y"]], self.local)

    def keep_begin(self):
        self.keep_in().start()

    def keep_turn(self):
        self.keep_in().wait()
        self.keep_out().start()

    def finish(self):
        y = self.me["y"]
        for n in range(len(self.parts)):
            self.copy(n, 1 - y, 1 - y).wait_recv()
            self.copy(n, 1 - y, y).wait_send()
        self.keep_out().wait()


OPENING_ORDERS = ("yzxc", "zyxc", "z", "z")


def opening_kernel(tok_ref, qkv_ref, *rest):
    early, rest = rest[:2], rest[2:]
    x_ref, full_ref, rest = rest[0], rest[1], rest[2:]
    early_out, (bounce, send, recv, local) = rest[:2], rest[2:]
    me = place()
    greet(me)
    rows = tok_ref.shape[1]
    swap = Swap(me, tok_ref, x_ref, bounce, send, recv, local.at[0], 0, ((0, rows // 8), (rows // 8, rows - rows // 8)))
    half = qkv_ref.shape[-1] // 2
    sources = [(qkv_ref.at[:, pl.ds(n * half, half)], full_ref, (n * half, half)) for n in range(2)]
    sources += [(a, b, None) for a, b in zip(early, early_out)]
    gathers, base = [], 2
    for i, (source, full, columns) in enumerate(sources):
        order = OPENING_ORDERS[i]
        gathers.append(
            Gather(me, source, full, send, recv, local.at[1 + i], base, order, "", columns)
        )
        base += Gather.sems(order)
    first, second, later = gathers[0], gathers[1], gathers[2:]
    first.start()
    second.start()
    swap.give(0)
    swap.keep_begin()
    first.step(1)
    second.step(1)
    swap.give(1)
    swap.keep_turn()
    first.step(2)
    for g in later:
        g.start()
    second.step(2)
    first.step(3)
    second.step(3)
    first.step(4)
    second.step(4)
    for g in later:
        g.step(1)
    for g in gathers:
        g.finish()
    swap.finish()


def opening_call(tokens, w_qkv, early):
    hbm = pl.BlockSpec(memory_space=pl.ANY)
    sems = 2 + sum(map(Gather.sems, OPENING_ORDERS))
    return pl.pallas_call(
        opening_kernel,
        in_specs=[hbm] + [pl.BlockSpec(memory_space=pltpu.VMEM)] * 3,
        out_specs=[hbm] * 4,
        out_shape=[
            jax.ShapeDtypeStruct(tokens.shape, BF),
            jax.ShapeDtypeStruct((4, 2, 2, 2) + w_qkv.shape, BF),
        ]
        + [jax.ShapeDtypeStruct((4,) + a.shape, BF) for a in early],
        scratch_shapes=[
            pltpu.VMEM(tokens.shape[1:], BF),
            pltpu.SemaphoreType.DMA((sems,)),
            pltpu.SemaphoreType.DMA((sems,)),
            pltpu.SemaphoreType.DMA((5,)),
        ],
        compiler_params=pltpu.CompilerParams(
            vmem_limit_bytes=VMEM_LIMIT, collective_id=0, has_side_effects=True
        ),
        name="opening",
    )(tokens, w_qkv, *early)


QKV_ORDERS = ("y", "x", "z", "y", "x")
QKV_HELD = ("z", "z", "", "", "")


def halves(ref):
    half = ref.shape[-1] // 2
    return [ref.at[:, pl.ds(n * half, half)] for n in range(2)]


def stages(me, shards, fulls, orders, held, columns, send, recv, local):
    out, base = [], 0
    for i, order in enumerate(orders):
        out.append(
            Gather(me, shards[i], fulls[i], send, recv, local.at[i], base, order, held[i], columns[i])
        )
        base += Gather.sems(order)
    return out


def qkv_kernel(moves, x_ref, w_ref, cos_ref, sin_ref, *rest):
    shards, rest = rest[:moves], rest[moves:]
    q_ref, k_ref, v_ref, xt_ref, rest = rest[0], rest[1], rest[2], rest[3], rest[4:]
    if moves:
        fulls, (send, recv, local) = rest[:5], rest[5:]
        me = place()
        shards = list(shards[:3]) + halves(shards[3])
        gathers = stages(me, shards, fulls, QKV_ORDERS, QKV_HELD, (None,) * 5, send, recv, local)

        @pl.when(pl.program_id(0) == 0)
        def _():
            greet(me)
            for i in (3, 4, 0, 1, 2):
                gathers[i].start()

    x = x_ref[...]
    width = x.shape[1]
    cosine, sine = cos_ref[...], sin_ref[...]
    for part, out in ((0, q_ref), (1, k_ref), (2, v_ref)):
        for pair in range(width // PAIR):
            at = part * width + pair * PAIR
            if pair % 2 == 0:
                u2 = dot(x, w_ref[:, at : at + 2 * PAIR])
            u = u2[:, (pair % 2) * PAIR : (pair % 2 + 1) * PAIR]
            if part < 2:
                u = u * cosine + turn(u) * sine
            if part == 0:
                u = u * (0.125 * LOG2E)
            out[:, pair * PAIR : (pair + 1) * PAIR] = u.astype(BF)
    xt_ref[...] = x.T
    if moves:

        @pl.when(pl.program_id(0) == pl.num_programs(0) - 1)
        def _():
            for g in gathers:
                g.step(1)
            for g in gathers:
                g.finish()


def qkv_call(x, w, cosine, sine, moving=(), tile=512):
    tokens, width = x.shape
    span = cosine.shape[0]
    tile = min(tile, span)
    moves = len(moving)
    row = pl.BlockSpec((tile, width), lambda i: (i, 0))
    table = pl.BlockSpec((tile, PAIR), lambda i: (i % (span // tile), 0))
    results, extra, more = [], [], {}
    if moves:
        for i, order in enumerate(QKV_ORDERS):
            a = moving[min(i, 3)]
            spans = tuple(SIZE[n] for n in AXES if n in QKV_HELD[i] + order)
            block = (a.shape[-2], a.shape[-1] // (2 if i >= 3 else 1))
            results.append(jax.ShapeDtypeStruct(spans + block, BF))
        sems = sum(map(Gather.sems, QKV_ORDERS))
        extra = [pltpu.SemaphoreType.DMA((n,)) for n in (sems, sems, len(QKV_ORDERS))]
        more = dict(collective_id=6, has_side_effects=True)
    return pl.pallas_call(
        functools.partial(qkv_kernel, moves),
        grid=(tokens // tile,),
        in_specs=[
            row,
            pl.BlockSpec(w.shape, lambda i: (0, 0), pipeline_mode=pl.Buffered(1)),
            table,
            table,
        ]
        + [
            pl.BlockSpec(a.shape, lambda i, n=a.ndim: (0,) * n, pipeline_mode=pl.Buffered(1))
            for a in moving
        ],
        out_specs=[row, row, row, pl.BlockSpec((width, tile), lambda i: (0, i))]
        + [pl.BlockSpec(memory_space=pl.ANY)] * len(results),
        out_shape=[jax.ShapeDtypeStruct((tokens, width), BF)] * 3
        + [jax.ShapeDtypeStruct((width, tokens), BF)]
        + results,
        scratch_shapes=extra,
        compiler_params=pltpu.CompilerParams(vmem_limit_bytes=VMEM_LIMIT, **more),
        name="qkv",
    )(x, w, cosine, sine, *moving)


def attend_kernel(tile, chunk, moves, q_ref, k_ref, v_ref, bias_ref, *rest):
    inputs, rest = rest[:moves], rest[moves:]
    o_ref, aug_ref, rest = rest[0], rest[1], rest[2:]
    results = max(moves - 1, 0)
    outputs, rest = rest[:results], rest[results:]
    ka, va, s_scr, m_scr = rest[:4]
    keys, span = k_ref.shape[1], q_ref.shape[1]
    tiles = span // tile
    events = {}
    if moves:
        events = attend_events(inputs, outputs, *rest[4:])

    @pl.when(pl.program_id(1) == 0)
    def _():
        ka[:, PAIR:] = bias_ref[0]
        va[:, PAIR:] = jnp.ones((keys, PAIR), BF)

    ka[:, :PAIR] = k_ref[0]
    va[:, :PAIR] = v_ref[0]
    lane = lanes((tile, PAIR))
    side = lanes((tile, 2 * PAIR)) // HEAD % 2
    ones = (lane % HEAD == 3).astype(F32).astype(BF)
    chunks = keys // chunk

    def query(i, h):
        at = pl.ds(pl.multiple_of(i * tile, tile), tile)
        both = jnp.concatenate([q_ref[0, at, :], ones], axis=1)
        return jnp.where(side == h, both, jnp.zeros_like(both))

    def score(qa, h, c, top):
        s = dot_nt(qa, ka[c * chunk : (c + 1) * chunk, :])
        s_scr[h, :, c * chunk : (c + 1) * chunk] = s
        for b in range(chunk // PAIR):
            part = s[:, b * PAIR : (b + 1) * PAIR]
            top = part if top is None else jnp.maximum(top, part)
        return top

    def close(h, top):
        m_scr[h] = jnp.broadcast_to(jnp.max(top, axis=1, keepdims=True), (tile, PAIR))

    def unit(h, later, other):
        m = m_scr[h]
        wide = jnp.concatenate([m] * (chunk // PAIR), axis=1)
        qa = query(later, other)
        acc, top = None, None
        for c in range(chunks):
            top = score(qa, other, c, top)
            p = jnp.exp2(s_scr[h, :, c * chunk : (c + 1) * chunk] - wide).astype(BF)
            part = dot(p, va[c * chunk : (c + 1) * chunk, :])
            acc = part if acc is None else acc + part
        return acc, top, m

    top = None
    qa = query(0, 0)
    for c in range(chunks):
        top = score(qa, 0, c, top)
    close(0, top)

    def step(i, _):
        acc0, top, m0 = unit(0, i, 1)
        close(1, top)
        acc1, top, m1 = unit(1, jnp.minimum(i + 1, tiles - 1), 0)
        close(0, top)
        mine = lane < HEAD
        total = jnp.where(mine, acc0[:, PAIR:], acc1[:, PAIR:])
        at = pl.ds(pl.multiple_of(i * tile, tile), tile)
        o_ref[0, at, :] = (jnp.where(mine, acc0[:, :PAIR], acc1[:, :PAIR]) / total).astype(BF)
        lse = jnp.where(mine, m0, m1) + jnp.log2(total)
        aug_ref[0, at, :] = spread(lse, jnp.where(lane % HEAD == 3, 1.0, 0.0))
        return 0

    unroll = 2 if tiles % 2 == 0 else 1

    def group(n, _):
        now = pl.program_id(1) * (tiles // unroll) + n
        for at_step, acts in events.items():

            @pl.when(now == at_step)
            def _():
                for act in acts:
                    act()

        for j in range(unroll):
            step(n * unroll + j, 0)
        return 0

    lax.fori_loop(0, tiles // unroll, group, 0)
    if moves:

        @pl.when(pl.program_id(1) == pl.num_programs(1) - 1)
        def _():
            for act in events.last:
                act()


class Events(dict):
    def __init__(self):
        self.last = []

    def put(self, at, *acts):
        self.setdefault(at, []).extend(acts)


ATTEND_HELD = ("zy", "zx", "z", "y", "x")
ATTEND_ORDERS = ("xc", "yc", "yxc", "zxc", "zyc")
ATTEND_PLAN = ((2, 0, 1), (4, 2, 1), (4, 3, 1), (7, 4, 1), (10, 1, 1), (10, 2, 2))
ATTEND_FIRST = (2, 1, 0, 3, 4)


def attend_events(inputs, outputs, send, recv, local):
    me = place()
    half = inputs[3].shape[-1]
    columns = (None, None, None, (0, half), (half, half))
    fulls = tuple(outputs) + (outputs[3],)
    gathers = stages(me, inputs, fulls, ATTEND_ORDERS, ATTEND_HELD, columns, send, recv, local)
    events = Events()
    events.put(0, functools.partial(greet, me), *(gathers[i].start for i in ATTEND_FIRST))
    done = [1] * len(gathers)
    for at, i, stage in ATTEND_PLAN:
        events.put(at, functools.partial(gathers[i].step, stage))
        done[i] = stage + 1
    for stage in range(1, 4):
        for i, g in enumerate(gathers):
            if done[i] <= stage <= len(ATTEND_ORDERS[i]):
                events.last.append(functools.partial(g.step, stage))
    events.last += [g.finish for g in gathers]
    return events


def spread(value, other):
    high = value.astype(BF).astype(F32)
    rest = value - high
    mid = rest.astype(BF).astype(F32)
    low = rest - mid
    sub = lanes(value.shape) % HEAD
    return jnp.where(
        sub == 0, high, jnp.where(sub == 1, mid, jnp.where(sub == 2, low, other))
    ).astype(BF)


def attend_call(q, k, v, bias, moving=(), tile=512, chunk=512):
    rows, span, width = q.shape
    keys = k.shape[1]
    tile = min(tile, span)
    moves = len(moving)
    qs = pl.BlockSpec((1, span, PAIR), lambda r, p: (r, 0, p))
    ks = pl.BlockSpec((1, keys, PAIR), lambda r, p: (r, 0, p))
    hbm = pl.BlockSpec(memory_space=pl.ANY)
    moved_shapes = [jax.ShapeDtypeStruct((4, 2, 2, 2) + a.shape[-2:], a.dtype) for a in moving[:3]]
    for a in moving[3:4]:
        moved_shapes.append(jax.ShapeDtypeStruct((4, 2, 2, 2, a.shape[-2], 2 * a.shape[-1]), a.dtype))
    sems = sum(map(Gather.sems, ATTEND_ORDERS))
    extra = [pltpu.SemaphoreType.DMA((sems,))] * 2 + [pltpu.SemaphoreType.DMA((len(ATTEND_ORDERS),))]
    held = [
        pl.BlockSpec(a.shape, lambda r, p, n=a.ndim: (0,) * n, pipeline_mode=pl.Buffered(1))
        for a in moving
    ]
    more = dict(collective_id=1, has_side_effects=True) if moves else {}
    return pl.pallas_call(
        functools.partial(attend_kernel, tile, chunk, moves),
        grid=(rows, width // PAIR),
        in_specs=[qs, ks, ks, pl.BlockSpec((1, keys, PAIR), lambda r, p: (r, 0, 0))]
        + held,
        out_specs=[qs, qs] + [hbm] * len(moved_shapes),
        out_shape=[jax.ShapeDtypeStruct(q.shape, BF)] * 2 + moved_shapes,
        scratch_shapes=[
            pltpu.VMEM((keys, 2 * PAIR), BF),
            pltpu.VMEM((keys, 2 * PAIR), BF),
            pltpu.VMEM((2, tile, keys), F32),
            pltpu.VMEM((2, tile, PAIR), F32),
        ]
        + (extra if moves else []),
        compiler_params=pltpu.CompilerParams(vmem_limit_bytes=VMEM_LIMIT, **more),
        name="attend",
    )(q, k, v, bias, *moving)


def attend_back_kernel(
    tq, unroll, moves, q_ref, k_ref, v_ref, bias_ref, o_ref, do_ref, aug_ref, cos_ref, sin_ref, *rest
):
    inputs, rest = rest[:moves], rest[moves:]
    dq_ref, dk_ref, dv_ref, rest = rest[0], rest[1], rest[2], rest[3:]
    outputs, rest = rest[:moves], rest[moves:]
    qa, da, ka, va, kt, dk_acc, dv_acc = rest[:7]
    keys, span = k_ref.shape[1], q_ref.shape[1]
    tiles = span // tq
    events = {}
    if moves:
        events = back_events(inputs, outputs, *rest[7:])

    @pl.when(pl.program_id(1) == 0)
    def _():
        minus = jnp.where(lanes((keys, PAIR)) % HEAD < 3, -1.0, 0.0)
        ka[:, PAIR:] = (minus + bias_ref[0].astype(F32)).astype(BF)
        va[:, PAIR:] = minus.astype(BF)

    k, do = k_ref[0], do_ref[0]
    ka[:, :PAIR] = k
    va[:, :PAIR] = v_ref[0]
    kt[...] = k.T
    prod = do.astype(F32) * o_ref[0].astype(F32)
    first = prod.astype(BF)
    second = (prod - first.astype(F32)).astype(BF)
    block = (
        (lax.broadcasted_iota(jnp.int32, (PAIR, PAIR), 0) // HEAD)
        == (lax.broadcasted_iota(jnp.int32, (PAIR, PAIR), 1) // HEAD)
    ).astype(F32).astype(BF)
    delta = dot(first, block) + dot(second, block)
    q_both = jnp.concatenate([q_ref[0], aug_ref[0]], axis=1)
    d_both = jnp.concatenate([do, spread(delta, jnp.zeros_like(delta))], axis=1)
    side = lanes(q_both.shape) // HEAD % 2
    for h in range(2):
        qa[h] = jnp.where(side == h, q_both, jnp.zeros_like(q_both))
        da[h] = jnp.where(side == h, d_both, jnp.zeros_like(d_both))
    dk_acc[...] = jnp.zeros_like(dk_acc)
    dv_acc[...] = jnp.zeros_like(dv_acc)

    def query_step(i, _):
        at_q = pl.ds(pl.multiple_of(i * tq, tq), tq)
        dv, dk, dq = None, None, []
        for h in range(2):
            st = dot_nt(ka[...], qa[h, at_q, :])
            dpt = dot_nt(va[...], da[h, at_q, :])
            p = jnp.exp2(st)
            ds = (p * dpt).astype(BF)
            pv = dot(p.astype(BF), da[h, at_q, :PAIR])
            pk = dot(ds, qa[h, at_q, :PAIR])
            dv = pv if dv is None else dv + pv
            dk = pk if dk is None else dk + pk
            dq.append(dot(kt[h * HEAD : (h + 1) * HEAD, :], ds))
        dv_acc[...] += dv
        dk_acc[...] += dk
        g = jnp.concatenate(dq, axis=0).T * 0.125
        dq_ref[0, at_q, :] = back_turn(g, cos_ref[at_q, :], sin_ref[at_q, :]).astype(BF)
        return 0

    def group(n, _):
        now = pl.program_id(1) * (tiles // unroll) + n
        for at_step, acts in events.items():

            @pl.when(now == at_step)
            def _():
                for act in acts:
                    act()

        for j in range(unroll):
            query_step(n * unroll + j, 0)
        return 0

    lax.fori_loop(0, tiles // unroll, group, 0)
    dv_ref[0] = dv_acc[...].astype(dv_ref.dtype)
    g = dk_acc[...] * LN2
    if dk_ref.dtype == BF:
        g = back_turn(g, cos_ref[...], sin_ref[...])
    dk_ref[0] = g.astype(dk_ref.dtype)
    if moves:

        @pl.when(pl.program_id(1) == pl.num_programs(1) - 1)
        def _():
            for act in events.last:
                act()


def back_turn(g, cosine, sine):
    return g * cosine - turn(g * sine)


def wide_piece(source, columns):
    return lambda c, y: source.at[:, :, c, :, pl.ds(y * columns, columns)]


def tall_piece(source):
    return lambda c, y: source.at[:, :, c, y]


BACK_ORDERS = ("yx", "yx", "xy", "xy")
BACK_PLAN = (
    (1, 0, 1), (1, 2, 1), (1, 1, 1), (1, 3, 1), (3, 0, 2), (3, 2, 2), (3, 3, 2), (4, 0, 3), (4, 2, 3), (4, 1, 2),
    (5, 1, 3), (5, 3, 3), (5, 0, 4),
)


def back_events(inputs, outputs, send, recv, local, *bufs):
    me = place()
    reduces = []
    for i, (source, out) in enumerate(zip(inputs, outputs)):
        piece = wide_piece(source, source.shape[-1] // 2) if len(source.shape) == 5 else tall_piece(source)
        reduces.append(
            Reduce(
                me, piece, bufs[5 * i : 5 * i + 5], out, send, recv,
                local.at[pl.ds(2 * i, 2)], i * Reduce.SEMS, BACK_ORDERS[i],
            )
        )
    events = Events()
    events.put(0, functools.partial(greet, me), *(reduces[i].start for i in (0, 2, 1, 3)))
    for at, i, stage in BACK_PLAN:
        events.put(at, functools.partial(reduces[i].step, stage))
    events.last += [functools.partial(reduces[i].step, 4) for i in (2, 1, 3)]
    events.last += [r.finish for r in reduces]
    return events


def attend_back_call(q, k, v, bias, o, do, aug, cosine, sine, whole, moving=(), tq=512, unroll=4):
    rows, span, width = q.shape
    keys = k.shape[1]
    tq = min(tq, span)
    unroll = min(unroll, span // tq)
    moves = len(moving)
    qs = pl.BlockSpec((1, span, PAIR), lambda r, p: (r, 0, p))
    ks = pl.BlockSpec((1, keys, PAIR), lambda r, p: (r, 0, p))
    table = pl.BlockSpec((span, PAIR), lambda r, p: (0, 0), pipeline_mode=pl.Buffered(1))
    hbm = pl.BlockSpec(memory_space=pl.ANY)
    kv_type = BF if whole else F32
    results, result_specs, extra, more = [], [], [], {}
    if moves:
        extra = [pltpu.SemaphoreType.DMA((Reduce.SEMS * moves,))] * 2
        extra += [pltpu.SemaphoreType.DMA((2 * moves,))]
        for a, order in zip(moving, BACK_ORDERS):
            block = (a.shape[-2], a.shape[-1] // (2 if a.ndim == 5 else 1))
            results.append(jax.ShapeDtypeStruct(block, F32))
            result_specs.append(pl.BlockSpec(block, lambda r, p: (0, 0), pipeline_mode=pl.Buffered(1)))
            extra += Reduce.scratch(*block, a.dtype, order)
        more = dict(collective_id=2, has_side_effects=True)
    return pl.pallas_call(
        functools.partial(attend_back_kernel, tq, unroll, moves),
        grid=(rows, width // PAIR),
        in_specs=[
            qs, ks, ks,
            pl.BlockSpec((1, keys, PAIR), lambda r, p: (r, 0, 0), pipeline_mode=pl.Buffered(1)),
            qs, qs, qs, table, table,
        ]
        + [hbm] * moves,
        out_specs=[qs, ks, ks] + result_specs,
        out_shape=[
            jax.ShapeDtypeStruct(q.shape, BF),
            jax.ShapeDtypeStruct(k.shape, kv_type),
            jax.ShapeDtypeStruct(k.shape, kv_type),
        ]
        + results,
        scratch_shapes=[
            pltpu.VMEM((2, span, 2 * PAIR), BF),
            pltpu.VMEM((2, span, 2 * PAIR), BF),
            pltpu.VMEM((keys, 2 * PAIR), BF),
            pltpu.VMEM((keys, 2 * PAIR), BF),
            pltpu.VMEM((PAIR, keys), BF),
            pltpu.VMEM((keys, PAIR), F32),
            pltpu.VMEM((keys, PAIR), F32),
        ]
        + extra,
        compiler_params=pltpu.CompilerParams(vmem_limit_bytes=VMEM_LIMIT, **more),
        name="attend_back",
    )(q, k, v, bias, o, do, aug, cosine, sine, *moving)


def middle_kernel(
    chunk, moves, x_ref, att_ref, cot_ref, wo_ref, wg_ref, wu_ref, wd_ref, g1_ref, g2_ref, *rest
):
    source, rest = rest[:moves], rest[moves:]
    (out_ref, dfirst_ref, datt_ref, act_ref, dg_ref, du_ref, ht_ref, dft_ref, at_ref, gg1_ref, gg2_ref) = rest[:11]
    ca, cb = rest[11:13]
    if moves:
        arrived, dy_ref, send, recv = rest[13:]
        me = place()
        now, per = pl.program_id(0), pl.num_programs(0) // 2
        tile = dy_ref.shape[0]
        give = pltpu.make_async_remote_copy(
            src_ref=source[0].at[1 - me["y"]],
            dst_ref=arrived,
            send_sem=send.at[0],
            recv_sem=recv.at[0],
            device_id=device(moved(me, "y", 1)),
            device_id_type=MESH,
        )

        @pl.when(now == 0)
        def _():
            greet(me)
            give.start()

        pl.when(now == per)(give.wait)

        @pl.when(now < per)
        def _():
            dy_ref[...] = cot_ref[...]

        @pl.when(now >= per)
        def _():
            dy_ref[...] = arrived[pl.ds(pl.multiple_of((now - per) * tile, tile), tile), :]

    else:
        dy_ref = cot_ref

    @pl.when(pl.program_id(0) == 0)
    def _():
        gg1_ref[...] = jnp.zeros_like(gg1_ref)
        gg2_ref[...] = jnp.zeros_like(gg2_ref)

    gain1, gain2 = g1_ref[...], g2_ref[...]
    att = att_ref[...]
    at_ref[...] = att.T
    first = x_ref[...].astype(F32) + dot(att, wo_ref[:, : att.shape[1]])
    centered = first - jnp.mean(first, axis=1, keepdims=True)
    s1 = lax.rsqrt(jnp.mean(centered * centered, axis=1, keepdims=True) + EPS)
    n1 = centered * s1
    hidden = n1 * gain1
    low = hidden.astype(BF)
    ht_ref[...] = low.T
    hidden_width = wg_ref.shape[1]
    second = hidden
    for c in range(hidden_width // chunk):
        at = slice(c * chunk, (c + 1) * chunk)
        g = dot(low, wg_ref[:, at])
        u = dot(low, wu_ref[:, at])
        sig = jax.nn.sigmoid(g)
        silu = g * sig
        act = (silu * u).astype(BF)
        act_ref[:, at] = act
        ca[:, at] = (u * (sig + silu * (1.0 - sig))).astype(ca.dtype)
        cb[:, at] = silu.astype(cb.dtype)
        second = second + dot(act, wd_ref[at, :])
    centered = second - jnp.mean(second, axis=1, keepdims=True)
    s2 = lax.rsqrt(jnp.mean(centered * centered, axis=1, keepdims=True) + EPS)
    n2 = centered * s2
    out_ref[...] = (n2 * gain2).astype(BF)
    dy = dy_ref[...].astype(F32)
    gg2_ref[...] += jnp.sum(dy * n2, axis=0, keepdims=True)
    inner = dy * gain2
    d_second = s2 * (
        inner - jnp.mean(inner, axis=1, keepdims=True) - n2 * jnp.mean(inner * n2, axis=1, keepdims=True)
    )
    d_ffn = d_second.astype(BF)
    dft_ref[...] = d_ffn.T
    d_hidden = d_second
    for c in range(hidden_width // chunk):
        at = slice(c * chunk, (c + 1) * chunk)
        d_act = dot_nt(d_ffn, wd_ref[at, :])
        dg = (d_act * ca[:, at]).astype(BF)
        du = (d_act * cb[:, at]).astype(BF)
        dg_ref[:, at] = dg
        du_ref[:, at] = du
        d_hidden = d_hidden + dot_nt(dg, wg_ref[:, at]) + dot_nt(du, wu_ref[:, at])
    gg1_ref[...] += jnp.sum(d_hidden * n1, axis=0, keepdims=True)
    inner = d_hidden * gain1
    d_first = s1 * (
        inner - jnp.mean(inner, axis=1, keepdims=True) - n1 * jnp.mean(inner * n1, axis=1, keepdims=True)
    )
    low = d_first.astype(BF)
    dfirst_ref[...] = low
    datt_ref[...] = dot_nt(low, wo_ref[:, : low.shape[1]]).astype(BF)


def middle_call(x, att, cot, wo, wg, wu, wd, g1, g2, tile=256, chunk=768):
    tokens, width = x.shape
    hidden_width = wg.shape[1]
    tile = min(tile, tokens)
    moves = cot.ndim - 2
    per = tokens // tile // 2

    def place_of(i):
        if not moves:
            return i
        return lax.rem(lax.axis_index("blk") + i // per, 2) * per + lax.rem(i, per)

    row = pl.BlockSpec((tile, width), lambda i: (place_of(i), 0))
    wide = pl.BlockSpec((tile, hidden_width), lambda i: (place_of(i), 0))
    column = pl.BlockSpec((width, tile), lambda i: (0, place_of(i)))
    cot_row, extra, more = row, [], {}
    if moves:
        cot_row = pl.BlockSpec(
            (None, tile, width), lambda i: (lax.axis_index("blk"), jnp.minimum(i, per - 1), 0)
        )
        extra = [pltpu.VMEM((tokens // 2, width), BF), pltpu.VMEM((tile, width), BF)]
        extra += [pltpu.SemaphoreType.DMA((1,))] * 2
        more = dict(collective_id=5, has_side_effects=True)

    def whole(a):
        return pl.BlockSpec(a.shape, lambda i: (0, 0), pipeline_mode=pl.Buffered(1))

    gain = pl.BlockSpec((1, width), lambda i: (0, 0))
    return pl.pallas_call(
        functools.partial(middle_kernel, chunk, moves),
        grid=(tokens // tile,),
        in_specs=[row, row, cot_row, whole(wo), whole(wg), whole(wu), whole(wd), gain, gain]
        + [pl.BlockSpec(memory_space=pl.ANY)] * moves,
        out_specs=[row, row, row, wide, wide, wide, column, column, column, gain, gain],
        out_shape=[jax.ShapeDtypeStruct((tokens, width), BF)] * 3
        + [jax.ShapeDtypeStruct((tokens, hidden_width), BF)] * 3
        + [jax.ShapeDtypeStruct((width, tokens), BF)] * 3
        + [jax.ShapeDtypeStruct((1, width), F32)] * 2,
        scratch_shapes=[pltpu.VMEM((tile, hidden_width), F32)] * 2 + extra,
        compiler_params=pltpu.CompilerParams(vmem_limit_bytes=VMEM_LIMIT, **more),
        name="middle",
    )(x, att, cot, wo, wg, wu, wd, g1, g2, *([cot] * moves))


def outer_kernel(a_ref, b_ref, o_ref):
    o_ref[...] = dot(a_ref[...], b_ref[...]).astype(o_ref.dtype)


def outer_call(a, b, out_type, tile=512):
    rows, tokens = a.shape
    columns = b.shape[1]
    tile = tile if columns % tile == 0 else 256
    return pl.pallas_call(
        outer_kernel,
        grid=(columns // tile,),
        in_specs=[
            pl.BlockSpec((rows, tokens), lambda i: (0, 0), pipeline_mode=pl.Buffered(1)),
            pl.BlockSpec((tokens, tile), lambda i: (0, i)),
        ],
        out_specs=pl.BlockSpec((rows, tile), lambda i: (0, i)),
        out_shape=jax.ShapeDtypeStruct((rows, columns), out_type),
        compiler_params=params(),
        name="outer",
    )(a, b)


def outers_kernel(steps, moves, a1_ref, a2_ref, a3_ref, b1_ref, b2_ref, b3_ref, b4_ref, gains_ref, *rest):
    source, rest = rest[:moves], rest[moves:]
    o1_ref, o2_ref, o3_ref, o4_ref, rest = rest[0], rest[1], rest[2], rest[3], rest[4:]
    now = pl.program_id(0)
    if moves:
        target, bounce, send, recv, local = rest
        me = place()
        swap = Swap(me, source[0], target, bounce, send, recv, local.at[0], 0, ((0, target.shape[1]),))

        @pl.when(now == 0)
        def _():
            greet(me)
            swap.give(0)
            swap.keep_begin()

        pl.when(now == 3)(swap.keep_turn)
        pl.when(now == 3 * steps)(swap.finish)

    @pl.when(now < steps)
    def _():
        o1_ref[...] = dot(a1_ref[...], b1_ref[...]).astype(BF)

    @pl.when((now >= steps) & (now < 2 * steps))
    def _():
        o2_ref[...] = dot(a1_ref[...], b2_ref[...]).astype(BF)

    @pl.when((now >= 2 * steps) & (now < 3 * steps))
    def _():
        o3_ref[...] = dot(a2_ref[...], b3_ref[...]).astype(BF)

    @pl.when(now == 3 * steps)
    def _():
        width = b4_ref.shape[1]
        o4_ref[:, :width] = dot(a3_ref[...], b4_ref[...])
        o4_ref[:, width:] = gains_ref[...]


def outers_call(h_t, df_t, att_t, d_gate, d_up, act, d_first, gains, moving=(), tile=512):
    width, tokens = h_t.shape
    hidden = d_gate.shape[1]
    steps = hidden // tile

    def whole(a):
        return pl.BlockSpec(a.shape, lambda i: (0, 0), pipeline_mode=pl.Buffered(1))

    def part(rows, n):
        return pl.BlockSpec((rows, tile), lambda i: (0, jnp.clip(i - n * steps, 0, steps - 1)))

    moves = len(moving)
    hbm = pl.BlockSpec(memory_space=pl.ANY)
    extra = [pltpu.VMEM(a.shape[1:], BF) for a in moving]
    extra += [pltpu.SemaphoreType.DMA((1,))] * (3 * moves)
    more = dict(collective_id=4, has_side_effects=True) if moves else {}
    return pl.pallas_call(
        functools.partial(outers_kernel, steps, moves),
        grid=(3 * steps + 1,),
        in_specs=[whole(h_t), whole(df_t), whole(att_t)]
        + [part(tokens, n) for n in range(3)]
        + [whole(d_first), whole(gains)]
        + [hbm] * moves,
        out_specs=[part(width, n) for n in range(3)]
        + [pl.BlockSpec((width, width + gains.shape[1]), lambda i: (0, 0), pipeline_mode=pl.Buffered(1))]
        + [hbm] * moves,
        out_shape=[jax.ShapeDtypeStruct((width, hidden), BF)] * 3
        + [jax.ShapeDtypeStruct((width, width + gains.shape[1]), F32)]
        + [jax.ShapeDtypeStruct(a.shape, BF) for a in moving],
        scratch_shapes=extra,
        compiler_params=pltpu.CompilerParams(vmem_limit_bytes=VMEM_LIMIT, **more),
        name="outers",
    )(h_t, df_t, att_t, d_gate, d_up, act, d_first, gains, *moving)


CLOSING_ORDERS = ("xy", "xy", "xy")


def closing_kernel(
    dq_hbm, dk_hbm, dv_hbm, first_hbm, xt_hbm, w_hbm, g_out, sum_ref,
    dq, dk, dv, first, xt, w, g, w0, w1, w2, send, recv, local, mine_sem, *bufs,
):
    me = place()
    y = me["y"]
    loads = [
        pltpu.make_async_copy(a, b, local.at[i])
        for i, (a, b) in enumerate(
            ((w_hbm, w), (dq_hbm, dq), (dk_hbm, dk), (dv_hbm, dv), (first_hbm, first), (xt_hbm, xt))
        )
    ]
    for load in loads:
        load.start()
    greet(me)
    width = dq.shape[1]
    half = g.shape[1]
    tile = half // 2

    def rows_of(which, t):
        at = pl.ds(pl.multiple_of(which * half + t * tile, tile), tile)
        total = first[at, :].astype(F32)
        for n, a in enumerate((dq, dk, dv)):
            total += dot_nt(a[at, :], w[:, n * width : (n + 1) * width])
        g[which, pl.ds(t * tile, tile), :] = total.astype(BF)

    for load in loads[:5]:
        load.wait()
    quarter = half // 4

    def give(n, target_half):
        part = pl.ds(n * quarter, quarter)
        return pltpu.make_async_remote_copy(
            src_ref=g.at[1 - y, part],
            dst_ref=g_out.at[target_half, part],
            send_sem=send.at[n],
            recv_sem=recv.at[n],
            device_id=device(moved(me, "y", 1)),
            device_id_type=MESH,
        )

    rows_of(1 - y, 0)
    give(0, y).start()
    give(1, y).start()
    rows_of(1 - y, 1)
    loads[5].wait()
    reduces = []
    for n, (a, target) in enumerate(((dq, w0), (dk, w1), (dv, w2))):
        reduces.append(
            Reduce(
                me, tall_piece(target), bufs[5 * n : 5 * n + 5], sum_ref.at[:, pl.ds(n * width, width)],
                send, recv, mine_sem.at[pl.ds(2 * n, 2)], 4 + n * Reduce.SEMS, CLOSING_ORDERS[n],
            )
        )

    def products(n, a, target):
        step = 2 * PAIR

        def part(i, _):
            at = pl.ds(pl.multiple_of(i * step, step), step)
            value = dot(xt[...], a[:, at])
            target[:, :, :, :, :, at] = value.reshape(target.shape[:-1] + (step,)).astype(BF)
            return 0

        lax.fori_loop(0, width // step, part, 0)

    products(0, dq, w0)
    reduces[0].start()
    give(2, y).start()
    products(1, dk, w1)
    reduces[1].start()
    reduces[0].step(1)
    products(2, dv, w2)
    reduces[2].start()
    reduces[1].step(1)
    reduces[0].step(2)
    reduces[2].step(1)
    rows_of(y, 0)
    reduces[1].step(2)
    reduces[0].step(3)
    rows_of(y, 1)
    keep = pltpu.make_async_copy(g.at[y], g_out.at[y], local.at[0])
    keep.start()
    reduces[2].step(2)
    give(3, y).start()
    reduces[1].step(3)
    reduces[0].step(4)
    reduces[2].step(3)
    reduces[1].step(4)
    reduces[2].step(4)
    for r in reduces:
        r.finish()
    for n in range(4):
        give(n, 1 - y).wait_recv()
        give(n, y).wait_send()
    keep.wait()


def closing_call(dq, dk, dv, first, xt, w):
    tokens, width = dq.shape
    hbm = pl.BlockSpec(memory_space=pl.ANY)
    block = (width // 32, width)
    full = pltpu.VMEM((4, 2, 2, 2) + block, BF)
    scratch = [pltpu.VMEM(a.shape, BF) for a in (dq, dk, dv, first, xt, w)]
    scratch += [pltpu.VMEM((2, tokens // 2, width), BF), full, full, full]
    sems = 4 + 3 * Reduce.SEMS
    scratch += [pltpu.SemaphoreType.DMA((sems,))] * 2
    scratch += [pltpu.SemaphoreType.DMA((6,)), pltpu.SemaphoreType.DMA((6,))]
    for order in CLOSING_ORDERS:
        scratch += Reduce.scratch(*block, BF, order)
    return pl.pallas_call(
        closing_kernel,
        in_specs=[hbm] * 6,
        out_specs=[hbm, pl.BlockSpec(memory_space=pltpu.VMEM)],
        out_shape=[
            jax.ShapeDtypeStruct((2, tokens // 2, width), BF),
            jax.ShapeDtypeStruct((block[0], 3 * width), F32),
        ],
        scratch_shapes=scratch,
        compiler_params=pltpu.CompilerParams(
            vmem_limit_bytes=VMEM_LIMIT, collective_id=3, has_side_effects=True
        ),
        name="closing",
    )(dq, dk, dv, first, xt, w)


def tokens_kernel(dq_ref, dk_ref, dv_ref, dfirst_ref, w_ref, o_ref):
    width = dq_ref.shape[1]
    total = dfirst_ref[...].astype(F32)
    total += dot_nt(dq_ref[...], w_ref[:, :width])
    total += dot_nt(dk_ref[...], w_ref[:, width : 2 * width])
    total += dot_nt(dv_ref[...], w_ref[:, 2 * width :])
    o_ref[...] = total.astype(BF)


def tokens_call(dq, dk, dv, dfirst, w, tile=512):
    tokens, width = dq.shape
    tile = min(tile, tokens)
    row = pl.BlockSpec((tile, width), lambda i: (i, 0))
    return pl.pallas_call(
        tokens_kernel,
        grid=(tokens // tile,),
        in_specs=[row] * 4 + [pl.BlockSpec(w.shape, lambda i: (0, 0), pipeline_mode=pl.Buffered(1))],
        out_specs=row,
        out_shape=jax.ShapeDtypeStruct((tokens, width), BF),
        compiler_params=params(),
        name="grad_tokens",
    )(dq, dk, dv, dfirst, w)


def angle_tables(span):
    index = np.arange(HEAD // 2, dtype=np.float64)
    inverse = np.power(1000.0, -2.0 * index / HEAD)
    angles = np.arange(span, dtype=np.float64)[:, None] * inverse[None, :]
    repeat = (1, PAIR // (HEAD // 2))
    return (
        np.tile(np.cos(angles), repeat).astype(np.float32),
        np.tile(np.sin(angles), repeat).astype(np.float32),
    )


def body(tokens, lengths, w_qkv, w_out, w_gate, w_up, w_down, gain_one, gain_two, cotangent):
    axes = ("dp", "blk")
    blk = lax.axis_size("blk")
    mine = lax.axis_index("blk")
    rows, span, width = tokens.shape
    seq = span * blk
    own = blk == 2 and rows == 2 and lax.axis_size("dp") == 16

    def gather(a):
        return lax.all_gather(a, axes, axis=0, tiled=True)

    cosine, sine = map(jnp.asarray, angle_tables(seq))
    gains = jnp.stack([gain_one, gain_two], 1)
    if own:
        w_out = jnp.pad(jnp.concatenate([w_out, gains], 1), ((0, 0), (0, PAIR - 2)))
        x, f_qkv, w_out, w_gate = opening_call(tokens, w_qkv, (w_out, w_gate))
        x = x.reshape(1, seq, width)
        f_qkv = f_qkv.reshape(width, -1)
        length = lax.dynamic_slice_in_dim(lengths, mine, 1, 0)
        cq, sq = cosine, sine
    else:
        f_qkv, f_out, f_gate, f_up, f_down = map(gather, (w_qkv, w_out, w_gate, w_up, w_down))
        f_gains = gather(gains).astype(F32)
        x, cot, length = tokens, cotangent.reshape(rows * span, width), lengths
        cq = lax.dynamic_slice_in_dim(cosine, mine * span, span, 0)
        sq = lax.dynamic_slice_in_dim(sine, mine * span, span, 0)
    n, t = x.shape[:2]
    flat = x.reshape(n * t, width)
    q, k, v, xt, *moving = qkv_call(
        flat, f_qkv, cq, sq, (w_out, w_gate, w_up, w_down) if own else ()
    )
    q, k, v = (a.reshape(n, t, width) for a in (q, k, v))
    if not own:
        k = lax.all_gather(k, "blk", axis=1, tiled=True)
        v = lax.all_gather(v, "blk", axis=1, tiled=True)
    position = jnp.arange(seq, dtype=jnp.int32)[None, :, None]
    lane = jnp.arange(PAIR, dtype=jnp.int32)[None, None, :]
    bias = jnp.where((lane % HEAD == 3) & (position >= length[:, None, None]), NEG, 0.0).astype(BF)
    if own:
        att, aug, f_out, f_gate, f_up, f_down = attend_call(
            q, k, v, bias, moving
        )
        f_out = f_out.reshape(width, -1)
        f_gains = f_out[:, width : width + 2].astype(F32)
        cot = cotangent
        f_gate, f_up = f_gate.reshape(width, -1), f_up.reshape(width, -1)
        f_down = f_down.reshape(-1, width)
    else:
        att, aug = attend_call(q, k, v, bias)
    g1, g2 = f_gains[:, 0][None], f_gains[:, 1][None]
    out, d_first, d_att, act, d_gate, d_up, h_t, df_t, att_t, gg1, gg2 = middle_call(
        flat, att.reshape(n * t, width), cot, f_out, f_gate, f_up, f_down, g1, g2
    )
    gains = jnp.pad(jnp.concatenate([gg1, gg2]).T, ((0, 0), (0, PAIR - 2)))
    moving = (out.reshape(2, span, width),) if own else ()
    gw_gate, gw_up, gw_down_t, gw_out, *moving = outers_call(
        h_t, df_t, att_t, d_gate, d_up, act, d_first, gains, moving
    )
    d_att = d_att.reshape(n, t, width)
    if own:
        wide = tuple(g.reshape(4, 2, 2, width // 16, -1) for g in (gw_gate, gw_up, gw_down_t))
        out = moving[0]
        dq, dk, dv, s_gate, s_up, s_down_t, s_out = attend_back_call(
            q, k, v, bias, att, d_att, aug, cq, sq, True,
            wide + (gw_out.reshape(4, 2, 2, 2, width // 32, -1),),
        )
    else:

        def scatter_wide(g):
            g = lax.psum_scatter(g, "blk", scatter_dimension=1, tiled=True)
            return lax.psum_scatter(g, "dp", scatter_dimension=0, tiled=True).astype(F32)

        s_gate, s_up, s_down_t = map(scatter_wide, (gw_gate, gw_up, gw_down_t))
        s_out = lax.psum_scatter(gw_out, axes, scatter_dimension=0, tiled=True)
        dq, dk, dv = attend_back_call(q, k, v, bias, att, d_att, aug, cq, sq, False)
        dk = lax.psum_scatter(dk, "blk", scatter_dimension=1, tiled=True)
        dv = lax.psum_scatter(dv, "blk", scatter_dimension=1, tiled=True)
        heads = (dk * jnp.tile(sq, (1, width // PAIR))).reshape(n, t, HEADS, HEAD)
        half = jnp.concatenate([heads[..., HEAD // 2 :], -heads[..., : HEAD // 2]], -1)
        dk = dk * jnp.tile(cq, (1, width // PAIR)) + half.reshape(n, t, width)
        dk, dv = dk.astype(BF), dv.astype(BF)
    s_down = s_down_t.T
    s_out, s_gg = s_out[:, :width], s_out[:, width : width + 2]
    dq, dk, dv = (a.reshape(n * t, width) for a in (dq, dk, dv))
    if own:
        g_tokens, s_qkv = closing_call(dq, dk, dv, d_first, xt, f_qkv)
    else:
        gw_qkv = jnp.concatenate([outer_call(xt, a, BF, 256) for a in (dq, dk, dv)], 1)
        s_qkv = lax.psum_scatter(gw_qkv, axes, scatter_dimension=0, tiled=True).astype(F32)
        g_tokens = tokens_call(dq, dk, dv, d_first, f_qkv).reshape(tokens.shape)
        out = out.reshape(tokens.shape)
    return (out, g_tokens, s_qkv, s_out, s_gate, s_up, s_down, s_gg[:, 0], s_gg[:, 1])


def solution(mesh):
    both = ("dp", "blk")
    return jax.shard_map(
        body,
        mesh=mesh,
        in_specs=(
            P("dp", "blk", None),
            P("dp"),
            P(both, None),
            P(both, None),
            P(both, None),
            P(both, None),
            P(both, None),
            P(both),
            P(both),
            P("dp", "blk", None),
        ),
        out_specs=(
            P("dp", "blk", None),
            P("dp", "blk", None),
            P(both, None),
            P(both, None),
            P("dp", "blk"),
            P("dp", "blk"),
            P("blk", "dp"),
            P(both),
            P(both),
        ),
        check_vma=False,
    )
```

```python
import functools

import jax
import jax.numpy as jnp
import numpy as np
from jax import lax
from jax.experimental import pallas as pl
from jax.experimental.pallas import tpu as pltpu
from jax.sharding import PartitionSpec as P

HEADS = 12
HEAD = 64
PAIR = 2 * HEAD
EPS = 1e-05
NEG = -1e30
LOG2E = 1.4426950408889634
LN2 = 0.6931471805599453
VMEM_LIMIT = 60 * 1024 * 1024

BF = jnp.bfloat16
F32 = jnp.float32


def dot(a, b):
    return lax.dot_general(a, b, (((1,), (0,)), ((), ())), preferred_element_type=F32)


def dot_nt(a, b):
    return lax.dot_general(a, b, (((1,), (1,)), ((), ())), preferred_element_type=F32)


def params(limit=VMEM_LIMIT):
    return pltpu.CompilerParams(vmem_limit_bytes=limit)


def lanes(shape):
    return lax.broadcasted_iota(jnp.int32, shape, 1)


def turn(u):
    low_half = (lanes(u.shape) % HEAD) < HEAD // 2
    return jnp.where(low_half, -pltpu.roll(u, PAIR - HEAD // 2, 1), pltpu.roll(u, HEAD // 2, 1))


MESH = pl.DeviceIdType.MESH
AXES = "zxcy"
SIZE = {"z": 4, "x": 2, "c": 2, "y": 2}


def place():
    dp, y = lax.axis_index("dp"), lax.axis_index("blk")
    return {"z": dp // 4, "x": dp // 2 % 2, "c": dp % 2, "y": y}


def moved(me, axis, by):
    return {**me, axis: lax.rem(me[axis] + by, SIZE[axis])}


def device(at):
    return ((at["z"] * 2 + at["x"]) * 2 + at["c"], at["y"])


def greet(me):
    barrier = pltpu.get_barrier_semaphore()
    peers = [moved(me, "y", 1), moved(me, "x", 1), moved(me, "c", 1)]
    peers += [moved(me, "z", d) for d in range(1, 4)]
    for peer in peers:
        pl.semaphore_signal(barrier, inc=1, device_id=device(peer), device_id_type=MESH)
    pl.semaphore_wait(barrier, len(peers))


class Gather:
    def __init__(self, me, shard, full, send, recv, local, base, order, held="", columns=None):
        self.me, self.shard, self.full, self.held = me, shard, full, held
        self.part = () if columns is None else (slice(None), pl.ds(*columns))
        self.spans = [a for a in AXES if a in held + order]
        self.send, self.recv, self.local, self.base, self.order = send, recv, local, base, order

    @staticmethod
    def sems(order):
        return sum(SIZE[a] - 1 for a in order)

    def view(self, at, got):
        return self.full.at[tuple(slice(None) if a in got else at[a] for a in self.spans) + self.part]

    def at_stage(self, stage):
        got = self.held + self.order[:stage]
        return got, self.order[stage], self.base + self.sems(self.order[:stage])

    def copies(self, stage):
        got, axis, slot = self.at_stage(stage)
        here = self.view(self.me, got)
        return [
            pltpu.make_async_remote_copy(
                src_ref=self.shard if stage == 0 else here,
                dst_ref=here,
                send_sem=self.send.at[slot + d - 1],
                recv_sem=self.recv.at[slot + d - 1],
                device_id=device(moved(self.me, axis, d)),
                device_id_type=MESH,
            )
            for d in range(1, SIZE[axis])
        ]

    def own(self):
        return pltpu.make_async_copy(self.shard, self.view(self.me, self.held), self.local)

    def arrivals(self, stage):
        got, axis, slot = self.at_stage(stage)
        for d in range(1, SIZE[axis]):
            there = self.view(moved(self.me, axis, SIZE[axis] - d), got)
            pltpu.make_async_remote_copy(
                src_ref=there,
                dst_ref=there,
                send_sem=self.send.at[slot + d - 1],
                recv_sem=self.recv.at[slot + d - 1],
                device_id=device(moved(self.me, axis, d)),
                device_id_type=MESH,
            ).wait_recv()

    def start(self):
        self.own().start()
        for copy in self.copies(0):
            copy.start()

    def step(self, stage):
        self.arrivals(stage - 1)
        if stage == 1:
            self.own().wait()
        if stage < len(self.order):
            for copy in self.copies(stage):
                copy.start()

    def finish(self):
        for stage in range(len(self.order)):
            for copy in self.copies(stage):
                copy.wait_send()


class Reduce:
    SEMS = 7

    def __init__(self, me, piece, bufs, out, send, recv, local, base, order):
        self.me, self.piece, self.out, self.order = me, piece, out, order
        self.b, self.r0, self.r1, self.r2, self.r3 = bufs
        self.send, self.recv, self.local, self.base = send, recv, local, base

    def copy(self, source, target, slot, axis, by=1):
        return pltpu.make_async_remote_copy(
            src_ref=source,
            dst_ref=target,
            send_sem=self.send.at[self.base + slot],
            recv_sem=self.recv.at[self.base + slot],
            device_id=device(moved(self.me, axis, by)),
            device_id_type=MESH,
        )

    def mine(self):
        c = self.me["c"]
        return [
            pltpu.make_async_copy(self.piece(c, y), self.b.at[y], self.local.at[y]) for y in range(2)
        ]

    def copies(self, stage):
        x, y, z = self.me["x"], self.me["y"], self.me["z"]
        if stage == 0:
            other = 1 - self.me["c"]
            return [self.copy(self.piece(other, i), self.r0.at[i], i, "c") for i in range(2)]
        if stage == 1:
            source = self.b.at[1 - y] if self.order[0] == "y" else self.b.at[:, :, 1 - x]
            return [self.copy(source, self.r1, 2, self.order[0])]
        if stage == 2:
            source = self.b.at[y, :, 1 - x] if self.order[0] == "y" else self.b.at[1 - y, :, x]
            return [self.copy(source, self.r2, 3, self.order[1])]
        return [
            self.copy(self.b.at[y, lax.rem(z + d, 4), x], self.r3.at[d - 1], 3 + d, "z", d)
            for d in range(1, 4)
        ]

    def start(self):
        for copy in self.copies(0) + self.mine():
            copy.start()

    def step(self, stage):
        x, y, z = self.me["x"], self.me["y"], self.me["z"]
        for copy in self.copies(stage - 1):
            copy.wait_recv()
        b = self.b
        if stage == 1:
            for copy in self.mine():
                copy.wait()

            def add(i, _):
                at = (i // 4, i % 4)
                b[at] = b[at] + self.r0[at]
                return 0

            lax.fori_loop(0, 8, add, 0)
        if stage == 2:

            def add(i, _):
                if self.order[0] == "y":
                    for j in range(2):
                        b[y, i, j] = b[y, i, j] + self.r1[i, j]
                else:
                    for j in range(2):
                        b[j, i, x] = b[j, i, x] + self.r1[j, i]
                return 0

            lax.fori_loop(0, 4, add, 0)
        if stage == 3:

            def add(i, _):
                b[y, i, x] = b[y, i, x] + self.r2[i]
                return 0

            lax.fori_loop(0, 4, add, 0)
        if stage == 4:
            total = b[y, z, x].astype(F32)
            for d in range(3):
                total = total + self.r3[d].astype(F32)
            self.out[...] = total
            return
        for copy in self.copies(stage):
            copy.start()

    def finish(self):
        for stage in range(4):
            for copy in self.copies(stage):
                copy.wait_send()

    @staticmethod
    def scratch(rows, columns, kind, order):
        lead = (4, 2) if order[0] == "y" else (2, 4)
        return [
            pltpu.VMEM(shape + (rows, columns), kind)
            for shape in ((2, 4, 2), (2, 4, 2), lead, (4,), (3,))
        ]


class Swap:
    def __init__(self, me, source, target, bounce, send, recv, local, slots, parts):
        self.me, self.source, self.target, self.bounce = me, source, target, bounce
        self.send, self.recv, self.local, self.slots, self.parts = send, recv, local, slots, parts

    def copy(self, n, row, half):
        begin, size = self.parts[n]
        part = pl.ds(begin, size)
        return pltpu.make_async_remote_copy(
            src_ref=self.source.at[row, part],
            dst_ref=self.target.at[half, part],
            send_sem=self.send.at[self.slots + n],
            recv_sem=self.recv.at[self.slots + n],
            device_id=device(moved(self.me, "y", 1)),
            device_id_type=MESH,
        )

    def give(self, n):
        y = self.me["y"]
        self.copy(n, 1 - y, y).start()

    def keep_in(self):
        return pltpu.make_async_copy(self.source.at[self.me["y"]], self.bounce, self.local)

    def keep_out(self):
        return pltpu.make_async_copy(self.bounce, self.target.at[self.me["y"]], self.local)

    def keep_begin(self):
        self.keep_in().start()

    def keep_turn(self):
        self.keep_in().wait()
        self.keep_out().start()

    def finish(self):
        y = self.me["y"]
        for n in range(len(self.parts)):
            self.copy(n, 1 - y, 1 - y).wait_recv()
            self.copy(n, 1 - y, y).wait_send()
        self.keep_out().wait()


def halves(ref):
    half = ref.shape[-1] // 2
    return [ref.at[(slice(None),) * (len(ref.shape) - 1) + (pl.ds(n * half, half),)] for n in range(2)]


def stages(me, shards, fulls, orders, held, columns, send, recv, local, base=0):
    out = []
    for i, order in enumerate(orders):
        out.append(
            Gather(me, shards[i], fulls[i], send, recv, local.at[i], base, order, held[i], columns[i])
        )
        base += Gather.sems(order)
    return out


def project(x, w_ref, cosine, sine, put):
    width = x.shape[1]
    for part in range(3):
        for pair in range(width // PAIR):
            at = part * width + pair * PAIR
            if pair % 2 == 0:
                u2 = dot(x, w_ref[:, at : at + 2 * PAIR])
            u = u2[:, (pair % 2) * PAIR : (pair % 2 + 1) * PAIR]
            if part < 2:
                u = u * cosine + turn(u) * sine
            if part == 0:
                u = u * (0.125 * LOG2E)
            put(part, slice(pair * PAIR, (pair + 1) * PAIR), u.astype(BF))


def qkv_kernel(x_ref, w_ref, cos_ref, sin_ref, q_ref, k_ref, v_ref, xt_ref):
    x = x_ref[...]

    def put(part, columns, value):
        (q_ref, k_ref, v_ref)[part][:, columns] = value

    project(x, w_ref, cos_ref[...], sin_ref[...], put)
    xt_ref[...] = x.T


def qkv_call(x, w, cosine, sine, tile=512):
    tokens, width = x.shape
    span = cosine.shape[0]
    tile = min(tile, span)
    row = pl.BlockSpec((tile, width), lambda i: (i, 0))
    table = pl.BlockSpec((tile, PAIR), lambda i: (i % (span // tile), 0))
    return pl.pallas_call(
        qkv_kernel,
        grid=(tokens // tile,),
        in_specs=[
            row,
            pl.BlockSpec(w.shape, lambda i: (0, 0), pipeline_mode=pl.Buffered(1)),
            table,
            table,
        ],
        out_specs=[row, row, row, pl.BlockSpec((width, tile), lambda i: (0, i))],
        out_shape=[jax.ShapeDtypeStruct((tokens, width), BF)] * 3
        + [jax.ShapeDtypeStruct((width, tokens), BF)],
        compiler_params=params(),
        name="qkv",
    )(x, w, cosine, sine)


OPENING_ORDERS = ("yzxc", "zyxc", "zy", "zx", "z", "y", "x")


def opening_kernel(
    tok_hbm, w_shard, out_shard, gate_shard, up_shard, down_shard, cos_ref, sin_ref,
    x_hbm, w_hbm, q_hbm, k_hbm, v_hbm, xt_hbm, out_part, gate_part, up_part, left_part, right_part,
    x, w_blocks, w, q, k, v, xt, send, recv, local, load, store,
):
    me = place()
    y = me["y"]
    greet(me)
    rows = x.shape[1]
    begin = rows // 8
    parts = ((0, begin), (begin, rows - begin))

    def token_copy(n, row, half):
        part = pl.ds(*parts[n])
        return pltpu.make_async_remote_copy(
            src_ref=tok_hbm.at[row, part],
            dst_ref=x.at[half, part],
            send_sem=send.at[n],
            recv_sem=recv.at[n],
            device_id=device(moved(me, "y", 1)),
            device_id_type=MESH,
        )

    width = w.shape[1] // 2
    g = stages(
        me,
        halves(w_shard) + [out_shard, gate_shard, up_shard] + halves(down_shard),
        [w_blocks, w_blocks, out_part, gate_part, up_part, left_part, right_part],
        OPENING_ORDERS,
        ("",) * 7,
        ((0, width), (width, width)) + (None,) * 5,
        send, recv, local, 2,
    )
    mine = pltpu.make_async_copy(tok_hbm.at[y], x.at[y], load.at[0])
    g[0].start()
    g[1].start()
    token_copy(0, 1 - y, y).start()
    mine.start()
    g[0].step(1)
    g[1].step(1)
    token_copy(1, 1 - y, y).start()
    g[0].step(2)
    for n in (2, 3, 4):
        g[n].start()
    g[1].step(2)
    g[6].start()
    g[5].start()
    g[0].step(3)
    g[1].step(3)
    g[0].step(4)
    g[1].step(4)
    g[2].step(1)
    g[3].step(1)
    for n in range(3):
        part = slice(n * w.shape[0], (n + 1) * w.shape[0])
        block = w_blocks[:, :, :, :, :, part].astype(F32)
        w[:, part] = block.reshape(w.shape[0], w.shape[0]).astype(BF)
    keep_w = pltpu.make_async_copy(w, w_hbm, load.at[1])
    keep_w.start()
    mine.wait()
    tile = 512

    def stores(n):
        half = lax.rem(y + n // 2, 2)
        at = pl.ds(pl.multiple_of(half * rows + lax.rem(n, 2) * tile, tile), tile)
        pairs = [(a.at[at], b.at[at]) for a, b in ((q, q_hbm), (k, k_hbm), (v, v_hbm))]
        pairs.append((xt.at[:, at], xt_hbm.at[:, at]))
        return [pltpu.make_async_copy(a, b, store.at[n, i]) for i, (a, b) in enumerate(pairs)]

    def tile_step(n, _):
        half = lax.rem(y + n // 2, 2)
        start = pl.multiple_of(half * rows + lax.rem(n, 2) * tile, tile)
        at = pl.ds(start, tile)

        @pl.when(n == 2)
        def _():
            for m in range(2):
                token_copy(m, 1 - y, 1 - y).wait_recv()

        value = x[half, pl.ds(pl.multiple_of(lax.rem(n, 2) * tile, tile), tile), :]

        def put(part, columns, u):
            (q, k, v)[part][at, columns] = u

        project(value, w, cos_ref[at, :], sin_ref[at, :], put)
        xt[:, at] = value.T
        for copy in stores(n):
            copy.start()
        return 0

    lax.fori_loop(0, 4, tile_step, 0)
    keep_x = pltpu.make_async_copy(x, x_hbm, load.at[2])
    keep_x.start()
    g[2].step(2)
    g[3].step(2)
    for n in (4, 5, 6):
        g[n].step(1)
    for gather in g:
        gather.finish()
    for m in range(2):
        token_copy(m, 1 - y, y).wait_send()
    for n in range(4):
        for copy in stores(n):
            copy.wait()
    keep_w.wait()
    keep_x.wait()


def opening_call(tokens, w_qkv, w_out, w_gate, w_up, w_down, cosine, sine):
    rows, span, width = tokens.shape
    total = rows * span
    hbm = pl.BlockSpec(memory_space=pl.ANY)
    held = pl.BlockSpec(memory_space=pltpu.VMEM)
    whole = (width, w_qkv.shape[1])
    flat = (total, width)
    shapes = [tokens.shape, whole, flat, flat, flat, (width, total)]
    shapes += [(4, 2) + w_out.shape, (4, 2) + w_gate.shape, (4,) + w_up.shape]
    shapes += [(2, w_down.shape[0], w_down.shape[1] // 2)] * 2
    sems = 2 + sum(map(Gather.sems, OPENING_ORDERS))
    return pl.pallas_call(
        opening_kernel,
        in_specs=[hbm] + [held] * 7,
        out_specs=[hbm] * len(shapes),
        out_shape=[jax.ShapeDtypeStruct(shape, BF) for shape in shapes],
        scratch_shapes=[
            pltpu.VMEM(tokens.shape, BF),
            pltpu.VMEM((4, 2, 2, 2) + w_qkv.shape, BF),
            pltpu.VMEM(whole, BF),
            pltpu.VMEM(flat, BF),
            pltpu.VMEM(flat, BF),
            pltpu.VMEM(flat, BF),
            pltpu.VMEM((width, total), BF),
            pltpu.SemaphoreType.DMA((sems,)),
            pltpu.SemaphoreType.DMA((sems,)),
            pltpu.SemaphoreType.DMA((len(OPENING_ORDERS),)),
            pltpu.SemaphoreType.DMA((3,)),
            pltpu.SemaphoreType.DMA((4, 4)),
        ],
        compiler_params=pltpu.CompilerParams(
            vmem_limit_bytes=VMEM_LIMIT, collective_id=0, has_side_effects=True
        ),
        name="opening",
    )(tokens, w_qkv, w_out, w_gate, w_up, w_down, cosine, sine)


def attend_kernel(tile, chunk, moves, q_ref, k_ref, v_ref, bias_ref, *rest):
    inputs, rest = rest[:moves], rest[moves:]
    o_ref, aug_ref, rest = rest[0], rest[1], rest[2:]
    results = max(moves - 1, 0)
    outputs, rest = rest[:results], rest[results:]
    ka, va, s_scr, m_scr = rest[:4]
    keys, span = k_ref.shape[1], q_ref.shape[1]
    tiles = span // tile
    events = {}
    if moves:
        events = attend_events(inputs, outputs, *rest[4:])

    @pl.when(pl.program_id(1) == 0)
    def _():
        ka[:, PAIR:] = bias_ref[0]
        va[:, PAIR:] = jnp.ones((keys, PAIR), BF)

    ka[:, :PAIR] = k_ref[0]
    va[:, :PAIR] = v_ref[0]
    lane = lanes((tile, PAIR))
    side = lanes((tile, 2 * PAIR)) // HEAD % 2
    ones = (lane % HEAD == 3).astype(F32).astype(BF)
    chunks = keys // chunk

    def query(i, h):
        at = pl.ds(pl.multiple_of(i * tile, tile), tile)
        both = jnp.concatenate([q_ref[0, at, :], ones], axis=1)
        return jnp.where(side == h, both, jnp.zeros_like(both))

    def score(qa, h, c, top):
        s = dot_nt(qa, ka[c * chunk : (c + 1) * chunk, :])
        s_scr[h, :, c * chunk : (c + 1) * chunk] = s
        for b in range(chunk // PAIR):
            part = s[:, b * PAIR : (b + 1) * PAIR]
            top = part if top is None else jnp.maximum(top, part)
        return top

    def close(h, top):
        m_scr[h] = jnp.broadcast_to(jnp.max(top, axis=1, keepdims=True), (tile, PAIR))

    def unit(h, later, other):
        m = m_scr[h]
        wide = jnp.concatenate([m] * (chunk // PAIR), axis=1)
        qa = query(later, other)
        acc, top = None, None
        for c in range(chunks):
            top = score(qa, other, c, top)
            p = jnp.exp2(s_scr[h, :, c * chunk : (c + 1) * chunk] - wide).astype(BF)
            part = dot(p, va[c * chunk : (c + 1) * chunk, :])
            acc = part if acc is None else acc + part
        return acc, top, m

    top = None
    qa = query(0, 0)
    for c in range(chunks):
        top = score(qa, 0, c, top)
    close(0, top)

    def step(i, _):
        acc0, top, m0 = unit(0, i, 1)
        close(1, top)
        acc1, top, m1 = unit(1, jnp.minimum(i + 1, tiles - 1), 0)
        close(0, top)
        mine = lane < HEAD
        total = jnp.where(mine, acc0[:, PAIR:], acc1[:, PAIR:])
        at = pl.ds(pl.multiple_of(i * tile, tile), tile)
        o_ref[0, at, :] = (jnp.where(mine, acc0[:, :PAIR], acc1[:, :PAIR]) / total).astype(BF)
        lse = jnp.where(mine, m0, m1) + jnp.log2(total)
        aug_ref[0, at, :] = spread(lse, jnp.where(lane % HEAD == 3, 1.0, 0.0))
        return 0

    unroll = 2 if tiles % 2 == 0 else 1

    def group(n, _):
        now = pl.program_id(1) * (tiles // unroll) + n
        for at_step, acts in events.items():

            @pl.when(now == at_step)
            def _():
                for act in acts:
                    act()

        for j in range(unroll):
            step(n * unroll + j, 0)
        return 0

    lax.fori_loop(0, tiles // unroll, group, 0)
    if moves:

        @pl.when(pl.program_id(1) == pl.num_programs(1) - 1)
        def _():
            for act in events.last:
                act()


class Events(dict):
    def __init__(self):
        self.last = []

    def put(self, at, *acts):
        self.setdefault(at, []).extend(acts)


ATTEND_HELD = ("zy", "zx", "z", "y", "x")
ATTEND_ORDERS = ("xc", "yc", "yxc", "zxc", "zyc")
ATTEND_PLAN = ((2, 0, 1), (4, 2, 1), (4, 3, 1), (7, 4, 1), (10, 1, 1), (10, 2, 2), (11, 3, 2), (11, 4, 2))
ATTEND_FIRST = (2, 1, 0, 3, 4)


def attend_events(inputs, outputs, send, recv, local):
    me = place()
    half = inputs[3].shape[-1]
    columns = (None, None, None, (0, half), (half, half))
    fulls = tuple(outputs) + (outputs[3],)
    gathers = stages(me, inputs, fulls, ATTEND_ORDERS, ATTEND_HELD, columns, send, recv, local)
    events = Events()
    events.put(0, functools.partial(greet, me), *(gathers[i].start for i in ATTEND_FIRST))
    done = [1] * len(gathers)
    for at, i, stage in ATTEND_PLAN:
        events.put(at, functools.partial(gathers[i].step, stage))
        done[i] = stage + 1
    for stage in range(1, 4):
        for i, g in enumerate(gathers):
            if done[i] <= stage <= len(ATTEND_ORDERS[i]):
                events.last.append(functools.partial(g.step, stage))
    events.last += [g.finish for g in gathers]
    return events


def spread(value, other):
    high = value.astype(BF).astype(F32)
    rest = value - high
    mid = rest.astype(BF).astype(F32)
    low = rest - mid
    sub = lanes(value.shape) % HEAD
    return jnp.where(
        sub == 0, high, jnp.where(sub == 1, mid, jnp.where(sub == 2, low, other))
    ).astype(BF)


def attend_call(q, k, v, bias, moving=(), tile=512, chunk=512):
    rows, span, width = q.shape
    keys = k.shape[1]
    tile = min(tile, span)
    moves = len(moving)
    qs = pl.BlockSpec((1, span, PAIR), lambda r, p: (r, 0, p))
    ks = pl.BlockSpec((1, keys, PAIR), lambda r, p: (r, 0, p))
    hbm = pl.BlockSpec(memory_space=pl.ANY)
    moved_shapes = [jax.ShapeDtypeStruct((4, 2, 2, 2) + a.shape[-2:], a.dtype) for a in moving[:3]]
    for a in moving[3:4]:
        moved_shapes.append(jax.ShapeDtypeStruct((4, 2, 2, 2, a.shape[-2], 2 * a.shape[-1]), a.dtype))
    sems = sum(map(Gather.sems, ATTEND_ORDERS))
    extra = [pltpu.SemaphoreType.DMA((sems,))] * 2 + [pltpu.SemaphoreType.DMA((len(ATTEND_ORDERS),))]
    held = [
        pl.BlockSpec(a.shape, lambda r, p, n=a.ndim: (0,) * n, pipeline_mode=pl.Buffered(1))
        for a in moving
    ]
    more = dict(collective_id=1, has_side_effects=True) if moves else {}
    return pl.pallas_call(
        functools.partial(attend_kernel, tile, chunk, moves),
        grid=(rows, width // PAIR),
        in_specs=[qs, ks, ks, pl.BlockSpec((1, keys, PAIR), lambda r, p: (r, 0, 0))]
        + held,
        out_specs=[qs, qs] + [hbm] * len(moved_shapes),
        out_shape=[jax.ShapeDtypeStruct(q.shape, BF)] * 2 + moved_shapes,
        scratch_shapes=[
            pltpu.VMEM((keys, 2 * PAIR), BF),
            pltpu.VMEM((keys, 2 * PAIR), BF),
            pltpu.VMEM((2, tile, keys), F32),
            pltpu.VMEM((2, tile, PAIR), F32),
        ]
        + (extra if moves else []),
        compiler_params=pltpu.CompilerParams(vmem_limit_bytes=VMEM_LIMIT, **more),
        name="attend",
    )(q, k, v, bias, *moving)


def attend_back_kernel(
    tq, unroll, moves, q_ref, k_ref, v_ref, bias_ref, o_ref, do_ref, aug_ref, cos_ref, sin_ref, *rest
):
    inputs, rest = rest[:moves], rest[moves:]
    dq_ref, dk_ref, dv_ref, rest = rest[0], rest[1], rest[2], rest[3:]
    outputs, rest = rest[:moves], rest[moves:]
    qa, da, ka, va, kt, dk_acc, dv_acc = rest[:7]
    keys, span = k_ref.shape[1], q_ref.shape[1]
    tiles = span // tq
    events = {}
    if moves:
        events = back_events(inputs, outputs, *rest[7:])

    @pl.when(pl.program_id(1) == 0)
    def _():
        minus = jnp.where(lanes((keys, PAIR)) % HEAD < 3, -1.0, 0.0)
        ka[:, PAIR:] = (minus + bias_ref[0].astype(F32)).astype(BF)
        va[:, PAIR:] = minus.astype(BF)

    k, do = k_ref[0], do_ref[0]
    ka[:, :PAIR] = k
    va[:, :PAIR] = v_ref[0]
    kt[...] = k.T
    prod = do.astype(F32) * o_ref[0].astype(F32)
    first = prod.astype(BF)
    second = (prod - first.astype(F32)).astype(BF)
    block = (
        (lax.broadcasted_iota(jnp.int32, (PAIR, PAIR), 0) // HEAD)
        == (lax.broadcasted_iota(jnp.int32, (PAIR, PAIR), 1) // HEAD)
    ).astype(F32).astype(BF)
    delta = dot(first, block) + dot(second, block)
    q_both = jnp.concatenate([q_ref[0], aug_ref[0]], axis=1)
    d_both = jnp.concatenate([do, spread(delta, jnp.zeros_like(delta))], axis=1)
    side = lanes(q_both.shape) // HEAD % 2
    for h in range(2):
        qa[h] = jnp.where(side == h, q_both, jnp.zeros_like(q_both))
        da[h] = jnp.where(side == h, d_both, jnp.zeros_like(d_both))
    dk_acc[...] = jnp.zeros_like(dk_acc)
    dv_acc[...] = jnp.zeros_like(dv_acc)

    def query_step(i, _):
        at_q = pl.ds(pl.multiple_of(i * tq, tq), tq)
        dv, dk, dq = None, None, []
        for h in range(2):
            st = dot_nt(ka[...], qa[h, at_q, :])
            dpt = dot_nt(va[...], da[h, at_q, :])
            p = jnp.exp2(st)
            ds = (p * dpt).astype(BF)
            pv = dot(p.astype(BF), da[h, at_q, :PAIR])
            pk = dot(ds, qa[h, at_q, :PAIR])
            dv = pv if dv is None else dv + pv
            dk = pk if dk is None else dk + pk
            dq.append(dot(kt[h * HEAD : (h + 1) * HEAD, :], ds))
        dv_acc[...] += dv
        dk_acc[...] += dk
        g = jnp.concatenate(dq, axis=0).T * 0.125
        dq_ref[0, at_q, :] = back_turn(g, cos_ref[at_q, :], sin_ref[at_q, :]).astype(BF)
        return 0

    def group(n, _):
        now = pl.program_id(1) * (tiles // unroll) + n
        for at_step, acts in events.items():

            @pl.when(now == at_step)
            def _():
                for act in acts:
                    act()

        for j in range(unroll):
            query_step(n * unroll + j, 0)
        return 0

    lax.fori_loop(0, tiles // unroll, group, 0)
    dv_ref[0] = dv_acc[...].astype(dv_ref.dtype)
    g = dk_acc[...] * LN2
    if dk_ref.dtype == BF:
        g = back_turn(g, cos_ref[...], sin_ref[...])
    dk_ref[0] = g.astype(dk_ref.dtype)
    if moves:

        @pl.when(pl.program_id(1) == pl.num_programs(1) - 1)
        def _():
            for act in events.last:
                act()


def back_turn(g, cosine, sine):
    return g * cosine - turn(g * sine)


def wide_piece(source, columns):
    return lambda c, y: source.at[:, :, c, :, pl.ds(y * columns, columns)]


def tall_piece(source):
    return lambda c, y: source.at[:, :, c, y]


BACK_ORDERS = ("yx", "yx", "xy", "xy")
BACK_PLAN = (
    (1, 0, 1), (1, 2, 1), (1, 1, 1), (1, 3, 1), (3, 0, 2), (3, 2, 2), (3, 3, 2), (4, 0, 3), (4, 2, 3), (4, 1, 2),
    (5, 1, 3), (5, 3, 3), (5, 0, 4),
)


def back_events(inputs, outputs, send, recv, local, *bufs):
    me = place()
    reduces = []
    for i, (source, out) in enumerate(zip(inputs, outputs)):
        piece = wide_piece(source, source.shape[-1] // 2) if len(source.shape) == 5 else tall_piece(source)
        reduces.append(
            Reduce(
                me, piece, bufs[5 * i : 5 * i + 5], out, send, recv,
                local.at[pl.ds(2 * i, 2)], i * Reduce.SEMS, BACK_ORDERS[i],
            )
        )
    events = Events()
    events.put(0, functools.partial(greet, me), *(reduces[i].start for i in (0, 2, 1, 3)))
    for at, i, stage in BACK_PLAN:
        events.put(at, functools.partial(reduces[i].step, stage))
    events.last += [functools.partial(reduces[i].step, 4) for i in (2, 1, 3)]
    events.last += [r.finish for r in reduces]
    return events


def attend_back_call(q, k, v, bias, o, do, aug, cosine, sine, whole, moving=(), tq=512, unroll=4):
    rows, span, width = q.shape
    keys = k.shape[1]
    tq = min(tq, span)
    unroll = min(unroll, span // tq)
    moves = len(moving)
    qs = pl.BlockSpec((1, span, PAIR), lambda r, p: (r, 0, p))
    ks = pl.BlockSpec((1, keys, PAIR), lambda r, p: (r, 0, p))
    table = pl.BlockSpec((span, PAIR), lambda r, p: (0, 0), pipeline_mode=pl.Buffered(1))
    hbm = pl.BlockSpec(memory_space=pl.ANY)
    kv_type = BF if whole else F32
    results, result_specs, extra, more = [], [], [], {}
    if moves:
        extra = [pltpu.SemaphoreType.DMA((Reduce.SEMS * moves,))] * 2
        extra += [pltpu.SemaphoreType.DMA((2 * moves,))]
        for a, order in zip(moving, BACK_ORDERS):
            block = (a.shape[-2], a.shape[-1] // (2 if a.ndim == 5 else 1))
            results.append(jax.ShapeDtypeStruct(block, F32))
            result_specs.append(pl.BlockSpec(block, lambda r, p: (0, 0), pipeline_mode=pl.Buffered(1)))
            extra += Reduce.scratch(*block, a.dtype, order)
        more = dict(collective_id=2, has_side_effects=True)
    return pl.pallas_call(
        functools.partial(attend_back_kernel, tq, unroll, moves),
        grid=(rows, width // PAIR),
        in_specs=[
            qs, ks, ks,
            pl.BlockSpec((1, keys, PAIR), lambda r, p: (r, 0, 0), pipeline_mode=pl.Buffered(1)),
            qs, qs, qs, table, table,
        ]
        + [hbm] * moves,
        out_specs=[qs, ks, ks] + result_specs,
        out_shape=[
            jax.ShapeDtypeStruct(q.shape, BF),
            jax.ShapeDtypeStruct(k.shape, kv_type),
            jax.ShapeDtypeStruct(k.shape, kv_type),
        ]
        + results,
        scratch_shapes=[
            pltpu.VMEM((2, span, 2 * PAIR), BF),
            pltpu.VMEM((2, span, 2 * PAIR), BF),
            pltpu.VMEM((keys, 2 * PAIR), BF),
            pltpu.VMEM((keys, 2 * PAIR), BF),
            pltpu.VMEM((PAIR, keys), BF),
            pltpu.VMEM((keys, PAIR), F32),
            pltpu.VMEM((keys, PAIR), F32),
        ]
        + extra,
        compiler_params=pltpu.CompilerParams(vmem_limit_bytes=VMEM_LIMIT, **more),
        name="attend_back",
    )(q, k, v, bias, o, do, aug, cosine, sine, *moving)


def middle_kernel(
    chunk, moves, x_ref, att_ref, cot_ref, wo_ref, wg_ref, wu_ref, wd_ref, g1_ref, g2_ref, *rest
):
    source, rest = rest[:moves], rest[moves:]
    (out_ref, dfirst_ref, datt_ref, act_ref, dg_ref, du_ref, ht_ref, dft_ref, at_ref, gg1_ref, gg2_ref) = rest[:11]
    ca, cb = rest[11:13]
    if moves:
        arrived, dy_ref, send, recv = rest[13:]
        me = place()
        now, per = pl.program_id(0), pl.num_programs(0) // 2
        tile = dy_ref.shape[0]
        give = pltpu.make_async_remote_copy(
            src_ref=source[0].at[1 - me["y"]],
            dst_ref=arrived,
            send_sem=send.at[0],
            recv_sem=recv.at[0],
            device_id=device(moved(me, "y", 1)),
            device_id_type=MESH,
        )

        @pl.when(now == 0)
        def _():
            greet(me)
            give.start()

        pl.when(now == per)(give.wait)

        @pl.when(now < per)
        def _():
            dy_ref[...] = cot_ref[...]

        @pl.when(now >= per)
        def _():
            dy_ref[...] = arrived[pl.ds(pl.multiple_of((now - per) * tile, tile), tile), :]

    else:
        dy_ref = cot_ref

    @pl.when(pl.program_id(0) == 0)
    def _():
        gg1_ref[...] = jnp.zeros_like(gg1_ref)
        gg2_ref[...] = jnp.zeros_like(gg2_ref)

    gain1, gain2 = g1_ref[...], g2_ref[...]
    att = att_ref[...]
    at_ref[...] = att.T
    first = x_ref[...].astype(F32) + dot(att, wo_ref[:, : att.shape[1]])
    centered = first - jnp.mean(first, axis=1, keepdims=True)
    s1 = lax.rsqrt(jnp.mean(centered * centered, axis=1, keepdims=True) + EPS)
    n1 = centered * s1
    hidden = n1 * gain1
    low = hidden.astype(BF)
    ht_ref[...] = low.T
    hidden_width = wg_ref.shape[1]
    second = hidden
    for c in range(hidden_width // chunk):
        at = slice(c * chunk, (c + 1) * chunk)
        g = dot(low, wg_ref[:, at])
        u = dot(low, wu_ref[:, at])
        sig = jax.nn.sigmoid(g)
        silu = g * sig
        act = (silu * u).astype(BF)
        act_ref[:, at] = act
        ca[:, at] = (u * (sig + silu * (1.0 - sig))).astype(ca.dtype)
        cb[:, at] = silu.astype(cb.dtype)
        second = second + dot(act, wd_ref[at, :])
    centered = second - jnp.mean(second, axis=1, keepdims=True)
    s2 = lax.rsqrt(jnp.mean(centered * centered, axis=1, keepdims=True) + EPS)
    n2 = centered * s2
    out_ref[...] = (n2 * gain2).astype(BF)
    dy = dy_ref[...].astype(F32)
    gg2_ref[...] += jnp.sum(dy * n2, axis=0, keepdims=True)
    inner = dy * gain2
    d_second = s2 * (
        inner - jnp.mean(inner, axis=1, keepdims=True) - n2 * jnp.mean(inner * n2, axis=1, keepdims=True)
    )
    d_ffn = d_second.astype(BF)
    dft_ref[...] = d_ffn.T
    d_hidden = d_second
    for c in range(hidden_width // chunk):
        at = slice(c * chunk, (c + 1) * chunk)
        d_act = dot_nt(d_ffn, wd_ref[at, :])
        dg = (d_act * ca[:, at]).astype(BF)
        du = (d_act * cb[:, at]).astype(BF)
        dg_ref[:, at] = dg
        du_ref[:, at] = du
        d_hidden = d_hidden + dot_nt(dg, wg_ref[:, at]) + dot_nt(du, wu_ref[:, at])
    gg1_ref[...] += jnp.sum(d_hidden * n1, axis=0, keepdims=True)
    inner = d_hidden * gain1
    d_first = s1 * (
        inner - jnp.mean(inner, axis=1, keepdims=True) - n1 * jnp.mean(inner * n1, axis=1, keepdims=True)
    )
    low = d_first.astype(BF)
    dfirst_ref[...] = low
    datt_ref[...] = dot_nt(low, wo_ref[:, : low.shape[1]]).astype(BF)


def middle_call(x, att, cot, wo, wg, wu, wd, g1, g2, tile=256, chunk=768):
    tokens, width = x.shape
    hidden_width = wg.shape[1]
    tile = min(tile, tokens)
    moves = cot.ndim - 2
    per = tokens // tile // 2

    def place_of(i):
        if not moves:
            return i
        return lax.rem(lax.axis_index("blk") + i // per, 2) * per + lax.rem(i, per)

    row = pl.BlockSpec((tile, width), lambda i: (place_of(i), 0))
    wide = pl.BlockSpec((tile, hidden_width), lambda i: (place_of(i), 0))
    column = pl.BlockSpec((width, tile), lambda i: (0, place_of(i)))
    cot_row, extra, more = row, [], {}
    if moves:
        cot_row = pl.BlockSpec(
            (None, tile, width), lambda i: (lax.axis_index("blk"), jnp.minimum(i, per - 1), 0)
        )
        extra = [pltpu.VMEM((tokens // 2, width), BF), pltpu.VMEM((tile, width), BF)]
        extra += [pltpu.SemaphoreType.DMA((1,))] * 2
        more = dict(collective_id=5, has_side_effects=True)

    def whole(a):
        return pl.BlockSpec(a.shape, lambda i: (0, 0), pipeline_mode=pl.Buffered(1))

    gain = pl.BlockSpec((1, width), lambda i: (0, 0))
    return pl.pallas_call(
        functools.partial(middle_kernel, chunk, moves),
        grid=(tokens // tile,),
        in_specs=[row, row, cot_row, whole(wo), whole(wg), whole(wu), whole(wd), gain, gain]
        + [pl.BlockSpec(memory_space=pl.ANY)] * moves,
        out_specs=[row, row, row, wide, wide, wide, column, column, column, gain, gain],
        out_shape=[jax.ShapeDtypeStruct((tokens, width), BF)] * 3
        + [jax.ShapeDtypeStruct((tokens, hidden_width), BF)] * 3
        + [jax.ShapeDtypeStruct((width, tokens), BF)] * 3
        + [jax.ShapeDtypeStruct((1, width), F32)] * 2,
        scratch_shapes=[pltpu.VMEM((tile, hidden_width), F32)] * 2 + extra,
        compiler_params=pltpu.CompilerParams(vmem_limit_bytes=VMEM_LIMIT, **more),
        name="middle",
    )(x, att, cot, wo, wg, wu, wd, g1, g2, *([cot] * moves))


def outer_kernel(a_ref, b_ref, o_ref):
    o_ref[...] = dot(a_ref[...], b_ref[...]).astype(o_ref.dtype)


def outer_call(a, b, out_type, tile=512):
    rows, tokens = a.shape
    columns = b.shape[1]
    tile = tile if columns % tile == 0 else 256
    return pl.pallas_call(
        outer_kernel,
        grid=(columns // tile,),
        in_specs=[
            pl.BlockSpec((rows, tokens), lambda i: (0, 0), pipeline_mode=pl.Buffered(1)),
            pl.BlockSpec((tokens, tile), lambda i: (0, i)),
        ],
        out_specs=pl.BlockSpec((rows, tile), lambda i: (0, i)),
        out_shape=jax.ShapeDtypeStruct((rows, columns), out_type),
        compiler_params=params(),
        name="outer",
    )(a, b)


def outers_kernel(steps, moves, a1_ref, a2_hbm, a3_hbm, b1_ref, b2_ref, b3_ref, b4_hbm, gains_ref, *rest):
    source, rest = rest[:moves], rest[moves:]
    o1_ref, o2_ref, o3_ref, o4_ref, rest = rest[0], rest[1], rest[2], rest[3], rest[4:]
    now = pl.program_id(0)
    target, rest = rest[:moves], rest[moves:]
    a2_ref, a3_ref, b4_ref, load, rest = rest[0], rest[1], rest[2], rest[3], rest[4:]
    late = [
        pltpu.make_async_copy(a, b, load.at[i])
        for i, (a, b) in enumerate(((a2_hbm, a2_ref), (a3_hbm, a3_ref), (b4_hbm, b4_ref)))
    ]

    @pl.when(now == 0)
    def _():
        for copy in late:
            copy.start()

    @pl.when(now == 2 * steps)
    def _():
        for copy in late:
            copy.wait()

    if moves:
        target, (bounce, send, recv, local) = target[0], rest
        me = place()
        swap = Swap(me, source[0], target, bounce, send, recv, local.at[0], 0, ((0, target.shape[1]),))

        @pl.when(now == 0)
        def _():
            greet(me)
            swap.give(0)
            swap.keep_begin()

        pl.when(now == 3)(swap.keep_turn)
        pl.when(now == 3 * steps)(swap.finish)

    @pl.when(now < steps)
    def _():
        o1_ref[...] = dot(a1_ref[...], b1_ref[...]).astype(BF)

    @pl.when((now >= steps) & (now < 2 * steps))
    def _():
        o2_ref[...] = dot(a1_ref[...], b2_ref[...]).astype(BF)

    @pl.when((now >= 2 * steps) & (now < 3 * steps))
    def _():
        o3_ref[...] = dot(a2_ref[...], b3_ref[...]).astype(BF)

    @pl.when(now == 3 * steps)
    def _():
        width = b4_ref.shape[1]
        o4_ref[:, :width] = dot(a3_ref[...], b4_ref[...])
        o4_ref[:, width:] = gains_ref[...]


def outers_call(h_t, df_t, att_t, d_gate, d_up, act, d_first, gains, moving=(), tile=512):
    width, tokens = h_t.shape
    hidden = d_gate.shape[1]
    steps = hidden // tile

    def whole(a):
        return pl.BlockSpec(a.shape, lambda i: (0, 0), pipeline_mode=pl.Buffered(1))

    def part(rows, n):
        return pl.BlockSpec((rows, tile), lambda i: (0, jnp.clip(i - n * steps, 0, steps - 1)))

    moves = len(moving)
    hbm = pl.BlockSpec(memory_space=pl.ANY)
    extra = [pltpu.VMEM(a.shape, BF) for a in (df_t, att_t, d_first)] + [pltpu.SemaphoreType.DMA((3,))]
    extra += [pltpu.VMEM(a.shape[1:], BF) for a in moving]
    extra += [pltpu.SemaphoreType.DMA((1,))] * (3 * moves)
    more = dict(collective_id=4, has_side_effects=True) if moves else {}
    return pl.pallas_call(
        functools.partial(outers_kernel, steps, moves),
        grid=(3 * steps + 1,),
        in_specs=[whole(h_t), hbm, hbm] + [part(tokens, n) for n in range(3)] + [hbm, whole(gains)]
        + [hbm] * moves,
        out_specs=[part(width, n) for n in range(3)]
        + [pl.BlockSpec((width, width + gains.shape[1]), lambda i: (0, 0), pipeline_mode=pl.Buffered(1))]
        + [hbm] * moves,
        out_shape=[jax.ShapeDtypeStruct((width, hidden), BF)] * 3
        + [jax.ShapeDtypeStruct((width, width + gains.shape[1]), F32)]
        + [jax.ShapeDtypeStruct(a.shape, BF) for a in moving],
        scratch_shapes=extra,
        compiler_params=pltpu.CompilerParams(vmem_limit_bytes=VMEM_LIMIT, **more),
        name="outers",
    )(h_t, df_t, att_t, d_gate, d_up, act, d_first, gains, *moving)


CLOSING_ORDERS = ("xy", "xy", "xy")


def closing_kernel(
    dq_hbm, dk_hbm, dv_hbm, first_hbm, xt_hbm, w_hbm, g_out, sum_ref,
    dq, dk, dv, first, xt, w, g, w0, w1, w2, send, recv, local, mine_sem, *bufs,
):
    me = place()
    y = me["y"]
    loads = [
        pltpu.make_async_copy(a, b, local.at[i])
        for i, (a, b) in enumerate(
            ((w_hbm, w), (dq_hbm, dq), (dk_hbm, dk), (dv_hbm, dv), (first_hbm, first), (xt_hbm, xt))
        )
    ]
    for load in loads:
        load.start()
    greet(me)
    width = dq.shape[1]
    half = g.shape[1]
    tile = half // 2

    def rows_of(which, t):
        at = pl.ds(pl.multiple_of(which * half + t * tile, tile), tile)
        total = first[at, :].astype(F32)
        for n, a in enumerate((dq, dk, dv)):
            total += dot_nt(a[at, :], w[:, n * width : (n + 1) * width])
        g[which, pl.ds(t * tile, tile), :] = total.astype(BF)

    for load in loads[:5]:
        load.wait()
    quarter = half // 4

    def give(n, target_half):
        part = pl.ds(n * quarter, quarter)
        return pltpu.make_async_remote_copy(
            src_ref=g.at[1 - y, part],
            dst_ref=g_out.at[target_half, part],
            send_sem=send.at[n],
            recv_sem=recv.at[n],
            device_id=device(moved(me, "y", 1)),
            device_id_type=MESH,
        )

    rows_of(1 - y, 0)
    give(0, y).start()
    give(1, y).start()
    rows_of(1 - y, 1)
    loads[5].wait()
    reduces = []
    for n, (a, target) in enumerate(((dq, w0), (dk, w1), (dv, w2))):
        reduces.append(
            Reduce(
                me, tall_piece(target), bufs[5 * n : 5 * n + 5], sum_ref.at[:, pl.ds(n * width, width)],
                send, recv, mine_sem.at[pl.ds(2 * n, 2)], 4 + n * Reduce.SEMS, CLOSING_ORDERS[n],
            )
        )

    def products(n, a, target):
        step = 2 * PAIR

        def part(i, _):
            at = pl.ds(pl.multiple_of(i * step, step), step)
            value = dot(xt[...], a[:, at])
            target[:, :, :, :, :, at] = value.reshape(target.shape[:-1] + (step,)).astype(BF)
            return 0

        lax.fori_loop(0, width // step, part, 0)

    products(0, dq, w0)
    reduces[0].start()
    give(2, y).start()
    products(1, dk, w1)
    reduces[1].start()
    reduces[0].step(1)
    products(2, dv, w2)
    reduces[2].start()
    reduces[1].step(1)
    reduces[0].step(2)
    reduces[2].step(1)
    rows_of(y, 0)
    reduces[1].step(2)
    reduces[0].step(3)
    rows_of(y, 1)
    keep = pltpu.make_async_copy(g.at[y], g_out.at[y], local.at[0])
    keep.start()
    reduces[2].step(2)
    give(3, y).start()
    reduces[1].step(3)
    reduces[0].step(4)
    reduces[2].step(3)
    reduces[1].step(4)
    reduces[2].step(4)
    for r in reduces:
        r.finish()
    for n in range(4):
        give(n, 1 - y).wait_recv()
        give(n, y).wait_send()
    keep.wait()


def closing_call(dq, dk, dv, first, xt, w):
    tokens, width = dq.shape
    hbm = pl.BlockSpec(memory_space=pl.ANY)
    block = (width // 32, width)
    full = pltpu.VMEM((4, 2, 2, 2) + block, BF)
    scratch = [pltpu.VMEM(a.shape, BF) for a in (dq, dk, dv, first, xt, w)]
    scratch += [pltpu.VMEM((2, tokens // 2, width), BF), full, full, full]
    sems = 4 + 3 * Reduce.SEMS
    scratch += [pltpu.SemaphoreType.DMA((sems,))] * 2
    scratch += [pltpu.SemaphoreType.DMA((6,)), pltpu.SemaphoreType.DMA((6,))]
    for order in CLOSING_ORDERS:
        scratch += Reduce.scratch(*block, BF, order)
    return pl.pallas_call(
        closing_kernel,
        in_specs=[hbm] * 6,
        out_specs=[hbm, pl.BlockSpec(memory_space=pltpu.VMEM)],
        out_shape=[
            jax.ShapeDtypeStruct((2, tokens // 2, width), BF),
            jax.ShapeDtypeStruct((block[0], 3 * width), F32),
        ],
        scratch_shapes=scratch,
        compiler_params=pltpu.CompilerParams(
            vmem_limit_bytes=VMEM_LIMIT, collective_id=3, has_side_effects=True
        ),
        name="closing",
    )(dq, dk, dv, first, xt, w)


def tokens_kernel(dq_ref, dk_ref, dv_ref, dfirst_ref, w_ref, o_ref):
    width = dq_ref.shape[1]
    total = dfirst_ref[...].astype(F32)
    total += dot_nt(dq_ref[...], w_ref[:, :width])
    total += dot_nt(dk_ref[...], w_ref[:, width : 2 * width])
    total += dot_nt(dv_ref[...], w_ref[:, 2 * width :])
    o_ref[...] = total.astype(BF)


def tokens_call(dq, dk, dv, dfirst, w, tile=512):
    tokens, width = dq.shape
    tile = min(tile, tokens)
    row = pl.BlockSpec((tile, width), lambda i: (i, 0))
    return pl.pallas_call(
        tokens_kernel,
        grid=(tokens // tile,),
        in_specs=[row] * 4 + [pl.BlockSpec(w.shape, lambda i: (0, 0), pipeline_mode=pl.Buffered(1))],
        out_specs=row,
        out_shape=jax.ShapeDtypeStruct((tokens, width), BF),
        compiler_params=params(),
        name="grad_tokens",
    )(dq, dk, dv, dfirst, w)


def angle_tables(span):
    index = np.arange(HEAD // 2, dtype=np.float64)
    inverse = np.power(1000.0, -2.0 * index / HEAD)
    angles = np.arange(span, dtype=np.float64)[:, None] * inverse[None, :]
    repeat = (1, PAIR // (HEAD // 2))
    return (
        np.tile(np.cos(angles), repeat).astype(np.float32),
        np.tile(np.sin(angles), repeat).astype(np.float32),
    )


def body(tokens, lengths, w_qkv, w_out, w_gate, w_up, w_down, gain_one, gain_two, cotangent):
    axes = ("dp", "blk")
    blk = lax.axis_size("blk")
    mine = lax.axis_index("blk")
    rows, span, width = tokens.shape
    seq = span * blk
    own = blk == 2 and rows == 2 and lax.axis_size("dp") == 16

    def gather(a):
        return lax.all_gather(a, axes, axis=0, tiled=True)

    cosine, sine = map(jnp.asarray, angle_tables(seq))
    gains = jnp.stack([gain_one, gain_two], 1)
    if own:
        w_out = jnp.pad(jnp.concatenate([w_out, gains], 1), ((0, 0), (0, PAIR - 2)))
        x, f_qkv, q, k, v, xt, *moving = opening_call(
            tokens, w_qkv, w_out, w_gate, w_up, w_down, cosine, sine
        )
        x = x.reshape(1, seq, width)
        length = lax.dynamic_slice_in_dim(lengths, mine, 1, 0)
        cq, sq = cosine, sine
    else:
        f_qkv, f_out, f_gate, f_up, f_down = map(gather, (w_qkv, w_out, w_gate, w_up, w_down))
        f_gains = gather(gains).astype(F32)
        x, cot, length = tokens, cotangent.reshape(rows * span, width), lengths
        cq = lax.dynamic_slice_in_dim(cosine, mine * span, span, 0)
        sq = lax.dynamic_slice_in_dim(sine, mine * span, span, 0)
    n, t = x.shape[:2]
    flat = x.reshape(n * t, width)
    if not own:
        q, k, v, xt = qkv_call(flat, f_qkv, cq, sq)
    q, k, v = (a.reshape(n, t, width) for a in (q, k, v))
    if not own:
        k = lax.all_gather(k, "blk", axis=1, tiled=True)
        v = lax.all_gather(v, "blk", axis=1, tiled=True)
    position = jnp.arange(seq, dtype=jnp.int32)[None, :, None]
    lane = jnp.arange(PAIR, dtype=jnp.int32)[None, None, :]
    bias = jnp.where((lane % HEAD == 3) & (position >= length[:, None, None]), NEG, 0.0).astype(BF)
    if own:
        att, aug, f_out, f_gate, f_up, f_down = attend_call(
            q, k, v, bias, moving
        )
        f_out = f_out.reshape(width, -1)
        f_gains = f_out[:, width : width + 2].astype(F32)
        cot = cotangent
        f_gate, f_up = f_gate.reshape(width, -1), f_up.reshape(width, -1)
        f_down = f_down.reshape(-1, width)
    else:
        att, aug = attend_call(q, k, v, bias)
    g1, g2 = f_gains[:, 0][None], f_gains[:, 1][None]
    out, d_first, d_att, act, d_gate, d_up, h_t, df_t, att_t, gg1, gg2 = middle_call(
        flat, att.reshape(n * t, width), cot, f_out, f_gate, f_up, f_down, g1, g2
    )
    gains = jnp.pad(jnp.concatenate([gg1, gg2]).T, ((0, 0), (0, PAIR - 2)))
    moving = (out.reshape(2, span, width),) if own else ()
    gw_gate, gw_up, gw_down_t, gw_out, *moving = outers_call(
        h_t, df_t, att_t, d_gate, d_up, act, d_first, gains, moving
    )
    d_att = d_att.reshape(n, t, width)
    if own:
        wide = tuple(g.reshape(4, 2, 2, width // 16, -1) for g in (gw_gate, gw_up, gw_down_t))
        out = moving[0]
        dq, dk, dv, s_gate, s_up, s_down_t, s_out = attend_back_call(
            q, k, v, bias, att, d_att, aug, cq, sq, True,
            wide + (gw_out.reshape(4, 2, 2, 2, width // 32, -1),),
        )
    else:

        def scatter_wide(g):
            g = lax.psum_scatter(g, "blk", scatter_dimension=1, tiled=True)
            return lax.psum_scatter(g, "dp", scatter_dimension=0, tiled=True).astype(F32)

        s_gate, s_up, s_down_t = map(scatter_wide, (gw_gate, gw_up, gw_down_t))
        s_out = lax.psum_scatter(gw_out, axes, scatter_dimension=0, tiled=True)
        dq, dk, dv = attend_back_call(q, k, v, bias, att, d_att, aug, cq, sq, False)
        dk = lax.psum_scatter(dk, "blk", scatter_dimension=1, tiled=True)
        dv = lax.psum_scatter(dv, "blk", scatter_dimension=1, tiled=True)
        heads = (dk * jnp.tile(sq, (1, width // PAIR))).reshape(n, t, HEADS, HEAD)
        half = jnp.concatenate([heads[..., HEAD // 2 :], -heads[..., : HEAD // 2]], -1)
        dk = dk * jnp.tile(cq, (1, width // PAIR)) + half.reshape(n, t, width)
        dk, dv = dk.astype(BF), dv.astype(BF)
    s_down = s_down_t.T
    s_out, s_gg = s_out[:, :width], s_out[:, width : width + 2]
    dq, dk, dv = (a.reshape(n * t, width) for a in (dq, dk, dv))
    if own:
        g_tokens, s_qkv = closing_call(dq, dk, dv, d_first, xt, f_qkv)
    else:
        gw_qkv = jnp.concatenate([outer_call(xt, a, BF, 256) for a in (dq, dk, dv)], 1)
        s_qkv = lax.psum_scatter(gw_qkv, axes, scatter_dimension=0, tiled=True).astype(F32)
        g_tokens = tokens_call(dq, dk, dv, d_first, f_qkv).reshape(tokens.shape)
        out = out.reshape(tokens.shape)
    return (out, g_tokens, s_qkv, s_out, s_gate, s_up, s_down, s_gg[:, 0], s_gg[:, 1])


def solution(mesh):
    both = ("dp", "blk")
    return jax.shard_map(
        body,
        mesh=mesh,
        in_specs=(
            P("dp", "blk", None),
            P("dp"),
            P(both, None),
            P(both, None),
            P(both, None),
            P(both, None),
            P(both, None),
            P(both),
            P(both),
            P("dp", "blk", None),
        ),
        out_specs=(
            P("dp", "blk", None),
            P("dp", "blk", None),
            P(both, None),
            P(both, None),
            P("dp", "blk"),
            P("dp", "blk"),
            P("blk", "dp"),
            P(both),
            P(both),
        ),
        check_vma=False,
    )
```

```python
import functools

import jax
import jax.numpy as jnp
import numpy as np
from jax import lax
from jax.experimental import pallas as pl
from jax.experimental.pallas import tpu as pltpu
from jax.sharding import PartitionSpec as P

HEADS = 12
HEAD = 64
PAIR = 2 * HEAD
EPS = 1e-05
NEG = -1e30
LOG2E = 1.4426950408889634
LN2 = 0.6931471805599453
VMEM_LIMIT = 60 * 1024 * 1024

BF = jnp.bfloat16
F32 = jnp.float32


def dot(a, b):
    return lax.dot_general(a, b, (((1,), (0,)), ((), ())), preferred_element_type=F32)


def dot_nt(a, b):
    return lax.dot_general(a, b, (((1,), (1,)), ((), ())), preferred_element_type=F32)


def params(limit=VMEM_LIMIT):
    return pltpu.CompilerParams(vmem_limit_bytes=limit)


def lanes(shape):
    return lax.broadcasted_iota(jnp.int32, shape, 1)


def turn(u):
    low_half = (lanes(u.shape) % HEAD) < HEAD // 2
    return jnp.where(low_half, -pltpu.roll(u, PAIR - HEAD // 2, 1), pltpu.roll(u, HEAD // 2, 1))


MESH = pl.DeviceIdType.MESH
AXES = "zxcy"
SIZE = {"z": 4, "x": 2, "c": 2, "y": 2}


def place():
    dp, y = lax.axis_index("dp"), lax.axis_index("blk")
    return {"z": dp // 4, "x": dp // 2 % 2, "c": dp % 2, "y": y}


def moved(me, axis, by):
    return {**me, axis: lax.rem(me[axis] + by, SIZE[axis])}


def device(at):
    return ((at["z"] * 2 + at["x"]) * 2 + at["c"], at["y"])


def greet(me):
    barrier = pltpu.get_barrier_semaphore()
    peers = [moved(me, "y", 1), moved(me, "x", 1), moved(me, "c", 1)]
    peers += [moved(me, "z", d) for d in range(1, 4)]
    for peer in peers:
        pl.semaphore_signal(barrier, inc=1, device_id=device(peer), device_id_type=MESH)
    pl.semaphore_wait(barrier, len(peers))


class Gather:
    def __init__(self, me, shard, full, send, recv, local, base, order, held="", columns=None):
        self.me, self.shard, self.full, self.held = me, shard, full, held
        self.part = () if columns is None else (slice(None), pl.ds(*columns))
        self.spans = [a for a in AXES if a in held + order]
        self.send, self.recv, self.local, self.base, self.order = send, recv, local, base, order

    @staticmethod
    def sems(order):
        return sum(SIZE[a] - 1 for a in order)

    def view(self, at, got):
        return self.full.at[tuple(slice(None) if a in got else at[a] for a in self.spans) + self.part]

    def at_stage(self, stage):
        got = self.held + self.order[:stage]
        return got, self.order[stage], self.base + self.sems(self.order[:stage])

    def copies(self, stage):
        got, axis, slot = self.at_stage(stage)
        here = self.view(self.me, got)
        return [
            pltpu.make_async_remote_copy(
                src_ref=self.shard if stage == 0 else here,
                dst_ref=here,
                send_sem=self.send.at[slot + d - 1],
                recv_sem=self.recv.at[slot + d - 1],
                device_id=device(moved(self.me, axis, d)),
                device_id_type=MESH,
            )
            for d in range(1, SIZE[axis])
        ]

    def own(self):
        return pltpu.make_async_copy(self.shard, self.view(self.me, self.held), self.local)

    def arrivals(self, stage):
        got, axis, slot = self.at_stage(stage)
        for d in range(1, SIZE[axis]):
            there = self.view(moved(self.me, axis, SIZE[axis] - d), got)
            pltpu.make_async_remote_copy(
                src_ref=there,
                dst_ref=there,
                send_sem=self.send.at[slot + d - 1],
                recv_sem=self.recv.at[slot + d - 1],
                device_id=device(moved(self.me, axis, d)),
                device_id_type=MESH,
            ).wait_recv()

    def start(self):
        self.own().start()
        for copy in self.copies(0):
            copy.start()

    def step(self, stage):
        self.arrivals(stage - 1)
        if stage == 1:
            self.own().wait()
        if stage < len(self.order):
            for copy in self.copies(stage):
                copy.start()

    def finish(self):
        for stage in range(len(self.order)):
            for copy in self.copies(stage):
                copy.wait_send()


class Reduce:
    SEMS = 7

    def __init__(self, me, piece, bufs, out, send, recv, local, base, order):
        self.me, self.piece, self.out, self.order = me, piece, out, order
        self.b, self.r0, self.r1, self.r2, self.r3 = bufs
        self.send, self.recv, self.local, self.base = send, recv, local, base

    def copy(self, source, target, slot, axis, by=1):
        return pltpu.make_async_remote_copy(
            src_ref=source,
            dst_ref=target,
            send_sem=self.send.at[self.base + slot],
            recv_sem=self.recv.at[self.base + slot],
            device_id=device(moved(self.me, axis, by)),
            device_id_type=MESH,
        )

    def mine(self):
        c = self.me["c"]
        return [
            pltpu.make_async_copy(self.piece(c, y), self.b.at[y], self.local.at[y]) for y in range(2)
        ]

    def copies(self, stage):
        x, y, z = self.me["x"], self.me["y"], self.me["z"]
        if stage == 0:
            other = 1 - self.me["c"]
            return [self.copy(self.piece(other, i), self.r0.at[i], i, "c") for i in range(2)]
        if self.order[0] == "z":
            if stage == 1:
                return [
                    self.copy(self.b.at[:, lax.rem(z + d, 4)], self.r1.at[d - 1], 3 + d, "z", d)
                    for d in range(1, 4)
                ]
            if stage == 2:
                return [self.copy(self.b.at[1 - y, z], self.r2, 2, "y")]
            return [self.copy(self.b.at[y, z, 1 - x], self.r3, 3, "x")]
        if stage == 1:
            source = self.b.at[1 - y] if self.order[0] == "y" else self.b.at[:, :, 1 - x]
            return [self.copy(source, self.r1, 2, self.order[0])]
        if stage == 2:
            source = self.b.at[y, :, 1 - x] if self.order[0] == "y" else self.b.at[1 - y, :, x]
            return [self.copy(source, self.r2, 3, self.order[1])]
        return [
            self.copy(self.b.at[y, lax.rem(z + d, 4), x], self.r3.at[d - 1], 3 + d, "z", d)
            for d in range(1, 4)
        ]

    def start(self):
        for copy in self.copies(0) + self.mine():
            copy.start()

    def step(self, stage):
        x, y, z = self.me["x"], self.me["y"], self.me["z"]
        for copy in self.copies(stage - 1):
            copy.wait_recv()
        b = self.b
        if stage == 1:
            for copy in self.mine():
                copy.wait()

            def add(i, _):
                at = (i // 4, i % 4)
                b[at] = b[at] + self.r0[at]
                return 0

            lax.fori_loop(0, 8, add, 0)
        if self.order[0] == "z" and stage > 1:
            if stage == 2:

                def add(i, _):
                    at = (i // 2, i % 2)
                    total = b[at[0], z, at[1]].astype(F32)
                    for d in range(3):
                        total = total + self.r1[d, at[0], at[1]].astype(F32)
                    b[at[0], z, at[1]] = total.astype(b.dtype)
                    return 0

                lax.fori_loop(0, 4, add, 0)
            if stage == 3:
                for i in range(2):
                    b[y, z, i] = b[y, z, i] + self.r2[i]
            if stage == 4:
                self.out[...] = b[y, z, x].astype(F32) + self.r3[...].astype(F32)
                return
            for copy in self.copies(stage):
                copy.start()
            return
        if stage == 2:

            def add(i, _):
                if self.order[0] == "y":
                    for j in range(2):
                        b[y, i, j] = b[y, i, j] + self.r1[i, j]
                else:
                    for j in range(2):
                        b[j, i, x] = b[j, i, x] + self.r1[j, i]
                return 0

            lax.fori_loop(0, 4, add, 0)
        if stage == 3:

            def add(i, _):
                b[y, i, x] = b[y, i, x] + self.r2[i]
                return 0

            lax.fori_loop(0, 4, add, 0)
        if stage == 4:
            total = b[y, z, x].astype(F32)
            for d in range(3):
                total = total + self.r3[d].astype(F32)
            self.out[...] = total
            return
        for copy in self.copies(stage):
            copy.start()

    def finish(self):
        for stage in range(4):
            for copy in self.copies(stage):
                copy.wait_send()

    @staticmethod
    def scratch(rows, columns, kind, order):
        if order[0] == "z":
            return [
                pltpu.VMEM(shape + (rows, columns), kind)
                for shape in ((2, 4, 2), (2, 4, 2), (3, 2, 2), (2,), ())
            ]
        lead = (4, 2) if order[0] == "y" else (2, 4)
        return [
            pltpu.VMEM(shape + (rows, columns), kind)
            for shape in ((2, 4, 2), (2, 4, 2), lead, (4,), (3,))
        ]


class Swap:
    def __init__(self, me, source, target, bounce, send, recv, local, slots, parts):
        self.me, self.source, self.target, self.bounce = me, source, target, bounce
        self.send, self.recv, self.local, self.slots, self.parts = send, recv, local, slots, parts

    def copy(self, n, row, half):
        begin, size = self.parts[n]
        part = pl.ds(begin, size)
        return pltpu.make_async_remote_copy(
            src_ref=self.source.at[row, part],
            dst_ref=self.target.at[half, part],
            send_sem=self.send.at[self.slots + n],
            recv_sem=self.recv.at[self.slots + n],
            device_id=device(moved(self.me, "y", 1)),
            device_id_type=MESH,
        )

    def give(self, n):
        y = self.me["y"]
        self.copy(n, 1 - y, y).start()

    def keep_in(self):
        return pltpu.make_async_copy(self.source.at[self.me["y"]], self.bounce, self.local)

    def keep_out(self):
        return pltpu.make_async_copy(self.bounce, self.target.at[self.me["y"]], self.local)

    def keep_begin(self):
        self.keep_in().start()

    def keep_turn(self):
        self.keep_in().wait()
        self.keep_out().start()

    def finish(self):
        y = self.me["y"]
        for n in range(len(self.parts)):
            self.copy(n, 1 - y, 1 - y).wait_recv()
            self.copy(n, 1 - y, y).wait_send()
        self.keep_out().wait()


def halves(ref):
    half = ref.shape[-1] // 2
    return [ref.at[(slice(None),) * (len(ref.shape) - 1) + (pl.ds(n * half, half),)] for n in range(2)]


def stages(me, shards, fulls, orders, held, columns, send, recv, local, base=0):
    out = []
    for i, order in enumerate(orders):
        out.append(
            Gather(me, shards[i], fulls[i], send, recv, local.at[i], base, order, held[i], columns[i])
        )
        base += Gather.sems(order)
    return out


def project(x, w_ref, cosine, sine, put):
    width = x.shape[1]
    for part in range(3):
        for pair in range(width // PAIR):
            at = part * width + pair * PAIR
            if pair % 2 == 0:
                u2 = dot(x, w_ref[:, at : at + 2 * PAIR])
            u = u2[:, (pair % 2) * PAIR : (pair % 2 + 1) * PAIR]
            if part < 2:
                u = u * cosine + turn(u) * sine
            if part == 0:
                u = u * (0.125 * LOG2E)
            put(part, slice(pair * PAIR, (pair + 1) * PAIR), u.astype(BF))


def qkv_kernel(x_ref, w_ref, cos_ref, sin_ref, q_ref, k_ref, v_ref, xt_ref):
    x = x_ref[...]

    def put(part, columns, value):
        (q_ref, k_ref, v_ref)[part][:, columns] = value

    project(x, w_ref, cos_ref[...], sin_ref[...], put)
    xt_ref[...] = x.T


def qkv_call(x, w, cosine, sine, tile=512):
    tokens, width = x.shape
    span = cosine.shape[0]
    tile = min(tile, span)
    row = pl.BlockSpec((tile, width), lambda i: (i, 0))
    table = pl.BlockSpec((tile, PAIR), lambda i: (i % (span // tile), 0))
    return pl.pallas_call(
        qkv_kernel,
        grid=(tokens // tile,),
        in_specs=[
            row,
            pl.BlockSpec(w.shape, lambda i: (0, 0), pipeline_mode=pl.Buffered(1)),
            table,
            table,
        ],
        out_specs=[row, row, row, pl.BlockSpec((width, tile), lambda i: (0, i))],
        out_shape=[jax.ShapeDtypeStruct((tokens, width), BF)] * 3
        + [jax.ShapeDtypeStruct((width, tokens), BF)],
        compiler_params=params(),
        name="qkv",
    )(x, w, cosine, sine)


OPENING_ORDERS = ("yzxc", "zyxc", "zy", "zx", "z", "y", "x")


def opening_kernel(
    tok_hbm, w_shard, out_shard, gate_shard, up_shard, down_shard, cos_ref, sin_ref,
    x_hbm, w_hbm, q_hbm, k_hbm, v_hbm, xt_hbm, out_part, gate_part, up_part, left_part, right_part,
    x, w_blocks, w, q, k, v, xt, send, recv, local, load, store,
):
    me = place()
    y = me["y"]
    greet(me)
    rows = x.shape[1]
    begin = rows // 8
    parts = ((0, begin), (begin, rows - begin))

    def token_copy(n, row, half):
        part = pl.ds(*parts[n])
        return pltpu.make_async_remote_copy(
            src_ref=tok_hbm.at[row, part],
            dst_ref=x.at[half, part],
            send_sem=send.at[n],
            recv_sem=recv.at[n],
            device_id=device(moved(me, "y", 1)),
            device_id_type=MESH,
        )

    width = w.shape[1] // 2
    g = stages(
        me,
        halves(w_shard) + [out_shard, gate_shard, up_shard] + halves(down_shard),
        [w_blocks, w_blocks, out_part, gate_part, up_part, left_part, right_part],
        OPENING_ORDERS,
        ("",) * 7,
        ((0, width), (width, width)) + (None,) * 5,
        send, recv, local, 2,
    )
    mine = pltpu.make_async_copy(tok_hbm.at[y], x.at[y], load.at[0])
    g[0].start()
    g[1].start()
    token_copy(0, 1 - y, y).start()
    mine.start()
    g[0].step(1)
    g[1].step(1)
    token_copy(1, 1 - y, y).start()
    g[0].step(2)
    for n in (2, 3, 4):
        g[n].start()
    g[1].step(2)
    g[6].start()
    g[5].start()
    g[0].step(3)
    g[1].step(3)
    g[0].step(4)
    g[1].step(4)
    g[2].step(1)
    g[3].step(1)
    for n in range(3):
        part = slice(n * w.shape[0], (n + 1) * w.shape[0])
        block = w_blocks[:, :, :, :, :, part].astype(F32)
        w[:, part] = block.reshape(w.shape[0], w.shape[0]).astype(BF)
    keep_w = pltpu.make_async_copy(w, w_hbm, load.at[1])
    keep_w.start()
    mine.wait()
    tile = 512

    def stores(n):
        half = lax.rem(y + n // 2, 2)
        at = pl.ds(pl.multiple_of(half * rows + lax.rem(n, 2) * tile, tile), tile)
        pairs = [(a.at[at], b.at[at]) for a, b in ((q, q_hbm), (k, k_hbm), (v, v_hbm))]
        pairs.append((xt.at[:, at], xt_hbm.at[:, at]))
        return [pltpu.make_async_copy(a, b, store.at[n, i]) for i, (a, b) in enumerate(pairs)]

    def tile_step(n, _):
        half = lax.rem(y + n // 2, 2)
        start = pl.multiple_of(half * rows + lax.rem(n, 2) * tile, tile)
        at = pl.ds(start, tile)

        @pl.when(n == 2)
        def _():
            for m in range(2):
                token_copy(m, 1 - y, 1 - y).wait_recv()

        value = x[half, pl.ds(pl.multiple_of(lax.rem(n, 2) * tile, tile), tile), :]

        def put(part, columns, u):
            (q, k, v)[part][at, columns] = u

        project(value, w, cos_ref[at, :], sin_ref[at, :], put)
        xt[:, at] = value.T
        for copy in stores(n):
            copy.start()
        return 0

    lax.fori_loop(0, 4, tile_step, 0)
    keep_x = pltpu.make_async_copy(x, x_hbm, load.at[2])
    keep_x.start()
    g[2].step(2)
    g[3].step(2)
    for n in (4, 5, 6):
        g[n].step(1)
    for gather in g:
        gather.finish()
    for m in range(2):
        token_copy(m, 1 - y, y).wait_send()
    for n in range(4):
        for copy in stores(n):
            copy.wait()
    keep_w.wait()
    keep_x.wait()


def opening_call(tokens, w_qkv, w_out, w_gate, w_up, w_down, cosine, sine):
    rows, span, width = tokens.shape
    total = rows * span
    hbm = pl.BlockSpec(memory_space=pl.ANY)
    held = pl.BlockSpec(memory_space=pltpu.VMEM)
    whole = (width, w_qkv.shape[1])
    flat = (total, width)
    shapes = [tokens.shape, whole, flat, flat, flat, (width, total)]
    shapes += [(4, 2) + w_out.shape, (4, 2) + w_gate.shape, (4,) + w_up.shape]
    shapes += [(2, w_down.shape[0], w_down.shape[1] // 2)] * 2
    sems = 2 + sum(map(Gather.sems, OPENING_ORDERS))
    return pl.pallas_call(
        opening_kernel,
        in_specs=[hbm] + [held] * 7,
        out_specs=[hbm] * len(shapes),
        out_shape=[jax.ShapeDtypeStruct(shape, BF) for shape in shapes],
        scratch_shapes=[
            pltpu.VMEM(tokens.shape, BF),
            pltpu.VMEM((4, 2, 2, 2) + w_qkv.shape, BF),
            pltpu.VMEM(whole, BF),
            pltpu.VMEM(flat, BF),
            pltpu.VMEM(flat, BF),
            pltpu.VMEM(flat, BF),
            pltpu.VMEM((width, total), BF),
            pltpu.SemaphoreType.DMA((sems,)),
            pltpu.SemaphoreType.DMA((sems,)),
            pltpu.SemaphoreType.DMA((len(OPENING_ORDERS),)),
            pltpu.SemaphoreType.DMA((3,)),
            pltpu.SemaphoreType.DMA((4, 4)),
        ],
        compiler_params=pltpu.CompilerParams(
            vmem_limit_bytes=VMEM_LIMIT, collective_id=0, has_side_effects=True
        ),
        name="opening",
    )(tokens, w_qkv, w_out, w_gate, w_up, w_down, cosine, sine)


def key_mask(len_ref, own, keys, other):
    length = len_ref[lax.axis_index("blk") if own else pl.program_id(0)]
    sub = lanes((keys, PAIR)) % HEAD
    past = lax.broadcasted_iota(jnp.int32, (keys, PAIR), 0) >= length
    return jnp.where(sub < 3, other, jnp.where((sub == 3) & past, NEG, 0.0))


def attend_kernel(tile, chunk, moves, len_ref, q_ref, k_ref, v_ref, *rest):
    inputs, rest = rest[:moves], rest[moves:]
    o_ref, aug_ref, rest = rest[0], rest[1], rest[2:]
    results = max(moves - 1, 0)
    outputs, rest = rest[:results], rest[results:]
    ka, va, s_scr, m_scr = rest[:4]
    keys, span = k_ref.shape[1], q_ref.shape[1]
    tiles = span // tile
    events = {}
    if moves:
        events = attend_events(inputs, outputs, *rest[4:])

    @pl.when(pl.program_id(1) == 0)
    def _():
        ka[:, PAIR:] = key_mask(len_ref, moves, keys, 0.0).astype(BF)
        va[:, PAIR:] = jnp.ones((keys, PAIR), BF)

    ka[:, :PAIR] = k_ref[0]
    va[:, :PAIR] = v_ref[0]
    lane = lanes((tile, PAIR))
    side = lanes((tile, 2 * PAIR)) // HEAD % 2
    ones = (lane % HEAD == 3).astype(F32).astype(BF)
    chunks = keys // chunk

    def query(i, h):
        at = pl.ds(pl.multiple_of(i * tile, tile), tile)
        both = jnp.concatenate([q_ref[0, at, :], ones], axis=1)
        return jnp.where(side == h, both, jnp.zeros_like(both))

    def score(qa, h, c, top):
        s = dot_nt(qa, ka[c * chunk : (c + 1) * chunk, :])
        s_scr[h, :, c * chunk : (c + 1) * chunk] = s
        for b in range(chunk // PAIR):
            part = s[:, b * PAIR : (b + 1) * PAIR]
            top = part if top is None else jnp.maximum(top, part)
        return top

    def close(h, top):
        m_scr[h] = jnp.broadcast_to(jnp.max(top, axis=1, keepdims=True), (tile, PAIR))

    def unit(h, later, other):
        m = m_scr[h]
        wide = jnp.concatenate([m] * (chunk // PAIR), axis=1)
        qa = query(later, other)
        acc, top = None, None
        for c in range(chunks):
            top = score(qa, other, c, top)
            p = jnp.exp2(s_scr[h, :, c * chunk : (c + 1) * chunk] - wide).astype(BF)
            part = dot(p, va[c * chunk : (c + 1) * chunk, :])
            acc = part if acc is None else acc + part
        return acc, top, m

    top = None
    qa = query(0, 0)
    for c in range(chunks):
        top = score(qa, 0, c, top)
    close(0, top)

    def step(i, _):
        acc0, top, m0 = unit(0, i, 1)
        close(1, top)
        acc1, top, m1 = unit(1, jnp.minimum(i + 1, tiles - 1), 0)
        close(0, top)
        mine = lane < HEAD
        total = jnp.where(mine, acc0[:, PAIR:], acc1[:, PAIR:])
        at = pl.ds(pl.multiple_of(i * tile, tile), tile)
        o_ref[0, at, :] = (jnp.where(mine, acc0[:, :PAIR], acc1[:, :PAIR]) / total).astype(BF)
        lse = jnp.where(mine, m0, m1) + jnp.log2(total)
        aug_ref[0, at, :] = spread(lse, jnp.where(lane % HEAD == 3, 1.0, 0.0))
        return 0

    unroll = 2 if tiles % 2 == 0 else 1

    def group(n, _):
        now = pl.program_id(1) * (tiles // unroll) + n
        for at_step, acts in events.items():

            @pl.when(now == at_step)
            def _():
                for act in acts:
                    act()

        for j in range(unroll):
            step(n * unroll + j, 0)
        return 0

    lax.fori_loop(0, tiles // unroll, group, 0)
    if moves:

        @pl.when(pl.program_id(1) == pl.num_programs(1) - 1)
        def _():
            for act in events.last:
                act()


class Events(dict):
    def __init__(self):
        self.last = []

    def put(self, at, *acts):
        self.setdefault(at, []).extend(acts)


ATTEND_HELD = ("zy", "zx", "z", "y", "x")
ATTEND_ORDERS = ("xc", "yc", "yxc", "zxc", "zyc")
ATTEND_PLAN = ((2, 0, 1), (4, 2, 1), (4, 3, 1), (7, 4, 1), (10, 1, 1), (10, 2, 2), (11, 3, 2), (11, 4, 2))
ATTEND_FIRST = (2, 1, 0, 3, 4)


def attend_events(inputs, outputs, send, recv, local):
    me = place()
    half = inputs[3].shape[-1]
    columns = (None, None, None, (0, half), (half, half))
    fulls = tuple(outputs) + (outputs[3],)
    gathers = stages(me, inputs, fulls, ATTEND_ORDERS, ATTEND_HELD, columns, send, recv, local)
    events = Events()
    events.put(0, functools.partial(greet, me), *(gathers[i].start for i in ATTEND_FIRST))
    done = [1] * len(gathers)
    for at, i, stage in ATTEND_PLAN:
        events.put(at, functools.partial(gathers[i].step, stage))
        done[i] = stage + 1
    for stage in range(1, 4):
        for i, g in enumerate(gathers):
            if done[i] <= stage <= len(ATTEND_ORDERS[i]):
                events.last.append(functools.partial(g.step, stage))
    events.last += [g.finish for g in gathers]
    return events


def spread(value, other):
    high = value.astype(BF).astype(F32)
    rest = value - high
    mid = rest.astype(BF).astype(F32)
    low = rest - mid
    sub = lanes(value.shape) % HEAD
    return jnp.where(
        sub == 0, high, jnp.where(sub == 1, mid, jnp.where(sub == 2, low, other))
    ).astype(BF)


def attend_call(q, k, v, lengths, moving=(), tile=512, chunk=512):
    rows, span, width = q.shape
    keys = k.shape[1]
    tile = min(tile, span)
    moves = len(moving)
    qs = pl.BlockSpec((1, span, PAIR), lambda r, p: (r, 0, p))
    ks = pl.BlockSpec((1, keys, PAIR), lambda r, p: (r, 0, p))
    hbm = pl.BlockSpec(memory_space=pl.ANY)
    moved_shapes = [jax.ShapeDtypeStruct((4, 2, 2, 2) + a.shape[-2:], a.dtype) for a in moving[:3]]
    for a in moving[3:4]:
        moved_shapes.append(jax.ShapeDtypeStruct((4, 2, 2, 2, a.shape[-2], 2 * a.shape[-1]), a.dtype))
    sems = sum(map(Gather.sems, ATTEND_ORDERS))
    extra = [pltpu.SemaphoreType.DMA((sems,))] * 2 + [pltpu.SemaphoreType.DMA((len(ATTEND_ORDERS),))]
    held = [
        pl.BlockSpec(a.shape, lambda r, p, n=a.ndim: (0,) * n, pipeline_mode=pl.Buffered(1))
        for a in moving
    ]
    more = dict(collective_id=1, has_side_effects=True) if moves else {}
    return pl.pallas_call(
        functools.partial(attend_kernel, tile, chunk, moves),
        grid=(rows, width // PAIR),
        in_specs=[pl.BlockSpec(memory_space=pltpu.SMEM), qs, ks, ks] + held,
        out_specs=[qs, qs] + [hbm] * len(moved_shapes),
        out_shape=[jax.ShapeDtypeStruct(q.shape, BF)] * 2 + moved_shapes,
        scratch_shapes=[
            pltpu.VMEM((keys, 2 * PAIR), BF),
            pltpu.VMEM((keys, 2 * PAIR), BF),
            pltpu.VMEM((2, tile, keys), F32),
            pltpu.VMEM((2, tile, PAIR), F32),
        ]
        + (extra if moves else []),
        compiler_params=pltpu.CompilerParams(vmem_limit_bytes=VMEM_LIMIT, **more),
        name="attend",
    )(lengths, q, k, v, *moving)


def attend_back_kernel(
    tq, unroll, moves, len_ref, q_ref, k_ref, v_ref, o_ref, do_ref, aug_ref, cos_ref, sin_ref, *rest
):
    inputs, rest = rest[:moves], rest[moves:]
    dq_ref, dk_ref, dv_ref, rest = rest[0], rest[1], rest[2], rest[3:]
    outputs, rest = rest[:moves], rest[moves:]
    qa, da, ka, va, kt, dk_acc, dv_acc = rest[:7]
    keys, span = k_ref.shape[1], q_ref.shape[1]
    tiles = span // tq
    events = {}
    if moves:
        events = back_events(inputs, outputs, *rest[7:])

    @pl.when(pl.program_id(1) == 0)
    def _():
        ka[:, PAIR:] = key_mask(len_ref, moves, keys, -1.0).astype(BF)
        va[:, PAIR:] = jnp.where(lanes((keys, PAIR)) % HEAD < 3, -1.0, 0.0).astype(BF)

    k, do = k_ref[0], do_ref[0]
    ka[:, :PAIR] = k
    va[:, :PAIR] = v_ref[0]
    kt[...] = k.T
    prod = do.astype(F32) * o_ref[0].astype(F32)
    first = prod.astype(BF)
    second = (prod - first.astype(F32)).astype(BF)
    block = (
        (lax.broadcasted_iota(jnp.int32, (PAIR, PAIR), 0) // HEAD)
        == (lax.broadcasted_iota(jnp.int32, (PAIR, PAIR), 1) // HEAD)
    ).astype(F32).astype(BF)
    delta = dot(first, block) + dot(second, block)
    q_both = jnp.concatenate([q_ref[0], aug_ref[0]], axis=1)
    d_both = jnp.concatenate([do, spread(delta, jnp.zeros_like(delta))], axis=1)
    side = lanes(q_both.shape) // HEAD % 2
    for h in range(2):
        qa[h] = jnp.where(side == h, q_both, jnp.zeros_like(q_both))
        da[h] = jnp.where(side == h, d_both, jnp.zeros_like(d_both))
    dk_acc[...] = jnp.zeros_like(dk_acc)
    dv_acc[...] = jnp.zeros_like(dv_acc)

    def query_step(i, _):
        at_q = pl.ds(pl.multiple_of(i * tq, tq), tq)
        dv, dk, dq = None, None, []
        for h in range(2):
            st = dot_nt(ka[...], qa[h, at_q, :])
            dpt = dot_nt(va[...], da[h, at_q, :])
            p = jnp.exp2(st)
            ds = (p * dpt).astype(BF)
            pv = dot(p.astype(BF), da[h, at_q, :PAIR])
            pk = dot(ds, qa[h, at_q, :PAIR])
            dv = pv if dv is None else dv + pv
            dk = pk if dk is None else dk + pk
            dq.append(dot(kt[h * HEAD : (h + 1) * HEAD, :], ds))
        dv_acc[...] += dv
        dk_acc[...] += dk
        g = jnp.concatenate(dq, axis=0).T * 0.125
        dq_ref[0, at_q, :] = back_turn(g, cos_ref[at_q, :], sin_ref[at_q, :]).astype(BF)
        return 0

    def group(n, _):
        now = pl.program_id(1) * (tiles // unroll) + n
        for at_step, acts in events.items():

            @pl.when(now == at_step)
            def _():
                for act in acts:
                    act()

        for j in range(unroll):
            query_step(n * unroll + j, 0)
        return 0

    lax.fori_loop(0, tiles // unroll, group, 0)
    dv_ref[0] = dv_acc[...].astype(dv_ref.dtype)
    g = dk_acc[...] * LN2
    if dk_ref.dtype == BF:
        g = back_turn(g, cos_ref[...], sin_ref[...])
    dk_ref[0] = g.astype(dk_ref.dtype)
    if moves:

        @pl.when(pl.program_id(1) == pl.num_programs(1) - 1)
        def _():
            for act in events.last:
                act()


def back_turn(g, cosine, sine):
    return g * cosine - turn(g * sine)


def wide_piece(source, columns):
    return lambda c, y: source.at[:, :, c, :, pl.ds(y * columns, columns)]


def tall_piece(source):
    return lambda c, y: source.at[:, :, c, y]


BACK_ORDERS = ("yx", "xy", "zyx", "xy")
BACK_PLAN = (
    (1, 0, 1), (1, 1, 1), (1, 2, 1), (1, 3, 1), (3, 0, 2), (3, 1, 2), (3, 3, 2), (4, 0, 3), (4, 1, 3), (4, 2, 2),
    (4, 3, 3), (5, 0, 4), (5, 2, 3),
)
BACK_LAST = (2, 1, 3)


def back_events(inputs, outputs, send, recv, local, *bufs):
    me = place()
    reduces = []
    for i, (source, out) in enumerate(zip(inputs, outputs)):
        piece = wide_piece(source, source.shape[-1] // 2) if len(source.shape) == 5 else tall_piece(source)
        reduces.append(
            Reduce(
                me, piece, bufs[5 * i : 5 * i + 5], out, send, recv,
                local.at[pl.ds(2 * i, 2)], i * Reduce.SEMS, BACK_ORDERS[i],
            )
        )
    events = Events()
    events.put(0, functools.partial(greet, me), *(reduces[i].start for i in (2, 0, 1, 3)))
    for at, i, stage in BACK_PLAN:
        events.put(at, functools.partial(reduces[i].step, stage))
    events.last += [functools.partial(reduces[i].step, 4) for i in BACK_LAST]
    events.last += [r.finish for r in reduces]
    return events


def attend_back_call(q, k, v, lengths, o, do, aug, cosine, sine, whole, moving=(), tq=512, unroll=4):
    rows, span, width = q.shape
    keys = k.shape[1]
    tq = min(tq, span)
    unroll = min(unroll, span // tq)
    moves = len(moving)
    qs = pl.BlockSpec((1, span, PAIR), lambda r, p: (r, 0, p))
    ks = pl.BlockSpec((1, keys, PAIR), lambda r, p: (r, 0, p))
    table = pl.BlockSpec((span, PAIR), lambda r, p: (0, 0), pipeline_mode=pl.Buffered(1))
    hbm = pl.BlockSpec(memory_space=pl.ANY)
    kv_type = BF if whole else F32
    results, result_specs, extra, more = [], [], [], {}
    if moves:
        extra = [pltpu.SemaphoreType.DMA((Reduce.SEMS * moves,))] * 2
        extra += [pltpu.SemaphoreType.DMA((2 * moves,))]
        for a, order in zip(moving, BACK_ORDERS):
            block = (a.shape[-2], a.shape[-1] // (2 if a.ndim == 5 else 1))
            results.append(jax.ShapeDtypeStruct(block, F32))
            result_specs.append(pl.BlockSpec(block, lambda r, p: (0, 0), pipeline_mode=pl.Buffered(1)))
            extra += Reduce.scratch(*block, a.dtype, order)
        more = dict(collective_id=2, has_side_effects=True)
    return pl.pallas_call(
        functools.partial(attend_back_kernel, tq, unroll, moves),
        grid=(rows, width // PAIR),
        in_specs=[pl.BlockSpec(memory_space=pltpu.SMEM), qs, ks, ks, qs, qs, qs, table, table]
        + [hbm] * moves,
        out_specs=[qs, ks, ks] + result_specs,
        out_shape=[
            jax.ShapeDtypeStruct(q.shape, BF),
            jax.ShapeDtypeStruct(k.shape, kv_type),
            jax.ShapeDtypeStruct(k.shape, kv_type),
        ]
        + results,
        scratch_shapes=[
            pltpu.VMEM((2, span, 2 * PAIR), BF),
            pltpu.VMEM((2, span, 2 * PAIR), BF),
            pltpu.VMEM((keys, 2 * PAIR), BF),
            pltpu.VMEM((keys, 2 * PAIR), BF),
            pltpu.VMEM((PAIR, keys), BF),
            pltpu.VMEM((keys, PAIR), F32),
            pltpu.VMEM((keys, PAIR), F32),
        ]
        + extra,
        compiler_params=pltpu.CompilerParams(vmem_limit_bytes=VMEM_LIMIT, **more),
        name="attend_back",
    )(lengths, q, k, v, o, do, aug, cosine, sine, *moving)


def middle_kernel(
    chunk, moves, x_ref, att_ref, cot_ref, wo_ref, wg_ref, wu_ref, wd_ref, *rest
):
    source, rest = rest[:moves], rest[moves:]
    (out_ref, dfirst_ref, datt_ref, act_ref, dg_ref, du_ref, ht_ref, dft_ref, at_ref, gg_ref) = rest[:10]
    ca, cb, gains = rest[10:13]
    if moves:
        arrived, dy_ref, send, recv = rest[13:]
        me = place()
        now, per = pl.program_id(0), pl.num_programs(0) // 2
        tile = dy_ref.shape[0]
        give = pltpu.make_async_remote_copy(
            src_ref=source[0].at[1 - me["y"]],
            dst_ref=arrived,
            send_sem=send.at[0],
            recv_sem=recv.at[0],
            device_id=device(moved(me, "y", 1)),
            device_id_type=MESH,
        )

        @pl.when(now == 0)
        def _():
            greet(me)
            give.start()

        pl.when(now == per)(give.wait)

        @pl.when(now < per)
        def _():
            dy_ref[...] = cot_ref[...]

        @pl.when(now >= per)
        def _():
            dy_ref[...] = arrived[pl.ds(pl.multiple_of((now - per) * tile, tile), tile), :]

    else:
        dy_ref = cot_ref

    @pl.when(pl.program_id(0) == 0)
    def _():
        gg_ref[...] = jnp.zeros_like(gg_ref)
        gains[...] = wo_ref[:, x_ref.shape[1] :].astype(F32).T[:8]

    gain1, gain2 = gains[0:1, :], gains[1:2, :]
    att = att_ref[...]
    at_ref[...] = att.T
    first = x_ref[...].astype(F32) + dot(att, wo_ref[:, : att.shape[1]])
    centered = first - jnp.mean(first, axis=1, keepdims=True)
    s1 = lax.rsqrt(jnp.mean(centered * centered, axis=1, keepdims=True) + EPS)
    n1 = centered * s1
    hidden = n1 * gain1
    low = hidden.astype(BF)
    ht_ref[...] = low.T
    hidden_width = wg_ref.shape[1]
    second = hidden
    for c in range(hidden_width // chunk):
        at = slice(c * chunk, (c + 1) * chunk)
        g = dot(low, wg_ref[:, at])
        u = dot(low, wu_ref[:, at])
        sig = jax.nn.sigmoid(g)
        silu = g * sig
        act = (silu * u).astype(BF)
        act_ref[:, at] = act
        ca[:, at] = (u * (sig + silu * (1.0 - sig))).astype(ca.dtype)
        cb[:, at] = silu.astype(cb.dtype)
        second = second + dot(act, wd_ref[at, :])
    centered = second - jnp.mean(second, axis=1, keepdims=True)
    s2 = lax.rsqrt(jnp.mean(centered * centered, axis=1, keepdims=True) + EPS)
    n2 = centered * s2
    out_ref[...] = (n2 * gain2).astype(BF)
    dy = dy_ref[...].astype(F32)
    gg_ref[1:2, :] += jnp.sum(dy * n2, axis=0, keepdims=True)
    inner = dy * gain2
    d_second = s2 * (
        inner - jnp.mean(inner, axis=1, keepdims=True) - n2 * jnp.mean(inner * n2, axis=1, keepdims=True)
    )
    d_ffn = d_second.astype(BF)
    dft_ref[...] = d_ffn.T
    d_hidden = d_second
    for c in range(hidden_width // chunk):
        at = slice(c * chunk, (c + 1) * chunk)
        d_act = dot_nt(d_ffn, wd_ref[at, :])
        dg = (d_act * ca[:, at]).astype(BF)
        du = (d_act * cb[:, at]).astype(BF)
        dg_ref[:, at] = dg
        du_ref[:, at] = du
        d_hidden = d_hidden + dot_nt(dg, wg_ref[:, at]) + dot_nt(du, wu_ref[:, at])
    gg_ref[0:1, :] += jnp.sum(d_hidden * n1, axis=0, keepdims=True)
    inner = d_hidden * gain1
    d_first = s1 * (
        inner - jnp.mean(inner, axis=1, keepdims=True) - n1 * jnp.mean(inner * n1, axis=1, keepdims=True)
    )
    low = d_first.astype(BF)
    dfirst_ref[...] = low
    datt_ref[...] = dot_nt(low, wo_ref[:, : low.shape[1]]).astype(BF)


def middle_call(x, att, cot, wo, wg, wu, wd, tile=256, chunk=768):
    tokens, width = x.shape
    hidden_width = wg.shape[1]
    tile = min(tile, tokens)
    moves = cot.ndim - 2
    per = tokens // tile // 2

    def place_of(i):
        if not moves:
            return i
        return lax.rem(lax.axis_index("blk") + i // per, 2) * per + lax.rem(i, per)

    row = pl.BlockSpec((tile, width), lambda i: (place_of(i), 0))
    wide = pl.BlockSpec((tile, hidden_width), lambda i: (place_of(i), 0))
    column = pl.BlockSpec((width, tile), lambda i: (0, place_of(i)))
    cot_row, extra, more = row, [], {}
    if moves:
        cot_row = pl.BlockSpec(
            (None, tile, width), lambda i: (lax.axis_index("blk"), jnp.minimum(i, per - 1), 0)
        )
        extra = [pltpu.VMEM((tokens // 2, width), BF), pltpu.VMEM((tile, width), BF)]
        extra += [pltpu.SemaphoreType.DMA((1,))] * 2
        more = dict(collective_id=5, has_side_effects=True)

    def whole(a):
        return pl.BlockSpec(a.shape, lambda i: (0, 0), pipeline_mode=pl.Buffered(1))

    return pl.pallas_call(
        functools.partial(middle_kernel, chunk, moves),
        grid=(tokens // tile,),
        in_specs=[row, row, cot_row, whole(wo), whole(wg), whole(wu), whole(wd)]
        + [pl.BlockSpec(memory_space=pl.ANY)] * moves,
        out_specs=[row, row, row, wide, wide, wide, column, column, column]
        + [pl.BlockSpec((PAIR, width), lambda i: (0, 0))],
        out_shape=[jax.ShapeDtypeStruct((tokens, width), BF)] * 3
        + [jax.ShapeDtypeStruct((tokens, hidden_width), BF)] * 3
        + [jax.ShapeDtypeStruct((width, tokens), BF)] * 3
        + [jax.ShapeDtypeStruct((PAIR, width), F32)],
        scratch_shapes=[pltpu.VMEM((tile, hidden_width), F32)] * 2 + [pltpu.VMEM((8, width), F32)] + extra,
        compiler_params=pltpu.CompilerParams(vmem_limit_bytes=VMEM_LIMIT, **more),
        name="middle",
    )(x, att, cot, wo, wg, wu, wd, *([cot] * moves))


def outer_kernel(a_ref, b_ref, o_ref):
    o_ref[...] = dot(a_ref[...], b_ref[...]).astype(o_ref.dtype)


def outer_call(a, b, out_type, tile=512):
    rows, tokens = a.shape
    columns = b.shape[1]
    tile = tile if columns % tile == 0 else 256
    return pl.pallas_call(
        outer_kernel,
        grid=(columns // tile,),
        in_specs=[
            pl.BlockSpec((rows, tokens), lambda i: (0, 0), pipeline_mode=pl.Buffered(1)),
            pl.BlockSpec((tokens, tile), lambda i: (0, i)),
        ],
        out_specs=pl.BlockSpec((rows, tile), lambda i: (0, i)),
        out_shape=jax.ShapeDtypeStruct((rows, columns), out_type),
        compiler_params=params(),
        name="outer",
    )(a, b)


def outers_kernel(steps, moves, a1_ref, a2_hbm, a3_hbm, b1_ref, b2_ref, b3_ref, b4_hbm, gains_ref, *rest):
    source, rest = rest[:moves], rest[moves:]
    o1_ref, o2_ref, o3_ref, o4_ref, rest = rest[0], rest[1], rest[2], rest[3], rest[4:]
    now = pl.program_id(0)
    target, rest = rest[:moves], rest[moves:]
    a2_ref, a3_ref, b4_ref, load, rest = rest[0], rest[1], rest[2], rest[3], rest[4:]
    late = [
        pltpu.make_async_copy(a, b, load.at[i])
        for i, (a, b) in enumerate(((a2_hbm, a2_ref), (a3_hbm, a3_ref), (b4_hbm, b4_ref)))
    ]

    @pl.when(now == 0)
    def _():
        for copy in late:
            copy.start()

    @pl.when(now == 2 * steps)
    def _():
        for copy in late:
            copy.wait()

    if moves:
        target, (bounce, send, recv, local) = target[0], rest
        me = place()
        swap = Swap(me, source[0], target, bounce, send, recv, local.at[0], 0, ((0, target.shape[1]),))

        @pl.when(now == 0)
        def _():
            greet(me)
            swap.give(0)
            swap.keep_begin()

        pl.when(now == 3)(swap.keep_turn)
        pl.when(now == 3 * steps)(swap.finish)

    @pl.when(now < steps)
    def _():
        o1_ref[...] = dot(a1_ref[...], b1_ref[...]).astype(BF)

    @pl.when((now >= steps) & (now < 2 * steps))
    def _():
        o2_ref[...] = dot(a1_ref[...], b2_ref[...]).astype(BF)

    @pl.when((now >= 2 * steps) & (now < 3 * steps))
    def _():
        o3_ref[...] = dot(a2_ref[...], b3_ref[...]).astype(BF)

    @pl.when(now == 3 * steps)
    def _():
        width = b4_ref.shape[1]
        o4_ref[:, :width] = dot(a3_ref[...], b4_ref[...])
        o4_ref[:, width:] = gains_ref[...].T


def outers_call(h_t, df_t, att_t, d_gate, d_up, act, d_first, gains, moving=(), tile=512):
    width, tokens = h_t.shape
    hidden = d_gate.shape[1]
    steps = hidden // tile

    def whole(a):
        return pl.BlockSpec(a.shape, lambda i: (0, 0), pipeline_mode=pl.Buffered(1))

    def part(rows, n):
        return pl.BlockSpec((rows, tile), lambda i: (0, jnp.clip(i - n * steps, 0, steps - 1)))

    moves = len(moving)
    hbm = pl.BlockSpec(memory_space=pl.ANY)
    extra = [pltpu.VMEM(a.shape, BF) for a in (df_t, att_t, d_first)] + [pltpu.SemaphoreType.DMA((3,))]
    extra += [pltpu.VMEM(a.shape[1:], BF) for a in moving]
    extra += [pltpu.SemaphoreType.DMA((1,))] * (3 * moves)
    more = dict(collective_id=4, has_side_effects=True) if moves else {}
    return pl.pallas_call(
        functools.partial(outers_kernel, steps, moves),
        grid=(3 * steps + 1,),
        in_specs=[whole(h_t), hbm, hbm] + [part(tokens, n) for n in range(3)] + [hbm, whole(gains)]
        + [hbm] * moves,
        out_specs=[part(width, n) for n in range(3)]
        + [pl.BlockSpec((width, width + PAIR), lambda i: (0, 0), pipeline_mode=pl.Buffered(1))]
        + [hbm] * moves,
        out_shape=[jax.ShapeDtypeStruct((width, hidden), BF)] * 3
        + [jax.ShapeDtypeStruct((width, width + PAIR), F32)]
        + [jax.ShapeDtypeStruct(a.shape, BF) for a in moving],
        scratch_shapes=extra,
        compiler_params=pltpu.CompilerParams(vmem_limit_bytes=VMEM_LIMIT, **more),
        name="outers",
    )(h_t, df_t, att_t, d_gate, d_up, act, d_first, gains, *moving)


CLOSING_ORDERS = ("xy", "xy", "xy")


def closing_kernel(
    dq_hbm, dk_hbm, dv_hbm, first_hbm, xt_hbm, w_hbm, g_out, sum_ref,
    dq, dk, dv, first, xt, w, g, w0, w1, w2, send, recv, local, mine_sem, *bufs,
):
    me = place()
    y = me["y"]
    half = g.shape[1]

    def load(n, a, b, which=None):
        if which is not None:
            at = pl.ds(pl.multiple_of(which * half, half), half)
            a, b = a.at[at], b.at[at]
        return pltpu.make_async_copy(a, b, local.at[n])

    rows_hbm = ((dq_hbm, dq), (dk_hbm, dk), (dv_hbm, dv), (first_hbm, first))
    early = [load(0, w_hbm, w)] + [load(1 + n, a, b, 1 - y) for n, (a, b) in enumerate(rows_hbm)]
    later = [load(5, xt_hbm, xt)] + [load(6 + n, a, b, y) for n, (a, b) in enumerate(rows_hbm)]
    for copy in early + later:
        copy.start()
    greet(me)
    width = dq.shape[1]
    tile = half // 4

    def rows_of(which, t):
        at = pl.ds(pl.multiple_of(which * half + t * tile, tile), tile)
        total = first[at, :].astype(F32)
        for n, a in enumerate((dq, dk, dv)):
            total += dot_nt(a[at, :], w[:, n * width : (n + 1) * width])
        g[which, pl.ds(t * tile, tile), :] = total.astype(BF)

    for copy in early:
        copy.wait()
    quarter = half // 4

    def give(n, target_half):
        part = pl.ds(n * quarter, quarter)
        return pltpu.make_async_remote_copy(
            src_ref=g.at[1 - y, part],
            dst_ref=g_out.at[target_half, part],
            send_sem=send.at[n],
            recv_sem=recv.at[n],
            device_id=device(moved(me, "y", 1)),
            device_id_type=MESH,
        )

    for t in range(4):
        rows_of(1 - y, t)
        if t < 2:
            give(t, y).start()
    for copy in later:
        copy.wait()
    reduces = []
    for n, (a, target) in enumerate(((dq, w0), (dk, w1), (dv, w2))):
        reduces.append(
            Reduce(
                me, tall_piece(target), bufs[5 * n : 5 * n + 5], sum_ref.at[:, pl.ds(n * width, width)],
                send, recv, mine_sem.at[pl.ds(2 * n, 2)], 4 + n * Reduce.SEMS, CLOSING_ORDERS[n],
            )
        )

    def products(n, a, target):
        step = 2 * PAIR

        def part(i, _):
            at = pl.ds(pl.multiple_of(i * step, step), step)
            value = dot(xt[...], a[:, at])
            target[:, :, :, :, :, at] = value.reshape(target.shape[:-1] + (step,)).astype(BF)
            return 0

        lax.fori_loop(0, width // step, part, 0)

    products(0, dq, w0)
    reduces[0].start()
    give(2, y).start()
    products(1, dk, w1)
    reduces[1].start()
    reduces[0].step(1)
    products(2, dv, w2)
    reduces[2].start()
    reduces[1].step(1)
    reduces[0].step(2)
    reduces[2].step(1)
    rows_of(y, 0)
    rows_of(y, 1)
    reduces[1].step(2)
    reduces[0].step(3)
    rows_of(y, 2)
    rows_of(y, 3)
    keep = pltpu.make_async_copy(g.at[y], g_out.at[y], local.at[0])
    keep.start()
    reduces[2].step(2)
    give(3, y).start()
    reduces[1].step(3)
    reduces[0].step(4)
    reduces[2].step(3)
    reduces[1].step(4)
    reduces[2].step(4)
    for r in reduces:
        r.finish()
    for n in range(4):
        give(n, 1 - y).wait_recv()
        give(n, y).wait_send()
    keep.wait()


def closing_call(dq, dk, dv, first, xt, w):
    tokens, width = dq.shape
    hbm = pl.BlockSpec(memory_space=pl.ANY)
    block = (width // 32, width)
    full = pltpu.VMEM((4, 2, 2, 2) + block, BF)
    scratch = [pltpu.VMEM(a.shape, BF) for a in (dq, dk, dv, first, xt, w)]
    scratch += [pltpu.VMEM((2, tokens // 2, width), BF), full, full, full]
    sems = 4 + 3 * Reduce.SEMS
    scratch += [pltpu.SemaphoreType.DMA((sems,))] * 2
    scratch += [pltpu.SemaphoreType.DMA((10,)), pltpu.SemaphoreType.DMA((6,))]
    for order in CLOSING_ORDERS:
        scratch += Reduce.scratch(*block, BF, order)
    return pl.pallas_call(
        closing_kernel,
        in_specs=[hbm] * 6,
        out_specs=[hbm, pl.BlockSpec(memory_space=pltpu.VMEM)],
        out_shape=[
            jax.ShapeDtypeStruct((2, tokens // 2, width), BF),
            jax.ShapeDtypeStruct((block[0], 3 * width), F32),
        ],
        scratch_shapes=scratch,
        compiler_params=pltpu.CompilerParams(
            vmem_limit_bytes=VMEM_LIMIT, collective_id=3, has_side_effects=True
        ),
        name="closing",
    )(dq, dk, dv, first, xt, w)


def tokens_kernel(dq_ref, dk_ref, dv_ref, dfirst_ref, w_ref, o_ref):
    width = dq_ref.shape[1]
    total = dfirst_ref[...].astype(F32)
    total += dot_nt(dq_ref[...], w_ref[:, :width])
    total += dot_nt(dk_ref[...], w_ref[:, width : 2 * width])
    total += dot_nt(dv_ref[...], w_ref[:, 2 * width :])
    o_ref[...] = total.astype(BF)


def tokens_call(dq, dk, dv, dfirst, w, tile=512):
    tokens, width = dq.shape
    tile = min(tile, tokens)
    row = pl.BlockSpec((tile, width), lambda i: (i, 0))
    return pl.pallas_call(
        tokens_kernel,
        grid=(tokens // tile,),
        in_specs=[row] * 4 + [pl.BlockSpec(w.shape, lambda i: (0, 0), pipeline_mode=pl.Buffered(1))],
        out_specs=row,
        out_shape=jax.ShapeDtypeStruct((tokens, width), BF),
        compiler_params=params(),
        name="grad_tokens",
    )(dq, dk, dv, dfirst, w)


def angle_tables(span):
    index = np.arange(HEAD // 2, dtype=np.float64)
    inverse = np.power(1000.0, -2.0 * index / HEAD)
    angles = np.arange(span, dtype=np.float64)[:, None] * inverse[None, :]
    repeat = (1, PAIR // (HEAD // 2))
    return (
        np.tile(np.cos(angles), repeat).astype(np.float32),
        np.tile(np.sin(angles), repeat).astype(np.float32),
    )


def body(tokens, lengths, w_qkv, w_out, w_gate, w_up, w_down, gain_one, gain_two, cotangent):
    axes = ("dp", "blk")
    blk = lax.axis_size("blk")
    mine = lax.axis_index("blk")
    rows, span, width = tokens.shape
    seq = span * blk
    own = blk == 2 and rows == 2 and lax.axis_size("dp") == 16

    def gather(a):
        return lax.all_gather(a, axes, axis=0, tiled=True)

    cosine, sine = map(jnp.asarray, angle_tables(seq))
    gains = jnp.stack([gain_one, gain_two], 1)
    w_out = jnp.pad(jnp.concatenate([w_out, gains], 1), ((0, 0), (0, PAIR - 2)))
    if own:
        x, f_qkv, q, k, v, xt, *moving = opening_call(
            tokens, w_qkv, w_out, w_gate, w_up, w_down, cosine, sine
        )
        x = x.reshape(1, seq, width)
        cq, sq = cosine, sine
    else:
        f_qkv, f_out, f_gate, f_up, f_down = map(gather, (w_qkv, w_out, w_gate, w_up, w_down))
        x, cot = tokens, cotangent.reshape(rows * span, width)
        cq = lax.dynamic_slice_in_dim(cosine, mine * span, span, 0)
        sq = lax.dynamic_slice_in_dim(sine, mine * span, span, 0)
    n, t = x.shape[:2]
    flat = x.reshape(n * t, width)
    if not own:
        q, k, v, xt = qkv_call(flat, f_qkv, cq, sq)
    q, k, v = (a.reshape(n, t, width) for a in (q, k, v))
    if not own:
        k = lax.all_gather(k, "blk", axis=1, tiled=True)
        v = lax.all_gather(v, "blk", axis=1, tiled=True)
    if own:
        att, aug, f_out, f_gate, f_up, f_down = attend_call(
            q, k, v, lengths, moving
        )
        f_out = f_out.reshape(width, -1)
        cot = cotangent
        f_gate, f_up = f_gate.reshape(width, -1), f_up.reshape(width, -1)
        f_down = f_down.reshape(-1, width)
    else:
        att, aug = attend_call(q, k, v, lengths)
    out, d_first, d_att, act, d_gate, d_up, h_t, df_t, att_t, gains = middle_call(
        flat, att.reshape(n * t, width), cot, f_out, f_gate, f_up, f_down
    )
    moving = (out.reshape(2, span, width),) if own else ()
    gw_gate, gw_up, gw_down_t, gw_out, *moving = outers_call(
        h_t, df_t, att_t, d_gate, d_up, act, d_first, gains, moving
    )
    d_att = d_att.reshape(n, t, width)
    if own:
        wide = tuple(g.reshape(4, 2, 2, width // 16, -1) for g in (gw_gate, gw_up, gw_down_t))
        out = moving[0]
        dq, dk, dv, s_gate, s_up, s_down_t, s_out = attend_back_call(
            q, k, v, lengths, att, d_att, aug, cq, sq, True,
            wide + (gw_out.reshape(4, 2, 2, 2, width // 32, -1),),
        )
    else:

        def scatter_wide(g):
            g = lax.psum_scatter(g, "blk", scatter_dimension=1, tiled=True)
            return lax.psum_scatter(g, "dp", scatter_dimension=0, tiled=True).astype(F32)

        s_gate, s_up, s_down_t = map(scatter_wide, (gw_gate, gw_up, gw_down_t))
        s_out = lax.psum_scatter(gw_out, axes, scatter_dimension=0, tiled=True)
        dq, dk, dv = attend_back_call(q, k, v, lengths, att, d_att, aug, cq, sq, False)
        dk = lax.psum_scatter(dk, "blk", scatter_dimension=1, tiled=True)
        dv = lax.psum_scatter(dv, "blk", scatter_dimension=1, tiled=True)
        heads = (dk * jnp.tile(sq, (1, width // PAIR))).reshape(n, t, HEADS, HEAD)
        half = jnp.concatenate([heads[..., HEAD // 2 :], -heads[..., : HEAD // 2]], -1)
        dk = dk * jnp.tile(cq, (1, width // PAIR)) + half.reshape(n, t, width)
        dk, dv = dk.astype(BF), dv.astype(BF)
    s_down = s_down_t.T
    s_out, s_gg = s_out[:, :width], s_out[:, width : width + 2]
    dq, dk, dv = (a.reshape(n * t, width) for a in (dq, dk, dv))
    if own:
        g_tokens, s_qkv = closing_call(dq, dk, dv, d_first, xt, f_qkv)
    else:
        gw_qkv = jnp.concatenate([outer_call(xt, a, BF, 256) for a in (dq, dk, dv)], 1)
        s_qkv = lax.psum_scatter(gw_qkv, axes, scatter_dimension=0, tiled=True).astype(F32)
        g_tokens = tokens_call(dq, dk, dv, d_first, f_qkv).reshape(tokens.shape)
        out = out.reshape(tokens.shape)
    return (out, g_tokens, s_qkv, s_out, s_gate, s_up, s_down, s_gg[:, 0], s_gg[:, 1])


def solution(mesh):
    both = ("dp", "blk")
    return jax.shard_map(
        body,
        mesh=mesh,
        in_specs=(
            P("dp", "blk", None),
            P("dp"),
            P(both, None),
            P(both, None),
            P(both, None),
            P(both, None),
            P(both, None),
            P(both),
            P(both),
            P("dp", "blk", None),
        ),
        out_specs=(
            P("dp", "blk", None),
            P("dp", "blk", None),
            P(both, None),
            P(both, None),
            P("dp", "blk"),
            P("dp", "blk"),
            P("blk", "dp"),
            P(both),
            P(both),
        ),
        check_vma=False,
    )
```

```python
import functools

import jax
import jax.numpy as jnp
import numpy as np
from jax import lax
from jax.experimental import pallas as pl
from jax.experimental.pallas import tpu as pltpu
from jax.sharding import PartitionSpec as P

HEADS = 12
HEAD = 64
PAIR = 2 * HEAD
EPS = 1e-05
NEG = -1e30
LOG2E = 1.4426950408889634
LN2 = 0.6931471805599453
VMEM_LIMIT = 60 * 1024 * 1024

BF = jnp.bfloat16
F32 = jnp.float32


def dot(a, b):
    return lax.dot_general(a, b, (((1,), (0,)), ((), ())), preferred_element_type=F32)


def dot_nt(a, b):
    return lax.dot_general(a, b, (((1,), (1,)), ((), ())), preferred_element_type=F32)


def params(limit=VMEM_LIMIT):
    return pltpu.CompilerParams(vmem_limit_bytes=limit)


def lanes(shape):
    return lax.broadcasted_iota(jnp.int32, shape, 1)


def turn(u):
    low_half = (lanes(u.shape) % HEAD) < HEAD // 2
    return jnp.where(low_half, -pltpu.roll(u, PAIR - HEAD // 2, 1), pltpu.roll(u, HEAD // 2, 1))


MESH = pl.DeviceIdType.MESH
AXES = "zxcy"
SIZE = {"z": 4, "x": 2, "c": 2, "y": 2}


def place():
    dp, y = lax.axis_index("dp"), lax.axis_index("blk")
    return {"z": dp // 4, "x": dp // 2 % 2, "c": dp % 2, "y": y}


def moved(me, axis, by):
    return {**me, axis: lax.rem(me[axis] + by, SIZE[axis])}


def device(at):
    return ((at["z"] * 2 + at["x"]) * 2 + at["c"], at["y"])


def greet(me):
    barrier = pltpu.get_barrier_semaphore()
    peers = [moved(me, "y", 1), moved(me, "x", 1), moved(me, "c", 1)]
    peers += [moved(me, "z", d) for d in range(1, 4)]
    for peer in peers:
        pl.semaphore_signal(barrier, inc=1, device_id=device(peer), device_id_type=MESH)
    pl.semaphore_wait(barrier, len(peers))


class Gather:
    def __init__(self, me, shard, full, send, recv, local, base, order, held="", columns=None):
        self.me, self.shard, self.full, self.held = me, shard, full, held
        self.part = () if columns is None else (slice(None), pl.ds(*columns))
        self.spans = [a for a in AXES if a in held + order]
        self.send, self.recv, self.local, self.base, self.order = send, recv, local, base, order

    @staticmethod
    def sems(order):
        return sum(SIZE[a] - 1 for a in order)

    def view(self, at, got):
        return self.full.at[tuple(slice(None) if a in got else at[a] for a in self.spans) + self.part]

    def at_stage(self, stage):
        got = self.held + self.order[:stage]
        return got, self.order[stage], self.base + self.sems(self.order[:stage])

    def copies(self, stage):
        got, axis, slot = self.at_stage(stage)
        here = self.view(self.me, got)
        return [
            pltpu.make_async_remote_copy(
                src_ref=self.shard if stage == 0 else here,
                dst_ref=here,
                send_sem=self.send.at[slot + d - 1],
                recv_sem=self.recv.at[slot + d - 1],
                device_id=device(moved(self.me, axis, d)),
                device_id_type=MESH,
            )
            for d in range(1, SIZE[axis])
        ]

    def own(self):
        return pltpu.make_async_copy(self.shard, self.view(self.me, self.held), self.local)

    def arrivals(self, stage):
        got, axis, slot = self.at_stage(stage)
        for d in range(1, SIZE[axis]):
            there = self.view(moved(self.me, axis, SIZE[axis] - d), got)
            pltpu.make_async_remote_copy(
                src_ref=there,
                dst_ref=there,
                send_sem=self.send.at[slot + d - 1],
                recv_sem=self.recv.at[slot + d - 1],
                device_id=device(moved(self.me, axis, d)),
                device_id_type=MESH,
            ).wait_recv()

    def start(self):
        self.own().start()
        for copy in self.copies(0):
            copy.start()

    def step(self, stage):
        self.arrivals(stage - 1)
        if stage == 1:
            self.own().wait()
        if stage < len(self.order):
            for copy in self.copies(stage):
                copy.start()

    def finish(self):
        for stage in range(len(self.order)):
            for copy in self.copies(stage):
                copy.wait_send()


class Reduce:
    SEMS = 7

    def __init__(self, me, piece, bufs, out, send, recv, local, base, order):
        self.me, self.piece, self.out, self.order = me, piece, out, order
        self.b, self.r0, self.r1, self.r2, self.r3 = bufs
        self.send, self.recv, self.local, self.base = send, recv, local, base

    def copy(self, source, target, slot, axis, by=1):
        return pltpu.make_async_remote_copy(
            src_ref=source,
            dst_ref=target,
            send_sem=self.send.at[self.base + slot],
            recv_sem=self.recv.at[self.base + slot],
            device_id=device(moved(self.me, axis, by)),
            device_id_type=MESH,
        )

    def mine(self):
        c = self.me["c"]
        return [
            pltpu.make_async_copy(self.piece(c, y), self.b.at[y], self.local.at[y]) for y in range(2)
        ]

    def copies(self, stage):
        x, y, z = self.me["x"], self.me["y"], self.me["z"]
        if stage == 0:
            other = 1 - self.me["c"]
            return [self.copy(self.piece(other, i), self.r0.at[i], i, "c") for i in range(2)]
        if self.order[0] == "z":
            if stage == 1:
                return [
                    self.copy(self.b.at[:, lax.rem(z + d, 4)], self.r1.at[d - 1], 3 + d, "z", d)
                    for d in range(1, 4)
                ]
            if stage == 2:
                return [self.copy(self.b.at[1 - y, z], self.r2, 2, "y")]
            return [self.copy(self.b.at[y, z, 1 - x], self.r3, 3, "x")]
        if stage == 1:
            source = self.b.at[1 - y] if self.order[0] == "y" else self.b.at[:, :, 1 - x]
            return [self.copy(source, self.r1, 2, self.order[0])]
        if stage == 2:
            source = self.b.at[y, :, 1 - x] if self.order[0] == "y" else self.b.at[1 - y, :, x]
            return [self.copy(source, self.r2, 3, self.order[1])]
        return [
            self.copy(self.b.at[y, lax.rem(z + d, 4), x], self.r3.at[d - 1], 3 + d, "z", d)
            for d in range(1, 4)
        ]

    def start(self):
        for copy in self.copies(0) + self.mine():
            copy.start()

    def step(self, stage):
        x, y, z = self.me["x"], self.me["y"], self.me["z"]
        for copy in self.copies(stage - 1):
            copy.wait_recv()
        b = self.b
        if stage == 1:
            for copy in self.mine():
                copy.wait()

            def add(i, _):
                at = (i // 4, i % 4)
                b[at] = b[at] + self.r0[at]
                return 0

            lax.fori_loop(0, 8, add, 0)
        if self.order[0] == "z" and stage > 1:
            if stage == 2:

                def add(i, _):
                    at = (i // 2, i % 2)
                    total = b[at[0], z, at[1]].astype(F32)
                    for d in range(3):
                        total = total + self.r1[d, at[0], at[1]].astype(F32)
                    b[at[0], z, at[1]] = total.astype(b.dtype)
                    return 0

                lax.fori_loop(0, 4, add, 0)
            if stage == 3:
                for i in range(2):
                    b[y, z, i] = b[y, z, i] + self.r2[i]
            if stage == 4:
                self.out[...] = b[y, z, x].astype(F32) + self.r3[...].astype(F32)
                return
            for copy in self.copies(stage):
                copy.start()
            return
        if stage == 2:

            def add(i, _):
                if self.order[0] == "y":
                    for j in range(2):
                        b[y, i, j] = b[y, i, j] + self.r1[i, j]
                else:
                    for j in range(2):
                        b[j, i, x] = b[j, i, x] + self.r1[j, i]
                return 0

            lax.fori_loop(0, 4, add, 0)
        if stage == 3:

            def add(i, _):
                b[y, i, x] = b[y, i, x] + self.r2[i]
                return 0

            lax.fori_loop(0, 4, add, 0)
        if stage == 4:
            total = b[y, z, x].astype(F32)
            for d in range(3):
                total = total + self.r3[d].astype(F32)
            self.out[...] = total
            return
        for copy in self.copies(stage):
            copy.start()

    def finish(self):
        for stage in range(4):
            for copy in self.copies(stage):
                copy.wait_send()

    @staticmethod
    def scratch(rows, columns, kind, order):
        if order[0] == "z":
            return [
                pltpu.VMEM(shape + (rows, columns), kind)
                for shape in ((2, 4, 2), (2, 4, 2), (3, 2, 2), (2,), ())
            ]
        lead = (4, 2) if order[0] == "y" else (2, 4)
        return [
            pltpu.VMEM(shape + (rows, columns), kind)
            for shape in ((2, 4, 2), (2, 4, 2), lead, (4,), (3,))
        ]


class Swap:
    def __init__(self, me, source, target, bounce, send, recv, local, slots, parts):
        self.me, self.source, self.target, self.bounce = me, source, target, bounce
        self.send, self.recv, self.local, self.slots, self.parts = send, recv, local, slots, parts

    def copy(self, n, row, half):
        begin, size = self.parts[n]
        part = pl.ds(begin, size)
        return pltpu.make_async_remote_copy(
            src_ref=self.source.at[row, part],
            dst_ref=self.target.at[half, part],
            send_sem=self.send.at[self.slots + n],
            recv_sem=self.recv.at[self.slots + n],
            device_id=device(moved(self.me, "y", 1)),
            device_id_type=MESH,
        )

    def give(self, n):
        y = self.me["y"]
        self.copy(n, 1 - y, y).start()

    def keep_in(self):
        return pltpu.make_async_copy(self.source.at[self.me["y"]], self.bounce, self.local)

    def keep_out(self):
        return pltpu.make_async_copy(self.bounce, self.target.at[self.me["y"]], self.local)

    def keep_begin(self):
        self.keep_in().start()

    def keep_turn(self):
        self.keep_in().wait()
        self.keep_out().start()

    def finish(self):
        y = self.me["y"]
        for n in range(len(self.parts)):
            self.copy(n, 1 - y, 1 - y).wait_recv()
            self.copy(n, 1 - y, y).wait_send()
        self.keep_out().wait()


def halves(ref):
    half = ref.shape[-1] // 2
    return [ref.at[(slice(None),) * (len(ref.shape) - 1) + (pl.ds(n * half, half),)] for n in range(2)]


def stages(me, shards, fulls, orders, held, columns, send, recv, local, base=0):
    out = []
    for i, order in enumerate(orders):
        out.append(
            Gather(me, shards[i], fulls[i], send, recv, local.at[i], base, order, held[i], columns[i])
        )
        base += Gather.sems(order)
    return out


def project(x, w_ref, cosine, sine, put):
    width = x.shape[1]
    for part in range(3):
        for pair in range(width // PAIR):
            at = part * width + pair * PAIR
            if pair % 2 == 0:
                u2 = dot(x, w_ref[:, at : at + 2 * PAIR])
            u = u2[:, (pair % 2) * PAIR : (pair % 2 + 1) * PAIR]
            if part < 2:
                u = u * cosine + turn(u) * sine
            if part == 0:
                u = u * (0.125 * LOG2E)
            put(part, slice(pair * PAIR, (pair + 1) * PAIR), u.astype(BF))


def qkv_kernel(x_ref, w_ref, cos_ref, sin_ref, q_ref, k_ref, v_ref, xt_ref):
    x = x_ref[...]

    def put(part, columns, value):
        (q_ref, k_ref, v_ref)[part][:, columns] = value

    project(x, w_ref, cos_ref[...], sin_ref[...], put)
    xt_ref[...] = x.T


def qkv_call(x, w, cosine, sine, tile=512):
    tokens, width = x.shape
    span = cosine.shape[0]
    tile = min(tile, span)
    row = pl.BlockSpec((tile, width), lambda i: (i, 0))
    table = pl.BlockSpec((tile, PAIR), lambda i: (i % (span // tile), 0))
    return pl.pallas_call(
        qkv_kernel,
        grid=(tokens // tile,),
        in_specs=[
            row,
            pl.BlockSpec(w.shape, lambda i: (0, 0), pipeline_mode=pl.Buffered(1)),
            table,
            table,
        ],
        out_specs=[row, row, row, pl.BlockSpec((width, tile), lambda i: (0, i))],
        out_shape=[jax.ShapeDtypeStruct((tokens, width), BF)] * 3
        + [jax.ShapeDtypeStruct((width, tokens), BF)],
        compiler_params=params(),
        name="qkv",
    )(x, w, cosine, sine)


OPENING_ORDERS = ("yzxc", "zyxc", "zy", "zx", "z", "y", "x")


def opening_kernel(
    tok_hbm, w_shard, out_shard, gate_shard, up_shard, down_shard, cos_ref, sin_ref,
    x_hbm, w_hbm, q_hbm, k_hbm, v_hbm, xt_hbm, out_part, gate_part, up_part, left_part, right_part,
    x, w_blocks, w, q, k, v, xt, send, recv, local, load, store,
):
    me = place()
    y = me["y"]
    greet(me)
    rows = x.shape[1]
    begin = rows // 8
    parts = ((0, begin), (begin, rows - begin))

    def token_copy(n, row, half):
        part = pl.ds(*parts[n])
        return pltpu.make_async_remote_copy(
            src_ref=tok_hbm.at[row, part],
            dst_ref=x.at[half, part],
            send_sem=send.at[n],
            recv_sem=recv.at[n],
            device_id=device(moved(me, "y", 1)),
            device_id_type=MESH,
        )

    width = w.shape[1] // 2
    g = stages(
        me,
        halves(w_shard) + [out_shard, gate_shard, up_shard] + halves(down_shard),
        [w_blocks, w_blocks, out_part, gate_part, up_part, left_part, right_part],
        OPENING_ORDERS,
        ("",) * 7,
        ((0, width), (width, width)) + (None,) * 5,
        send, recv, local, 2,
    )
    mine = pltpu.make_async_copy(tok_hbm.at[y], x.at[y], load.at[0])
    g[0].start()
    g[1].start()
    token_copy(0, 1 - y, y).start()
    mine.start()
    g[0].step(1)
    g[1].step(1)
    token_copy(1, 1 - y, y).start()
    g[0].step(2)
    for n in (2, 3, 4):
        g[n].start()
    g[1].step(2)
    g[6].start()
    g[5].start()
    g[0].step(3)
    g[1].step(3)
    g[0].step(4)
    g[1].step(4)
    g[2].step(1)
    g[3].step(1)
    for n in range(3):
        part = slice(n * w.shape[0], (n + 1) * w.shape[0])
        block = w_blocks[:, :, :, :, :, part].astype(F32)
        w[:, part] = block.reshape(w.shape[0], w.shape[0]).astype(BF)
    keep_w = pltpu.make_async_copy(w, w_hbm, load.at[1])
    keep_w.start()
    mine.wait()
    tile = 512

    def stores(n):
        half = lax.rem(y + n // 2, 2)
        at = pl.ds(pl.multiple_of(half * rows + lax.rem(n, 2) * tile, tile), tile)
        pairs = [(a.at[at], b.at[at]) for a, b in ((q, q_hbm), (k, k_hbm), (v, v_hbm))]
        pairs.append((xt.at[:, at], xt_hbm.at[:, at]))
        return [pltpu.make_async_copy(a, b, store.at[n, i]) for i, (a, b) in enumerate(pairs)]

    def tile_step(n, _):
        half = lax.rem(y + n // 2, 2)
        start = pl.multiple_of(half * rows + lax.rem(n, 2) * tile, tile)
        at = pl.ds(start, tile)

        @pl.when(n == 2)
        def _():
            for m in range(2):
                token_copy(m, 1 - y, 1 - y).wait_recv()

        value = x[half, pl.ds(pl.multiple_of(lax.rem(n, 2) * tile, tile), tile), :]

        def put(part, columns, u):
            (q, k, v)[part][at, columns] = u

        project(value, w, cos_ref[at, :], sin_ref[at, :], put)
        xt[:, at] = value.T
        for copy in stores(n):
            copy.start()
        return 0

    lax.fori_loop(0, 4, tile_step, 0)
    keep_x = pltpu.make_async_copy(x, x_hbm, load.at[2])
    keep_x.start()
    g[2].step(2)
    g[3].step(2)
    for n in (4, 5, 6):
        g[n].step(1)
    for gather in g:
        gather.finish()
    for m in range(2):
        token_copy(m, 1 - y, y).wait_send()
    for n in range(4):
        for copy in stores(n):
            copy.wait()
    keep_w.wait()
    keep_x.wait()


def opening_call(tokens, w_qkv, w_out, w_gate, w_up, w_down, cosine, sine):
    rows, span, width = tokens.shape
    total = rows * span
    hbm = pl.BlockSpec(memory_space=pl.ANY)
    held = pl.BlockSpec(memory_space=pltpu.VMEM)
    whole = (width, w_qkv.shape[1])
    flat = (total, width)
    shapes = [tokens.shape, whole, flat, flat, flat, (width, total)]
    shapes += [(4, 2) + w_out.shape, (4, 2) + w_gate.shape, (4,) + w_up.shape]
    shapes += [(2, w_down.shape[0], w_down.shape[1] // 2)] * 2
    sems = 2 + sum(map(Gather.sems, OPENING_ORDERS))
    return pl.pallas_call(
        opening_kernel,
        in_specs=[hbm] + [held] * 7,
        out_specs=[hbm] * len(shapes),
        out_shape=[jax.ShapeDtypeStruct(shape, BF) for shape in shapes],
        scratch_shapes=[
            pltpu.VMEM(tokens.shape, BF),
            pltpu.VMEM((4, 2, 2, 2) + w_qkv.shape, BF),
            pltpu.VMEM(whole, BF),
            pltpu.VMEM(flat, BF),
            pltpu.VMEM(flat, BF),
            pltpu.VMEM(flat, BF),
            pltpu.VMEM((width, total), BF),
            pltpu.SemaphoreType.DMA((sems,)),
            pltpu.SemaphoreType.DMA((sems,)),
            pltpu.SemaphoreType.DMA((len(OPENING_ORDERS),)),
            pltpu.SemaphoreType.DMA((3,)),
            pltpu.SemaphoreType.DMA((4, 4)),
        ],
        compiler_params=pltpu.CompilerParams(
            vmem_limit_bytes=VMEM_LIMIT, collective_id=0, has_side_effects=True
        ),
        name="opening",
    )(tokens, w_qkv, w_out, w_gate, w_up, w_down, cosine, sine)


def key_mask(len_ref, own, keys, other):
    length = len_ref[lax.axis_index("blk") if own else pl.program_id(0)]
    sub = lanes((keys, PAIR)) % HEAD
    past = lax.broadcasted_iota(jnp.int32, (keys, PAIR), 0) >= length
    return jnp.where(sub < 3, other, jnp.where((sub == 3) & past, NEG, 0.0))


def attend_kernel(tile, chunk, moves, len_ref, q_ref, k_ref, v_ref, *rest):
    inputs, rest = rest[:moves], rest[moves:]
    o_ref, aug_ref, rest = rest[0], rest[1], rest[2:]
    results = max(moves - 1, 0)
    outputs, rest = rest[:results], rest[results:]
    ka, va, s_scr, m_scr = rest[:4]
    keys, span = k_ref.shape[1], q_ref.shape[1]
    tiles = span // tile
    events = {}
    if moves:
        events = attend_events(inputs, outputs, *rest[4:])

    @pl.when(pl.program_id(1) == 0)
    def _():
        ka[:, PAIR:] = key_mask(len_ref, moves, keys, 0.0).astype(BF)
        va[:, PAIR:] = jnp.ones((keys, PAIR), BF)

    ka[:, :PAIR] = k_ref[0]
    va[:, :PAIR] = v_ref[0]
    lane = lanes((tile, PAIR))
    side = lanes((tile, 2 * PAIR)) // HEAD % 2
    ones = (lane % HEAD == 3).astype(F32).astype(BF)
    chunks = keys // chunk

    def query(i, h):
        at = pl.ds(pl.multiple_of(i * tile, tile), tile)
        both = jnp.concatenate([q_ref[0, at, :], ones], axis=1)
        return jnp.where(side == h, both, jnp.zeros_like(both))

    def score(qa, h, c, top):
        s = dot_nt(qa, ka[c * chunk : (c + 1) * chunk, :])
        s_scr[h, :, c * chunk : (c + 1) * chunk] = s
        for b in range(chunk // PAIR):
            part = s[:, b * PAIR : (b + 1) * PAIR]
            top = part if top is None else jnp.maximum(top, part)
        return top

    def close(h, top):
        m_scr[h] = jnp.broadcast_to(jnp.max(top, axis=1, keepdims=True), (tile, PAIR))

    def unit(h, later, other):
        m = m_scr[h]
        wide = jnp.concatenate([m] * (chunk // PAIR), axis=1)
        qa = query(later, other)
        acc, top = None, None
        for c in range(chunks):
            top = score(qa, other, c, top)
            p = jnp.exp2(s_scr[h, :, c * chunk : (c + 1) * chunk] - wide).astype(BF)
            part = dot(p, va[c * chunk : (c + 1) * chunk, :])
            acc = part if acc is None else acc + part
        return acc, top, m

    top = None
    qa = query(0, 0)
    for c in range(chunks):
        top = score(qa, 0, c, top)
    close(0, top)

    def step(i, _):
        acc0, top, m0 = unit(0, i, 1)
        close(1, top)
        acc1, top, m1 = unit(1, jnp.minimum(i + 1, tiles - 1), 0)
        close(0, top)
        mine = lane < HEAD
        total = jnp.where(mine, acc0[:, PAIR:], acc1[:, PAIR:])
        at = pl.ds(pl.multiple_of(i * tile, tile), tile)
        o_ref[0, at, :] = (jnp.where(mine, acc0[:, :PAIR], acc1[:, :PAIR]) / total).astype(BF)
        lse = jnp.where(mine, m0, m1) + jnp.log2(total)
        aug_ref[0, at, :] = spread(lse, jnp.where(lane % HEAD == 3, 1.0, 0.0))
        return 0

    unroll = 2 if tiles % 2 == 0 else 1

    def group(n, _):
        now = pl.program_id(1) * (tiles // unroll) + n
        for at_step, acts in events.items():

            @pl.when(now == at_step)
            def _():
                for act in acts:
                    act()

        for j in range(unroll):
            step(n * unroll + j, 0)
        return 0

    lax.fori_loop(0, tiles // unroll, group, 0)
    if moves:

        @pl.when(pl.program_id(1) == pl.num_programs(1) - 1)
        def _():
            for act in events.last:
                act()


class Events(dict):
    def __init__(self):
        self.last = []

    def put(self, at, *acts):
        self.setdefault(at, []).extend(acts)


ATTEND_HELD = ("zy", "zx", "z", "y", "x")
ATTEND_ORDERS = ("xc", "yc", "yxc", "zxc", "zyc")
ATTEND_PLAN = ((2, 0, 1), (4, 2, 1), (4, 3, 1), (7, 4, 1), (10, 1, 1), (10, 2, 2), (11, 3, 2), (11, 4, 2))
ATTEND_FIRST = (2, 1, 0, 3, 4)


def attend_events(inputs, outputs, send, recv, local):
    me = place()
    half = inputs[3].shape[-1]
    columns = (None, None, None, (0, half), (half, half))
    fulls = tuple(outputs) + (outputs[3],)
    gathers = stages(me, inputs, fulls, ATTEND_ORDERS, ATTEND_HELD, columns, send, recv, local)
    events = Events()
    events.put(0, functools.partial(greet, me), *(gathers[i].start for i in ATTEND_FIRST))
    done = [1] * len(gathers)
    for at, i, stage in ATTEND_PLAN:
        events.put(at, functools.partial(gathers[i].step, stage))
        done[i] = stage + 1
    for stage in range(1, 4):
        for i, g in enumerate(gathers):
            if done[i] <= stage <= len(ATTEND_ORDERS[i]):
                events.last.append(functools.partial(g.step, stage))
    events.last += [g.finish for g in gathers]
    return events


def spread(value, other):
    high = value.astype(BF).astype(F32)
    rest = value - high
    mid = rest.astype(BF).astype(F32)
    low = rest - mid
    sub = lanes(value.shape) % HEAD
    return jnp.where(
        sub == 0, high, jnp.where(sub == 1, mid, jnp.where(sub == 2, low, other))
    ).astype(BF)


def attend_call(q, k, v, lengths, moving=(), tile=512, chunk=512):
    rows, span, width = q.shape
    keys = k.shape[1]
    tile = min(tile, span)
    moves = len(moving)
    qs = pl.BlockSpec((1, span, PAIR), lambda r, p: (r, 0, p))
    ks = pl.BlockSpec((1, keys, PAIR), lambda r, p: (r, 0, p))
    hbm = pl.BlockSpec(memory_space=pl.ANY)
    moved_shapes = [jax.ShapeDtypeStruct((4, 2, 2, 2) + a.shape[-2:], a.dtype) for a in moving[:3]]
    for a in moving[3:4]:
        moved_shapes.append(jax.ShapeDtypeStruct((4, 2, 2, 2, a.shape[-2], 2 * a.shape[-1]), a.dtype))
    sems = sum(map(Gather.sems, ATTEND_ORDERS))
    extra = [pltpu.SemaphoreType.DMA((sems,))] * 2 + [pltpu.SemaphoreType.DMA((len(ATTEND_ORDERS),))]
    held = [
        pl.BlockSpec(a.shape, lambda r, p, n=a.ndim: (0,) * n, pipeline_mode=pl.Buffered(1))
        for a in moving
    ]
    more = dict(collective_id=1, has_side_effects=True) if moves else {}
    return pl.pallas_call(
        functools.partial(attend_kernel, tile, chunk, moves),
        grid=(rows, width // PAIR),
        in_specs=[pl.BlockSpec(memory_space=pltpu.SMEM), qs, ks, ks] + held,
        out_specs=[qs, qs] + [hbm] * len(moved_shapes),
        out_shape=[jax.ShapeDtypeStruct(q.shape, BF)] * 2 + moved_shapes,
        scratch_shapes=[
            pltpu.VMEM((keys, 2 * PAIR), BF),
            pltpu.VMEM((keys, 2 * PAIR), BF),
            pltpu.VMEM((2, tile, keys), F32),
            pltpu.VMEM((2, tile, PAIR), F32),
        ]
        + (extra if moves else []),
        compiler_params=pltpu.CompilerParams(vmem_limit_bytes=VMEM_LIMIT, **more),
        name="attend",
    )(lengths, q, k, v, *moving)


def attend_back_kernel(
    tq, unroll, moves, len_ref, q_ref, k_ref, v_ref, o_ref, do_ref, aug_ref, cos_ref, sin_ref, *rest
):
    inputs, rest = rest[:moves], rest[moves:]
    dq_ref, dk_ref, dv_ref, rest = rest[0], rest[1], rest[2], rest[3:]
    outputs, rest = rest[:moves], rest[moves:]
    qa, da, ka, va, kt, dk_acc, dv_acc = rest[:7]
    keys, span = k_ref.shape[1], q_ref.shape[1]
    tiles = span // tq
    events = {}
    if moves:
        events = back_events(inputs, outputs, *rest[7:])

    @pl.when(pl.program_id(1) == 0)
    def _():
        ka[:, PAIR:] = key_mask(len_ref, moves, keys, -1.0).astype(BF)
        va[:, PAIR:] = jnp.where(lanes((keys, PAIR)) % HEAD < 3, -1.0, 0.0).astype(BF)

    k, do = k_ref[0], do_ref[0]
    ka[:, :PAIR] = k
    va[:, :PAIR] = v_ref[0]
    kt[...] = k.T
    prod = do.astype(F32) * o_ref[0].astype(F32)
    first = prod.astype(BF)
    second = (prod - first.astype(F32)).astype(BF)
    block = (
        (lax.broadcasted_iota(jnp.int32, (PAIR, PAIR), 0) // HEAD)
        == (lax.broadcasted_iota(jnp.int32, (PAIR, PAIR), 1) // HEAD)
    ).astype(F32).astype(BF)
    delta = dot(first, block) + dot(second, block)
    q_both = jnp.concatenate([q_ref[0], aug_ref[0]], axis=1)
    d_both = jnp.concatenate([do, spread(delta, jnp.zeros_like(delta))], axis=1)
    side = lanes(q_both.shape) // HEAD % 2
    for h in range(2):
        qa[h] = jnp.where(side == h, q_both, jnp.zeros_like(q_both))
        da[h] = jnp.where(side == h, d_both, jnp.zeros_like(d_both))
    dk_acc[...] = jnp.zeros_like(dk_acc)
    dv_acc[...] = jnp.zeros_like(dv_acc)

    def query_step(i, _):
        at_q = pl.ds(pl.multiple_of(i * tq, tq), tq)
        dv, dk, dq = None, None, []
        for h in range(2):
            st = dot_nt(ka[...], qa[h, at_q, :])
            dpt = dot_nt(va[...], da[h, at_q, :])
            p = jnp.exp2(st)
            ds = (p * dpt).astype(BF)
            pv = dot(p.astype(BF), da[h, at_q, :PAIR])
            pk = dot(ds, qa[h, at_q, :PAIR])
            dv = pv if dv is None else dv + pv
            dk = pk if dk is None else dk + pk
            dq.append(dot(kt[h * HEAD : (h + 1) * HEAD, :], ds))
        dv_acc[...] += dv
        dk_acc[...] += dk
        g = jnp.concatenate(dq, axis=0).T * 0.125
        dq_ref[0, at_q, :] = back_turn(g, cos_ref[at_q, :], sin_ref[at_q, :]).astype(BF)
        return 0

    def group(n, _):
        now = pl.program_id(1) * (tiles // unroll) + n
        for at_step, acts in events.items():

            @pl.when(now == at_step)
            def _():
                for act in acts:
                    act()

        for j in range(unroll):
            query_step(n * unroll + j, 0)
        return 0

    lax.fori_loop(0, tiles // unroll, group, 0)
    dv_ref[0] = dv_acc[...].astype(dv_ref.dtype)
    g = dk_acc[...] * LN2
    if dk_ref.dtype == BF:
        g = back_turn(g, cos_ref[...], sin_ref[...])
    dk_ref[0] = g.astype(dk_ref.dtype)
    if moves:

        @pl.when(pl.program_id(1) == pl.num_programs(1) - 1)
        def _():
            for act in events.last:
                act()


def back_turn(g, cosine, sine):
    return g * cosine - turn(g * sine)


def wide_piece(source, columns):
    return lambda c, y: source.at[:, :, c, :, pl.ds(y * columns, columns)]


def tall_piece(source):
    return lambda c, y: source.at[:, :, c, y]


BACK_ORDERS = ("yx", "xy", "zyx", "xy")
BACK_PLAN = (
    (1, 0, 1), (1, 1, 1), (1, 2, 1), (1, 3, 1), (3, 0, 2), (3, 1, 2), (4, 0, 3), (4, 1, 3), (4, 2, 2), (4, 3, 2),
    (5, 0, 4), (5, 2, 3), (5, 3, 3),
)
BACK_LAST = (2, 1, 3)


def back_events(inputs, outputs, send, recv, local, *bufs):
    me = place()
    reduces = []
    for i, (source, out) in enumerate(zip(inputs, outputs)):
        piece = wide_piece(source, source.shape[-1] // 2) if len(source.shape) == 5 else tall_piece(source)
        reduces.append(
            Reduce(
                me, piece, bufs[5 * i : 5 * i + 5], out, send, recv,
                local.at[pl.ds(2 * i, 2)], i * Reduce.SEMS, BACK_ORDERS[i],
            )
        )
    events = Events()
    events.put(0, functools.partial(greet, me), *(reduces[i].start for i in (2, 0, 1, 3)))
    for at, i, stage in BACK_PLAN:
        events.put(at, functools.partial(reduces[i].step, stage))
    events.last += [functools.partial(reduces[i].step, 4) for i in BACK_LAST]
    events.last += [r.finish for r in reduces]
    return events


def attend_back_call(q, k, v, lengths, o, do, aug, cosine, sine, whole, moving=(), tq=512, unroll=4):
    rows, span, width = q.shape
    keys = k.shape[1]
    tq = min(tq, span)
    unroll = min(unroll, span // tq)
    moves = len(moving)
    qs = pl.BlockSpec((1, span, PAIR), lambda r, p: (r, 0, p))
    ks = pl.BlockSpec((1, keys, PAIR), lambda r, p: (r, 0, p))
    table = pl.BlockSpec((span, PAIR), lambda r, p: (0, 0), pipeline_mode=pl.Buffered(1))
    hbm = pl.BlockSpec(memory_space=pl.ANY)
    kv_type = BF if whole else F32
    results, result_specs, extra, more = [], [], [], {}
    if moves:
        extra = [pltpu.SemaphoreType.DMA((Reduce.SEMS * moves,))] * 2
        extra += [pltpu.SemaphoreType.DMA((2 * moves,))]
        for a, order in zip(moving, BACK_ORDERS):
            block = (a.shape[-2], a.shape[-1] // (2 if a.ndim == 5 else 1))
            results.append(jax.ShapeDtypeStruct(block, F32))
            result_specs.append(pl.BlockSpec(block, lambda r, p: (0, 0), pipeline_mode=pl.Buffered(1)))
            extra += Reduce.scratch(*block, a.dtype, order)
        more = dict(collective_id=2, has_side_effects=True)
    return pl.pallas_call(
        functools.partial(attend_back_kernel, tq, unroll, moves),
        grid=(rows, width // PAIR),
        in_specs=[pl.BlockSpec(memory_space=pltpu.SMEM), qs, ks, ks, qs, qs, qs, table, table]
        + [hbm] * moves,
        out_specs=[qs, ks, ks] + result_specs,
        out_shape=[
            jax.ShapeDtypeStruct(q.shape, BF),
            jax.ShapeDtypeStruct(k.shape, kv_type),
            jax.ShapeDtypeStruct(k.shape, kv_type),
        ]
        + results,
        scratch_shapes=[
            pltpu.VMEM((2, span, 2 * PAIR), BF),
            pltpu.VMEM((2, span, 2 * PAIR), BF),
            pltpu.VMEM((keys, 2 * PAIR), BF),
            pltpu.VMEM((keys, 2 * PAIR), BF),
            pltpu.VMEM((PAIR, keys), BF),
            pltpu.VMEM((keys, PAIR), F32),
            pltpu.VMEM((keys, PAIR), F32),
        ]
        + extra,
        compiler_params=pltpu.CompilerParams(vmem_limit_bytes=VMEM_LIMIT, **more),
        name="attend_back",
    )(lengths, q, k, v, o, do, aug, cosine, sine, *moving)


def middle_kernel(
    chunk, moves, x_ref, att_ref, cot_ref, wo_ref, wg_ref, wu_ref, wd_ref, *rest
):
    source, rest = rest[:moves], rest[moves:]
    (out_ref, dfirst_ref, datt_ref, act_ref, dg_ref, du_ref, ht_ref, dft_ref, at_ref, gg_ref) = rest[:10]
    ca, cb, gains = rest[10:13]
    if moves:
        arrived, dy_ref, send, recv = rest[13:]
        me = place()
        now, per = pl.program_id(0), pl.num_programs(0) // 2
        tile = dy_ref.shape[0]
        give = pltpu.make_async_remote_copy(
            src_ref=source[0].at[1 - me["y"]],
            dst_ref=arrived,
            send_sem=send.at[0],
            recv_sem=recv.at[0],
            device_id=device(moved(me, "y", 1)),
            device_id_type=MESH,
        )

        @pl.when(now == 0)
        def _():
            greet(me)
            give.start()

        pl.when(now == per)(give.wait)

        @pl.when(now < per)
        def _():
            dy_ref[...] = cot_ref[...]

        @pl.when(now >= per)
        def _():
            dy_ref[...] = arrived[pl.ds(pl.multiple_of((now - per) * tile, tile), tile), :]

    else:
        dy_ref = cot_ref

    @pl.when(pl.program_id(0) == 0)
    def _():
        gg_ref[...] = jnp.zeros_like(gg_ref)
        gains[...] = wo_ref[:, x_ref.shape[1] :].astype(F32).T[:8]

    gain1, gain2 = gains[0:1, :], gains[1:2, :]
    att = att_ref[...]
    at_ref[...] = att.T
    first = x_ref[...].astype(F32) + dot(att, wo_ref[:, : att.shape[1]])
    centered = first - jnp.mean(first, axis=1, keepdims=True)
    s1 = lax.rsqrt(jnp.mean(centered * centered, axis=1, keepdims=True) + EPS)
    n1 = centered * s1
    hidden = n1 * gain1
    low = hidden.astype(BF)
    ht_ref[...] = low.T
    hidden_width = wg_ref.shape[1]
    second = hidden
    for c in range(hidden_width // chunk):
        at = slice(c * chunk, (c + 1) * chunk)
        g = dot(low, wg_ref[:, at])
        u = dot(low, wu_ref[:, at])
        sig = jax.nn.sigmoid(g)
        silu = g * sig
        act = (silu * u).astype(BF)
        act_ref[:, at] = act
        ca[:, at] = (u * (sig + silu * (1.0 - sig))).astype(ca.dtype)
        cb[:, at] = silu.astype(cb.dtype)
        second = second + dot(act, wd_ref[at, :])
    centered = second - jnp.mean(second, axis=1, keepdims=True)
    s2 = lax.rsqrt(jnp.mean(centered * centered, axis=1, keepdims=True) + EPS)
    n2 = centered * s2
    out_ref[...] = (n2 * gain2).astype(BF)
    dy = dy_ref[...].astype(F32)
    gg_ref[1:2, :] += jnp.sum(dy * n2, axis=0, keepdims=True)
    inner = dy * gain2
    d_second = s2 * (
        inner - jnp.mean(inner, axis=1, keepdims=True) - n2 * jnp.mean(inner * n2, axis=1, keepdims=True)
    )
    d_ffn = d_second.astype(BF)
    dft_ref[...] = d_ffn.T
    d_hidden = d_second
    for c in range(hidden_width // chunk):
        at = slice(c * chunk, (c + 1) * chunk)
        d_act = dot_nt(d_ffn, wd_ref[at, :])
        dg = (d_act * ca[:, at]).astype(BF)
        du = (d_act * cb[:, at]).astype(BF)
        dg_ref[:, at] = dg
        du_ref[:, at] = du
        d_hidden = d_hidden + dot_nt(dg, wg_ref[:, at]) + dot_nt(du, wu_ref[:, at])
    gg_ref[0:1, :] += jnp.sum(d_hidden * n1, axis=0, keepdims=True)
    inner = d_hidden * gain1
    d_first = s1 * (
        inner - jnp.mean(inner, axis=1, keepdims=True) - n1 * jnp.mean(inner * n1, axis=1, keepdims=True)
    )
    low = d_first.astype(BF)
    dfirst_ref[...] = low
    datt_ref[...] = dot_nt(low, wo_ref[:, : low.shape[1]]).astype(BF)


def middle_call(x, att, cot, wo, wg, wu, wd, tile=256, chunk=768):
    tokens, width = x.shape
    hidden_width = wg.shape[1]
    tile = min(tile, tokens)
    moves = cot.ndim - 2
    per = tokens // tile // 2

    def place_of(i):
        if not moves:
            return i
        return lax.rem(lax.axis_index("blk") + i // per, 2) * per + lax.rem(i, per)

    row = pl.BlockSpec((tile, width), lambda i: (place_of(i), 0))
    wide = pl.BlockSpec((tile, hidden_width), lambda i: (place_of(i), 0))
    column = pl.BlockSpec((width, tile), lambda i: (0, place_of(i)))
    cot_row, extra, more = row, [], {}
    if moves:
        cot_row = pl.BlockSpec(
            (None, tile, width), lambda i: (lax.axis_index("blk"), jnp.minimum(i, per - 1), 0)
        )
        extra = [pltpu.VMEM((tokens // 2, width), BF), pltpu.VMEM((tile, width), BF)]
        extra += [pltpu.SemaphoreType.DMA((1,))] * 2
        more = dict(collective_id=5, has_side_effects=True)

    def whole(a):
        return pl.BlockSpec(a.shape, lambda i: (0, 0), pipeline_mode=pl.Buffered(1))

    return pl.pallas_call(
        functools.partial(middle_kernel, chunk, moves),
        grid=(tokens // tile,),
        in_specs=[row, row, cot_row, whole(wo), whole(wg), whole(wu), whole(wd)]
        + [pl.BlockSpec(memory_space=pl.ANY)] * moves,
        out_specs=[row, row, row, wide, wide, wide, column, column, column]
        + [pl.BlockSpec((PAIR, width), lambda i: (0, 0))],
        out_shape=[jax.ShapeDtypeStruct((tokens, width), BF)] * 3
        + [jax.ShapeDtypeStruct((tokens, hidden_width), BF)] * 3
        + [jax.ShapeDtypeStruct((width, tokens), BF)] * 3
        + [jax.ShapeDtypeStruct((PAIR, width), F32)],
        scratch_shapes=[pltpu.VMEM((tile, hidden_width), F32)] * 2 + [pltpu.VMEM((8, width), F32)] + extra,
        compiler_params=pltpu.CompilerParams(vmem_limit_bytes=VMEM_LIMIT, **more),
        name="middle",
    )(x, att, cot, wo, wg, wu, wd, *([cot] * moves))


def outer_kernel(a_ref, b_ref, o_ref):
    o_ref[...] = dot(a_ref[...], b_ref[...]).astype(o_ref.dtype)


def outer_call(a, b, out_type, tile=512):
    rows, tokens = a.shape
    columns = b.shape[1]
    tile = tile if columns % tile == 0 else 256
    return pl.pallas_call(
        outer_kernel,
        grid=(columns // tile,),
        in_specs=[
            pl.BlockSpec((rows, tokens), lambda i: (0, 0), pipeline_mode=pl.Buffered(1)),
            pl.BlockSpec((tokens, tile), lambda i: (0, i)),
        ],
        out_specs=pl.BlockSpec((rows, tile), lambda i: (0, i)),
        out_shape=jax.ShapeDtypeStruct((rows, columns), out_type),
        compiler_params=params(),
        name="outer",
    )(a, b)


def outers_kernel(steps, moves, a1_ref, a2_hbm, a3_hbm, b1_ref, b2_ref, b3_ref, b4_hbm, gains_ref, *rest):
    source, rest = rest[:moves], rest[moves:]
    o1_ref, o2_ref, o3_ref, o4_ref, rest = rest[0], rest[1], rest[2], rest[3], rest[4:]
    now = pl.program_id(0)
    target, rest = rest[:moves], rest[moves:]
    a2_ref, a3_ref, b4_ref, load, rest = rest[0], rest[1], rest[2], rest[3], rest[4:]
    late = [
        pltpu.make_async_copy(a, b, load.at[i])
        for i, (a, b) in enumerate(((a2_hbm, a2_ref), (a3_hbm, a3_ref), (b4_hbm, b4_ref)))
    ]

    @pl.when(now == 0)
    def _():
        for copy in late:
            copy.start()

    @pl.when(now == 2 * steps)
    def _():
        for copy in late:
            copy.wait()

    if moves:
        target, (bounce, send, recv, local) = target[0], rest
        me = place()
        swap = Swap(me, source[0], target, bounce, send, recv, local.at[0], 0, ((0, target.shape[1]),))

        @pl.when(now == 0)
        def _():
            greet(me)
            swap.give(0)
            swap.keep_begin()

        pl.when(now == 3)(swap.keep_turn)
        pl.when(now == 3 * steps)(swap.finish)

    @pl.when(now < steps)
    def _():
        o1_ref[...] = dot(a1_ref[...], b1_ref[...]).astype(BF)

    @pl.when((now >= steps) & (now < 2 * steps))
    def _():
        o2_ref[...] = dot(a1_ref[...], b2_ref[...]).astype(BF)

    @pl.when((now >= 2 * steps) & (now < 3 * steps))
    def _():
        o3_ref[...] = dot(a2_ref[...], b3_ref[...]).astype(BF)

    @pl.when(now == 3 * steps)
    def _():
        width = b4_ref.shape[1]
        o4_ref[:, :width] = dot(a3_ref[...], b4_ref[...])
        o4_ref[:, width:] = gains_ref[...].T


def outers_call(h_t, df_t, att_t, d_gate, d_up, act, d_first, gains, moving=(), tile=512):
    width, tokens = h_t.shape
    hidden = d_gate.shape[1]
    steps = hidden // tile

    def whole(a):
        return pl.BlockSpec(a.shape, lambda i: (0, 0), pipeline_mode=pl.Buffered(1))

    def part(rows, n):
        return pl.BlockSpec((rows, tile), lambda i: (0, jnp.clip(i - n * steps, 0, steps - 1)))

    moves = len(moving)
    hbm = pl.BlockSpec(memory_space=pl.ANY)
    extra = [pltpu.VMEM(a.shape, BF) for a in (df_t, att_t, d_first)] + [pltpu.SemaphoreType.DMA((3,))]
    extra += [pltpu.VMEM(a.shape[1:], BF) for a in moving]
    extra += [pltpu.SemaphoreType.DMA((1,))] * (3 * moves)
    more = dict(collective_id=4, has_side_effects=True) if moves else {}
    return pl.pallas_call(
        functools.partial(outers_kernel, steps, moves),
        grid=(3 * steps + 1,),
        in_specs=[whole(h_t), hbm, hbm] + [part(tokens, n) for n in range(3)] + [hbm, whole(gains)]
        + [hbm] * moves,
        out_specs=[part(width, n) for n in range(3)]
        + [pl.BlockSpec((width, width + PAIR), lambda i: (0, 0), pipeline_mode=pl.Buffered(1))]
        + [hbm] * moves,
        out_shape=[jax.ShapeDtypeStruct((width, hidden), BF)] * 3
        + [jax.ShapeDtypeStruct((width, width + PAIR), F32)]
        + [jax.ShapeDtypeStruct(a.shape, BF) for a in moving],
        scratch_shapes=extra,
        compiler_params=pltpu.CompilerParams(vmem_limit_bytes=VMEM_LIMIT, **more),
        name="outers",
    )(h_t, df_t, att_t, d_gate, d_up, act, d_first, gains, *moving)


CLOSING_ORDERS = ("xy", "xy", "xy")


def closing_kernel(
    dq_hbm, dk_hbm, dv_hbm, first_hbm, xt_hbm, w_hbm, g_out, sum_ref,
    dq, dk, dv, first, xt, w, g, w0, w1, w2, send, recv, local, mine_sem, *bufs,
):
    me = place()
    y = me["y"]
    half = g.shape[1]

    def load(n, a, b, which=None):
        if which is not None:
            at = pl.ds(pl.multiple_of(which * half, half), half)
            a, b = a.at[at], b.at[at]
        return pltpu.make_async_copy(a, b, local.at[n])

    rows_hbm = ((dq_hbm, dq), (dk_hbm, dk), (dv_hbm, dv), (first_hbm, first))
    early = [load(0, w_hbm, w)] + [load(1 + n, a, b, 1 - y) for n, (a, b) in enumerate(rows_hbm)]
    later = [load(5, xt_hbm, xt)] + [load(6 + n, a, b, y) for n, (a, b) in enumerate(rows_hbm)]
    for copy in early + later:
        copy.start()
    greet(me)
    width = dq.shape[1]
    tile = half // 4

    def rows_of(which, t):
        at = pl.ds(pl.multiple_of(which * half + t * tile, tile), tile)
        total = first[at, :].astype(F32)
        for n, a in enumerate((dq, dk, dv)):
            total += dot_nt(a[at, :], w[:, n * width : (n + 1) * width])
        g[which, pl.ds(pl.multiple_of(t * tile, tile), tile), :] = total.astype(BF)

    for copy in early:
        copy.wait()
    quarter = half // 4

    def give(n, target_half):
        part = pl.ds(n * quarter if isinstance(n, int) else pl.multiple_of(n * quarter, quarter), quarter)
        return pltpu.make_async_remote_copy(
            src_ref=g.at[1 - y, part],
            dst_ref=g_out.at[target_half, part],
            send_sem=send.at[n],
            recv_sem=recv.at[n],
            device_id=device(moved(me, "y", 1)),
            device_id_type=MESH,
        )

    def away(t, _):
        rows_of(1 - y, t)
        pl.when(t < 2)(lambda: give(t, y).start())
        return 0

    def home(t, _):
        rows_of(y, t)
        return 0

    lax.fori_loop(0, 4, away, 0)
    for copy in later:
        copy.wait()
    reduces = []
    for n, (a, target) in enumerate(((dq, w0), (dk, w1), (dv, w2))):
        reduces.append(
            Reduce(
                me, tall_piece(target), bufs[5 * n : 5 * n + 5], sum_ref.at[:, pl.ds(n * width, width)],
                send, recv, mine_sem.at[pl.ds(2 * n, 2)], 4 + n * Reduce.SEMS, CLOSING_ORDERS[n],
            )
        )

    def products(n, a, target):
        step = 2 * PAIR

        def part(i, _):
            at = pl.ds(pl.multiple_of(i * step, step), step)
            value = dot(xt[...], a[:, at])
            target[:, :, :, :, :, at] = value.reshape(target.shape[:-1] + (step,)).astype(BF)
            return 0

        lax.fori_loop(0, width // step, part, 0)

    products(0, dq, w0)
    reduces[0].start()
    give(2, y).start()
    products(1, dk, w1)
    reduces[1].start()
    reduces[0].step(1)
    products(2, dv, w2)
    reduces[2].start()
    reduces[1].step(1)
    reduces[0].step(2)
    reduces[2].step(1)
    lax.fori_loop(0, 2, home, 0)
    reduces[1].step(2)
    reduces[0].step(3)
    lax.fori_loop(2, 4, home, 0)
    keep = pltpu.make_async_copy(g.at[y], g_out.at[y], local.at[0])
    keep.start()
    reduces[2].step(2)
    give(3, y).start()
    reduces[1].step(3)
    reduces[0].step(4)
    reduces[2].step(3)
    reduces[1].step(4)
    reduces[2].step(4)
    for r in reduces:
        r.finish()
    for n in range(4):
        give(n, 1 - y).wait_recv()
        give(n, y).wait_send()
    keep.wait()


def closing_call(dq, dk, dv, first, xt, w):
    tokens, width = dq.shape
    hbm = pl.BlockSpec(memory_space=pl.ANY)
    block = (width // 32, width)
    full = pltpu.VMEM((4, 2, 2, 2) + block, BF)
    scratch = [pltpu.VMEM(a.shape, BF) for a in (dq, dk, dv, first, xt, w)]
    scratch += [pltpu.VMEM((2, tokens // 2, width), BF), full, full, full]
    sems = 4 + 3 * Reduce.SEMS
    scratch += [pltpu.SemaphoreType.DMA((sems,))] * 2
    scratch += [pltpu.SemaphoreType.DMA((10,)), pltpu.SemaphoreType.DMA((6,))]
    for order in CLOSING_ORDERS:
        scratch += Reduce.scratch(*block, BF, order)
    return pl.pallas_call(
        closing_kernel,
        in_specs=[hbm] * 6,
        out_specs=[hbm, pl.BlockSpec(memory_space=pltpu.VMEM)],
        out_shape=[
            jax.ShapeDtypeStruct((2, tokens // 2, width), BF),
            jax.ShapeDtypeStruct((block[0], 3 * width), F32),
        ],
        scratch_shapes=scratch,
        compiler_params=pltpu.CompilerParams(
            vmem_limit_bytes=VMEM_LIMIT, collective_id=3, has_side_effects=True
        ),
        name="closing",
    )(dq, dk, dv, first, xt, w)


def tokens_kernel(dq_ref, dk_ref, dv_ref, dfirst_ref, w_ref, o_ref):
    width = dq_ref.shape[1]
    total = dfirst_ref[...].astype(F32)
    total += dot_nt(dq_ref[...], w_ref[:, :width])
    total += dot_nt(dk_ref[...], w_ref[:, width : 2 * width])
    total += dot_nt(dv_ref[...], w_ref[:, 2 * width :])
    o_ref[...] = total.astype(BF)


def tokens_call(dq, dk, dv, dfirst, w, tile=512):
    tokens, width = dq.shape
    tile = min(tile, tokens)
    row = pl.BlockSpec((tile, width), lambda i: (i, 0))
    return pl.pallas_call(
        tokens_kernel,
        grid=(tokens // tile,),
        in_specs=[row] * 4 + [pl.BlockSpec(w.shape, lambda i: (0, 0), pipeline_mode=pl.Buffered(1))],
        out_specs=row,
        out_shape=jax.ShapeDtypeStruct((tokens, width), BF),
        compiler_params=params(),
        name="grad_tokens",
    )(dq, dk, dv, dfirst, w)


def angle_tables(span):
    index = np.arange(HEAD // 2, dtype=np.float64)
    inverse = np.power(1000.0, -2.0 * index / HEAD)
    angles = np.arange(span, dtype=np.float64)[:, None] * inverse[None, :]
    repeat = (1, PAIR // (HEAD // 2))
    return (
        np.tile(np.cos(angles), repeat).astype(np.float32),
        np.tile(np.sin(angles), repeat).astype(np.float32),
    )


def body(tokens, lengths, w_qkv, w_out, w_gate, w_up, w_down, gain_one, gain_two, cotangent):
    axes = ("dp", "blk")
    blk = lax.axis_size("blk")
    mine = lax.axis_index("blk")
    rows, span, width = tokens.shape
    seq = span * blk
    own = blk == 2 and rows == 2 and lax.axis_size("dp") == 16

    def gather(a):
        return lax.all_gather(a, axes, axis=0, tiled=True)

    cosine, sine = map(jnp.asarray, angle_tables(seq))
    gains = jnp.stack([gain_one, gain_two], 1)
    w_out = jnp.pad(jnp.concatenate([w_out, gains], 1), ((0, 0), (0, PAIR - 2)))
    if own:
        x, f_qkv, q, k, v, xt, *moving = opening_call(
            tokens, w_qkv, w_out, w_gate, w_up, w_down, cosine, sine
        )
        x = x.reshape(1, seq, width)
        cq, sq = cosine, sine
    else:
        f_qkv, f_out, f_gate, f_up, f_down = map(gather, (w_qkv, w_out, w_gate, w_up, w_down))
        x, cot = tokens, cotangent.reshape(rows * span, width)
        cq = lax.dynamic_slice_in_dim(cosine, mine * span, span, 0)
        sq = lax.dynamic_slice_in_dim(sine, mine * span, span, 0)
    n, t = x.shape[:2]
    flat = x.reshape(n * t, width)
    if not own:
        q, k, v, xt = qkv_call(flat, f_qkv, cq, sq)
    q, k, v = (a.reshape(n, t, width) for a in (q, k, v))
    if not own:
        k = lax.all_gather(k, "blk", axis=1, tiled=True)
        v = lax.all_gather(v, "blk", axis=1, tiled=True)
    if own:
        att, aug, f_out, f_gate, f_up, f_down = attend_call(
            q, k, v, lengths, moving
        )
        f_out = f_out.reshape(width, -1)
        cot = cotangent
        f_gate, f_up = f_gate.reshape(width, -1), f_up.reshape(width, -1)
        f_down = f_down.reshape(-1, width)
    else:
        att, aug = attend_call(q, k, v, lengths)
    out, d_first, d_att, act, d_gate, d_up, h_t, df_t, att_t, gains = middle_call(
        flat, att.reshape(n * t, width), cot, f_out, f_gate, f_up, f_down
    )
    moving = (out.reshape(2, span, width),) if own else ()
    gw_gate, gw_up, gw_down_t, gw_out, *moving = outers_call(
        h_t, df_t, att_t, d_gate, d_up, act, d_first, gains, moving
    )
    d_att = d_att.reshape(n, t, width)
    if own:
        wide = tuple(g.reshape(4, 2, 2, width // 16, -1) for g in (gw_gate, gw_up, gw_down_t))
        out = moving[0]
        dq, dk, dv, s_gate, s_up, s_down_t, s_out = attend_back_call(
            q, k, v, lengths, att, d_att, aug, cq, sq, True,
            wide + (gw_out.reshape(4, 2, 2, 2, width // 32, -1),),
        )
    else:

        def scatter_wide(g):
            g = lax.psum_scatter(g, "blk", scatter_dimension=1, tiled=True)
            return lax.psum_scatter(g, "dp", scatter_dimension=0, tiled=True).astype(F32)

        s_gate, s_up, s_down_t = map(scatter_wide, (gw_gate, gw_up, gw_down_t))
        s_out = lax.psum_scatter(gw_out, axes, scatter_dimension=0, tiled=True)
        dq, dk, dv = attend_back_call(q, k, v, lengths, att, d_att, aug, cq, sq, False)
        dk = lax.psum_scatter(dk, "blk", scatter_dimension=1, tiled=True)
        dv = lax.psum_scatter(dv, "blk", scatter_dimension=1, tiled=True)
        heads = (dk * jnp.tile(sq, (1, width // PAIR))).reshape(n, t, HEADS, HEAD)
        half = jnp.concatenate([heads[..., HEAD // 2 :], -heads[..., : HEAD // 2]], -1)
        dk = dk * jnp.tile(cq, (1, width // PAIR)) + half.reshape(n, t, width)
        dk, dv = dk.astype(BF), dv.astype(BF)
    s_down = s_down_t.T
    s_out, s_gg = s_out[:, :width], s_out[:, width : width + 2]
    dq, dk, dv = (a.reshape(n * t, width) for a in (dq, dk, dv))
    if own:
        g_tokens, s_qkv = closing_call(dq, dk, dv, d_first, xt, f_qkv)
    else:
        gw_qkv = jnp.concatenate([outer_call(xt, a, BF, 256) for a in (dq, dk, dv)], 1)
        s_qkv = lax.psum_scatter(gw_qkv, axes, scatter_dimension=0, tiled=True).astype(F32)
        g_tokens = tokens_call(dq, dk, dv, d_first, f_qkv).reshape(tokens.shape)
        out = out.reshape(tokens.shape)
    return (out, g_tokens, s_qkv, s_out, s_gate, s_up, s_down, s_gg[:, 0], s_gg[:, 1])


def solution(mesh):
    both = ("dp", "blk")
    return jax.shard_map(
        body,
        mesh=mesh,
        in_specs=(
            P("dp", "blk", None),
            P("dp"),
            P(both, None),
            P(both, None),
            P(both, None),
            P(both, None),
            P(both, None),
            P(both),
            P(both),
            P("dp", "blk", None),
        ),
        out_specs=(
            P("dp", "blk", None),
            P("dp", "blk", None),
            P(both, None),
            P(both, None),
            P("dp", "blk"),
            P("dp", "blk"),
            P("blk", "dp"),
            P(both),
            P(both),
        ),
        check_vma=False,
    )
```

```python
import functools

import jax
import jax.numpy as jnp
import numpy as np
from jax import lax
from jax.experimental import pallas as pl
from jax.experimental.pallas import tpu as pltpu
from jax.sharding import PartitionSpec as P

HEADS = 12
HEAD = 64
PAIR = 2 * HEAD
EPS = 1e-05
NEG = -1e30
LOG2E = 1.4426950408889634
LN2 = 0.6931471805599453
VMEM_LIMIT = 60 * 1024 * 1024

BF = jnp.bfloat16
F32 = jnp.float32


def dot(a, b):
    return lax.dot_general(a, b, (((1,), (0,)), ((), ())), preferred_element_type=F32)


def dot_nt(a, b):
    return lax.dot_general(a, b, (((1,), (1,)), ((), ())), preferred_element_type=F32)


def params(limit=VMEM_LIMIT):
    return pltpu.CompilerParams(vmem_limit_bytes=limit)


def lanes(shape):
    return lax.broadcasted_iota(jnp.int32, shape, 1)


def turn(u):
    low_half = (lanes(u.shape) % HEAD) < HEAD // 2
    return jnp.where(low_half, -pltpu.roll(u, PAIR - HEAD // 2, 1), pltpu.roll(u, HEAD // 2, 1))


MESH = pl.DeviceIdType.MESH
AXES = "zxcy"
SIZE = {"z": 4, "x": 2, "c": 2, "y": 2}


def place():
    dp, y = lax.axis_index("dp"), lax.axis_index("blk")
    return {"z": dp // 4, "x": dp // 2 % 2, "c": dp % 2, "y": y}


def moved(me, axis, by):
    return {**me, axis: lax.rem(me[axis] + by, SIZE[axis])}


def device(at):
    return ((at["z"] * 2 + at["x"]) * 2 + at["c"], at["y"])


def greet(me):
    barrier = pltpu.get_barrier_semaphore()
    peers = [moved(me, "y", 1), moved(me, "x", 1), moved(me, "c", 1)]
    peers += [moved(me, "z", d) for d in range(1, 4)]
    for peer in peers:
        pl.semaphore_signal(barrier, inc=1, device_id=device(peer), device_id_type=MESH)
    pl.semaphore_wait(barrier, len(peers))


class Gather:
    def __init__(self, me, shard, full, send, recv, local, base, order, held="", columns=None):
        self.me, self.shard, self.full, self.held = me, shard, full, held
        self.part = () if columns is None else (slice(None), pl.ds(*columns))
        self.spans = [a for a in AXES if a in held + order]
        self.send, self.recv, self.local, self.base, self.order = send, recv, local, base, order

    @staticmethod
    def sems(order):
        return sum(SIZE[a] - 1 for a in order)

    def view(self, at, got):
        return self.full.at[tuple(slice(None) if a in got else at[a] for a in self.spans) + self.part]

    def at_stage(self, stage):
        got = self.held + self.order[:stage]
        return got, self.order[stage], self.base + self.sems(self.order[:stage])

    def copies(self, stage):
        got, axis, slot = self.at_stage(stage)
        here = self.view(self.me, got)
        return [
            pltpu.make_async_remote_copy(
                src_ref=self.shard if stage == 0 else here,
                dst_ref=here,
                send_sem=self.send.at[slot + d - 1],
                recv_sem=self.recv.at[slot + d - 1],
                device_id=device(moved(self.me, axis, d)),
                device_id_type=MESH,
            )
            for d in range(1, SIZE[axis])
        ]

    def own(self):
        return pltpu.make_async_copy(self.shard, self.view(self.me, self.held), self.local)

    def arrivals(self, stage):
        got, axis, slot = self.at_stage(stage)
        for d in range(1, SIZE[axis]):
            there = self.view(moved(self.me, axis, SIZE[axis] - d), got)
            pltpu.make_async_remote_copy(
                src_ref=there,
                dst_ref=there,
                send_sem=self.send.at[slot + d - 1],
                recv_sem=self.recv.at[slot + d - 1],
                device_id=device(moved(self.me, axis, d)),
                device_id_type=MESH,
            ).wait_recv()

    def start(self):
        self.own().start()
        for copy in self.copies(0):
            copy.start()

    def step(self, stage):
        self.arrivals(stage - 1)
        if stage == 1:
            self.own().wait()
        if stage < len(self.order):
            for copy in self.copies(stage):
                copy.start()

    def finish(self):
        for stage in range(len(self.order)):
            for copy in self.copies(stage):
                copy.wait_send()


class Reduce:
    SEMS = 7

    def __init__(self, me, piece, bufs, out, send, recv, local, base, order):
        self.me, self.piece, self.out, self.order = me, piece, out, order
        self.b, self.r0, self.r1, self.r2, self.r3 = bufs
        self.send, self.recv, self.local, self.base = send, recv, local, base

    def copy(self, source, target, slot, axis, by=1):
        return pltpu.make_async_remote_copy(
            src_ref=source,
            dst_ref=target,
            send_sem=self.send.at[self.base + slot],
            recv_sem=self.recv.at[self.base + slot],
            device_id=device(moved(self.me, axis, by)),
            device_id_type=MESH,
        )

    def mine(self):
        c = self.me["c"]
        return [
            pltpu.make_async_copy(self.piece(c, y), self.b.at[y], self.local.at[y]) for y in range(2)
        ]

    def copies(self, stage):
        x, y, z = self.me["x"], self.me["y"], self.me["z"]
        if stage == 0:
            other = 1 - self.me["c"]
            return [self.copy(self.piece(other, i), self.r0.at[i], i, "c") for i in range(2)]
        if self.order[0] == "z":
            if stage == 1:
                return [
                    self.copy(self.b.at[:, lax.rem(z + d, 4)], self.r1.at[d - 1], 3 + d, "z", d)
                    for d in range(1, 4)
                ]
            if stage == 2:
                return [self.copy(self.b.at[1 - y, z], self.r2, 2, "y")]
            return [self.copy(self.b.at[y, z, 1 - x], self.r3, 3, "x")]
        if stage == 1:
            source = self.b.at[1 - y] if self.order[0] == "y" else self.b.at[:, :, 1 - x]
            return [self.copy(source, self.r1, 2, self.order[0])]
        if stage == 2:
            source = self.b.at[y, :, 1 - x] if self.order[0] == "y" else self.b.at[1 - y, :, x]
            return [self.copy(source, self.r2, 3, self.order[1])]
        return [
            self.copy(self.b.at[y, lax.rem(z + d, 4), x], self.r3.at[d - 1], 3 + d, "z", d)
            for d in range(1, 4)
        ]

    def start(self):
        for copy in self.copies(0) + self.mine():
            copy.start()

    def step(self, stage):
        x, y, z = self.me["x"], self.me["y"], self.me["z"]
        for copy in self.copies(stage - 1):
            copy.wait_recv()
        b = self.b
        if stage == 1:
            for copy in self.mine():
                copy.wait()

            def add(i, _):
                at = (i // 4, i % 4)
                b[at] = b[at] + self.r0[at]
                return 0

            lax.fori_loop(0, 8, add, 0)
        if self.order[0] == "z" and stage > 1:
            if stage == 2:

                def add(i, _):
                    at = (i // 2, i % 2)
                    total = b[at[0], z, at[1]].astype(F32)
                    for d in range(3):
                        total = total + self.r1[d, at[0], at[1]].astype(F32)
                    b[at[0], z, at[1]] = total.astype(b.dtype)
                    return 0

                lax.fori_loop(0, 4, add, 0)
            if stage == 3:
                for i in range(2):
                    b[y, z, i] = b[y, z, i] + self.r2[i]
            if stage == 4:
                self.out[...] = b[y, z, x].astype(F32) + self.r3[...].astype(F32)
                return
            for copy in self.copies(stage):
                copy.start()
            return
        if stage == 2:

            def add(i, _):
                if self.order[0] == "y":
                    for j in range(2):
                        b[y, i, j] = b[y, i, j] + self.r1[i, j]
                else:
                    for j in range(2):
                        b[j, i, x] = b[j, i, x] + self.r1[j, i]
                return 0

            lax.fori_loop(0, 4, add, 0)
        if stage == 3:

            def add(i, _):
                b[y, i, x] = b[y, i, x] + self.r2[i]
                return 0

            lax.fori_loop(0, 4, add, 0)
        if stage == 4:
            total = b[y, z, x].astype(F32)
            for d in range(3):
                total = total + self.r3[d].astype(F32)
            self.out[...] = total
            return
        for copy in self.copies(stage):
            copy.start()

    def finish(self):
        for stage in range(4):
            for copy in self.copies(stage):
                copy.wait_send()

    @staticmethod
    def scratch(rows, columns, kind, order):
        if order[0] == "z":
            return [
                pltpu.VMEM(shape + (rows, columns), kind)
                for shape in ((2, 4, 2), (2, 4, 2), (3, 2, 2), (2,), ())
            ]
        lead = (4, 2) if order[0] == "y" else (2, 4)
        return [
            pltpu.VMEM(shape + (rows, columns), kind)
            for shape in ((2, 4, 2), (2, 4, 2), lead, (4,), (3,))
        ]


class Swap:
    def __init__(self, me, source, target, bounce, send, recv, local, slots, parts):
        self.me, self.source, self.target, self.bounce = me, source, target, bounce
        self.send, self.recv, self.local, self.slots, self.parts = send, recv, local, slots, parts

    def copy(self, n, row, half):
        begin, size = self.parts[n]
        part = pl.ds(begin, size)
        return pltpu.make_async_remote_copy(
            src_ref=self.source.at[row, part],
            dst_ref=self.target.at[half, part],
            send_sem=self.send.at[self.slots + n],
            recv_sem=self.recv.at[self.slots + n],
            device_id=device(moved(self.me, "y", 1)),
            device_id_type=MESH,
        )

    def give(self, n):
        y = self.me["y"]
        self.copy(n, 1 - y, y).start()

    def keep_in(self):
        return pltpu.make_async_copy(self.source.at[self.me["y"]], self.bounce, self.local)

    def keep_out(self):
        return pltpu.make_async_copy(self.bounce, self.target.at[self.me["y"]], self.local)

    def keep_begin(self):
        self.keep_in().start()

    def keep_turn(self):
        self.keep_in().wait()
        self.keep_out().start()

    def finish(self):
        y = self.me["y"]
        for n in range(len(self.parts)):
            self.copy(n, 1 - y, 1 - y).wait_recv()
            self.copy(n, 1 - y, y).wait_send()
        self.keep_out().wait()


def halves(ref):
    half = ref.shape[-1] // 2
    return [ref.at[(slice(None),) * (len(ref.shape) - 1) + (pl.ds(n * half, half),)] for n in range(2)]


def stages(me, shards, fulls, orders, held, columns, send, recv, local, base=0):
    out = []
    for i, order in enumerate(orders):
        out.append(
            Gather(me, shards[i], fulls[i], send, recv, local.at[i], base, order, held[i], columns[i])
        )
        base += Gather.sems(order)
    return out


def project(x, w_ref, cosine, sine, put):
    width = x.shape[1]
    for part in range(3):
        for pair in range(width // PAIR):
            at = part * width + pair * PAIR
            if pair % 2 == 0:
                u2 = dot(x, w_ref[:, at : at + 2 * PAIR])
            u = u2[:, (pair % 2) * PAIR : (pair % 2 + 1) * PAIR]
            if part < 2:
                u = u * cosine + turn(u) * sine
            if part == 0:
                u = u * (0.125 * LOG2E)
            put(part, slice(pair * PAIR, (pair + 1) * PAIR), u.astype(BF))


def qkv_kernel(x_ref, w_ref, cos_ref, sin_ref, q_ref, k_ref, v_ref, xt_ref):
    x = x_ref[...]

    def put(part, columns, value):
        (q_ref, k_ref, v_ref)[part][:, columns] = value

    project(x, w_ref, cos_ref[...], sin_ref[...], put)
    xt_ref[...] = x.T


def qkv_call(x, w, cosine, sine, tile=512):
    tokens, width = x.shape
    span = cosine.shape[0]
    tile = min(tile, span)
    row = pl.BlockSpec((tile, width), lambda i: (i, 0))
    table = pl.BlockSpec((tile, PAIR), lambda i: (i % (span // tile), 0))
    return pl.pallas_call(
        qkv_kernel,
        grid=(tokens // tile,),
        in_specs=[
            row,
            pl.BlockSpec(w.shape, lambda i: (0, 0), pipeline_mode=pl.Buffered(1)),
            table,
            table,
        ],
        out_specs=[row, row, row, pl.BlockSpec((width, tile), lambda i: (0, i))],
        out_shape=[jax.ShapeDtypeStruct((tokens, width), BF)] * 3
        + [jax.ShapeDtypeStruct((width, tokens), BF)],
        compiler_params=params(),
        name="qkv",
    )(x, w, cosine, sine)


OPENING_ORDERS = ("yzxc", "zyxc", "zy", "zx", "z", "y", "x")


def opening_kernel(
    tok_hbm, w_shard, out_ref, one_ref, two_ref, gate_shard, up_shard, down_shard, cos_ref, sin_ref,
    x_hbm, w_hbm, q_hbm, k_hbm, v_hbm, xt_hbm, out_part, gate_part, up_part, left_part, right_part,
    x, w_blocks, w, q, k, v, xt, out_shard, send, recv, local, load, store,
):
    count, columns = out_ref.shape
    square = (count, count)
    same = lax.broadcasted_iota(jnp.int32, square, 0) == lax.broadcasted_iota(jnp.int32, square, 1)
    one, two = (
        jnp.sum(jnp.where(same, ref[...].astype(F32), 0.0), axis=1, keepdims=True) for ref in (one_ref, two_ref)
    )
    lane = lanes((count, PAIR))
    out_shard[:, :columns] = out_ref[...]
    out_shard[:, columns:] = jnp.where(lane == 0, one, jnp.where(lane == 1, two, 0.0)).astype(BF)
    me = place()
    y = me["y"]
    greet(me)
    rows = x.shape[1]
    begin = rows // 8
    parts = ((0, begin), (begin, rows - begin))

    def token_copy(n, row, half):
        part = pl.ds(*parts[n])
        return pltpu.make_async_remote_copy(
            src_ref=tok_hbm.at[row, part],
            dst_ref=x.at[half, part],
            send_sem=send.at[n],
            recv_sem=recv.at[n],
            device_id=device(moved(me, "y", 1)),
            device_id_type=MESH,
        )

    width = w.shape[1] // 2
    g = stages(
        me,
        halves(w_shard) + [out_shard, gate_shard, up_shard] + halves(down_shard),
        [w_blocks, w_blocks, out_part, gate_part, up_part, left_part, right_part],
        OPENING_ORDERS,
        ("",) * 7,
        ((0, width), (width, width)) + (None,) * 5,
        send, recv, local, 2,
    )
    mine = pltpu.make_async_copy(tok_hbm.at[y], x.at[y], load.at[0])
    g[0].start()
    g[1].start()
    token_copy(0, 1 - y, y).start()
    mine.start()
    g[0].step(1)
    g[1].step(1)
    token_copy(1, 1 - y, y).start()
    g[0].step(2)
    for n in (2, 3, 4):
        g[n].start()
    g[1].step(2)
    g[6].start()
    g[5].start()
    g[0].step(3)
    g[1].step(3)
    g[0].step(4)
    g[1].step(4)
    g[2].step(1)
    g[3].step(1)
    for n in range(3):
        part = slice(n * w.shape[0], (n + 1) * w.shape[0])
        block = w_blocks[:, :, :, :, :, part].astype(F32)
        w[:, part] = block.reshape(w.shape[0], w.shape[0]).astype(BF)
    keep_w = pltpu.make_async_copy(w, w_hbm, load.at[1])
    keep_w.start()
    mine.wait()
    tile = 512

    def stores(n):
        half = lax.rem(y + n // 2, 2)
        at = pl.ds(pl.multiple_of(half * rows + lax.rem(n, 2) * tile, tile), tile)
        pairs = [(a.at[at], b.at[at]) for a, b in ((q, q_hbm), (k, k_hbm), (v, v_hbm))]
        pairs.append((xt.at[:, at], xt_hbm.at[:, at]))
        return [pltpu.make_async_copy(a, b, store.at[n, i]) for i, (a, b) in enumerate(pairs)]

    def tile_step(n, _):
        half = lax.rem(y + n // 2, 2)
        start = pl.multiple_of(half * rows + lax.rem(n, 2) * tile, tile)
        at = pl.ds(start, tile)

        @pl.when(n == 2)
        def _():
            for m in range(2):
                token_copy(m, 1 - y, 1 - y).wait_recv()

        value = x[half, pl.ds(pl.multiple_of(lax.rem(n, 2) * tile, tile), tile), :]

        def put(part, columns, u):
            (q, k, v)[part][at, columns] = u

        project(value, w, cos_ref[at, :], sin_ref[at, :], put)
        xt[:, at] = value.T
        for copy in stores(n):
            copy.start()
        return 0

    lax.fori_loop(0, 4, tile_step, 0)
    keep_x = pltpu.make_async_copy(x, x_hbm, load.at[2])
    keep_x.start()
    g[2].step(2)
    g[3].step(2)
    for n in (4, 5, 6):
        g[n].step(1)
    for gather in g:
        gather.finish()
    for m in range(2):
        token_copy(m, 1 - y, y).wait_send()
    for n in range(4):
        for copy in stores(n):
            copy.wait()
    keep_w.wait()
    keep_x.wait()


def opening_call(tokens, w_qkv, w_out, gain_one, gain_two, w_gate, w_up, w_down, cosine, sine):
    rows, span, width = tokens.shape
    total = rows * span
    hbm = pl.BlockSpec(memory_space=pl.ANY)
    held = pl.BlockSpec(memory_space=pltpu.VMEM)
    whole = (width, w_qkv.shape[1])
    flat = (total, width)
    shapes = [tokens.shape, whole, flat, flat, flat, (width, total)]
    out_shape = (w_out.shape[0], width + PAIR)
    shapes += [(4, 2) + out_shape, (4, 2) + w_gate.shape, (4,) + w_up.shape]
    shapes += [(2, w_down.shape[0], w_down.shape[1] // 2)] * 2
    sems = 2 + sum(map(Gather.sems, OPENING_ORDERS))
    return pl.pallas_call(
        opening_kernel,
        in_specs=[hbm] + [held] * 9,
        out_specs=[hbm] * len(shapes),
        out_shape=[jax.ShapeDtypeStruct(shape, BF) for shape in shapes],
        scratch_shapes=[
            pltpu.VMEM(tokens.shape, BF),
            pltpu.VMEM((4, 2, 2, 2) + w_qkv.shape, BF),
            pltpu.VMEM(whole, BF),
            pltpu.VMEM(flat, BF),
            pltpu.VMEM(flat, BF),
            pltpu.VMEM(flat, BF),
            pltpu.VMEM((width, total), BF),
            pltpu.VMEM(out_shape, BF),
            pltpu.SemaphoreType.DMA((sems,)),
            pltpu.SemaphoreType.DMA((sems,)),
            pltpu.SemaphoreType.DMA((len(OPENING_ORDERS),)),
            pltpu.SemaphoreType.DMA((3,)),
            pltpu.SemaphoreType.DMA((4, 4)),
        ],
        compiler_params=pltpu.CompilerParams(
            vmem_limit_bytes=VMEM_LIMIT, collective_id=0, has_side_effects=True
        ),
        name="opening",
    )(tokens, w_qkv, w_out, gain_one[None], gain_two[None], w_gate, w_up, w_down, cosine, sine)


def key_mask(len_ref, own, keys, other):
    length = len_ref[lax.axis_index("blk") if own else pl.program_id(0)]
    sub = lanes((keys, PAIR)) % HEAD
    past = lax.broadcasted_iota(jnp.int32, (keys, PAIR), 0) >= length
    return jnp.where(sub < 3, other, jnp.where((sub == 3) & past, NEG, 0.0))


def attend_kernel(tile, chunk, moves, len_ref, q_ref, k_ref, v_ref, *rest):
    inputs, rest = rest[:moves], rest[moves:]
    o_ref, aug_ref, rest = rest[0], rest[1], rest[2:]
    results = max(moves - 1, 0)
    outputs, rest = rest[:results], rest[results:]
    ka, va, s_scr, m_scr = rest[:4]
    keys, span = k_ref.shape[1], q_ref.shape[1]
    tiles = span // tile
    events = {}
    if moves:
        events = attend_events(inputs, outputs, *rest[4:])

    @pl.when(pl.program_id(1) == 0)
    def _():
        ka[:, PAIR:] = key_mask(len_ref, moves, keys, 0.0).astype(BF)
        va[:, PAIR:] = jnp.ones((keys, PAIR), BF)

    ka[:, :PAIR] = k_ref[0]
    va[:, :PAIR] = v_ref[0]
    lane = lanes((tile, PAIR))
    side = lanes((tile, 2 * PAIR)) // HEAD % 2
    ones = (lane % HEAD == 3).astype(F32).astype(BF)
    chunks = keys // chunk

    def query(i, h):
        at = pl.ds(pl.multiple_of(i * tile, tile), tile)
        both = jnp.concatenate([q_ref[0, at, :], ones], axis=1)
        return jnp.where(side == h, both, jnp.zeros_like(both))

    def score(qa, h, c, top):
        s = dot_nt(qa, ka[c * chunk : (c + 1) * chunk, :])
        s_scr[h, :, c * chunk : (c + 1) * chunk] = s
        for b in range(chunk // PAIR):
            part = s[:, b * PAIR : (b + 1) * PAIR]
            top = part if top is None else jnp.maximum(top, part)
        return top

    def close(h, top):
        m_scr[h] = jnp.broadcast_to(jnp.max(top, axis=1, keepdims=True), (tile, PAIR))

    def unit(h, later, other):
        m = m_scr[h]
        wide = jnp.concatenate([m] * (chunk // PAIR), axis=1)
        qa = query(later, other)
        acc, top = None, None
        for c in range(chunks):
            top = score(qa, other, c, top)
            p = jnp.exp2(s_scr[h, :, c * chunk : (c + 1) * chunk] - wide).astype(BF)
            part = dot(p, va[c * chunk : (c + 1) * chunk, :])
            acc = part if acc is None else acc + part
        return acc, top, m

    top = None
    qa = query(0, 0)
    for c in range(chunks):
        top = score(qa, 0, c, top)
    close(0, top)

    def step(i, _):
        acc0, top, m0 = unit(0, i, 1)
        close(1, top)
        acc1, top, m1 = unit(1, jnp.minimum(i + 1, tiles - 1), 0)
        close(0, top)
        mine = lane < HEAD
        total = jnp.where(mine, acc0[:, PAIR:], acc1[:, PAIR:])
        at = pl.ds(pl.multiple_of(i * tile, tile), tile)
        o_ref[0, at, :] = (jnp.where(mine, acc0[:, :PAIR], acc1[:, :PAIR]) / total).astype(BF)
        lse = jnp.where(mine, m0, m1) + jnp.log2(total)
        aug_ref[0, at, :] = spread(lse, jnp.where(lane % HEAD == 3, 1.0, 0.0))
        return 0

    unroll = 2 if tiles % 2 == 0 else 1

    def group(n, _):
        now = pl.program_id(1) * (tiles // unroll) + n
        for at_step, acts in events.items():

            @pl.when(now == at_step)
            def _():
                for act in acts:
                    act()

        for j in range(unroll):
            step(n * unroll + j, 0)
        return 0

    lax.fori_loop(0, tiles // unroll, group, 0)
    if moves:

        @pl.when(pl.program_id(1) == pl.num_programs(1) - 1)
        def _():
            for act in events.last:
                act()


class Events(dict):
    def __init__(self):
        self.last = []

    def put(self, at, *acts):
        self.setdefault(at, []).extend(acts)


ATTEND_HELD = ("zy", "zx", "z", "y", "x")
ATTEND_ORDERS = ("xc", "yc", "yxc", "zxc", "zyc")
ATTEND_PLAN = ((2, 0, 1), (4, 2, 1), (4, 3, 1), (7, 4, 1), (10, 1, 1), (10, 2, 2), (11, 3, 2), (11, 4, 2))
ATTEND_FIRST = (2, 1, 0, 3, 4)


def attend_events(inputs, outputs, send, recv, local):
    me = place()
    half = inputs[3].shape[-1]
    columns = (None, None, None, (0, half), (half, half))
    fulls = tuple(outputs) + (outputs[3],)
    gathers = stages(me, inputs, fulls, ATTEND_ORDERS, ATTEND_HELD, columns, send, recv, local)
    events = Events()
    events.put(0, functools.partial(greet, me), *(gathers[i].start for i in ATTEND_FIRST))
    done = [1] * len(gathers)
    for at, i, stage in ATTEND_PLAN:
        events.put(at, functools.partial(gathers[i].step, stage))
        done[i] = stage + 1
    for stage in range(1, 4):
        for i, g in enumerate(gathers):
            if done[i] <= stage <= len(ATTEND_ORDERS[i]):
                events.last.append(functools.partial(g.step, stage))
    events.last += [g.finish for g in gathers]
    return events


def spread(value, other):
    high = value.astype(BF).astype(F32)
    rest = value - high
    mid = rest.astype(BF).astype(F32)
    low = rest - mid
    sub = lanes(value.shape) % HEAD
    return jnp.where(
        sub == 0, high, jnp.where(sub == 1, mid, jnp.where(sub == 2, low, other))
    ).astype(BF)


def attend_call(q, k, v, lengths, moving=(), tile=512, chunk=512):
    rows, span, width = q.shape
    keys = k.shape[1]
    tile = min(tile, span)
    moves = len(moving)
    qs = pl.BlockSpec((1, span, PAIR), lambda r, p: (r, 0, p))
    ks = pl.BlockSpec((1, keys, PAIR), lambda r, p: (r, 0, p))
    hbm = pl.BlockSpec(memory_space=pl.ANY)
    moved_shapes = [jax.ShapeDtypeStruct((4, 2, 2, 2) + a.shape[-2:], a.dtype) for a in moving[:3]]
    for a in moving[3:4]:
        moved_shapes.append(jax.ShapeDtypeStruct((4, 2, 2, 2, a.shape[-2], 2 * a.shape[-1]), a.dtype))
    sems = sum(map(Gather.sems, ATTEND_ORDERS))
    extra = [pltpu.SemaphoreType.DMA((sems,))] * 2 + [pltpu.SemaphoreType.DMA((len(ATTEND_ORDERS),))]
    held = [
        pl.BlockSpec(a.shape, lambda r, p, n=a.ndim: (0,) * n, pipeline_mode=pl.Buffered(1))
        for a in moving
    ]
    more = dict(collective_id=1, has_side_effects=True) if moves else {}
    return pl.pallas_call(
        functools.partial(attend_kernel, tile, chunk, moves),
        grid=(rows, width // PAIR),
        in_specs=[pl.BlockSpec(memory_space=pltpu.SMEM), qs, ks, ks] + held,
        out_specs=[qs, qs] + [hbm] * len(moved_shapes),
        out_shape=[jax.ShapeDtypeStruct(q.shape, BF)] * 2 + moved_shapes,
        scratch_shapes=[
            pltpu.VMEM((keys, 2 * PAIR), BF),
            pltpu.VMEM((keys, 2 * PAIR), BF),
            pltpu.VMEM((2, tile, keys), F32),
            pltpu.VMEM((2, tile, PAIR), F32),
        ]
        + (extra if moves else []),
        compiler_params=pltpu.CompilerParams(vmem_limit_bytes=VMEM_LIMIT, **more),
        name="attend",
    )(lengths, q, k, v, *moving)


def attend_back_kernel(
    tq, unroll, moves, len_ref, q_ref, k_ref, v_ref, o_ref, do_ref, aug_ref, cos_ref, sin_ref, *rest
):
    inputs, rest = rest[:moves], rest[moves:]
    dq_ref, dk_ref, dv_ref, rest = rest[0], rest[1], rest[2], rest[3:]
    outputs, rest = rest[:moves], rest[moves:]
    qa, da, ka, va, kt, dk_acc, dv_acc = rest[:7]
    keys, span = k_ref.shape[1], q_ref.shape[1]
    tiles = span // tq
    events = {}
    if moves:
        events = back_events(inputs, outputs, *rest[7:])

    @pl.when(pl.program_id(1) == 0)
    def _():
        ka[:, PAIR:] = key_mask(len_ref, moves, keys, -1.0).astype(BF)
        va[:, PAIR:] = jnp.where(lanes((keys, PAIR)) % HEAD < 3, -1.0, 0.0).astype(BF)

    k, do = k_ref[0], do_ref[0]
    ka[:, :PAIR] = k
    va[:, :PAIR] = v_ref[0]
    kt[...] = k.T
    prod = do.astype(F32) * o_ref[0].astype(F32)
    first = prod.astype(BF)
    second = (prod - first.astype(F32)).astype(BF)
    block = (
        (lax.broadcasted_iota(jnp.int32, (PAIR, PAIR), 0) // HEAD)
        == (lax.broadcasted_iota(jnp.int32, (PAIR, PAIR), 1) // HEAD)
    ).astype(F32).astype(BF)
    delta = dot(first, block) + dot(second, block)
    q_both = jnp.concatenate([q_ref[0], aug_ref[0]], axis=1)
    d_both = jnp.concatenate([do, spread(delta, jnp.zeros_like(delta))], axis=1)
    side = lanes(q_both.shape) // HEAD % 2
    for h in range(2):
        qa[h] = jnp.where(side == h, q_both, jnp.zeros_like(q_both))
        da[h] = jnp.where(side == h, d_both, jnp.zeros_like(d_both))
    dk_acc[...] = jnp.zeros_like(dk_acc)
    dv_acc[...] = jnp.zeros_like(dv_acc)

    def query_step(i, _):
        at_q = pl.ds(pl.multiple_of(i * tq, tq), tq)
        dv, dk, dq = None, None, []
        for h in range(2):
            st = dot_nt(ka[...], qa[h, at_q, :])
            dpt = dot_nt(va[...], da[h, at_q, :])
            p = jnp.exp2(st)
            ds = (p * dpt).astype(BF)
            pv = dot(p.astype(BF), da[h, at_q, :PAIR])
            pk = dot(ds, qa[h, at_q, :PAIR])
            dv = pv if dv is None else dv + pv
            dk = pk if dk is None else dk + pk
            dq.append(dot(kt[h * HEAD : (h + 1) * HEAD, :], ds))
        dv_acc[...] += dv
        dk_acc[...] += dk
        g = jnp.concatenate(dq, axis=0).T * 0.125
        dq_ref[0, at_q, :] = back_turn(g, cos_ref[at_q, :], sin_ref[at_q, :]).astype(BF)
        return 0

    def group(n, _):
        now = pl.program_id(1) * (tiles // unroll) + n
        for at_step, acts in events.items():

            @pl.when(now == at_step)
            def _():
                for act in acts:
                    act()

        for j in range(unroll):
            query_step(n * unroll + j, 0)
        return 0

    lax.fori_loop(0, tiles // unroll, group, 0)
    dv_ref[0] = dv_acc[...].astype(dv_ref.dtype)
    g = dk_acc[...] * LN2
    if dk_ref.dtype == BF:
        g = back_turn(g, cos_ref[...], sin_ref[...])
    dk_ref[0] = g.astype(dk_ref.dtype)
    if moves:

        @pl.when(pl.program_id(1) == pl.num_programs(1) - 1)
        def _():
            for act in events.last:
                act()


def back_turn(g, cosine, sine):
    return g * cosine - turn(g * sine)


def wide_piece(source, columns):
    return lambda c, y: source.at[:, :, c, :, pl.ds(y * columns, columns)]


def tall_piece(source):
    return lambda c, y: source.at[:, :, c, y]


BACK_ORDERS = ("yx", "xy", "zyx", "xy")
BACK_PLAN = (
    (1, 0, 1), (1, 1, 1), (1, 2, 1), (1, 3, 1), (3, 0, 2), (3, 1, 2), (3, 3, 2), (4, 0, 3), (4, 1, 3), (4, 2, 2),
    (4, 3, 3), (5, 0, 4), (5, 2, 3),
)
BACK_LAST = (2, 1, 3)


def back_events(inputs, outputs, send, recv, local, *bufs):
    me = place()
    reduces = []
    for i, (source, out) in enumerate(zip(inputs, outputs)):
        piece = wide_piece(source, source.shape[-1] // 2) if len(source.shape) == 5 else tall_piece(source)
        reduces.append(
            Reduce(
                me, piece, bufs[5 * i : 5 * i + 5], out, send, recv,
                local.at[pl.ds(2 * i, 2)], i * Reduce.SEMS, BACK_ORDERS[i],
            )
        )
    events = Events()
    events.put(0, functools.partial(greet, me), *(reduces[i].start for i in (2, 0, 1, 3)))
    for at, i, stage in BACK_PLAN:
        events.put(at, functools.partial(reduces[i].step, stage))
    events.last += [functools.partial(reduces[i].step, 4) for i in BACK_LAST]
    events.last += [r.finish for r in reduces]
    return events


def attend_back_call(q, k, v, lengths, o, do, aug, cosine, sine, whole, moving=(), tq=512, unroll=4):
    rows, span, width = q.shape
    keys = k.shape[1]
    tq = min(tq, span)
    unroll = min(unroll, span // tq)
    moves = len(moving)
    qs = pl.BlockSpec((1, span, PAIR), lambda r, p: (r, 0, p))
    ks = pl.BlockSpec((1, keys, PAIR), lambda r, p: (r, 0, p))
    table = pl.BlockSpec((span, PAIR), lambda r, p: (0, 0), pipeline_mode=pl.Buffered(1))
    hbm = pl.BlockSpec(memory_space=pl.ANY)
    kv_type = BF if whole else F32
    results, result_specs, extra, more = [], [], [], {}
    if moves:
        extra = [pltpu.SemaphoreType.DMA((Reduce.SEMS * moves,))] * 2
        extra += [pltpu.SemaphoreType.DMA((2 * moves,))]
        for a, order in zip(moving, BACK_ORDERS):
            block = (a.shape[-2], a.shape[-1] // (2 if a.ndim == 5 else 1))
            results.append(jax.ShapeDtypeStruct(block, F32))
            result_specs.append(pl.BlockSpec(block, lambda r, p: (0, 0), pipeline_mode=pl.Buffered(1)))
            extra += Reduce.scratch(*block, a.dtype, order)
        more = dict(collective_id=2, has_side_effects=True)
    return pl.pallas_call(
        functools.partial(attend_back_kernel, tq, unroll, moves),
        grid=(rows, width // PAIR),
        in_specs=[pl.BlockSpec(memory_space=pltpu.SMEM), qs, ks, ks, qs, qs, qs, table, table]
        + [hbm] * moves,
        out_specs=[qs, ks, ks] + result_specs,
        out_shape=[
            jax.ShapeDtypeStruct(q.shape, BF),
            jax.ShapeDtypeStruct(k.shape, kv_type),
            jax.ShapeDtypeStruct(k.shape, kv_type),
        ]
        + results,
        scratch_shapes=[
            pltpu.VMEM((2, span, 2 * PAIR), BF),
            pltpu.VMEM((2, span, 2 * PAIR), BF),
            pltpu.VMEM((keys, 2 * PAIR), BF),
            pltpu.VMEM((keys, 2 * PAIR), BF),
            pltpu.VMEM((PAIR, keys), BF),
            pltpu.VMEM((keys, PAIR), F32),
            pltpu.VMEM((keys, PAIR), F32),
        ]
        + extra,
        compiler_params=pltpu.CompilerParams(vmem_limit_bytes=VMEM_LIMIT, **more),
        name="attend_back",
    )(lengths, q, k, v, o, do, aug, cosine, sine, *moving)


def middle_kernel(
    chunk, moves, x_ref, att_ref, cot_ref, wo_ref, wg_ref, wu_ref, wd_ref, *rest
):
    source, rest = rest[:moves], rest[moves:]
    (out_ref, dfirst_ref, datt_ref, act_ref, dg_ref, du_ref, ht_ref, dft_ref, at_ref, gg_ref) = rest[:10]
    ca, cb, gains = rest[10:13]
    if moves:
        arrived, dy_ref, send, recv = rest[13:]
        me = place()
        now, per = pl.program_id(0), pl.num_programs(0) // 2
        tile = dy_ref.shape[0]
        give = pltpu.make_async_remote_copy(
            src_ref=source[0].at[1 - me["y"]],
            dst_ref=arrived,
            send_sem=send.at[0],
            recv_sem=recv.at[0],
            device_id=device(moved(me, "y", 1)),
            device_id_type=MESH,
        )

        @pl.when(now == 0)
        def _():
            greet(me)
            give.start()

        pl.when(now == per)(give.wait)

        @pl.when(now < per)
        def _():
            dy_ref[...] = cot_ref[...]

        @pl.when(now >= per)
        def _():
            dy_ref[...] = arrived[pl.ds(pl.multiple_of((now - per) * tile, tile), tile), :]

    else:
        dy_ref = cot_ref

    @pl.when(pl.program_id(0) == 0)
    def _():
        gg_ref[...] = jnp.zeros_like(gg_ref)
        gains[...] = wo_ref[:, x_ref.shape[1] :].astype(F32).T[:8]

    gain1, gain2 = gains[0:1, :], gains[1:2, :]
    att = att_ref[...]
    at_ref[...] = att.T
    first = x_ref[...].astype(F32) + dot(att, wo_ref[:, : att.shape[1]])
    centered = first - jnp.mean(first, axis=1, keepdims=True)
    s1 = lax.rsqrt(jnp.mean(centered * centered, axis=1, keepdims=True) + EPS)
    n1 = centered * s1
    hidden = n1 * gain1
    low = hidden.astype(BF)
    ht_ref[...] = low.T
    hidden_width = wg_ref.shape[1]
    second = hidden
    for c in range(hidden_width // chunk):
        at = slice(c * chunk, (c + 1) * chunk)
        g = dot(low, wg_ref[:, at])
        u = dot(low, wu_ref[:, at])
        sig = jax.nn.sigmoid(g)
        silu = g * sig
        act = (silu * u).astype(BF)
        act_ref[:, at] = act
        ca[:, at] = (u * (sig + silu * (1.0 - sig))).astype(ca.dtype)
        cb[:, at] = silu.astype(cb.dtype)
        second = second + dot(act, wd_ref[at, :])
    centered = second - jnp.mean(second, axis=1, keepdims=True)
    s2 = lax.rsqrt(jnp.mean(centered * centered, axis=1, keepdims=True) + EPS)
    n2 = centered * s2
    out_ref[...] = (n2 * gain2).astype(BF)
    dy = dy_ref[...].astype(F32)
    gg_ref[1:2, :] += jnp.sum(dy * n2, axis=0, keepdims=True)
    inner = dy * gain2
    d_second = s2 * (
        inner - jnp.mean(inner, axis=1, keepdims=True) - n2 * jnp.mean(inner * n2, axis=1, keepdims=True)
    )
    d_ffn = d_second.astype(BF)
    dft_ref[...] = d_ffn.T
    d_hidden = d_second
    for c in range(hidden_width // chunk):
        at = slice(c * chunk, (c + 1) * chunk)
        d_act = dot_nt(d_ffn, wd_ref[at, :])
        dg = (d_act * ca[:, at]).astype(BF)
        du = (d_act * cb[:, at]).astype(BF)
        dg_ref[:, at] = dg
        du_ref[:, at] = du
        d_hidden = d_hidden + dot_nt(dg, wg_ref[:, at]) + dot_nt(du, wu_ref[:, at])
    gg_ref[0:1, :] += jnp.sum(d_hidden * n1, axis=0, keepdims=True)
    inner = d_hidden * gain1
    d_first = s1 * (
        inner - jnp.mean(inner, axis=1, keepdims=True) - n1 * jnp.mean(inner * n1, axis=1, keepdims=True)
    )
    low = d_first.astype(BF)
    dfirst_ref[...] = low
    datt_ref[...] = dot_nt(low, wo_ref[:, : low.shape[1]]).astype(BF)


def middle_call(x, att, cot, wo, wg, wu, wd, tile=256, chunk=768):
    tokens, width = x.shape
    hidden_width = wg.shape[1]
    tile = min(tile, tokens)
    moves = cot.ndim - 2
    per = tokens // tile // 2

    def place_of(i):
        if not moves:
            return i
        return lax.rem(lax.axis_index("blk") + i // per, 2) * per + lax.rem(i, per)

    row = pl.BlockSpec((tile, width), lambda i: (place_of(i), 0))
    wide = pl.BlockSpec((tile, hidden_width), lambda i: (place_of(i), 0))
    column = pl.BlockSpec((width, tile), lambda i: (0, place_of(i)))
    cot_row, extra, more = row, [], {}
    if moves:
        cot_row = pl.BlockSpec(
            (None, tile, width), lambda i: (lax.axis_index("blk"), jnp.minimum(i, per - 1), 0)
        )
        extra = [pltpu.VMEM((tokens // 2, width), BF), pltpu.VMEM((tile, width), BF)]
        extra += [pltpu.SemaphoreType.DMA((1,))] * 2
        more = dict(collective_id=5, has_side_effects=True)

    def whole(a):
        return pl.BlockSpec(a.shape, lambda i: (0, 0), pipeline_mode=pl.Buffered(1))

    return pl.pallas_call(
        functools.partial(middle_kernel, chunk, moves),
        grid=(tokens // tile,),
        in_specs=[row, row, cot_row, whole(wo), whole(wg), whole(wu), whole(wd)]
        + [pl.BlockSpec(memory_space=pl.ANY)] * moves,
        out_specs=[row, row, row, wide, wide, wide, column, column, column]
        + [pl.BlockSpec((PAIR, width), lambda i: (0, 0))],
        out_shape=[jax.ShapeDtypeStruct((tokens, width), BF)] * 3
        + [jax.ShapeDtypeStruct((tokens, hidden_width), BF)] * 3
        + [jax.ShapeDtypeStruct((width, tokens), BF)] * 3
        + [jax.ShapeDtypeStruct((PAIR, width), F32)],
        scratch_shapes=[pltpu.VMEM((tile, hidden_width), F32)] * 2 + [pltpu.VMEM((8, width), F32)] + extra,
        compiler_params=pltpu.CompilerParams(vmem_limit_bytes=VMEM_LIMIT, **more),
        name="middle",
    )(x, att, cot, wo, wg, wu, wd, *([cot] * moves))


def outer_kernel(a_ref, b_ref, o_ref):
    o_ref[...] = dot(a_ref[...], b_ref[...]).astype(o_ref.dtype)


def outer_call(a, b, out_type, tile=512):
    rows, tokens = a.shape
    columns = b.shape[1]
    tile = tile if columns % tile == 0 else 256
    return pl.pallas_call(
        outer_kernel,
        grid=(columns // tile,),
        in_specs=[
            pl.BlockSpec((rows, tokens), lambda i: (0, 0), pipeline_mode=pl.Buffered(1)),
            pl.BlockSpec((tokens, tile), lambda i: (0, i)),
        ],
        out_specs=pl.BlockSpec((rows, tile), lambda i: (0, i)),
        out_shape=jax.ShapeDtypeStruct((rows, columns), out_type),
        compiler_params=params(),
        name="outer",
    )(a, b)


def outers_kernel(steps, moves, a1_ref, a2_hbm, a3_hbm, b1_ref, b2_ref, b3_ref, b4_hbm, gains_ref, *rest):
    source, rest = rest[:moves], rest[moves:]
    o1_ref, o2_ref, o3_ref, o4_ref, rest = rest[0], rest[1], rest[2], rest[3], rest[4:]
    now = pl.program_id(0)
    target, rest = rest[:moves], rest[moves:]
    a2_ref, a3_ref, b4_ref, load, rest = rest[0], rest[1], rest[2], rest[3], rest[4:]
    late = [
        pltpu.make_async_copy(a, b, load.at[i])
        for i, (a, b) in enumerate(((a2_hbm, a2_ref), (a3_hbm, a3_ref), (b4_hbm, b4_ref)))
    ]

    @pl.when(now == 0)
    def _():
        for copy in late:
            copy.start()

    @pl.when(now == 2 * steps)
    def _():
        for copy in late:
            copy.wait()

    if moves:
        target, (bounce, send, recv, local) = target[0], rest
        me = place()
        swap = Swap(me, source[0], target, bounce, send, recv, local.at[0], 0, ((0, target.shape[1]),))

        @pl.when(now == 0)
        def _():
            greet(me)
            swap.give(0)
            swap.keep_begin()

        pl.when(now == 3)(swap.keep_turn)
        pl.when(now == 3 * steps)(swap.finish)

    @pl.when(now < steps)
    def _():
        o1_ref[...] = dot(a1_ref[...], b1_ref[...]).astype(BF)

    @pl.when((now >= steps) & (now < 2 * steps))
    def _():
        o2_ref[...] = dot(a1_ref[...], b2_ref[...]).astype(BF)

    @pl.when((now >= 2 * steps) & (now < 3 * steps))
    def _():
        o3_ref[...] = dot(a2_ref[...], b3_ref[...]).astype(BF)

    @pl.when(now == 3 * steps)
    def _():
        width = b4_ref.shape[1]
        o4_ref[:, :width] = dot(a3_ref[...], b4_ref[...])
        o4_ref[:, width:] = gains_ref[...].T


def outers_call(h_t, df_t, att_t, d_gate, d_up, act, d_first, gains, moving=(), tile=512):
    width, tokens = h_t.shape
    hidden = d_gate.shape[1]
    steps = hidden // tile

    def whole(a):
        return pl.BlockSpec(a.shape, lambda i: (0, 0), pipeline_mode=pl.Buffered(1))

    def part(rows, n):
        return pl.BlockSpec((rows, tile), lambda i: (0, jnp.clip(i - n * steps, 0, steps - 1)))

    moves = len(moving)
    hbm = pl.BlockSpec(memory_space=pl.ANY)
    extra = [pltpu.VMEM(a.shape, BF) for a in (df_t, att_t, d_first)] + [pltpu.SemaphoreType.DMA((3,))]
    extra += [pltpu.VMEM(a.shape[1:], BF) for a in moving]
    extra += [pltpu.SemaphoreType.DMA((1,))] * (3 * moves)
    more = dict(collective_id=4, has_side_effects=True) if moves else {}
    return pl.pallas_call(
        functools.partial(outers_kernel, steps, moves),
        grid=(3 * steps + 1,),
        in_specs=[whole(h_t), hbm, hbm] + [part(tokens, n) for n in range(3)] + [hbm, whole(gains)]
        + [hbm] * moves,
        out_specs=[part(width, n) for n in range(3)]
        + [pl.BlockSpec((width, width + PAIR), lambda i: (0, 0), pipeline_mode=pl.Buffered(1))]
        + [hbm] * moves,
        out_shape=[jax.ShapeDtypeStruct((width, hidden), BF)] * 3
        + [jax.ShapeDtypeStruct((width, width + PAIR), F32)]
        + [jax.ShapeDtypeStruct(a.shape, BF) for a in moving],
        scratch_shapes=extra,
        compiler_params=pltpu.CompilerParams(vmem_limit_bytes=VMEM_LIMIT, **more),
        name="outers",
    )(h_t, df_t, att_t, d_gate, d_up, act, d_first, gains, *moving)


CLOSING_ORDERS = ("xy", "xy", "xy")


def closing_kernel(
    dq_hbm, dk_hbm, dv_hbm, first_hbm, xt_hbm, w_hbm, g_out, sum_ref,
    dq, dk, dv, first, xt, w, g, w0, w1, w2, send, recv, local, mine_sem, *bufs,
):
    me = place()
    y = me["y"]
    half = g.shape[1]

    def load(n, a, b, which=None):
        if which is not None:
            at = pl.ds(pl.multiple_of(which * half, half), half)
            a, b = a.at[at], b.at[at]
        return pltpu.make_async_copy(a, b, local.at[n])

    rows_hbm = ((dq_hbm, dq), (dk_hbm, dk), (dv_hbm, dv), (first_hbm, first))
    early = [load(0, w_hbm, w)] + [load(1 + n, a, b, 1 - y) for n, (a, b) in enumerate(rows_hbm)]
    later = [load(5, xt_hbm, xt)] + [load(6 + n, a, b, y) for n, (a, b) in enumerate(rows_hbm)]
    for copy in early + later:
        copy.start()
    greet(me)
    width = dq.shape[1]
    tile = half // 4

    def rows_of(which, t):
        at = pl.ds(pl.multiple_of(which * half + t * tile, tile), tile)
        total = first[at, :].astype(F32)
        for n, a in enumerate((dq, dk, dv)):
            total += dot_nt(a[at, :], w[:, n * width : (n + 1) * width])
        g[which, pl.ds(t * tile, tile), :] = total.astype(BF)

    for copy in early:
        copy.wait()
    quarter = half // 4

    def give(n, target_half):
        part = pl.ds(n * quarter, quarter)
        return pltpu.make_async_remote_copy(
            src_ref=g.at[1 - y, part],
            dst_ref=g_out.at[target_half, part],
            send_sem=send.at[n],
            recv_sem=recv.at[n],
            device_id=device(moved(me, "y", 1)),
            device_id_type=MESH,
        )

    for t in range(4):
        rows_of(1 - y, t)
        if t < 2:
            give(t, y).start()
    for copy in later:
        copy.wait()
    reduces = []
    for n, (a, target) in enumerate(((dq, w0), (dk, w1), (dv, w2))):
        reduces.append(
            Reduce(
                me, tall_piece(target), bufs[5 * n : 5 * n + 5], sum_ref.at[:, pl.ds(n * width, width)],
                send, recv, mine_sem.at[pl.ds(2 * n, 2)], 4 + n * Reduce.SEMS, CLOSING_ORDERS[n],
            )
        )

    def products(n, a, target):
        step = 2 * PAIR

        def part(i, _):
            at = pl.ds(pl.multiple_of(i * step, step), step)
            value = dot(xt[...], a[:, at])
            target[:, :, :, :, :, at] = value.reshape(target.shape[:-1] + (step,)).astype(BF)
            return 0

        lax.fori_loop(0, width // step, part, 0)

    products(0, dq, w0)
    reduces[0].start()
    give(2, y).start()
    products(1, dk, w1)
    reduces[1].start()
    reduces[0].step(1)
    products(2, dv, w2)
    reduces[2].start()
    reduces[1].step(1)
    reduces[0].step(2)
    reduces[2].step(1)
    rows_of(y, 0)
    rows_of(y, 1)
    reduces[1].step(2)
    reduces[0].step(3)
    rows_of(y, 2)
    rows_of(y, 3)
    keep = pltpu.make_async_copy(g.at[y], g_out.at[y], local.at[0])
    keep.start()
    reduces[2].step(2)
    give(3, y).start()
    reduces[1].step(3)
    reduces[0].step(4)
    reduces[2].step(3)
    reduces[1].step(4)
    reduces[2].step(4)
    for r in reduces:
        r.finish()
    for n in range(4):
        give(n, 1 - y).wait_recv()
        give(n, y).wait_send()
    keep.wait()


def closing_call(dq, dk, dv, first, xt, w):
    tokens, width = dq.shape
    hbm = pl.BlockSpec(memory_space=pl.ANY)
    block = (width // 32, width)
    full = pltpu.VMEM((4, 2, 2, 2) + block, BF)
    scratch = [pltpu.VMEM(a.shape, BF) for a in (dq, dk, dv, first, xt, w)]
    scratch += [pltpu.VMEM((2, tokens // 2, width), BF), full, full, full]
    sems = 4 + 3 * Reduce.SEMS
    scratch += [pltpu.SemaphoreType.DMA((sems,))] * 2
    scratch += [pltpu.SemaphoreType.DMA((10,)), pltpu.SemaphoreType.DMA((6,))]
    for order in CLOSING_ORDERS:
        scratch += Reduce.scratch(*block, BF, order)
    return pl.pallas_call(
        closing_kernel,
        in_specs=[hbm] * 6,
        out_specs=[hbm, pl.BlockSpec(memory_space=pltpu.VMEM)],
        out_shape=[
            jax.ShapeDtypeStruct((2, tokens // 2, width), BF),
            jax.ShapeDtypeStruct((block[0], 3 * width), F32),
        ],
        scratch_shapes=scratch,
        compiler_params=pltpu.CompilerParams(
            vmem_limit_bytes=VMEM_LIMIT, collective_id=3, has_side_effects=True
        ),
        name="closing",
    )(dq, dk, dv, first, xt, w)


def tokens_kernel(dq_ref, dk_ref, dv_ref, dfirst_ref, w_ref, o_ref):
    width = dq_ref.shape[1]
    total = dfirst_ref[...].astype(F32)
    total += dot_nt(dq_ref[...], w_ref[:, :width])
    total += dot_nt(dk_ref[...], w_ref[:, width : 2 * width])
    total += dot_nt(dv_ref[...], w_ref[:, 2 * width :])
    o_ref[...] = total.astype(BF)


def tokens_call(dq, dk, dv, dfirst, w, tile=512):
    tokens, width = dq.shape
    tile = min(tile, tokens)
    row = pl.BlockSpec((tile, width), lambda i: (i, 0))
    return pl.pallas_call(
        tokens_kernel,
        grid=(tokens // tile,),
        in_specs=[row] * 4 + [pl.BlockSpec(w.shape, lambda i: (0, 0), pipeline_mode=pl.Buffered(1))],
        out_specs=row,
        out_shape=jax.ShapeDtypeStruct((tokens, width), BF),
        compiler_params=params(),
        name="grad_tokens",
    )(dq, dk, dv, dfirst, w)


def angle_tables(span):
    index = np.arange(HEAD // 2, dtype=np.float64)
    inverse = np.power(1000.0, -2.0 * index / HEAD)
    angles = np.arange(span, dtype=np.float64)[:, None] * inverse[None, :]
    repeat = (1, PAIR // (HEAD // 2))
    return (
        np.tile(np.cos(angles), repeat).astype(np.float32),
        np.tile(np.sin(angles), repeat).astype(np.float32),
    )


def body(tokens, lengths, w_qkv, w_out, w_gate, w_up, w_down, gain_one, gain_two, cotangent):
    axes = ("dp", "blk")
    blk = lax.axis_size("blk")
    mine = lax.axis_index("blk")
    rows, span, width = tokens.shape
    seq = span * blk
    own = blk == 2 and rows == 2 and lax.axis_size("dp") == 16

    def gather(a):
        return lax.all_gather(a, axes, axis=0, tiled=True)

    cosine, sine = map(jnp.asarray, angle_tables(seq))
    if own:
        x, f_qkv, q, k, v, xt, *moving = opening_call(
            tokens, w_qkv, w_out, gain_one, gain_two, w_gate, w_up, w_down, cosine, sine
        )
        x = x.reshape(1, seq, width)
        cq, sq = cosine, sine
    else:
        gains = jnp.stack([gain_one, gain_two], 1)
        w_out = jnp.pad(jnp.concatenate([w_out, gains], 1), ((0, 0), (0, PAIR - 2)))
        f_qkv, f_out, f_gate, f_up, f_down = map(gather, (w_qkv, w_out, w_gate, w_up, w_down))
        x, cot = tokens, cotangent.reshape(rows * span, width)
        cq = lax.dynamic_slice_in_dim(cosine, mine * span, span, 0)
        sq = lax.dynamic_slice_in_dim(sine, mine * span, span, 0)
    n, t = x.shape[:2]
    flat = x.reshape(n * t, width)
    if not own:
        q, k, v, xt = qkv_call(flat, f_qkv, cq, sq)
    q, k, v = (a.reshape(n, t, width) for a in (q, k, v))
    if not own:
        k = lax.all_gather(k, "blk", axis=1, tiled=True)
        v = lax.all_gather(v, "blk", axis=1, tiled=True)
    if own:
        att, aug, f_out, f_gate, f_up, f_down = attend_call(
            q, k, v, lengths, moving
        )
        f_out = f_out.reshape(width, -1)
        cot = cotangent
        f_gate, f_up = f_gate.reshape(width, -1), f_up.reshape(width, -1)
        f_down = f_down.reshape(-1, width)
    else:
        att, aug = attend_call(q, k, v, lengths)
    out, d_first, d_att, act, d_gate, d_up, h_t, df_t, att_t, gains = middle_call(
        flat, att.reshape(n * t, width), cot, f_out, f_gate, f_up, f_down
    )
    moving = (out.reshape(2, span, width),) if own else ()
    gw_gate, gw_up, gw_down_t, gw_out, *moving = outers_call(
        h_t, df_t, att_t, d_gate, d_up, act, d_first, gains, moving
    )
    d_att = d_att.reshape(n, t, width)
    if own:
        wide = tuple(g.reshape(4, 2, 2, width // 16, -1) for g in (gw_gate, gw_up, gw_down_t))
        out = moving[0]
        dq, dk, dv, s_gate, s_up, s_down_t, s_out = attend_back_call(
            q, k, v, lengths, att, d_att, aug, cq, sq, True,
            wide + (gw_out.reshape(4, 2, 2, 2, width // 32, -1),),
        )
    else:

        def scatter_wide(g):
            g = lax.psum_scatter(g, "blk", scatter_dimension=1, tiled=True)
            return lax.psum_scatter(g, "dp", scatter_dimension=0, tiled=True).astype(F32)

        s_gate, s_up, s_down_t = map(scatter_wide, (gw_gate, gw_up, gw_down_t))
        s_out = lax.psum_scatter(gw_out, axes, scatter_dimension=0, tiled=True)
        dq, dk, dv = attend_back_call(q, k, v, lengths, att, d_att, aug, cq, sq, False)
        dk = lax.psum_scatter(dk, "blk", scatter_dimension=1, tiled=True)
        dv = lax.psum_scatter(dv, "blk", scatter_dimension=1, tiled=True)
        heads = (dk * jnp.tile(sq, (1, width // PAIR))).reshape(n, t, HEADS, HEAD)
        half = jnp.concatenate([heads[..., HEAD // 2 :], -heads[..., : HEAD // 2]], -1)
        dk = dk * jnp.tile(cq, (1, width // PAIR)) + half.reshape(n, t, width)
        dk, dv = dk.astype(BF), dv.astype(BF)
    s_down = s_down_t.T
    s_out, s_gg = s_out[:, :width], s_out[:, width : width + 2]
    dq, dk, dv = (a.reshape(n * t, width) for a in (dq, dk, dv))
    if own:
        g_tokens, s_qkv = closing_call(dq, dk, dv, d_first, xt, f_qkv)
    else:
        gw_qkv = jnp.concatenate([outer_call(xt, a, BF, 256) for a in (dq, dk, dv)], 1)
        s_qkv = lax.psum_scatter(gw_qkv, axes, scatter_dimension=0, tiled=True).astype(F32)
        g_tokens = tokens_call(dq, dk, dv, d_first, f_qkv).reshape(tokens.shape)
        out = out.reshape(tokens.shape)
    return (out, g_tokens, s_qkv, s_out, s_gate, s_up, s_down, s_gg[:, 0], s_gg[:, 1])


def solution(mesh):
    both = ("dp", "blk")
    return jax.shard_map(
        body,
        mesh=mesh,
        in_specs=(
            P("dp", "blk", None),
            P("dp"),
            P(both, None),
            P(both, None),
            P(both, None),
            P(both, None),
            P(both, None),
            P(both),
            P(both),
            P("dp", "blk", None),
        ),
        out_specs=(
            P("dp", "blk", None),
            P("dp", "blk", None),
            P(both, None),
            P(both, None),
            P("dp", "blk"),
            P("dp", "blk"),
            P("blk", "dp"),
            P(both),
            P(both),
        ),
        check_vma=False,
    )
```
